32 devices in a mesh: dp: 4 (over x, core), seq: 8 (over z, y).
Axes of the slice: x: 2, y: 2, z: 4, core: 2. Of those that a mesh axis runs over, the one named last changes fastest.
Arguments:
- tokens: bfloat16 [8, 1024, 768], P('dp', 'seq'), may hold values from -6 to 6
- segments: int32 [8, 1024], P('dp', 'seq'), may hold values from 0 to 5, never falling along the last dimension, each value on 1 to 512 neighbouring positions
- cotangent: bfloat16 [8, 1024, 768], P('dp', 'seq'), may hold values from -6 to 6
- w_qkv: bfloat16 [1769472], P(('dp', 'seq')), may hold values from -0.21875 to 0.21875
- w_out: bfloat16 [589824], P(('dp', 'seq')), may hold values from -1.75 to 1.75
- w_fc1: bfloat16 [2359296], P(('dp', 'seq')), may hold values from -0.21875 to 0.21875
- w_fc2: bfloat16 [2359296], P(('dp', 'seq')), may hold values from -0.109375 to 0.109375
- norm_gains: bfloat16 [1536], P(('dp', 'seq')), may hold values from 0.5 to 1.5
- bias_pack: bfloat16 [7680], P(('dp', 'seq')), may hold values from -0.59765625 to 0.59765625
Outputs:
- block_out: bfloat16 [8, 1024, 768], P('dp', 'seq')
- input_grad: float32 [8, 1024, 768], P('dp', 'seq')
- grad_qkv: float32 [1769472], P(('dp', 'seq'))
- grad_out: float32 [589824], P(('dp', 'seq'))
- grad_fc1: float32 [2359296], P(('dp', 'seq'))
- grad_fc2: float32 [2359296], P(('dp', 'seq'))
- grad_gains: float32 [1536], P(('dp', 'seq'))
- grad_biases: float32 [6144], P(('dp', 'seq'))
- grad_shift_value: float32 [1536], P(('dp', 'seq'))
The draws below stay inside these ranges and needn't reach their ends.
Inputs may be any that keep to these rules, and one draw needn't show every extreme that they name: `segments`: along each sequence the segment numbers never fall; a segment is 1 to 512 positions long, and some segment is exactly that long.
All inputs are finite; a program needn't handle non-finite values.
Results may differ from the reference program's by a relative error of at most 0.015.
Values may be sent and summed in bfloat16 or wider, within the bound.
No kernel may reach another device: no remote copies, remote signals or barrier semaphores. Data moves between devices by JAX's collectives and lax.ppermute only.
A program may use at most 256 MiB of HBM per device.

```python
import math
import jax
import jax.numpy as jnp
import numpy as np
from jax import lax

D = 768
FF = 3072
HEADS = 12
HEAD_DIM = 64
LENGTH = 1024
SEQS = 8


def level_of(stream_key, shape, split, least, high):
    level, own = 1.0, jax.random.fold_in(stream_key, 6)
    for position, shards_of in split:
        heights = jnp.exp(jax.random.uniform(jax.random.fold_in(own, position), (shards_of,), jnp.float32, least / len(split), high / len(split)))
        level = level * jnp.repeat(heights, shape[position] // shards_of).reshape([-1 if axis == position else 1 for axis in range(len(shape))])
    return level


def split_up(number_of, total, reach, skew):
    portions = [(1 << 20) // math.isqrt(standing ** skew) + 1 for standing in range(2, number_of + 1)]
    rest, holding = total - reach - (number_of - 1), [1] * (number_of - 1)
    while rest > 0:
        movable = [i for i in range(number_of - 1) if holding[i] < reach]
        whole, budget = sum([portions[i] for i in movable]), rest
        for i in movable:
            extra = min(reach - holding[i], max(1, budget * portions[i] // whole), rest)
            holding[i] = holding[i] + extra
            rest = rest - extra
    return np.array([reach] + holding)


def ragged_sizes(stream_key, number_of, total, limit, lean):
    if number_of == 2:
        one = jax.random.randint(stream_key, (), max(1, total - limit), min(limit, total - 1) + 1)
        return jnp.stack([one, total - one])
    lengths = jnp.asarray(split_up(number_of, total, limit, lean), jnp.int32)
    pairs = (number_of - 1) // 2
    source_of, receiver = lengths[1:1 + 2 * pairs:2], lengths[2:2 + 2 * pairs:2]
    margin = jnp.minimum(source_of - 1, limit - receiver)
    shifted = jax.random.randint(jax.random.fold_in(stream_key, 1), (pairs,), 0, 1 << 20) % (margin + 1)
    lengths = lengths.at[1:1 + 2 * pairs:2].set(source_of - shifted).at[2:2 + 2 * pairs:2].set(receiver + shifted)
    return lengths[jax.random.permutation(jax.random.fold_in(stream_key, 2), number_of)]


def gaussian(stream_key, dims, spread, most, shards=(), held_as=jnp.bfloat16):
    entries = jax.random.normal(stream_key, dims, jnp.float32) * spread
    if len(shards) > 0:
        entries = level_of(stream_key, dims, shards, -0.22, 0.18) * entries
    return jnp.clip(entries, min=-most, max=most).astype(held_as)


def setup_inputs(seed: int = 0) -> dict:
    streams_of = jax.random.split(jax.random.key(seed), 10)
    tokens = gaussian(streams_of[0], (SEQS, LENGTH, D), 1.0, 6.0, ((0, 4), (1, 8)))
    segments = jax.vmap(lambda own: jnp.searchsorted(jnp.cumsum(ragged_sizes(own, 6, LENGTH, LENGTH // 2, 1)), jnp.arange(LENGTH), side="right"))(jax.random.split(streams_of[1], SEQS)).reshape((SEQS, LENGTH)).astype(jnp.int32)
    cotangent = gaussian(streams_of[2], (SEQS, LENGTH, D), 1.0, 6.0, ((0, 4), (1, 8)))
    w_qkv = gaussian(streams_of[3], (3 * D * D,), D ** -0.5, 0.21875, ((0, 32),))
    w_out = gaussian(streams_of[4], (D * D,), (max(1, 16 * D // LENGTH)) ** -0.5, 1.75, ((0, 32),))
    w_fc1 = gaussian(streams_of[5], (D * FF,), D ** -0.5, 0.21875, ((0, 32),))
    w_fc2 = gaussian(streams_of[6], (FF * D,), FF ** -0.5, 0.109375, ((0, 32),))
    norm_gains = jnp.clip(1.0 + 0.1 * jax.random.normal(streams_of[7], (2 * D,), jnp.float32), 0.5, 1.5).astype(jnp.bfloat16)
    bias_pack = gaussian(streams_of[8], (6 * D + FF,), 0.1, 0.59765625, ((0, 32),))
    return {"tokens": tokens, "segments": segments, "cotangent": cotangent, "w_qkv": w_qkv, "w_out": w_out, "w_fc1": w_fc1, "w_fc2": w_fc2, "norm_gains": norm_gains, "bias_pack": bias_pack}


epsilon = 1e-05
masked_value = -1000000000.0
highest = lax.Precision.HIGHEST

@jax.custom_vjp
def low(v):
    return lax.optimization_barrier(v.astype(jnp.bfloat16)).astype(jnp.float32)

@jax.custom_vjp
def low_back(v):
    return v

def low_keep(v):
    return (low(v), None)

def low_pass(kept, grad):
    return (grad,)

def back_keep(v):
    return (v, None)

def back_low(kept, grad):
    return (low(grad),)
low.defvjp(low_keep, low_pass)
low_back.defvjp(back_keep, back_low)

def layer_norm(field, scale_vec, shift_vec):
    center = field - lax.optimization_barrier(jnp.mean(field, axis=-1, keepdims=True))
    inverse = lax.rsqrt(lax.optimization_barrier(jnp.mean(center * center, axis=-1, keepdims=True)) + epsilon)
    return center * inverse * scale_vec + shift_vec

def product(left, right):
    return jnp.matmul(left, right, precision=highest)

def attend(queries, keys, values, doc_ids):
    length = queries.shape[0]
    block_rows = min(512, length)
    blocks = length // block_rows

    def one_block(block_item):
        query_rows, query_docs = block_item
        scores = jnp.einsum('qhd,khd->hqk', query_rows, keys, precision=highest) * 0.125
        scores = low_back(scores)
        same = (query_docs[:, None] == doc_ids[None, :])[None]
        scores = jnp.where(same, scores, masked_value)
        row_max = lax.optimization_barrier(jnp.max(scores, axis=-1, keepdims=True))
        weights = jnp.exp(scores - row_max)
        weights = low(weights / lax.optimization_barrier(jnp.sum(weights, axis=-1, keepdims=True)))
        return jnp.einsum('hqk,khd->qhd', weights, values, precision=highest)
    results = lax.map(jax.checkpoint(one_block), (queries.reshape(blocks, block_rows, HEADS, HEAD_DIM), doc_ids.reshape(blocks, block_rows)))
    return results.reshape(length, HEADS * HEAD_DIM)

def forward(inputs, w_qkv, w_out, w_fc1, w_fc2, norm_gains, bias_pack, doc_ids):
    width = inputs.shape[-1]
    hidden = w_fc1.shape[0] // width
    shift_one = bias_pack[:width]
    shift_two = bias_pack[width:2 * width]
    bias_query = bias_pack[2 * width:3 * width]
    bias_value = bias_pack[3 * width:4 * width]
    bias_proj = bias_pack[4 * width:5 * width]
    bias_down = bias_pack[5 * width:6 * width]
    bias_up = bias_pack[6 * width:]
    normed = layer_norm(inputs, norm_gains[:width], shift_one)
    mixed = product(low(normed), w_qkv.reshape(width, 3 * width))
    mixed = mixed + jnp.concatenate([bias_query, jnp.zeros_like(bias_query), bias_value])
    mixed = low(low_back(mixed))
    queries = mixed[:, :width].reshape(-1, HEADS, HEAD_DIM)
    keys = mixed[:, width:2 * width].reshape(-1, HEADS, HEAD_DIM)
    values = mixed[:, 2 * width:].reshape(-1, HEADS, HEAD_DIM)
    attended = attend(queries, keys, values, doc_ids)
    branch = low_back(product(low(low_back(attended)), w_out.reshape(width, width)) + bias_proj)
    middle = inputs + branch
    normed_two = layer_norm(middle, norm_gains[width:], shift_two)
    pre_act = low_back(product(low(normed_two), w_fc1.reshape(width, hidden)) + bias_up)
    activ = low(pre_act * jax.nn.sigmoid(1.702 * pre_act))
    return middle + product(activ, w_fc2.reshape(hidden, width)) + bias_down

def reference(tokens, segments, cotangent, w_qkv, w_out, w_fc1, w_fc2, norm_gains, bias_pack):
    params = (w_qkv.astype(jnp.float32), w_out.astype(jnp.float32), w_fc1.astype(jnp.float32), w_fc2.astype(jnp.float32), norm_gains.astype(jnp.float32), bias_pack.astype(jnp.float32))

    def one_sequence(running, seq_item):
        inputs, doc_ids, seed_grad = seq_item

        def apply(field, qkv_w, out_w, up_w, down_w, gain_w, bias_w):
            return forward(field, qkv_w, out_w, up_w, down_w, gain_w, bias_w, doc_ids)
        result, pullback = jax.vjp(apply, inputs.astype(jnp.float32), params[0], params[1], params[2], params[3], params[4], params[5])
        gradients = pullback(seed_grad.astype(jnp.float32))
        updated = (running[0] + gradients[1], running[1] + gradients[2], running[2] + gradients[3], running[3] + gradients[4], running[4] + gradients[5], running[5] + gradients[6])
        return (updated, (result.astype(jnp.bfloat16), gradients[0]))
    start_grads = (jnp.zeros_like(params[0]), jnp.zeros_like(params[1]), jnp.zeros_like(params[2]), jnp.zeros_like(params[3]), jnp.zeros_like(params[4]), jnp.zeros_like(params[5]))
    totals, (results, input_grads) = lax.scan(one_sequence, start_grads, (tokens, segments, cotangent))
    bias_total = totals[5]
    rest_grads = jnp.concatenate([bias_total[D:3 * D], bias_total[4 * D:]])
    lead_grads = jnp.concatenate([bias_total[:D], bias_total[3 * D:4 * D]])
    return (results, input_grads, totals[0], totals[1], totals[2], totals[3], totals[4], rest_grads, lead_grads)
```

```python
import functools
import itertools

import jax
import jax.numpy as jnp
import numpy as np
from jax import lax
from jax.experimental import pallas as pl
from jax.experimental.pallas import tpu as pltpu
from jax.sharding import Mesh
from jax.sharding import PartitionSpec as P

D = 768
FF = 3072
HEADS = 12
HEAD_DIM = 64
EPS = 1e-05
MASKED = -1000000000.0
BF = jnp.bfloat16
F32 = jnp.float32
AXES = ("x", "c", "zh", "zl", "yh", "yl")


class Net:
    def __init__(self, dims):
        self.dims = dims
        self.x, self.c, self.zh, self.zl, self.yh, self.yl = dims
        self.z, self.y = self.zh * self.zl, self.yh * self.yl
        self.chips = self.x * self.z * self.y
        bits = lambda axis, n: [(axis, 1 << b) for b in reversed(range(n.bit_length() - 1))]
        zs, xs, ys = bits("z", self.z), bits("x", self.x), bits("y", self.y)
        self.orders = (zs + xs + ys, zs + ys + xs)
        self.stages = len(self.orders[0])

    def perm(self, move):
        pairs = []
        for at in itertools.product(*(range(n) for n in self.dims)):
            to = move(*at)
            pairs.append(
                (int(np.ravel_multi_index(at, self.dims)), int(np.ravel_multi_index(to, self.dims)))
            )
        return pairs

    def flip(self, stage):
        def move(x, c, zh, zl, yh, yl):
            axis, bit = self.orders[c][stage]
            z, y = zh * self.zl + zl, yh * self.yl + yl
            if axis == "x":
                x ^= bit
            elif axis == "y":
                y ^= bit
            else:
                z ^= bit
            return (x, c, z // self.zl, z % self.zl, y // self.yl, y % self.yl)

        return self.perm(move)

    def across(self, value, stage):
        return lax.ppermute(value, AXES, self.flip(stage))

    def core(self, value):
        return lax.ppermute(value, "c", [(0, 1), (1, 0)])

    def pair(self, value):
        return lax.ppermute(value, "yl", [(0, 1), (1, 0)])

    def scatter_move(self, k):
        return self.perm(
            lambda x, c, zh, zl, yh, yl: (x, zh >> 1, 2 * c + (k ^ (zh & 1)), zl, yh, yl)
        )

    def table(self):
        me = {
            "x": lax.axis_index("x"),
            "z": lax.axis_index("zh") * self.zl + lax.axis_index("zl"),
            "y": lax.axis_index("yh") * self.yl + lax.axis_index("yl"),
        }
        grid = np.indices((self.x, self.z, self.y)).reshape(3, -1)
        axes = {"x": grid[0], "z": grid[1], "y": grid[2]}
        places = []
        for order in self.orders:
            place = jnp.zeros((self.chips,), jnp.int32)
            for stage, (axis, bit) in enumerate(order):
                differs = (jnp.asarray(axes[axis], jnp.int32) ^ me[axis]) & bit
                place = place + jnp.where(differs != 0, 1 << stage, 0)
            places.append(place)
        return jnp.where(lax.axis_index("c") == 0, places[0], places[1]).astype(jnp.int32)

    def gather(self, block):
        held = block[None]
        for stage in range(self.stages):
            held = jnp.concatenate([held, self.across(held, stage)])
        return held

    def scatter(self, held):
        for stage in reversed(range(self.stages)):
            half = held.shape[0] // 2
            got = self.across(held[half:], stage)
            held = held[:half].astype(F32) + got.astype(F32)
            if stage:
                held = held.astype(BF)
        return held[0]


def move_kernel(to_place, table, source, target, sems):
    copies = []
    for chip in range(source.shape[0]):
        place = table[chip]
        ends = (
            (source.at[chip], target.at[place])
            if to_place
            else (source.at[place], target.at[chip])
        )
        copies.append(pltpu.make_async_copy(*ends, sems.at[chip]))
    for copy in copies:
        copy.start()
    for copy in copies:
        copy.wait()


def reorder(blocks, table, to_place):
    rest = -blocks.shape[1] % 16
    if rest:
        rows = blocks.shape[1]
        blocks = jnp.pad(blocks, ((0, 0), (0, rest), (0, 0)))
        return reorder(blocks, table, to_place)[:, :rows]
    return pl.pallas_call(
        functools.partial(move_kernel, to_place),
        grid_spec=pltpu.PrefetchScalarGridSpec(
            num_scalar_prefetch=1,
            grid=(),
            in_specs=[pl.BlockSpec(memory_space=pl.ANY)],
            out_specs=pl.BlockSpec(memory_space=pl.ANY),
            scratch_shapes=[pltpu.SemaphoreType.DMA((blocks.shape[0],))],
        ),
        out_shape=jax.ShapeDtypeStruct(blocks.shape, blocks.dtype),
    )(table, blocks)


def normal(field):
    center = field - jnp.mean(field, axis=-1, keepdims=True)
    inverse = lax.rsqrt(jnp.mean(center * center, axis=-1, keepdims=True) + EPS)
    return center * inverse, inverse


def norm_back(upstream, unit, inverse, gain):
    scaled = upstream * gain
    return inverse * (
        scaled
        - jnp.mean(scaled, axis=-1, keepdims=True)
        - unit * jnp.mean(scaled * unit, axis=-1, keepdims=True)
    )


def dot(a, b):
    return jnp.dot(a, b, preferred_element_type=F32)


def dot_t(a, b):
    return lax.dot_general(a, b, (((1,), (1,)), ((), ())), preferred_element_type=F32)


def t_dot(a, b):
    return lax.dot_general(a, b, (((0,), (0,)), ((), ())), preferred_element_type=F32)


def fold(wide, parts):
    lead, rows, cols = wide.shape[:-2], wide.shape[-2], wide.shape[-1] // parts
    moved = jnp.moveaxis(wide.reshape(*lead, rows, parts, cols), -2, -3)
    return moved.reshape(*lead, parts * rows, cols)


def unfold(tall, parts):
    lead, rows, cols = tall.shape[:-2], tall.shape[-2] // parts, tall.shape[-1]
    moved = jnp.moveaxis(tall.reshape(*lead, parts, rows, cols), -3, -2)
    return moved.reshape(*lead, rows, parts * cols)


def body(net, tokens, segments, cotangent, w_qkv, w_out, w_fc1, w_fc2, norm_gains, bias_pack):
    local, cols, width = tokens.shape
    own = local * cols
    mine = 2 * own
    hidden = FF
    half_w, half_f = width // 2, hidden // 2
    devices = 2 * net.chips
    core = lax.axis_index("c")
    zodd = lax.axis_index("zh") & 1
    table = net.table()
    rows = width // devices
    frows = hidden // devices
    aligned = (width // (2 * net.x)) % HEAD_DIM == 0
    groups = net.x if aligned else 1

    def pick(array, parts, which):
        split = array.reshape(*array.shape[:-1], parts, 2, array.shape[-1] // (2 * parts))
        taken = jnp.where(which == 0, split[..., 0, :], split[..., 1, :])
        return taken.reshape(*array.shape[:-1], array.shape[-1] // 2)

    def spread(vector, parts):
        split = vector.reshape(parts, 1, vector.shape[-1] // parts)
        both = jnp.concatenate(
            [jnp.where(core == 0, split, 0.0), jnp.where(core == 1, split, 0.0)], axis=1
        )
        return both.reshape(-1)

    seg_row = jnp.pad(segments.astype(BF), ((0, 0), (0, width - cols)))[:, None, :]
    seg_rows = jnp.pad(seg_row, ((0, 0), (0, 7), (0, 0)))
    packed = jnp.concatenate([tokens, seg_rows], axis=1)

    def to_sequence(array):
        swapped = jnp.where(zodd == 0, array, array[::-1])
        return jnp.stack(
            [lax.ppermute(swapped[k], AXES, net.scatter_move(k)) for k in range(2)]
        )

    def from_sequence(array):
        back = jnp.stack(
            [
                lax.ppermute(array[k], AXES, [(b, a) for a, b in net.scatter_move(k)])
                for k in range(2)
            ]
        )
        return jnp.where(zodd == 0, back, back[::-1])

    def halves(which):
        qkv = fold(w_qkv.reshape(rows, 3 * width), 3).reshape(3, rows, width)
        up = w_fc1.reshape(rows, hidden)
        return pick(qkv, groups, which), pick(up, net.x, which)

    keep_qkv, keep_up = halves(core)
    give_qkv, give_up = halves(1 - core)
    small = jnp.concatenate([norm_gains, bias_pack])
    out_rows = w_out.reshape(rows, width)
    got_qkv, got_up, got_small, got_out = jax.tree.map(
        net.core, (give_qkv, give_up, small, out_rows)
    )

    def both(a, b, axis):
        return jnp.where(
            core == 0, jnp.concatenate([a, b], axis=axis), jnp.concatenate([b, a], axis=axis)
        )

    chip_qkv = both(keep_qkv, got_qkv, 1).reshape(6 * rows, half_w)
    chip_up = fold(both(keep_up, got_up, 0), 2)
    chip_out = fold(out_rows if aligned else both(out_rows, got_out, 0), 2)
    chip_small = jnp.pad(
        both(small[None], got_small[None], 0), ((0, 14), (0, half_w - small.shape[0]))
    )
    cut = np.cumsum([chip_qkv.shape[0], chip_out.shape[0]])
    blocks_a = reorder(
        net.gather(jnp.concatenate([chip_qkv, chip_out, chip_small])), table, False
    )
    blocks_up = reorder(net.gather(chip_up), table, False)
    blocks_down = reorder(net.gather(w_fc2.reshape(frows, width)), table, False)

    lead = (net.x, net.z, net.y)

    def natural(blocks):
        n = blocks.shape[-1]
        return jnp.moveaxis(blocks.reshape(*lead, 2, -1, n), 3, 1).reshape(-1, n)

    def by_chip(array):
        n = array.shape[-1]
        return jnp.moveaxis(array.reshape(net.x, 2, net.z, net.y, -1, n), 1, 3).reshape(
            net.chips, -1, n
        )

    qkv_blocks = blocks_a[:, : cut[0]].reshape(net.chips, 3, 2 * rows, half_w)
    w_q, w_k, w_v = (natural(qkv_blocks[:, i]) for i in range(3))
    out_blocks = unfold(blocks_a[:, cut[0] : cut[1]], 2)
    if aligned:
        w_proj = out_blocks.reshape(half_w, width)
    else:
        w_proj = lax.dynamic_slice_in_dim(natural(out_blocks), core * half_w, half_w)
    smalls = blocks_a[:, cut[1] : cut[1] + 2, : small.shape[0]].reshape(*lead, 2, -1)
    smalls = jnp.moveaxis(smalls, 3, 1).reshape(devices, -1).astype(F32)
    n_gain = norm_gains.shape[0]
    gains = smalls[:, :n_gain].reshape(-1)
    shifts = smalls[:, n_gain:].reshape(-1)
    w_up = natural(unfold(blocks_up, 2))
    w_down = blocks_down.reshape(half_f, width)
    gain1, gain2 = gains[:width], gains[width:]
    shift1, shift2, bias_q, bias_v, bias_proj, bias_down = (
        shifts[i * width : (i + 1) * width] for i in range(6)
    )
    bias_up = pick(shifts[6 * width :], net.x, core)
    bias_q, bias_v = pick(bias_q, groups, core), pick(bias_v, groups, core)

    x_own = to_sequence(packed)
    x_other = net.core(x_own)
    x_mine = jnp.concatenate([x_own, x_other])
    near = net.pair(x_own)
    near = jnp.concatenate([near, net.core(near)])
    x_seq = jnp.concatenate([x_mine, near])
    if net.zl * net.yh > 1:
        x_far = lax.all_gather(x_seq, ("zl", "yh"), axis=0, tiled=True)
        x_keys = x_far
    else:
        x_keys = x_seq
    g_own = to_sequence(cotangent)
    g_mine = jnp.concatenate([g_own, net.core(g_own)]).reshape(mine, width)
    docs = x_keys[:, cols, :cols].reshape(-1)
    query_docs = x_mine[:, cols, :cols].reshape(-1)
    x_all = x_keys[:, :cols].reshape(-1, width).astype(F32)
    x_q = x_mine[:, :cols].reshape(-1, width).astype(F32)

    unit_q, inverse_q = normal(x_q)
    a_q = (unit_q * gain1 + shift1).astype(BF)
    unit_all, _ = normal(x_all)
    a_all = (unit_all * gain1 + shift1).astype(BF)
    heads = HEADS // 2
    q = (dot(a_q, w_q) + bias_q).astype(BF)
    k = dot(a_all, w_k).astype(BF)
    v = (dot(a_all, w_v) + bias_v).astype(BF)
    by_head = lambda t: t.reshape(-1, heads, HEAD_DIM)
    same = (query_docs[:, None] == docs[None, :])[None]
    scores = (
        jnp.einsum("qhd,khd->hqk", by_head(q), by_head(k), preferred_element_type=F32) * 0.125
    )
    scores = jnp.where(same, scores, MASKED)
    weights = jnp.exp(scores - jnp.max(scores, axis=-1, keepdims=True))
    probs = weights / jnp.sum(weights, axis=-1, keepdims=True)
    probs_low = probs.astype(BF)
    att = jnp.einsum("hqk,khd->qhd", probs_low, by_head(v), preferred_element_type=F32)
    att = att.reshape(mine, half_w)
    att_low = att.astype(BF)

    def core_sum(partial):
        low = partial.astype(BF)
        got = net.core(low)
        return low.astype(F32) + jnp.concatenate([got[own:], got[:own]]).astype(F32)

    middle = x_q + core_sum(dot(att_low, w_proj)) + bias_proj
    unit2, inverse2 = normal(middle)
    a2 = (unit2 * gain2 + shift2).astype(BF)
    pre = dot(a2, w_up) + bias_up
    sig = jax.nn.sigmoid(1.702 * pre)
    activ = (pre * sig).astype(BF)
    down = dot(activ, w_down)
    down_got = net.core(down[own:].astype(BF)).astype(F32)
    out_own = (middle[:own] + down[:own] + down_got + bias_down).astype(BF)
    block_out = from_sequence(out_own.reshape(local, cols, width))

    grad_down = t_dot(activ, g_mine).astype(BF)
    grad_pre = (dot_t(g_mine, w_down) * (sig + 1.702 * pre * sig * (1.0 - sig))).astype(BF)
    shard_down = net.scatter(reorder(grad_down.reshape(net.chips, frows, width), table, True))
    grad_up = t_dot(a2, grad_pre).astype(BF)
    shard_up = net.scatter(reorder(fold(by_chip(grad_up), 2), table, True))
    e2 = core_sum(dot_t(grad_pre, w_up))
    grad_middle = g_mine.astype(F32) + norm_back(e2, unit2, inverse2, gain2)
    branch = grad_middle.astype(BF)
    grad_proj = t_dot(att_low, branch).astype(BF)
    d_heads = dot_t(branch, w_proj).astype(BF)
    dp = jnp.einsum("qhd,khd->hqk", by_head(d_heads), by_head(v), preferred_element_type=F32)
    delta = jnp.sum(probs * dp, axis=-1, keepdims=True)
    d_scores = (probs * (dp - delta)).astype(BF)
    dq = 0.125 * jnp.einsum("hqk,khd->qhd", d_scores, by_head(k), preferred_element_type=F32)
    dk = 0.125 * jnp.einsum("hqk,qhd->khd", d_scores, by_head(q), preferred_element_type=F32)
    dv = jnp.einsum("hqk,qhd->khd", probs_low, by_head(d_heads), preferred_element_type=F32)
    dq = dq.reshape(-1, half_w).astype(BF)
    dk = dk.reshape(-1, half_w).astype(BF)
    dv = dv.reshape(-1, half_w).astype(BF)
    grad_qkv = jnp.stack([t_dot(a_q, dq), t_dot(a_all, dk), t_dot(a_all, dv)]).astype(BF)

    e1_keys = (dot_t(dk, w_k) + dot_t(dv, w_v)).astype(BF)
    if net.zl * net.yh > 1:
        e1_keys = lax.psum_scatter(
            e1_keys, ("zl", "yh"), scatter_dimension=0, tiled=True
        )
    e1_near = e1_keys[mine:].reshape(2, own, width)
    e1_mine = e1_keys[:mine].astype(F32) + dot_t(dq, w_q)
    e1_mine = e1_mine.astype(BF).reshape(2, own, width)
    got = net.core(jnp.stack([e1_mine[1], e1_near[1]]))
    e1_near = e1_near[0].astype(F32) + got[1].astype(F32)
    e1 = e1_mine[0].astype(F32) + got[0].astype(F32) + net.pair(e1_near.astype(BF)).astype(F32)
    unit1 = unit_q[:own]
    in_own = grad_middle[:own] + norm_back(e1, unit1, inverse_q[:own], gain1)
    input_grad = from_sequence(in_own.astype(BF).reshape(local, cols, width)).astype(F32)

    total = lambda array: jnp.sum(array.astype(F32), axis=0)
    g_own = g_mine[:own]
    gain_sums = jnp.concatenate([total(e1 * unit1), total(e2[:own] * unit2[:own])])
    bias_sums = jnp.concatenate(
        [
            total(e2[:own]),
            spread(total(dq), groups),
            total(branch[:own]),
            total(g_own),
            spread(total(grad_pre), net.x),
        ]
    )
    lead_sums = jnp.concatenate([total(e1), spread(total(dv), groups)])
    sums = jnp.concatenate(
        [v.reshape(devices, -1) for v in (gain_sums, bias_sums, lead_sums)], axis=1
    )
    sums = sums + net.core(sums)
    sums = jnp.moveaxis(sums.reshape(net.x, 2, net.z, net.y, -1), 1, 0)
    sums = jnp.where(core == 0, sums[0], sums[1]).reshape(net.chips, 1, -1)
    n_sums = sums.shape[-1]
    sums = jnp.pad(sums, ((0, 0), (0, 15), (0, half_w - n_sums))).astype(BF)
    qkv_send = jnp.stack([by_chip(grad_qkv[i]) for i in range(3)], axis=1)
    qkv_send = qkv_send.reshape(net.chips, 6 * rows, half_w)
    if aligned:
        out_send = grad_proj.reshape(net.chips, rows, width)
    else:
        whole = jnp.zeros((width, width), BF)
        whole = lax.dynamic_update_slice(whole, grad_proj, (core * half_w, 0))
        out_send = by_chip(whole)
    sent = jnp.concatenate([qkv_send, fold(out_send, 2), sums], axis=1)
    shard_a = net.scatter(reorder(sent, table, True))

    def own_rows(chip):
        keep = jnp.where(core == 0, chip[..., 0, :, :], chip[..., 1, :, :])
        give = jnp.where(core == 0, chip[..., 1, :, :], chip[..., 0, :, :])
        return keep, net.core(give)

    def merge(keep, got, parts):
        split = lambda array: array.reshape(*array.shape[:-1], parts, 1, -1)
        first = jnp.where(core == 0, split(keep), split(got))
        second = jnp.where(core == 0, split(got), split(keep))
        return jnp.concatenate([first, second], axis=-2).reshape(*keep.shape[:-1], -1)

    qkv_own = merge(*own_rows(shard_a[: cut[0]].reshape(3, 2, rows, half_w)), groups)
    g_qkv = jnp.moveaxis(qkv_own, 0, 1).reshape(-1)
    out_own = unfold(shard_a[cut[0] : cut[1]], 2)
    if not aligned:
        keep, got = own_rows(out_own.reshape(2, rows, width))
        out_own = keep + got
    g_out = out_own.reshape(-1)
    up_own = merge(*own_rows(unfold(shard_up, 2).reshape(2, rows, half_f)), net.x)
    own_sums = shard_a[cut[1], :n_sums]
    n_gain = 2 * width // devices
    n_lead = n_sums - n_gain
    return (
        block_out,
        input_grad,
        g_qkv,
        g_out,
        up_own.reshape(-1),
        shard_down.reshape(-1),
        own_sums[:n_gain],
        own_sums[n_gain:n_lead],
        own_sums[n_lead:],
    )


def solution(mesh):
    dp, seq = mesh.shape["dp"], mesh.shape["seq"]
    y = 1 << (((seq.bit_length() - 1) - 1) // 2)
    z = seq // y
    dims = (dp // 2, 2, 4, z // 4, y // 2, 2)
    net = Net(dims)
    inner = Mesh(mesh.devices.reshape(dims), AXES)
    place = ("zh", "zl", "yh", "yl")
    cube = P(("x", "c"), place, None)
    flat = P(AXES)
    return jax.shard_map(
        functools.partial(body, net),
        mesh=inner,
        in_specs=(cube, P(("x", "c"), place), cube) + (flat,) * 6,
        out_specs=(cube, cube) + (flat,) * 7,
        check_vma=False,
    )
```

```python
import functools
import itertools

import jax
import jax.numpy as jnp
import numpy as np
from jax import lax
from jax.experimental import pallas as pl
from jax.experimental.pallas import tpu as pltpu
from jax.sharding import Mesh
from jax.sharding import PartitionSpec as P

D = 768
FF = 3072
HEADS = 12
HEAD_DIM = 64
EPS = 1e-05
MASKED = -1000000000.0
BF = jnp.bfloat16
F32 = jnp.float32
AXES = ("x", "c", "zh", "zl", "yh", "yl")


class Net:
    def __init__(self, dims):
        self.dims = dims
        self.x, self.c, self.zh, self.zl, self.yh, self.yl = dims
        self.z, self.y = self.zh * self.zl, self.yh * self.yl
        self.chips = self.x * self.z * self.y
        bits = lambda axis, n: [(axis, 1 << b) for b in reversed(range(n.bit_length() - 1))]
        zs, xs, ys = bits("z", self.z), bits("x", self.x), bits("y", self.y)
        self.orders = (zs + xs + ys, zs + ys + xs)
        self.stages = len(self.orders[0])

    def perm(self, move):
        pairs = []
        for at in itertools.product(*(range(n) for n in self.dims)):
            to = move(*at)
            pairs.append(
                (int(np.ravel_multi_index(at, self.dims)), int(np.ravel_multi_index(to, self.dims)))
            )
        return pairs

    def flip(self, stage):
        def move(x, c, zh, zl, yh, yl):
            axis, bit = self.orders[c][stage]
            z, y = zh * self.zl + zl, yh * self.yl + yl
            if axis == "x":
                x ^= bit
            elif axis == "y":
                y ^= bit
            else:
                z ^= bit
            return (x, c, z // self.zl, z % self.zl, y // self.yl, y % self.yl)

        return self.perm(move)

    def across(self, value, stage):
        return lax.ppermute(value, AXES, self.flip(stage))

    def core(self, value):
        return lax.ppermute(value, "c", [(0, 1), (1, 0)])

    def pair(self, value):
        return lax.ppermute(value, "yl", [(0, 1), (1, 0)])

    def scatter_move(self, k):
        return self.perm(
            lambda x, c, zh, zl, yh, yl: (x, zh >> 1, 2 * c + (k ^ (zh & 1)), zl, yh, yl)
        )

    def table(self):
        me = {
            "x": lax.axis_index("x"),
            "z": lax.axis_index("zh") * self.zl + lax.axis_index("zl"),
            "y": lax.axis_index("yh") * self.yl + lax.axis_index("yl"),
        }
        grid = np.indices((self.x, self.z, self.y)).reshape(3, -1)
        axes = {"x": grid[0], "z": grid[1], "y": grid[2]}
        places = []
        for order in self.orders:
            place = jnp.zeros((self.chips,), jnp.int32)
            for stage, (axis, bit) in enumerate(order):
                differs = (jnp.asarray(axes[axis], jnp.int32) ^ me[axis]) & bit
                place = place + jnp.where(differs != 0, 1 << stage, 0)
            places.append(place)
        return jnp.where(lax.axis_index("c") == 0, places[0], places[1]).astype(jnp.int32)

    def gather(self, block):
        held = block[None]
        for stage in range(self.stages):
            held = jnp.concatenate([held, self.across(held, stage)])
        return held

    def scatter(self, held):
        for stage in reversed(range(self.stages)):
            half = held.shape[0] // 2
            got = self.across(held[half:], stage)
            held = held[:half].astype(F32) + got.astype(F32)
            if stage:
                held = held.astype(BF)
        return held[0]


def move_kernel(table, source, target):
    target[...] = source[...]


def reorder(blocks, table, to_place):
    rest = -blocks.shape[1] % 16
    if rest:
        rows = blocks.shape[1]
        blocks = jnp.pad(blocks, ((0, 0), (0, rest), (0, 0)))
        return reorder(blocks, table, to_place)[:, :rows]
    chips, rows, cols = blocks.shape
    here = pl.BlockSpec((1, rows, cols), lambda chip, table: (chip, 0, 0))
    there = pl.BlockSpec((1, rows, cols), lambda chip, table: (table[chip], 0, 0))
    return pl.pallas_call(
        move_kernel,
        grid_spec=pltpu.PrefetchScalarGridSpec(
            num_scalar_prefetch=1,
            grid=(chips,),
            in_specs=[here if to_place else there],
            out_specs=there if to_place else here,
        ),
        out_shape=jax.ShapeDtypeStruct(blocks.shape, blocks.dtype),
    )(table, blocks)


def normal(field):
    center = field - jnp.mean(field, axis=-1, keepdims=True)
    inverse = lax.rsqrt(jnp.mean(center * center, axis=-1, keepdims=True) + EPS)
    return center * inverse, inverse


def norm_back(upstream, unit, inverse, gain):
    scaled = upstream * gain
    return inverse * (
        scaled
        - jnp.mean(scaled, axis=-1, keepdims=True)
        - unit * jnp.mean(scaled * unit, axis=-1, keepdims=True)
    )


def dot(a, b):
    return jnp.dot(a, b, preferred_element_type=F32)


def dot_t(a, b):
    return lax.dot_general(a, b, (((1,), (1,)), ((), ())), preferred_element_type=F32)


def t_dot(a, b):
    return lax.dot_general(a, b, (((0,), (0,)), ((), ())), preferred_element_type=F32)


def fold(wide, parts):
    lead, rows, cols = wide.shape[:-2], wide.shape[-2], wide.shape[-1] // parts
    moved = jnp.moveaxis(wide.reshape(*lead, rows, parts, cols), -2, -3)
    return moved.reshape(*lead, parts * rows, cols)


def unfold(tall, parts):
    lead, rows, cols = tall.shape[:-2], tall.shape[-2] // parts, tall.shape[-1]
    moved = jnp.moveaxis(tall.reshape(*lead, parts, rows, cols), -3, -2)
    return moved.reshape(*lead, rows, parts * cols)


def body(net, tokens, segments, cotangent, w_qkv, w_out, w_fc1, w_fc2, norm_gains, bias_pack):
    local, cols, width = tokens.shape
    own = local * cols
    mine = 2 * own
    hidden = FF
    half_w, half_f = width // 2, hidden // 2
    devices = 2 * net.chips
    core = lax.axis_index("c")
    zodd = lax.axis_index("zh") & 1
    table = net.table()
    rows = width // devices
    frows = hidden // devices
    aligned = (width // (2 * net.x)) % HEAD_DIM == 0
    groups = net.x if aligned else 1

    def pick(array, parts, which):
        split = array.reshape(*array.shape[:-1], parts, 2, array.shape[-1] // (2 * parts))
        taken = jnp.where(which == 0, split[..., 0, :], split[..., 1, :])
        return taken.reshape(*array.shape[:-1], array.shape[-1] // 2)

    def spread(vector, parts):
        split = vector.reshape(parts, 1, vector.shape[-1] // parts)
        both = jnp.concatenate(
            [jnp.where(core == 0, split, 0.0), jnp.where(core == 1, split, 0.0)], axis=1
        )
        return both.reshape(-1)

    seg_row = jnp.pad(segments.astype(BF), ((0, 0), (0, width - cols)))[:, None, :]
    seg_rows = jnp.pad(seg_row, ((0, 0), (0, 7), (0, 0)))
    packed = jnp.concatenate([tokens, seg_rows], axis=1)

    def to_sequence(array):
        swapped = jnp.where(zodd == 0, array, array[::-1])
        return jnp.stack(
            [lax.ppermute(swapped[k], AXES, net.scatter_move(k)) for k in range(2)]
        )

    def from_sequence(array):
        back = jnp.stack(
            [
                lax.ppermute(array[k], AXES, [(b, a) for a, b in net.scatter_move(k)])
                for k in range(2)
            ]
        )
        return jnp.where(zodd == 0, back, back[::-1])

    def halves(which):
        qkv = fold(w_qkv.reshape(rows, 3 * width), 3).reshape(3, rows, width)
        up = w_fc1.reshape(rows, hidden)
        return pick(qkv, groups, which), pick(up, net.x, which)

    keep_qkv, keep_up = halves(core)
    give_qkv, give_up = halves(1 - core)
    small = jnp.concatenate([norm_gains, bias_pack])
    out_rows = w_out.reshape(rows, width)
    got_qkv, got_up, got_small, got_out = jax.tree.map(
        net.core, (give_qkv, give_up, small, out_rows)
    )

    def both(a, b, axis):
        return jnp.where(
            core == 0, jnp.concatenate([a, b], axis=axis), jnp.concatenate([b, a], axis=axis)
        )

    chip_qkv = both(keep_qkv, got_qkv, 1).reshape(6 * rows, half_w)
    chip_up = fold(both(keep_up, got_up, 0), 2)
    chip_out = fold(out_rows if aligned else both(out_rows, got_out, 0), 2)
    chip_small = jnp.pad(
        both(small[None], got_small[None], 0), ((0, 14), (0, half_w - small.shape[0]))
    )
    cut = np.cumsum([chip_qkv.shape[0], chip_out.shape[0]])
    blocks_a = reorder(
        net.gather(jnp.concatenate([chip_qkv, chip_out, chip_small])), table, False
    )
    blocks_up = reorder(net.gather(chip_up), table, False)
    blocks_down = reorder(net.gather(w_fc2.reshape(frows, width)), table, False)

    lead = (net.x, net.z, net.y)

    def natural(blocks):
        n = blocks.shape[-1]
        return jnp.moveaxis(blocks.reshape(*lead, 2, -1, n), 3, 1).reshape(-1, n)

    def by_chip(array):
        n = array.shape[-1]
        return jnp.moveaxis(array.reshape(net.x, 2, net.z, net.y, -1, n), 1, 3).reshape(
            net.chips, -1, n
        )

    qkv_blocks = blocks_a[:, : cut[0]].reshape(net.chips, 3, 2 * rows, half_w)
    w_q, w_k, w_v = (natural(qkv_blocks[:, i]) for i in range(3))
    out_blocks = unfold(blocks_a[:, cut[0] : cut[1]], 2)
    if aligned:
        w_proj = out_blocks.reshape(half_w, width)
    else:
        w_proj = lax.dynamic_slice_in_dim(natural(out_blocks), core * half_w, half_w)
    smalls = blocks_a[:, cut[1] : cut[1] + 2, : small.shape[0]].reshape(*lead, 2, -1)
    smalls = jnp.moveaxis(smalls, 3, 1).reshape(devices, -1).astype(F32)
    n_gain = norm_gains.shape[0]
    gains = smalls[:, :n_gain].reshape(-1)
    shifts = smalls[:, n_gain:].reshape(-1)
    w_up = natural(unfold(blocks_up, 2))
    w_down = blocks_down.reshape(half_f, width)
    gain1, gain2 = gains[:width], gains[width:]
    shift1, shift2, bias_q, bias_v, bias_proj, bias_down = (
        shifts[i * width : (i + 1) * width] for i in range(6)
    )
    bias_up = pick(shifts[6 * width :], net.x, core)
    bias_q, bias_v = pick(bias_q, groups, core), pick(bias_v, groups, core)

    x_own = to_sequence(packed)
    x_other = net.core(x_own)
    x_mine = jnp.concatenate([x_own, x_other])
    near = net.pair(x_own)
    near = jnp.concatenate([near, net.core(near)])
    x_seq = jnp.concatenate([x_mine, near])
    if net.zl * net.yh > 1:
        x_far = lax.all_gather(x_seq, ("zl", "yh"), axis=0, tiled=True)
        x_keys = x_far
    else:
        x_keys = x_seq
    g_own = to_sequence(cotangent)
    g_mine = jnp.concatenate([g_own, net.core(g_own)]).reshape(mine, width)
    docs = x_keys[:, cols, :cols].reshape(-1)
    query_docs = x_mine[:, cols, :cols].reshape(-1)
    x_all = x_keys[:, :cols].reshape(-1, width).astype(F32)
    x_q = x_mine[:, :cols].reshape(-1, width).astype(F32)

    unit_q, inverse_q = normal(x_q)
    a_q = (unit_q * gain1 + shift1).astype(BF)
    unit_all, _ = normal(x_all)
    a_all = (unit_all * gain1 + shift1).astype(BF)
    heads = HEADS // 2
    q = (dot(a_q, w_q) + bias_q).astype(BF)
    k = dot(a_all, w_k).astype(BF)
    v = (dot(a_all, w_v) + bias_v).astype(BF)
    by_head = lambda t: t.reshape(-1, heads, HEAD_DIM)
    same = (query_docs[:, None] == docs[None, :])[None]
    scores = (
        jnp.einsum("qhd,khd->hqk", by_head(q), by_head(k), preferred_element_type=F32) * 0.125
    )
    scores = jnp.where(same, scores, MASKED)
    weights = jnp.exp(scores - jnp.max(scores, axis=-1, keepdims=True))
    probs = weights / jnp.sum(weights, axis=-1, keepdims=True)
    probs_low = probs.astype(BF)
    att = jnp.einsum("hqk,khd->qhd", probs_low, by_head(v), preferred_element_type=F32)
    att = att.reshape(mine, half_w)
    att_low = att.astype(BF)

    def core_sum(partial):
        low = partial.astype(BF)
        got = net.core(low)
        return low.astype(F32) + jnp.concatenate([got[own:], got[:own]]).astype(F32)

    middle = x_q + core_sum(dot(att_low, w_proj)) + bias_proj
    unit2, inverse2 = normal(middle)
    a2 = (unit2 * gain2 + shift2).astype(BF)
    pre = dot(a2, w_up) + bias_up
    sig = jax.nn.sigmoid(1.702 * pre)
    activ = (pre * sig).astype(BF)
    down = dot(activ, w_down)
    down_got = net.core(down[own:].astype(BF)).astype(F32)
    out_own = (middle[:own] + down[:own] + down_got + bias_down).astype(BF)
    block_out = from_sequence(out_own.reshape(local, cols, width))

    grad_down = t_dot(activ, g_mine).astype(BF)
    grad_pre = (dot_t(g_mine, w_down) * (sig + 1.702 * pre * sig * (1.0 - sig))).astype(BF)
    shard_down = net.scatter(reorder(grad_down.reshape(net.chips, frows, width), table, True))
    grad_up = t_dot(a2, grad_pre).astype(BF)
    shard_up = net.scatter(reorder(fold(by_chip(grad_up), 2), table, True))
    e2 = core_sum(dot_t(grad_pre, w_up))
    grad_middle = g_mine.astype(F32) + norm_back(e2, unit2, inverse2, gain2)
    branch = grad_middle.astype(BF)
    grad_proj = t_dot(att_low, branch).astype(BF)
    d_heads = dot_t(branch, w_proj).astype(BF)
    dp = jnp.einsum("qhd,khd->hqk", by_head(d_heads), by_head(v), preferred_element_type=F32)
    delta = jnp.sum(probs * dp, axis=-1, keepdims=True)
    d_scores = (probs * (dp - delta)).astype(BF)
    dq = 0.125 * jnp.einsum("hqk,khd->qhd", d_scores, by_head(k), preferred_element_type=F32)
    dk = 0.125 * jnp.einsum("hqk,qhd->khd", d_scores, by_head(q), preferred_element_type=F32)
    dv = jnp.einsum("hqk,qhd->khd", probs_low, by_head(d_heads), preferred_element_type=F32)
    dq = dq.reshape(-1, half_w).astype(BF)
    dk = dk.reshape(-1, half_w).astype(BF)
    dv = dv.reshape(-1, half_w).astype(BF)
    grad_qkv = jnp.stack([t_dot(a_q, dq), t_dot(a_all, dk), t_dot(a_all, dv)]).astype(BF)

    e1_keys = (dot_t(dk, w_k) + dot_t(dv, w_v)).astype(BF)
    if net.zl * net.yh > 1:
        e1_keys = lax.psum_scatter(
            e1_keys, ("zl", "yh"), scatter_dimension=0, tiled=True
        )
    e1_near = e1_keys[mine:].reshape(2, own, width)
    e1_mine = e1_keys[:mine].astype(F32) + dot_t(dq, w_q)
    e1_mine = e1_mine.astype(BF).reshape(2, own, width)
    got = net.core(jnp.stack([e1_mine[1], e1_near[1]]))
    e1_near = e1_near[0].astype(F32) + got[1].astype(F32)
    e1 = e1_mine[0].astype(F32) + got[0].astype(F32) + net.pair(e1_near.astype(BF)).astype(F32)
    unit1 = unit_q[:own]
    in_own = grad_middle[:own] + norm_back(e1, unit1, inverse_q[:own], gain1)
    input_grad = from_sequence(in_own.astype(BF).reshape(local, cols, width)).astype(F32)

    total = lambda array: jnp.sum(array.astype(F32), axis=0)
    g_own = g_mine[:own]
    gain_sums = jnp.concatenate([total(e1 * unit1), total(e2[:own] * unit2[:own])])
    bias_sums = jnp.concatenate(
        [
            total(e2[:own]),
            spread(total(dq), groups),
            total(branch[:own]),
            total(g_own),
            spread(total(grad_pre), net.x),
        ]
    )
    lead_sums = jnp.concatenate([total(e1), spread(total(dv), groups)])
    sums = jnp.concatenate(
        [v.reshape(devices, -1) for v in (gain_sums, bias_sums, lead_sums)], axis=1
    )
    sums = sums + net.core(sums)
    sums = jnp.moveaxis(sums.reshape(net.x, 2, net.z, net.y, -1), 1, 0)
    sums = jnp.where(core == 0, sums[0], sums[1]).reshape(net.chips, 1, -1)
    n_sums = sums.shape[-1]
    sums = jnp.pad(sums, ((0, 0), (0, 15), (0, half_w - n_sums))).astype(BF)
    qkv_send = jnp.stack([by_chip(grad_qkv[i]) for i in range(3)], axis=1)
    qkv_send = qkv_send.reshape(net.chips, 6 * rows, half_w)
    if aligned:
        out_send = grad_proj.reshape(net.chips, rows, width)
    else:
        whole = jnp.zeros((width, width), BF)
        whole = lax.dynamic_update_slice(whole, grad_proj, (core * half_w, 0))
        out_send = by_chip(whole)
    sent = jnp.concatenate([qkv_send, fold(out_send, 2), sums], axis=1)
    shard_a = net.scatter(reorder(sent, table, True))

    def own_rows(chip):
        keep = jnp.where(core == 0, chip[..., 0, :, :], chip[..., 1, :, :])
        give = jnp.where(core == 0, chip[..., 1, :, :], chip[..., 0, :, :])
        return keep, net.core(give)

    def merge(keep, got, parts):
        split = lambda array: array.reshape(*array.shape[:-1], parts, 1, -1)
        first = jnp.where(core == 0, split(keep), split(got))
        second = jnp.where(core == 0, split(got), split(keep))
        return jnp.concatenate([first, second], axis=-2).reshape(*keep.shape[:-1], -1)

    qkv_own = merge(*own_rows(shard_a[: cut[0]].reshape(3, 2, rows, half_w)), groups)
    g_qkv = jnp.moveaxis(qkv_own, 0, 1).reshape(-1)
    out_own = unfold(shard_a[cut[0] : cut[1]], 2)
    if not aligned:
        keep, got = own_rows(out_own.reshape(2, rows, width))
        out_own = keep + got
    g_out = out_own.reshape(-1)
    up_own = merge(*own_rows(unfold(shard_up, 2).reshape(2, rows, half_f)), net.x)
    own_sums = shard_a[cut[1], :n_sums]
    n_gain = 2 * width // devices
    n_lead = n_sums - n_gain
    return (
        block_out,
        input_grad,
        g_qkv,
        g_out,
        up_own.reshape(-1),
        shard_down.reshape(-1),
        own_sums[:n_gain],
        own_sums[n_gain:n_lead],
        own_sums[n_lead:],
    )


def solution(mesh):
    dp, seq = mesh.shape["dp"], mesh.shape["seq"]
    y = 1 << (((seq.bit_length() - 1) - 1) // 2)
    z = seq // y
    dims = (dp // 2, 2, 4, z // 4, y // 2, 2)
    net = Net(dims)
    inner = Mesh(mesh.devices.reshape(dims), AXES)
    place = ("zh", "zl", "yh", "yl")
    cube = P(("x", "c"), place, None)
    flat = P(AXES)
    return jax.shard_map(
        functools.partial(body, net),
        mesh=inner,
        in_specs=(cube, P(("x", "c"), place), cube) + (flat,) * 6,
        out_specs=(cube, cube) + (flat,) * 7,
        check_vma=False,
    )
```

```python
import functools
import itertools

import jax
import jax.numpy as jnp
import numpy as np
from jax import lax
from jax.experimental import pallas as pl
from jax.experimental.pallas import tpu as pltpu
from jax.sharding import Mesh
from jax.sharding import PartitionSpec as P

D = 768
FF = 3072
HEADS = 12
HEAD_DIM = 64
EPS = 1e-05
MASKED = -1000000000.0
BF = jnp.bfloat16
F32 = jnp.float32
AXES = ("x", "c", "zh", "zl", "yh", "yl")


class Net:
    def __init__(self, dims):
        self.dims = dims
        self.x, self.c, self.zh, self.zl, self.yh, self.yl = dims
        self.z, self.y = self.zh * self.zl, self.yh * self.yl
        self.chips = self.x * self.z * self.y
        bits = lambda axis, n: [(axis, 1 << b) for b in reversed(range(n.bit_length() - 1))]
        zs, xs, ys = bits("z", self.z), bits("x", self.x), bits("y", self.y)
        self.orders = (zs + xs + ys, zs + ys + xs)
        self.stages = len(self.orders[0])

    def perm(self, move):
        pairs = []
        for at in itertools.product(*(range(n) for n in self.dims)):
            to = move(*at)
            pairs.append(
                (int(np.ravel_multi_index(at, self.dims)), int(np.ravel_multi_index(to, self.dims)))
            )
        return pairs

    def flip(self, stage):
        def move(x, c, zh, zl, yh, yl):
            axis, bit = self.orders[c][stage]
            z, y = zh * self.zl + zl, yh * self.yl + yl
            if axis == "x":
                x ^= bit
            elif axis == "y":
                y ^= bit
            else:
                z ^= bit
            return (x, c, z // self.zl, z % self.zl, y // self.yl, y % self.yl)

        return self.perm(move)

    def across(self, value, stage):
        return lax.ppermute(value, AXES, self.flip(stage))

    def core(self, value):
        return lax.ppermute(value, "c", [(0, 1), (1, 0)])

    def pair(self, value):
        return lax.ppermute(value, "yl", [(0, 1), (1, 0)])

    def scatter_move(self, k):
        return self.perm(
            lambda x, c, zh, zl, yh, yl: (x, zh >> 1, 2 * c + (k ^ (zh & 1)), zl, yh, yl)
        )

    def table(self):
        me = {
            "x": lax.axis_index("x"),
            "z": lax.axis_index("zh") * self.zl + lax.axis_index("zl"),
            "y": lax.axis_index("yh") * self.yl + lax.axis_index("yl"),
        }
        grid = np.indices((self.x, self.z, self.y)).reshape(3, -1)
        axes = {"x": grid[0], "z": grid[1], "y": grid[2]}
        places = []
        for order in self.orders:
            place = jnp.zeros((self.chips,), jnp.int32)
            for stage, (axis, bit) in enumerate(order):
                differs = (jnp.asarray(axes[axis], jnp.int32) ^ me[axis]) & bit
                place = place + jnp.where(differs != 0, 1 << stage, 0)
            places.append(place)
        return jnp.where(lax.axis_index("c") == 0, places[0], places[1]).astype(jnp.int32)

    def gather(self, block):
        held = block[None]
        for stage in range(self.stages):
            held = jnp.concatenate([held, self.across(held, stage)])
        return held

    def scatter(self, held):
        for stage in reversed(range(self.stages)):
            half = held.shape[0] // 2
            got = self.across(held[half:], stage)
            held = held[:half].astype(F32) + got.astype(F32)
            if stage:
                held = held.astype(BF)
        return held[0]


def move_kernel(table, source, target):
    target[...] = source[...]


def reorder(blocks, table, to_place):
    rest = -blocks.shape[1] % 16
    if rest:
        rows = blocks.shape[1]
        blocks = jnp.pad(blocks, ((0, 0), (0, rest), (0, 0)))
        return reorder(blocks, table, to_place)[:, :rows]
    chips, rows, cols = blocks.shape
    here = pl.BlockSpec((1, rows, cols), lambda chip, table: (chip, 0, 0))
    there = pl.BlockSpec((1, rows, cols), lambda chip, table: (table[chip], 0, 0))
    return pl.pallas_call(
        move_kernel,
        grid_spec=pltpu.PrefetchScalarGridSpec(
            num_scalar_prefetch=1,
            grid=(chips,),
            in_specs=[here if to_place else there],
            out_specs=there if to_place else here,
        ),
        out_shape=jax.ShapeDtypeStruct(blocks.shape, blocks.dtype),
    )(table, blocks)


def normal(field):
    center = field - jnp.mean(field, axis=-1, keepdims=True)
    inverse = lax.rsqrt(jnp.mean(center * center, axis=-1, keepdims=True) + EPS)
    return center * inverse, inverse


def norm_back(upstream, unit, inverse, gain):
    scaled = upstream * gain
    return inverse * (
        scaled
        - jnp.mean(scaled, axis=-1, keepdims=True)
        - unit * jnp.mean(scaled * unit, axis=-1, keepdims=True)
    )


def dot(a, b):
    return jnp.dot(a, b, preferred_element_type=F32)


def dot_t(a, b):
    return lax.dot_general(a, b, (((1,), (1,)), ((), ())), preferred_element_type=F32)


def t_dot(a, b):
    return lax.dot_general(a, b, (((0,), (0,)), ((), ())), preferred_element_type=F32)


def fold(wide, parts):
    lead, rows, cols = wide.shape[:-2], wide.shape[-2], wide.shape[-1] // parts
    moved = jnp.moveaxis(wide.reshape(*lead, rows, parts, cols), -2, -3)
    return moved.reshape(*lead, parts * rows, cols)


def unfold(tall, parts):
    lead, rows, cols = tall.shape[:-2], tall.shape[-2] // parts, tall.shape[-1]
    moved = jnp.moveaxis(tall.reshape(*lead, parts, rows, cols), -3, -2)
    return moved.reshape(*lead, rows, parts * cols)


def body_any(net, tokens, segments, cotangent, w_qkv, w_out, w_fc1, w_fc2, norm_gains, bias_pack):
    local, cols, width = tokens.shape
    own = local * cols
    mine = 2 * own
    hidden = FF
    half_w, half_f = width // 2, hidden // 2
    devices = 2 * net.chips
    core = lax.axis_index("c")
    zodd = lax.axis_index("zh") & 1
    table = net.table()
    rows = width // devices
    frows = hidden // devices
    aligned = (width // (2 * net.x)) % HEAD_DIM == 0
    groups = net.x if aligned else 1

    def pick(array, parts, which):
        split = array.reshape(*array.shape[:-1], parts, 2, array.shape[-1] // (2 * parts))
        taken = jnp.where(which == 0, split[..., 0, :], split[..., 1, :])
        return taken.reshape(*array.shape[:-1], array.shape[-1] // 2)

    def spread(vector, parts):
        split = vector.reshape(parts, 1, vector.shape[-1] // parts)
        both = jnp.concatenate(
            [jnp.where(core == 0, split, 0.0), jnp.where(core == 1, split, 0.0)], axis=1
        )
        return both.reshape(-1)

    seg_row = jnp.pad(segments.astype(BF), ((0, 0), (0, width - cols)))[:, None, :]
    seg_rows = jnp.pad(seg_row, ((0, 0), (0, 7), (0, 0)))
    packed = jnp.concatenate([tokens, seg_rows], axis=1)

    def to_sequence(array):
        swapped = jnp.where(zodd == 0, array, array[::-1])
        return jnp.stack(
            [lax.ppermute(swapped[k], AXES, net.scatter_move(k)) for k in range(2)]
        )

    def from_sequence(array):
        back = jnp.stack(
            [
                lax.ppermute(array[k], AXES, [(b, a) for a, b in net.scatter_move(k)])
                for k in range(2)
            ]
        )
        return jnp.where(zodd == 0, back, back[::-1])

    def halves(which):
        qkv = fold(w_qkv.reshape(rows, 3 * width), 3).reshape(3, rows, width)
        up = w_fc1.reshape(rows, hidden)
        return pick(qkv, groups, which), pick(up, net.x, which)

    keep_qkv, keep_up = halves(core)
    give_qkv, give_up = halves(1 - core)
    small = jnp.concatenate([norm_gains, bias_pack])
    out_rows = w_out.reshape(rows, width)
    got_qkv, got_up, got_small, got_out = jax.tree.map(
        net.core, (give_qkv, give_up, small, out_rows)
    )

    def both(a, b, axis):
        return jnp.where(
            core == 0, jnp.concatenate([a, b], axis=axis), jnp.concatenate([b, a], axis=axis)
        )

    chip_qkv = both(keep_qkv, got_qkv, 1).reshape(6 * rows, half_w)
    chip_up = fold(both(keep_up, got_up, 0), 2)
    chip_out = fold(out_rows if aligned else both(out_rows, got_out, 0), 2)
    chip_small = jnp.pad(
        both(small[None], got_small[None], 0), ((0, 14), (0, half_w - small.shape[0]))
    )
    cut = np.cumsum([chip_qkv.shape[0], chip_out.shape[0]])
    blocks_a = reorder(
        net.gather(jnp.concatenate([chip_qkv, chip_out, chip_small])), table, False
    )
    blocks_up = reorder(net.gather(chip_up), table, False)
    blocks_down = reorder(net.gather(w_fc2.reshape(frows, width)), table, False)

    lead = (net.x, net.z, net.y)

    def natural(blocks):
        n = blocks.shape[-1]
        return jnp.moveaxis(blocks.reshape(*lead, 2, -1, n), 3, 1).reshape(-1, n)

    def by_chip(array):
        n = array.shape[-1]
        return jnp.moveaxis(array.reshape(net.x, 2, net.z, net.y, -1, n), 1, 3).reshape(
            net.chips, -1, n
        )

    qkv_blocks = blocks_a[:, : cut[0]].reshape(net.chips, 3, 2 * rows, half_w)
    w_q, w_k, w_v = (natural(qkv_blocks[:, i]) for i in range(3))
    out_blocks = unfold(blocks_a[:, cut[0] : cut[1]], 2)
    if aligned:
        w_proj = out_blocks.reshape(half_w, width)
    else:
        w_proj = lax.dynamic_slice_in_dim(natural(out_blocks), core * half_w, half_w)
    smalls = blocks_a[:, cut[1] : cut[1] + 2, : small.shape[0]].reshape(*lead, 2, -1)
    smalls = jnp.moveaxis(smalls, 3, 1).reshape(devices, -1).astype(F32)
    n_gain = norm_gains.shape[0]
    gains = smalls[:, :n_gain].reshape(-1)
    shifts = smalls[:, n_gain:].reshape(-1)
    w_up = natural(unfold(blocks_up, 2))
    w_down = blocks_down.reshape(half_f, width)
    gain1, gain2 = gains[:width], gains[width:]
    shift1, shift2, bias_q, bias_v, bias_proj, bias_down = (
        shifts[i * width : (i + 1) * width] for i in range(6)
    )
    bias_up = pick(shifts[6 * width :], net.x, core)
    bias_q, bias_v = pick(bias_q, groups, core), pick(bias_v, groups, core)

    x_own = to_sequence(packed)
    x_other = net.core(x_own)
    x_mine = jnp.concatenate([x_own, x_other])
    near = net.pair(x_own)
    near = jnp.concatenate([near, net.core(near)])
    x_seq = jnp.concatenate([x_mine, near])
    if net.zl * net.yh > 1:
        x_far = lax.all_gather(x_seq, ("zl", "yh"), axis=0, tiled=True)
        x_keys = x_far
    else:
        x_keys = x_seq
    g_own = to_sequence(cotangent)
    g_mine = jnp.concatenate([g_own, net.core(g_own)]).reshape(mine, width)
    docs = x_keys[:, cols, :cols].reshape(-1)
    query_docs = x_mine[:, cols, :cols].reshape(-1)
    x_all = x_keys[:, :cols].reshape(-1, width).astype(F32)
    x_q = x_mine[:, :cols].reshape(-1, width).astype(F32)

    unit_q, inverse_q = normal(x_q)
    a_q = (unit_q * gain1 + shift1).astype(BF)
    unit_all, _ = normal(x_all)
    a_all = (unit_all * gain1 + shift1).astype(BF)
    heads = HEADS // 2
    q = (dot(a_q, w_q) + bias_q).astype(BF)
    k = dot(a_all, w_k).astype(BF)
    v = (dot(a_all, w_v) + bias_v).astype(BF)
    by_head = lambda t: t.reshape(-1, heads, HEAD_DIM)
    same = (query_docs[:, None] == docs[None, :])[None]
    scores = (
        jnp.einsum("qhd,khd->hqk", by_head(q), by_head(k), preferred_element_type=F32) * 0.125
    )
    scores = jnp.where(same, scores, MASKED)
    weights = jnp.exp(scores - jnp.max(scores, axis=-1, keepdims=True))
    probs = weights / jnp.sum(weights, axis=-1, keepdims=True)
    probs_low = probs.astype(BF)
    att = jnp.einsum("hqk,khd->qhd", probs_low, by_head(v), preferred_element_type=F32)
    att = att.reshape(mine, half_w)
    att_low = att.astype(BF)

    def core_sum(partial):
        low = partial.astype(BF)
        got = net.core(low)
        return low.astype(F32) + jnp.concatenate([got[own:], got[:own]]).astype(F32)

    middle = x_q + core_sum(dot(att_low, w_proj)) + bias_proj
    unit2, inverse2 = normal(middle)
    a2 = (unit2 * gain2 + shift2).astype(BF)
    pre = dot(a2, w_up) + bias_up
    sig = jax.nn.sigmoid(1.702 * pre)
    activ = (pre * sig).astype(BF)
    down = dot(activ, w_down)
    down_got = net.core(down[own:].astype(BF)).astype(F32)
    out_own = (middle[:own] + down[:own] + down_got + bias_down).astype(BF)
    block_out = from_sequence(out_own.reshape(local, cols, width))

    grad_down = t_dot(activ, g_mine).astype(BF)
    grad_pre = (dot_t(g_mine, w_down) * (sig + 1.702 * pre * sig * (1.0 - sig))).astype(BF)
    shard_down = net.scatter(reorder(grad_down.reshape(net.chips, frows, width), table, True))
    grad_up = t_dot(a2, grad_pre).astype(BF)
    shard_up = net.scatter(reorder(fold(by_chip(grad_up), 2), table, True))
    e2 = core_sum(dot_t(grad_pre, w_up))
    grad_middle = g_mine.astype(F32) + norm_back(e2, unit2, inverse2, gain2)
    branch = grad_middle.astype(BF)
    grad_proj = t_dot(att_low, branch).astype(BF)
    d_heads = dot_t(branch, w_proj).astype(BF)
    dp = jnp.einsum("qhd,khd->hqk", by_head(d_heads), by_head(v), preferred_element_type=F32)
    delta = jnp.sum(probs * dp, axis=-1, keepdims=True)
    d_scores = (probs * (dp - delta)).astype(BF)
    dq = 0.125 * jnp.einsum("hqk,khd->qhd", d_scores, by_head(k), preferred_element_type=F32)
    dk = 0.125 * jnp.einsum("hqk,qhd->khd", d_scores, by_head(q), preferred_element_type=F32)
    dv = jnp.einsum("hqk,qhd->khd", probs_low, by_head(d_heads), preferred_element_type=F32)
    dq = dq.reshape(-1, half_w).astype(BF)
    dk = dk.reshape(-1, half_w).astype(BF)
    dv = dv.reshape(-1, half_w).astype(BF)
    grad_qkv = jnp.stack([t_dot(a_q, dq), t_dot(a_all, dk), t_dot(a_all, dv)]).astype(BF)

    e1_keys = (dot_t(dk, w_k) + dot_t(dv, w_v)).astype(BF)
    if net.zl * net.yh > 1:
        e1_keys = lax.psum_scatter(
            e1_keys, ("zl", "yh"), scatter_dimension=0, tiled=True
        )
    e1_near = e1_keys[mine:].reshape(2, own, width)
    e1_mine = e1_keys[:mine].astype(F32) + dot_t(dq, w_q)
    e1_mine = e1_mine.astype(BF).reshape(2, own, width)
    got = net.core(jnp.stack([e1_mine[1], e1_near[1]]))
    e1_near = e1_near[0].astype(F32) + got[1].astype(F32)
    e1 = e1_mine[0].astype(F32) + got[0].astype(F32) + net.pair(e1_near.astype(BF)).astype(F32)
    unit1 = unit_q[:own]
    in_own = grad_middle[:own] + norm_back(e1, unit1, inverse_q[:own], gain1)
    input_grad = from_sequence(in_own.astype(BF).reshape(local, cols, width)).astype(F32)

    total = lambda array: jnp.sum(array.astype(F32), axis=0)
    g_own = g_mine[:own]
    gain_sums = jnp.concatenate([total(e1 * unit1), total(e2[:own] * unit2[:own])])
    bias_sums = jnp.concatenate(
        [
            total(e2[:own]),
            spread(total(dq), groups),
            total(branch[:own]),
            total(g_own),
            spread(total(grad_pre), net.x),
        ]
    )
    lead_sums = jnp.concatenate([total(e1), spread(total(dv), groups)])
    sums = jnp.concatenate(
        [v.reshape(devices, -1) for v in (gain_sums, bias_sums, lead_sums)], axis=1
    )
    sums = sums + net.core(sums)
    sums = jnp.moveaxis(sums.reshape(net.x, 2, net.z, net.y, -1), 1, 0)
    sums = jnp.where(core == 0, sums[0], sums[1]).reshape(net.chips, 1, -1)
    n_sums = sums.shape[-1]
    sums = jnp.pad(sums, ((0, 0), (0, 15), (0, half_w - n_sums))).astype(BF)
    qkv_send = jnp.stack([by_chip(grad_qkv[i]) for i in range(3)], axis=1)
    qkv_send = qkv_send.reshape(net.chips, 6 * rows, half_w)
    if aligned:
        out_send = grad_proj.reshape(net.chips, rows, width)
    else:
        whole = jnp.zeros((width, width), BF)
        whole = lax.dynamic_update_slice(whole, grad_proj, (core * half_w, 0))
        out_send = by_chip(whole)
    sent = jnp.concatenate([qkv_send, fold(out_send, 2), sums], axis=1)
    shard_a = net.scatter(reorder(sent, table, True))

    def own_rows(chip):
        keep = jnp.where(core == 0, chip[..., 0, :, :], chip[..., 1, :, :])
        give = jnp.where(core == 0, chip[..., 1, :, :], chip[..., 0, :, :])
        return keep, net.core(give)

    def merge(keep, got, parts):
        split = lambda array: array.reshape(*array.shape[:-1], parts, 1, -1)
        first = jnp.where(core == 0, split(keep), split(got))
        second = jnp.where(core == 0, split(got), split(keep))
        return jnp.concatenate([first, second], axis=-2).reshape(*keep.shape[:-1], -1)

    qkv_own = merge(*own_rows(shard_a[: cut[0]].reshape(3, 2, rows, half_w)), groups)
    g_qkv = jnp.moveaxis(qkv_own, 0, 1).reshape(-1)
    out_own = unfold(shard_a[cut[0] : cut[1]], 2)
    if not aligned:
        keep, got = own_rows(out_own.reshape(2, rows, width))
        out_own = keep + got
    g_out = out_own.reshape(-1)
    up_own = merge(*own_rows(unfold(shard_up, 2).reshape(2, rows, half_f)), net.x)
    own_sums = shard_a[cut[1], :n_sums]
    n_gain = 2 * width // devices
    n_lead = n_sums - n_gain
    return (
        block_out,
        input_grad,
        g_qkv,
        g_out,
        up_own.reshape(-1),
        shard_down.reshape(-1),
        own_sums[:n_gain],
        own_sums[n_gain:n_lead],
        own_sums[n_lead:],
    )


SLAB = 128
PAIRS = HEADS // 4
DOUBLE = 2 * HEAD_DIM
PARTS = (
    ("gain1", D),
    ("gain2", D),
    ("shift1", D),
    ("shift2", D),
    ("bias_proj", D),
    ("bias_down", D),
    ("bias_q", D // 2),
    ("bias_v", D // 2),
    ("bias_up", FF // 2),
)
SUMS = (
    ("e1n", D),
    ("e2n", D),
    ("e2", D),
    ("dq", D // 2),
    ("branch", D),
    ("g", D),
    ("pre", FF // 2),
    ("e1", D),
    ("dv", D // 2),
)


def offsets(parts):
    ends = np.cumsum([n for _, n in parts])
    return {name: slice(int(end - n), int(end)) for (name, n), end in zip(parts, ends)}


AT = offsets(PARTS)


def dots(a, b, ca, cb):
    return lax.dot_general(a, b, (((ca,), (cb,)), ((), ())), preferred_element_type=F32)


def lane_half(e):
    lanes = lax.broadcasted_iota(jnp.int32, (1, DOUBLE), 1)
    inside = (lanes < HEAD_DIM) if e == 0 else (lanes >= HEAD_DIM)
    return inside.astype(F32).astype(BF)


def first_half(shape):
    return lax.broadcasted_iota(jnp.int32, shape, 1) < HEAD_DIM


def load_rows(inv, held, got, target, sems, pieces):
    half = held.shape[0]
    copies = []
    for r in range(2 * half):
        source = held if r < half else got
        for n, (first, rows, place) in enumerate(pieces):
            copies.append(
                pltpu.make_async_copy(
                    source.at[r % half, pl.ds(first, rows), :],
                    place(target, inv[r], rows),
                    sems.at[r, n],
                )
            )
    for copy in copies:
        copy.start()
    return copies


def attend_kernel(
    inv, xo, xt, xn, xm, row, col, vec, pi, held, got,
    a_ref, unit_ref, q_ref, k_ref, v_ref, o_ref, low_ref, lse_ref, w_ref,
    nat, w, bias, s, p_low, sems,
):
    place = lambda i: lambda t, chip, n: t.at[i, pl.ds(pl.multiple_of(chip * n, 16), n), :]
    copies = load_rows(inv, held, got, w, sems, [(48 * i, 48, place(i)) for i in range(3)])
    for i, (ref, j) in enumerate((ref, j) for ref in (xo, xt, xn, xm) for j in range(2)):
        unit, _ = normal(ref[j, :SLAB, :].astype(F32))
        at = pl.ds(i * SLAB, SLAB)
        unit_ref[at, :] = unit.astype(BF)
        nat[at, :] = (unit * vec[:, AT["gain1"]] + vec[:, AT["shift1"]]).astype(BF)
        bias[at, :] = jnp.where(col[at, :] == row[...], 0.0, MASKED)
    a_ref[...] = dot(nat[...], pi[...]).astype(BF)
    for copy in copies:
        copy.wait()
    w_ref[...] = w[...]
    mine = q_ref.shape[1]
    q = (dot(a_ref[:mine, :], w[0]) + vec[:, AT["bias_q"]]).astype(BF) * 0.125
    k = dot(a_ref[...], w[1]).astype(BF)
    v = (dot(a_ref[...], w[2]) + vec[:, AT["bias_v"]]).astype(BF)
    for i in range(PAIRS):
        lanes = slice(i * DOUBLE, (i + 1) * DOUBLE)
        q_ref[i], k_ref[i], v_ref[i] = q[:, lanes], k[:, lanes], v[:, lanes]
    keys = a_ref.shape[0]

    def pair(i, carry):
        outs = []
        for e in range(2):
            qm = q_ref[i] * lane_half(e)
            top = jnp.full((1, mine), -3e38, F32)
            for c in range(keys // SLAB):
                at = pl.ds(c * SLAB, SLAB)
                t = dots(k_ref[i, at, :], qm, 1, 1) + bias[at, :]
                s[at, :] = t
                top = jnp.maximum(top, jnp.max(t, axis=0, keepdims=True))
            total = jnp.zeros((1, mine), F32)
            for c in range(keys // SLAB):
                at = pl.ds(c * SLAB, SLAB)
                p = jnp.exp(s[at, :] - top)
                total = total + jnp.sum(p, axis=0, keepdims=True)
                p_low[at, :] = p.astype(BF)
            lse_ref[i, e : e + 1, :] = top + jnp.log(total)
            o = dots(p_low[...], v_ref[i], 0, 0)
            scale = jnp.broadcast_to(1.0 / total, (DOUBLE, mine)).T
            outs.append(o * scale)
        o = jnp.where(first_half(outs[0].shape), outs[0], outs[1])
        o_ref[i] = o
        low_ref[i] = o.astype(BF)
        return carry

    lax.fori_loop(0, PAIRS, pair, 0)


def project_kernel(inv, low, perm, held, got, part_ref, wo_ref, rel, sems):
    half = held.shape[0]
    copies = []
    for r in range(2 * half):
        source = held if r < half else got
        copies.append(
            pltpu.make_async_copy(
                source.at[r % half, pl.ds(96, 32), :], rel.at[pl.ds(r * 32, 32), :], sems.at[r]
            )
        )
    for copy in copies:
        copy.start()
    for copy in copies:
        copy.wait()
    wo_ref[...] = dot(perm[...], rel[...]).astype(BF)
    att = jnp.concatenate([low[i] for i in range(PAIRS)], axis=1)
    part_ref[...] = dot(att, wo_ref[...]).astype(BF)


def middle_kernel(
    inv, part, part_got, xo, xt, go, gt, vec, pi, held, got,
    mid_ref, a_ref, act_ref, fac_ref, w_ref, keep_ref, send_ref, sum_ref,
    nat, w, grad, sems,
):
    place = lambda h: lambda t, chip, n: t.at[
        pl.ds(pl.multiple_of(chip * n, 16), n), pl.ds(h * D, D)
    ]
    copies = load_rows(inv, held, got, w, sems, [(48 * h, 48, place(h)) for h in range(2)])
    mine = part.shape[0]
    own = mine // 2
    for i, (ref, j) in enumerate((ref, j) for ref in (xo, xt) for j in range(2)):
        at = pl.ds(i * SLAB, SLAB)
        other = pl.ds((i * SLAB + own) % mine, SLAB)
        mid = (
            ref[j, :SLAB, :].astype(F32)
            + (part[at, :].astype(F32) + part_got[other, :].astype(F32))
            + vec[:, AT["bias_proj"]]
        )
        mid_ref[at, :] = mid
        unit, _ = normal(mid)
        nat[at, :] = (unit * vec[:, AT["gain2"]] + vec[:, AT["shift2"]]).astype(BF)
    a_ref[...] = dot(nat[...], pi[...]).astype(BF)
    g = jnp.concatenate([go[0], go[1], gt[0], gt[1]], axis=0)
    sum_ref[...] = jnp.sum(g[:own].astype(F32), axis=0, keepdims=True)
    for copy in copies:
        copy.wait()
    w_ref[...] = w[...]
    step = 512
    for j in range(w.shape[1] // step):
        lanes = pl.ds(j * step, step)
        start = AT["bias_up"].start + j * step
        pre = dot(a_ref[...], w[:, lanes]) + vec[:, start : start + step]
        sig = 1.0 / (1.0 + jnp.exp(-1.702 * pre))
        act_ref[:, lanes] = (pre * sig).astype(BF)
        fac_ref[:, lanes] = sig + 1.702 * pre * sig * (1.0 - sig)
        grad[lanes, :] = dots(act_ref[:, lanes], g, 0, 0).astype(BF)
    spread_rows(inv, keep_ref, send_ref, lambda chip: [grad[pl.ds(pl.multiple_of(chip * 96, 16), 96), :]])


def spread_rows(inv, keep_ref, send_ref, rows_of):
    half = keep_ref.shape[0]
    for r in range(2 * half):
        target = keep_ref if r < half else send_ref
        first = 0
        for piece in rows_of(inv[r]):
            target[r % half, first : first + piece.shape[0], :] = piece
            first += piece.shape[0]


def slope_kernel(inv, go, gt, fac, w_up, pi, held, got, pre_ref, e_ref, w_ref, sum_ref, w, sems):
    place = lambda t, chip, n: t.at[pl.ds(pl.multiple_of(chip * n, 16), n), :]
    copies = load_rows(inv, held, got, w, sems, [(0, 96, place)])
    g = jnp.concatenate([go[0], go[1], gt[0], gt[1]], axis=0)
    for copy in copies:
        copy.wait()
    w_ref[...] = w[...]
    step = 512
    total = None
    for j in range(w.shape[0] // step):
        lanes = pl.ds(j * step, step)
        pre = (dots(g, w[lanes, :], 1, 1) * fac[:, lanes]).astype(BF)
        pre_ref[:, lanes] = pre
        sum_ref[:, lanes] = jnp.sum(pre.astype(F32), axis=0, keepdims=True)
        term = dots(pre, w_up[:, lanes], 1, 1)
        total = term if total is None else total + term
    e_ref[...] = dots(total.astype(BF), pi[...], 1, 1).astype(BF)


def update_kernel(inv, a, pre, act, w_down, keep_ref, send_ref, own_ref, give_ref, grad):
    step = 512
    for j in range(pre.shape[1] // step):
        lanes = pl.ds(j * step, step)
        grad[:, lanes] = dots(a[...], pre[:, lanes], 0, 0).astype(BF)
    rows = lambda chip: pl.ds(pl.multiple_of(chip * 48, 16), 48)
    spread_rows(
        inv, keep_ref, send_ref, lambda chip: [grad[rows(chip), :D], grad[rows(chip), D:]]
    )
    down = dot(act[...], w_down[...])
    own = own_ref.shape[0]
    own_ref[...] = down[:own]
    give_ref[...] = down[own:].astype(BF)


def back_kernel(
    e2, e2_got, mid, go, gt, vec, wo, q, k, v, o, lse, row, col, w, unit1, pi,
    gm_ref, branch_ref, dq_ref, dk_ref, dv_ref, keep_ref, give_ref,
    e2n_sum, e2_sum, branch_sum, dq_sum, dv_sum, e1n_sum, e1_sum,
    d_ref, p_low, s_low,
):
    mine = mid.shape[0]
    own = mine // 2
    sums = [jnp.zeros((1, D), F32) for _ in range(3)]
    for i, (ref, j) in enumerate((ref, j) for ref in (go, gt) for j in range(2)):
        at = pl.ds(i * SLAB, SLAB)
        other = pl.ds((i * SLAB + own) % mine, SLAB)
        e = e2[at, :].astype(F32) + e2_got[other, :].astype(F32)
        unit, inverse = normal(mid[at, :])
        gm = ref[j].astype(F32) + norm_back(e, unit, inverse, vec[:, AT["gain2"]])
        branch = gm.astype(BF)
        branch_ref[at, :] = branch
        if i < 2:
            gm_ref[at, :] = gm
            for n, term in enumerate((e * unit, e, branch.astype(F32))):
                sums[n] = sums[n] + jnp.sum(term, axis=0, keepdims=True)
    e2n_sum[...], e2_sum[...], branch_sum[...] = sums
    d = dots(branch_ref[...], wo[...], 1, 1).astype(BF)
    for i in range(PAIRS):
        d_ref[i] = d[:, i * DOUBLE : (i + 1) * DOUBLE]
    keys = k.shape[1]

    def pair(i, carry):
        both = (d_ref[i].astype(F32) * o[i]).T
        got = []
        for e in range(2):
            delta = jnp.sum(both[e * HEAD_DIM : (e + 1) * HEAD_DIM], axis=0, keepdims=True)
            qm = q[i] * lane_half(e)
            dm = d_ref[i] * lane_half(e)
            base = lse[i, e : e + 1, :]
            for c in range(keys // SLAB):
                at = pl.ds(c * SLAB, SLAB)
                t = dots(k[i, at, :], qm, 1, 1)
                p = jnp.where(col[at, :] == row[...], jnp.exp(t - base), 0.0)
                dp = dots(v[i, at, :], dm, 1, 1)
                p_low[at, :] = p.astype(BF)
                s_low[at, :] = (p * (dp - delta)).astype(BF)
            got.append(
                (
                    dots(s_low[...], k[i], 0, 0) * 0.125,
                    dot(s_low[...], q[i]),
                    dot(p_low[...], d_ref[i]),
                )
            )
        for n, ref in enumerate((dq_ref, dk_ref, dv_ref)):
            ref[i] = jnp.where(first_half(got[0][n].shape), got[0][n], got[1][n]).astype(BF)
        return carry

    lax.fori_loop(0, PAIRS, pair, 0)
    wide = lambda ref: jnp.concatenate([ref[i] for i in range(PAIRS)], axis=1)
    dq, dk, dv = wide(dq_ref), wide(dk_ref), wide(dv_ref)
    dq_sum[...] = jnp.sum(dq.astype(F32), axis=0, keepdims=True)
    dv_sum[...] = jnp.sum(dv.astype(F32), axis=0, keepdims=True)
    e1n = jnp.zeros((1, D), F32)
    e1s = jnp.zeros((1, D), F32)
    for part in range(keys // own):
        at = slice(part * own, (part + 1) * own)
        e = dots(dk[at], w[1], 1, 1) + dots(dv[at], w[2], 1, 1)
        if part < 2:
            e = e + dots(dq[at], w[0], 1, 1)
        e = dots(e.astype(BF), pi[...], 1, 1)
        e1s = e1s + jnp.sum(e, axis=0, keepdims=True)
        e1n = e1n + jnp.sum(e * unit1[pl.ds(part * own, own), :].astype(F32), axis=0, keepdims=True)
        target = keep_ref if part % 2 == 0 else give_ref
        target[part // 2] = e.astype(BF)
    e1n_sum[...] = e1n
    e1_sum[...] = e1s


def gather_grads_kernel(
    inv, a, dq, dk, dv, low, branch, perm, sums, keep_ref, send_ref, grad, out
):
    mine = dq.shape[1]
    wide = lambda ref: jnp.concatenate([ref[i] for i in range(PAIRS)], axis=1)
    grad[0] = dots(a[:mine, :], wide(dq), 0, 0).astype(BF)
    grad[1] = dots(a[...], wide(dk), 0, 0).astype(BF)
    grad[2] = dots(a[...], wide(dv), 0, 0).astype(BF)
    proj = dots(wide(low), branch[...], 0, 0).astype(BF)
    out[...] = dots(perm[...], proj, 0, 0).astype(BF)
    half = keep_ref.shape[0]
    for r in range(2 * half):
        target, at = (keep_ref if r < half else send_ref), r % half
        chip = inv[r]
        for i in range(3):
            target[at, 48 * i : 48 * i + 48, :] = grad[
                i, pl.ds(pl.multiple_of(chip * 48, 16), 48), :
            ]
        for h in range(2):
            lanes = slice(h * (D // 2), (h + 1) * (D // 2))
            target[at, 144 + 32 * h : 176 + 32 * h, :] = out[r * 32 : r * 32 + 32, lanes]
        target[at, 208:224, :] = sums[r]


def run(kernel, table, args, outs, scratch, anys=()):
    specs = [
        pl.BlockSpec(memory_space=pl.ANY) if i in anys else pl.BlockSpec(memory_space=pltpu.VMEM)
        for i in range(len(args))
    ]
    prefetch = () if table is None else (table,)
    return pl.pallas_call(
        kernel,
        grid_spec=pltpu.PrefetchScalarGridSpec(
            num_scalar_prefetch=len(prefetch),
            grid=(),
            in_specs=specs,
            out_specs=[pl.BlockSpec(memory_space=pltpu.VMEM) for _ in outs],
            scratch_shapes=scratch,
        ),
        out_shape=[jax.ShapeDtypeStruct(shape, dtype) for shape, dtype in outs],
        compiler_params=pltpu.CompilerParams(vmem_limit_bytes=44 * 2**20),
    )(*prefetch, *args)


def body(net, tokens, segments, cotangent, w_qkv, w_out, w_fc1, w_fc2, norm_gains, bias_pack):
    local, cols, width = tokens.shape
    own, mine = local * cols, 2 * local * cols
    keys = 2 * mine
    hidden = FF
    half_w, half_f = width // 2, hidden // 2
    chips, devices = net.chips, 2 * net.chips
    half = chips // 2
    rows, frows = width // devices, hidden // devices
    core = lax.axis_index("c")
    zodd = lax.axis_index("zh") & 1
    table = net.table()
    spots = jnp.arange(chips, dtype=jnp.int32)
    inv = jnp.sum(
        jnp.where(table[None, :] == spots[:, None], spots[None, :], 0), axis=1
    ).astype(jnp.int32)

    split = lambda n, parts: np.arange(n).reshape(parts, 2, n // (2 * parts))
    of_core = lambda n, parts: [split(n, parts)[:, c].reshape(-1) for c in range(2)]
    everywhere = lambda n: [np.arange(n)] * 2
    n_gain, n_bias = norm_gains.shape[0], bias_pack.shape[0]

    def owners(items):
        dev, place = [], []
        for c in range(2):
            flat = [(first + entry[c]) for first, entry, _, _ in items]
            dev.append(np.concatenate([f // n for f, (_, _, _, n) in zip(flat, items)]))
            place.append(
                np.concatenate([at + f % n for f, (_, _, at, n) in zip(flat, items)])
            )
        dev, place = np.array(dev, np.int32), np.array(place, np.int32)
        return (
            jnp.where(core == 0, dev[0], dev[1]),
            jnp.where(core == 0, place[0], place[1]),
        )

    chip_row = jnp.repeat(inv, 2)
    s_n = net.z * net.y
    row_device = ((chip_row // s_n) * 2 + jnp.tile(jnp.arange(2), chips)) * s_n + chip_row % s_n
    D_, W = everywhere(width), width

    def mapping(items):
        dev, place = owners(items)
        n_local = norm_gains.shape[0] + bias_pack.shape[0]
        pick_row = row_device[:, None] == dev[None, :]
        onehot = (jnp.arange(n_local, dtype=jnp.int32)[:, None] == place[None, :]).astype(BF)
        return pick_row, onehot

    gl, bl = n_gain, n_bias
    heads_c, ff_c = of_core(width, net.x), of_core(hidden, net.x)
    pick_in, hot_in = mapping(
        [
            (0, D_, 0, gl),
            (W, D_, 0, gl),
            (0, D_, gl, bl),
            (W, D_, gl, bl),
            (4 * W, D_, gl, bl),
            (5 * W, D_, gl, bl),
            (2 * W, heads_c, gl, bl),
            (3 * W, heads_c, gl, bl),
            (6 * W, ff_c, gl, bl),
        ]
    )
    ll = 2 * W // devices
    rl = n_gain + n_bias - 2 * ll
    pick_out, hot_out = mapping(
        [
            (0, D_, 0, ll),
            (W, D_, 0, ll),
            (0, D_, ll, rl),
            (W, heads_c, ll, rl),
            (2 * W, D_, ll, rl),
            (3 * W, D_, ll, rl),
            (4 * W, ff_c, ll, rl),
            (0, D_, ll + rl, ll),
            (W, heads_c, ll + rl, ll),
        ]
    )
    order = np.arange(width).reshape(net.x, 2, s_n, rows).transpose(0, 2, 1, 3).reshape(-1)
    pi = jnp.asarray((np.arange(width)[:, None] == order[None, :]), BF)
    rel_row = jnp.arange(chips * 32, dtype=jnp.int32)
    nat_row = jnp.where(rel_row % 32 < rows, jnp.repeat(inv, 32) * rows + rel_row % 32, -1)
    perm = (jnp.arange(half_w, dtype=jnp.int32)[:, None] == nat_row[None, :]).astype(BF)

    def pick(array, parts, which):
        view = array.reshape(*array.shape[:-1], parts, 2, array.shape[-1] // (2 * parts))
        taken = jnp.where(which == 0, view[..., 0, :], view[..., 1, :])
        return taken.reshape(*array.shape[:-1], array.shape[-1] // 2)

    def both(a, b, axis):
        return jnp.where(
            core == 0, jnp.concatenate([a, b], axis=axis), jnp.concatenate([b, a], axis=axis)
        )

    small = jnp.concatenate([norm_gains, bias_pack])
    qkv = w_qkv.reshape(rows, 3, width).swapaxes(0, 1)
    got_qkv, got_small = net.core(pick(qkv, net.x, 1 - core)), net.core(small)
    chip_qkv = both(pick(qkv, net.x, core), got_qkv, 1).reshape(6 * rows, half_w)
    chip_small = jnp.pad(
        both(small[None], got_small[None], 0), ((0, 14), (0, half_w - small.shape[0]))
    )

    def stages(block, start=None):
        held = block[None]
        for stage in range(net.stages - 1):
            held = jnp.concatenate([held, net.across(held, stage)])
            yield held
        yield held, net.across(held, net.stages - 1)

    q_steps = list(stages(jnp.concatenate([chip_qkv, chip_small])))
    q_held, q_got = q_steps[-1]

    seg_row = jnp.pad(segments.astype(BF), ((0, 0), (0, width - cols)))[:, None, :]
    packed = jnp.concatenate([tokens, jnp.pad(seg_row, ((0, 0), (0, 7), (0, 0)))], axis=1)

    def to_sequence(array):
        swapped = jnp.where(zodd == 0, array, array[::-1])
        return jnp.stack(
            [lax.ppermute(swapped[k], AXES, net.scatter_move(k)) for k in range(2)]
        )

    def from_sequence(array):
        back = jnp.stack(
            [
                lax.ppermute(array[k], AXES, [(b, a) for a, b in net.scatter_move(k)])
                for k in range(2)
            ]
        )
        return jnp.where(zodd == 0, back, back[::-1])

    def after(value, *others):
        return lax.optimization_barrier((value, *others))[0]

    x_o = to_sequence(packed)
    x_t = net.core(x_o)
    x_n = net.pair(x_o)
    x_m = net.core(x_n)

    up = w_fc1.reshape(rows, hidden)
    got_up = net.core(pick(up, net.x, 1 - core))
    chip_up = fold(both(pick(up, net.x, core), got_up, 0), 2)
    chip_up = jnp.concatenate([chip_up, jnp.pad(w_out.reshape(rows, width), ((0, 8), (0, 0)))])
    u_steps = list(stages(after(chip_up, q_steps[0])))
    u_held, u_got = u_steps[-1]
    d_steps = list(stages(after(w_fc2.reshape(frows, width), u_steps[0])))
    d_held, d_got = d_steps[-1]
    g_o = to_sequence(after(cotangent, q_steps[2]))
    g_t = net.core(g_o)

    doc = jnp.concatenate([a[:, cols, :cols].reshape(-1) for a in (x_o, x_t, x_n, x_m)])
    doc = doc.astype(F32)
    row, col = doc[None, :mine], doc[:, None]
    smalls = jnp.concatenate([q_held[:, 6 * rows : 6 * rows + 2], q_got[:, 6 * rows : 6 * rows + 2]])
    smalls = smalls.reshape(devices, half_w)[:, : small.shape[0]]
    vec = jnp.sum(jnp.where(pick_in, dot(smalls, hot_in), 0.0), axis=0, keepdims=True)

    dma = lambda *n: pltpu.SemaphoreType.DMA(n)
    vm = lambda shape, dtype: pltpu.VMEM(shape, dtype)
    by_pair = lambda n: (PAIRS, n, DOUBLE)
    a1, unit1, q, k, v, o, low, lse, w_mix = run(
        attend_kernel,
        inv,
        (x_o, x_t, x_n, x_m, row, col, vec, pi, q_held, q_got),
        (
            ((keys, width), BF),
            ((keys, width), BF),
            (by_pair(mine), BF),
            (by_pair(keys), BF),
            (by_pair(keys), BF),
            (by_pair(mine), F32),
            (by_pair(mine), BF),
            ((PAIRS, 8, mine), F32),
            ((3, width, half_w), BF),
        ),
        [
            vm((keys, width), BF),
            vm((3, width, half_w), BF),
            vm((keys, mine), F32),
            vm((keys, mine), F32),
            vm((keys, mine), BF),
            dma(chips, 3),
        ],
        anys=(8, 9),
    )
    part, wo = run(
        project_kernel,
        inv,
        (low, perm, u_held, u_got),
        (((mine, width), BF), ((half_w, width), BF)),
        [vm((chips * 32, width), BF), dma(chips)],
        anys=(2, 3),
    )
    part_got = net.core(part)
    blocks = ((half, 96, width), BF)
    mid, a2, act, fac, w_up, keep_d, send_d, g_sum = run(
        middle_kernel,
        inv,
        (part, part_got, x_o, x_t, g_o, g_t, vec, pi, u_held, u_got),
        (
            ((mine, width), F32),
            ((mine, width), BF),
            ((mine, half_f), BF),
            ((mine, half_f), F32),
            ((width, half_f), BF),
            blocks,
            blocks,
            ((1, width), F32),
        ),
        [
            vm((mine, width), BF),
            vm((width, half_f), BF),
            vm((half_f, width), BF),
            dma(chips, 2),
        ],
        anys=(8, 9),
    )

    def scatter(keep, send):
        for stage in reversed(range(net.stages)):
            got = net.across(send, stage)
            if stage == 0:
                return (keep.astype(F32) + got.astype(F32))[0]
            n = keep.shape[0] // 2
            send = (keep[n:].astype(F32) + got[n:].astype(F32)).astype(BF)
            keep = (keep[:n].astype(F32) + got[:n].astype(F32)).astype(BF)

    pre, e2, w_down, pre_sum = run(
        slope_kernel,
        inv,
        (g_o, g_t, fac, w_up, pi, d_held, d_got),
        (
            ((mine, half_f), BF),
            ((mine, width), BF),
            ((half_f, width), BF),
            ((1, half_f), F32),
        ),
        [vm((half_f, width), BF), dma(chips, 1)],
        anys=(5, 6),
    )
    e2_got = net.core(e2)
    keep_u, send_u, down_own, down_give = run(
        update_kernel,
        inv,
        (a2, pre, act, w_down),
        (blocks, blocks, ((own, width), F32), ((own, width), BF)),
        [vm((width, half_f), BF)],
    )
    shard_d = scatter(keep_d, send_d)
    shard_u = scatter(keep_u, send_u)
    down_got = net.core(down_give).astype(F32)
    out_own = (mid[:own] + down_own + down_got + vec[:, AT["bias_down"]]).astype(BF)
    block_out = from_sequence(out_own.reshape(local, cols, width))

    wide_sum, half_sum = ((1, width), F32), ((1, half_w), F32)
    quarter = ((2, own, width), BF)
    gm, branch, dq, dk, dv, keep_e, give_e, e2n, e2s, bs, dqs, dvs, e1n, e1s = run(
        back_kernel,
        None,
        (e2, e2_got, mid, g_o, g_t, vec, wo, q, k, v, o, lse, row, col, w_mix, unit1, pi),
        (
            ((own, width), F32),
            ((mine, width), BF),
            (by_pair(mine), BF),
            (by_pair(keys), BF),
            (by_pair(keys), BF),
            quarter,
            quarter,
            wide_sum,
            wide_sum,
            wide_sum,
            half_sum,
            half_sum,
            wide_sum,
            wide_sum,
        ),
        [vm(by_pair(mine), BF), vm((keys, mine), BF), vm((keys, mine), BF)],
    )
    got_e = net.core(give_e)
    e1_near = (keep_e[1].astype(F32) + got_e[1].astype(F32)).astype(BF)
    e1_near = net.pair(e1_near).astype(F32)

    sums = jnp.concatenate([e1n, e2n, e2s, dqs, bs, g_sum, pre_sum, e1s, dvs], axis=1)
    sums = dots(jnp.where(pick_out, sums, 0.0).astype(BF), hot_out, 1, 1).astype(BF)
    sums = jnp.pad(
        sums.reshape(chips, 2, -1), ((0, 0), (0, 14), (0, half_w - sums.shape[-1]))
    )
    blocks_q = ((half, 224, half_w), BF)
    keep_q, send_q = run(
        gather_grads_kernel,
        inv,
        (a1, dq, dk, dv, low, branch, perm, sums),
        (blocks_q, blocks_q),
        [vm((3, width, half_w), BF), vm((chips * 32, width), BF)],
    )
    shard_q = scatter(keep_q, send_q)

    e1 = keep_e[0].astype(F32) + got_e[0].astype(F32) + e1_near
    x_own = x_o[:, :cols].reshape(own, width).astype(F32)
    unit_own, inverse_own = normal(x_own)
    in_own = gm + norm_back(e1, unit_own, inverse_own, vec[:, AT["gain1"]])
    input_grad = from_sequence(in_own.astype(BF).reshape(local, cols, width)).astype(F32)

    def own_rows(chip):
        keep = jnp.where(core == 0, chip[..., 0, :, :], chip[..., 1, :, :])
        give = jnp.where(core == 0, chip[..., 1, :, :], chip[..., 0, :, :])
        return keep, net.core(give)

    def merge(keep, got, parts):
        view = lambda array: array.reshape(*array.shape[:-1], parts, 1, -1)
        first = jnp.where(core == 0, view(keep), view(got))
        second = jnp.where(core == 0, view(got), view(keep))
        return jnp.concatenate([first, second], axis=-2).reshape(*keep.shape[:-1], -1)

    qkv_own = merge(*own_rows(shard_q[: 6 * rows].reshape(3, 2, rows, half_w)), net.x)
    g_qkv = jnp.moveaxis(qkv_own, 0, 1).reshape(-1)
    g_out = unfold(shard_q[6 * rows : 6 * rows + 64], 2)[:rows].reshape(-1)
    up_own = merge(*own_rows(unfold(shard_u, 2).reshape(2, rows, half_f)), net.x)
    two = shard_q[6 * rows + 64 : 6 * rows + 66, : 2 * ll + rl]
    keep_s, got_s = own_rows(two.reshape(2, 1, -1))
    own_sums = (keep_s + got_s)[0]
    return (
        block_out,
        input_grad,
        g_qkv,
        g_out,
        up_own.reshape(-1),
        shard_d.reshape(-1),
        own_sums[:ll],
        own_sums[ll : ll + rl],
        own_sums[ll + rl :],
    )


def solution(mesh):
    dp, seq = mesh.shape["dp"], mesh.shape["seq"]
    y = 1 << (((seq.bit_length() - 1) - 1) // 2)
    z = seq // y
    dims = (dp // 2, 2, 4, z // 4, y // 2, 2)
    net = Net(dims)
    inner = Mesh(mesh.devices.reshape(dims), AXES)
    place = ("zh", "zl", "yh", "yl")
    cube = P(("x", "c"), place, None)
    flat = P(AXES)
    rows = D // (2 * net.chips)
    tiles = rows == 24 and net.chips == 16 and net.zl * net.yh == 1
    return jax.shard_map(
        functools.partial(body if tiles else body_any, net),
        mesh=inner,
        in_specs=(cube, P(("x", "c"), place), cube) + (flat,) * 6,
        out_specs=(cube, cube) + (flat,) * 7,
        check_vma=False,
    )
```

```python
import functools
import itertools

import jax
import jax.numpy as jnp
import numpy as np
from jax import lax
from jax.experimental import pallas as pl
from jax.experimental.pallas import tpu as pltpu
from jax.sharding import Mesh
from jax.sharding import PartitionSpec as P

D = 768
FF = 3072
HEADS = 12
HEAD_DIM = 64
EPS = 1e-05
MASKED = -1000000000.0
BF = jnp.bfloat16
F32 = jnp.float32
AXES = ("x", "c", "zh", "zl", "yh", "yl")


class Net:
    def __init__(self, dims):
        self.dims = dims
        self.x, self.c, self.zh, self.zl, self.yh, self.yl = dims
        self.z, self.y = self.zh * self.zl, self.yh * self.yl
        self.chips = self.x * self.z * self.y
        bits = lambda axis, n: [(axis, 1 << b) for b in reversed(range(n.bit_length() - 1))]
        zs, xs, ys = bits("z", self.z), bits("x", self.x), bits("y", self.y)
        self.orders = (zs + xs + ys, zs + ys + xs)
        self.mixed = (xs + zs + ys, ys + zs + xs)
        self.stages = len(self.orders[0])

    def perm(self, move):
        pairs = []
        for at in itertools.product(*(range(n) for n in self.dims)):
            to = move(*at)
            pairs.append(
                (int(np.ravel_multi_index(at, self.dims)), int(np.ravel_multi_index(to, self.dims)))
            )
        return pairs

    def flip(self, stage, orders):
        def move(x, c, zh, zl, yh, yl):
            axis, bit = orders[c][stage]
            z, y = zh * self.zl + zl, yh * self.yl + yl
            if axis == "x":
                x ^= bit
            elif axis == "y":
                y ^= bit
            else:
                z ^= bit
            return (x, c, z // self.zl, z % self.zl, y // self.yl, y % self.yl)

        return self.perm(move)

    def across(self, value, stage, orders=None):
        return lax.ppermute(value, AXES, self.flip(stage, orders or self.orders))

    def core(self, value):
        return lax.ppermute(value, "c", [(0, 1), (1, 0)])

    def pair(self, value):
        return lax.ppermute(value, "yl", [(0, 1), (1, 0)])

    def scatter_move(self, k):
        return self.perm(
            lambda x, c, zh, zl, yh, yl: (x, zh >> 1, 2 * c + (k ^ (zh & 1)), zl, yh, yl)
        )

    def table(self, orders=None):
        me = {
            "x": lax.axis_index("x"),
            "z": lax.axis_index("zh") * self.zl + lax.axis_index("zl"),
            "y": lax.axis_index("yh") * self.yl + lax.axis_index("yl"),
        }
        grid = np.indices((self.x, self.z, self.y)).reshape(3, -1)
        axes = {"x": grid[0], "z": grid[1], "y": grid[2]}
        places = []
        for order in orders or self.orders:
            place = jnp.zeros((self.chips,), jnp.int32)
            for stage, (axis, bit) in enumerate(order):
                differs = (jnp.asarray(axes[axis], jnp.int32) ^ me[axis]) & bit
                place = place + jnp.where(differs != 0, 1 << stage, 0)
            places.append(place)
        return jnp.where(lax.axis_index("c") == 0, places[0], places[1]).astype(jnp.int32)

    def gather(self, block):
        held = block[None]
        for stage in range(self.stages):
            held = jnp.concatenate([held, self.across(held, stage)])
        return held

    def scatter(self, held):
        for stage in reversed(range(self.stages)):
            half = held.shape[0] // 2
            got = self.across(held[half:], stage)
            held = held[:half].astype(F32) + got.astype(F32)
            if stage:
                held = held.astype(BF)
        return held[0]


def move_kernel(table, source, target):
    target[...] = source[...]


def reorder(blocks, table, to_place):
    rest = -blocks.shape[1] % 16
    if rest:
        rows = blocks.shape[1]
        blocks = jnp.pad(blocks, ((0, 0), (0, rest), (0, 0)))
        return reorder(blocks, table, to_place)[:, :rows]
    chips, rows, cols = blocks.shape
    here = pl.BlockSpec((1, rows, cols), lambda chip, table: (chip, 0, 0))
    there = pl.BlockSpec((1, rows, cols), lambda chip, table: (table[chip], 0, 0))
    return pl.pallas_call(
        move_kernel,
        grid_spec=pltpu.PrefetchScalarGridSpec(
            num_scalar_prefetch=1,
            grid=(chips,),
            in_specs=[here if to_place else there],
            out_specs=there if to_place else here,
        ),
        out_shape=jax.ShapeDtypeStruct(blocks.shape, blocks.dtype),
    )(table, blocks)


def normal(field):
    center = field - jnp.mean(field, axis=-1, keepdims=True)
    inverse = lax.rsqrt(jnp.mean(center * center, axis=-1, keepdims=True) + EPS)
    return center * inverse, inverse


def norm_back(upstream, unit, inverse, gain):
    scaled = upstream * gain
    return inverse * (
        scaled
        - jnp.mean(scaled, axis=-1, keepdims=True)
        - unit * jnp.mean(scaled * unit, axis=-1, keepdims=True)
    )


def dot(a, b):
    return jnp.dot(a, b, preferred_element_type=F32)


def dot_t(a, b):
    return lax.dot_general(a, b, (((1,), (1,)), ((), ())), preferred_element_type=F32)


def t_dot(a, b):
    return lax.dot_general(a, b, (((0,), (0,)), ((), ())), preferred_element_type=F32)


def fold(wide, parts):
    lead, rows, cols = wide.shape[:-2], wide.shape[-2], wide.shape[-1] // parts
    moved = jnp.moveaxis(wide.reshape(*lead, rows, parts, cols), -2, -3)
    return moved.reshape(*lead, parts * rows, cols)


def unfold(tall, parts):
    lead, rows, cols = tall.shape[:-2], tall.shape[-2] // parts, tall.shape[-1]
    moved = jnp.moveaxis(tall.reshape(*lead, parts, rows, cols), -3, -2)
    return moved.reshape(*lead, rows, parts * cols)


def body_any(net, tokens, segments, cotangent, w_qkv, w_out, w_fc1, w_fc2, norm_gains, bias_pack):
    local, cols, width = tokens.shape
    own = local * cols
    mine = 2 * own
    hidden = FF
    half_w, half_f = width // 2, hidden // 2
    devices = 2 * net.chips
    core = lax.axis_index("c")
    zodd = lax.axis_index("zh") & 1
    table = net.table()
    rows = width // devices
    frows = hidden // devices
    aligned = (width // (2 * net.x)) % HEAD_DIM == 0
    groups = net.x if aligned else 1

    def pick(array, parts, which):
        split = array.reshape(*array.shape[:-1], parts, 2, array.shape[-1] // (2 * parts))
        taken = jnp.where(which == 0, split[..., 0, :], split[..., 1, :])
        return taken.reshape(*array.shape[:-1], array.shape[-1] // 2)

    def spread(vector, parts):
        split = vector.reshape(parts, 1, vector.shape[-1] // parts)
        both = jnp.concatenate(
            [jnp.where(core == 0, split, 0.0), jnp.where(core == 1, split, 0.0)], axis=1
        )
        return both.reshape(-1)

    seg_row = jnp.pad(segments.astype(BF), ((0, 0), (0, width - cols)))[:, None, :]
    seg_rows = jnp.pad(seg_row, ((0, 0), (0, 7), (0, 0)))
    packed = jnp.concatenate([tokens, seg_rows], axis=1)

    def to_sequence(array):
        swapped = jnp.where(zodd == 0, array, array[::-1])
        return jnp.stack(
            [lax.ppermute(swapped[k], AXES, net.scatter_move(k)) for k in range(2)]
        )

    def from_sequence(array):
        back = jnp.stack(
            [
                lax.ppermute(array[k], AXES, [(b, a) for a, b in net.scatter_move(k)])
                for k in range(2)
            ]
        )
        return jnp.where(zodd == 0, back, back[::-1])

    def halves(which):
        qkv = fold(w_qkv.reshape(rows, 3 * width), 3).reshape(3, rows, width)
        up = w_fc1.reshape(rows, hidden)
        return pick(qkv, groups, which), pick(up, net.x, which)

    keep_qkv, keep_up = halves(core)
    give_qkv, give_up = halves(1 - core)
    small = jnp.concatenate([norm_gains, bias_pack])
    out_rows = w_out.reshape(rows, width)
    got_qkv, got_up, got_small, got_out = jax.tree.map(
        net.core, (give_qkv, give_up, small, out_rows)
    )

    def both(a, b, axis):
        return jnp.where(
            core == 0, jnp.concatenate([a, b], axis=axis), jnp.concatenate([b, a], axis=axis)
        )

    chip_qkv = both(keep_qkv, got_qkv, 1).reshape(6 * rows, half_w)
    chip_up = fold(both(keep_up, got_up, 0), 2)
    chip_out = fold(out_rows if aligned else both(out_rows, got_out, 0), 2)
    chip_small = jnp.pad(
        both(small[None], got_small[None], 0), ((0, 14), (0, half_w - small.shape[0]))
    )
    cut = np.cumsum([chip_qkv.shape[0], chip_out.shape[0]])
    blocks_a = reorder(
        net.gather(jnp.concatenate([chip_qkv, chip_out, chip_small])), table, False
    )
    blocks_up = reorder(net.gather(chip_up), table, False)
    blocks_down = reorder(net.gather(w_fc2.reshape(frows, width)), table, False)

    lead = (net.x, net.z, net.y)

    def natural(blocks):
        n = blocks.shape[-1]
        return jnp.moveaxis(blocks.reshape(*lead, 2, -1, n), 3, 1).reshape(-1, n)

    def by_chip(array):
        n = array.shape[-1]
        return jnp.moveaxis(array.reshape(net.x, 2, net.z, net.y, -1, n), 1, 3).reshape(
            net.chips, -1, n
        )

    qkv_blocks = blocks_a[:, : cut[0]].reshape(net.chips, 3, 2 * rows, half_w)
    w_q, w_k, w_v = (natural(qkv_blocks[:, i]) for i in range(3))
    out_blocks = unfold(blocks_a[:, cut[0] : cut[1]], 2)
    if aligned:
        w_proj = out_blocks.reshape(half_w, width)
    else:
        w_proj = lax.dynamic_slice_in_dim(natural(out_blocks), core * half_w, half_w)
    smalls = blocks_a[:, cut[1] : cut[1] + 2, : small.shape[0]].reshape(*lead, 2, -1)
    smalls = jnp.moveaxis(smalls, 3, 1).reshape(devices, -1).astype(F32)
    n_gain = norm_gains.shape[0]
    gains = smalls[:, :n_gain].reshape(-1)
    shifts = smalls[:, n_gain:].reshape(-1)
    w_up = natural(unfold(blocks_up, 2))
    w_down = blocks_down.reshape(half_f, width)
    gain1, gain2 = gains[:width], gains[width:]
    shift1, shift2, bias_q, bias_v, bias_proj, bias_down = (
        shifts[i * width : (i + 1) * width] for i in range(6)
    )
    bias_up = pick(shifts[6 * width :], net.x, core)
    bias_q, bias_v = pick(bias_q, groups, core), pick(bias_v, groups, core)

    x_own = to_sequence(packed)
    x_other = net.core(x_own)
    x_mine = jnp.concatenate([x_own, x_other])
    near = net.pair(x_own)
    near = jnp.concatenate([near, net.core(near)])
    x_seq = jnp.concatenate([x_mine, near])
    if net.zl * net.yh > 1:
        x_far = lax.all_gather(x_seq, ("zl", "yh"), axis=0, tiled=True)
        x_keys = x_far
    else:
        x_keys = x_seq
    g_own = to_sequence(cotangent)
    g_mine = jnp.concatenate([g_own, net.core(g_own)]).reshape(mine, width)
    docs = x_keys[:, cols, :cols].reshape(-1)
    query_docs = x_mine[:, cols, :cols].reshape(-1)
    x_all = x_keys[:, :cols].reshape(-1, width).astype(F32)
    x_q = x_mine[:, :cols].reshape(-1, width).astype(F32)

    unit_q, inverse_q = normal(x_q)
    a_q = (unit_q * gain1 + shift1).astype(BF)
    unit_all, _ = normal(x_all)
    a_all = (unit_all * gain1 + shift1).astype(BF)
    heads = HEADS // 2
    q = (dot(a_q, w_q) + bias_q).astype(BF)
    k = dot(a_all, w_k).astype(BF)
    v = (dot(a_all, w_v) + bias_v).astype(BF)
    by_head = lambda t: t.reshape(-1, heads, HEAD_DIM)
    same = (query_docs[:, None] == docs[None, :])[None]
    scores = (
        jnp.einsum("qhd,khd->hqk", by_head(q), by_head(k), preferred_element_type=F32) * 0.125
    )
    scores = jnp.where(same, scores, MASKED)
    weights = jnp.exp(scores - jnp.max(scores, axis=-1, keepdims=True))
    probs = weights / jnp.sum(weights, axis=-1, keepdims=True)
    probs_low = probs.astype(BF)
    att = jnp.einsum("hqk,khd->qhd", probs_low, by_head(v), preferred_element_type=F32)
    att = att.reshape(mine, half_w)
    att_low = att.astype(BF)

    def core_sum(partial):
        low = partial.astype(BF)
        got = net.core(low)
        return low.astype(F32) + jnp.concatenate([got[own:], got[:own]]).astype(F32)

    middle = x_q + core_sum(dot(att_low, w_proj)) + bias_proj
    unit2, inverse2 = normal(middle)
    a2 = (unit2 * gain2 + shift2).astype(BF)
    pre = dot(a2, w_up) + bias_up
    sig = jax.nn.sigmoid(1.702 * pre)
    activ = (pre * sig).astype(BF)
    down = dot(activ, w_down)
    down_got = net.core(down[own:].astype(BF)).astype(F32)
    out_own = (middle[:own] + down[:own] + down_got + bias_down).astype(BF)
    block_out = from_sequence(out_own.reshape(local, cols, width))

    grad_down = t_dot(activ, g_mine).astype(BF)
    grad_pre = (dot_t(g_mine, w_down) * (sig + 1.702 * pre * sig * (1.0 - sig))).astype(BF)
    shard_down = net.scatter(reorder(grad_down.reshape(net.chips, frows, width), table, True))
    grad_up = t_dot(a2, grad_pre).astype(BF)
    shard_up = net.scatter(reorder(fold(by_chip(grad_up), 2), table, True))
    e2 = core_sum(dot_t(grad_pre, w_up))
    grad_middle = g_mine.astype(F32) + norm_back(e2, unit2, inverse2, gain2)
    branch = grad_middle.astype(BF)
    grad_proj = t_dot(att_low, branch).astype(BF)
    d_heads = dot_t(branch, w_proj).astype(BF)
    dp = jnp.einsum("qhd,khd->hqk", by_head(d_heads), by_head(v), preferred_element_type=F32)
    delta = jnp.sum(probs * dp, axis=-1, keepdims=True)
    d_scores = (probs * (dp - delta)).astype(BF)
    dq = 0.125 * jnp.einsum("hqk,khd->qhd", d_scores, by_head(k), preferred_element_type=F32)
    dk = 0.125 * jnp.einsum("hqk,qhd->khd", d_scores, by_head(q), preferred_element_type=F32)
    dv = jnp.einsum("hqk,qhd->khd", probs_low, by_head(d_heads), preferred_element_type=F32)
    dq = dq.reshape(-1, half_w).astype(BF)
    dk = dk.reshape(-1, half_w).astype(BF)
    dv = dv.reshape(-1, half_w).astype(BF)
    grad_qkv = jnp.stack([t_dot(a_q, dq), t_dot(a_all, dk), t_dot(a_all, dv)]).astype(BF)

    e1_keys = (dot_t(dk, w_k) + dot_t(dv, w_v)).astype(BF)
    if net.zl * net.yh > 1:
        e1_keys = lax.psum_scatter(
            e1_keys, ("zl", "yh"), scatter_dimension=0, tiled=True
        )
    e1_near = e1_keys[mine:].reshape(2, own, width)
    e1_mine = e1_keys[:mine].astype(F32) + dot_t(dq, w_q)
    e1_mine = e1_mine.astype(BF).reshape(2, own, width)
    got = net.core(jnp.stack([e1_mine[1], e1_near[1]]))
    e1_near = e1_near[0].astype(F32) + got[1].astype(F32)
    e1 = e1_mine[0].astype(F32) + got[0].astype(F32) + net.pair(e1_near.astype(BF)).astype(F32)
    unit1 = unit_q[:own]
    in_own = grad_middle[:own] + norm_back(e1, unit1, inverse_q[:own], gain1)
    input_grad = from_sequence(in_own.astype(BF).reshape(local, cols, width)).astype(F32)

    total = lambda array: jnp.sum(array.astype(F32), axis=0)
    g_own = g_mine[:own]
    gain_sums = jnp.concatenate([total(e1 * unit1), total(e2[:own] * unit2[:own])])
    bias_sums = jnp.concatenate(
        [
            total(e2[:own]),
            spread(total(dq), groups),
            total(branch[:own]),
            total(g_own),
            spread(total(grad_pre), net.x),
        ]
    )
    lead_sums = jnp.concatenate([total(e1), spread(total(dv), groups)])
    sums = jnp.concatenate(
        [v.reshape(devices, -1) for v in (gain_sums, bias_sums, lead_sums)], axis=1
    )
    sums = sums + net.core(sums)
    sums = jnp.moveaxis(sums.reshape(net.x, 2, net.z, net.y, -1), 1, 0)
    sums = jnp.where(core == 0, sums[0], sums[1]).reshape(net.chips, 1, -1)
    n_sums = sums.shape[-1]
    sums = jnp.pad(sums, ((0, 0), (0, 15), (0, half_w - n_sums))).astype(BF)
    qkv_send = jnp.stack([by_chip(grad_qkv[i]) for i in range(3)], axis=1)
    qkv_send = qkv_send.reshape(net.chips, 6 * rows, half_w)
    if aligned:
        out_send = grad_proj.reshape(net.chips, rows, width)
    else:
        whole = jnp.zeros((width, width), BF)
        whole = lax.dynamic_update_slice(whole, grad_proj, (core * half_w, 0))
        out_send = by_chip(whole)
    sent = jnp.concatenate([qkv_send, fold(out_send, 2), sums], axis=1)
    shard_a = net.scatter(reorder(sent, table, True))

    def own_rows(chip):
        keep = jnp.where(core == 0, chip[..., 0, :, :], chip[..., 1, :, :])
        give = jnp.where(core == 0, chip[..., 1, :, :], chip[..., 0, :, :])
        return keep, net.core(give)

    def merge(keep, got, parts):
        split = lambda array: array.reshape(*array.shape[:-1], parts, 1, -1)
        first = jnp.where(core == 0, split(keep), split(got))
        second = jnp.where(core == 0, split(got), split(keep))
        return jnp.concatenate([first, second], axis=-2).reshape(*keep.shape[:-1], -1)

    qkv_own = merge(*own_rows(shard_a[: cut[0]].reshape(3, 2, rows, half_w)), groups)
    g_qkv = jnp.moveaxis(qkv_own, 0, 1).reshape(-1)
    out_own = unfold(shard_a[cut[0] : cut[1]], 2)
    if not aligned:
        keep, got = own_rows(out_own.reshape(2, rows, width))
        out_own = keep + got
    g_out = out_own.reshape(-1)
    up_own = merge(*own_rows(unfold(shard_up, 2).reshape(2, rows, half_f)), net.x)
    own_sums = shard_a[cut[1], :n_sums]
    n_gain = 2 * width // devices
    n_lead = n_sums - n_gain
    return (
        block_out,
        input_grad,
        g_qkv,
        g_out,
        up_own.reshape(-1),
        shard_down.reshape(-1),
        own_sums[:n_gain],
        own_sums[n_gain:n_lead],
        own_sums[n_lead:],
    )


SLAB = 128
PAIRS = HEADS // 4
DOUBLE = 2 * HEAD_DIM
PARTS = (
    ("gain1", D),
    ("gain2", D),
    ("shift1", D),
    ("shift2", D),
    ("bias_proj", D),
    ("bias_down", D),
    ("bias_q", D // 2),
    ("bias_v", D // 2),
    ("bias_up", FF // 2),
)
SUMS = (
    ("e1n", D),
    ("e2n", D),
    ("e2", D),
    ("dq", D // 2),
    ("branch", D),
    ("g", D),
    ("pre", FF // 2),
    ("e1", D),
    ("dv", D // 2),
)


def offsets(parts):
    ends = np.cumsum([n for _, n in parts])
    return {name: slice(int(end - n), int(end)) for (name, n), end in zip(parts, ends)}


AT = offsets(PARTS)


def dots(a, b, ca, cb):
    return lax.dot_general(a, b, (((ca,), (cb,)), ((), ())), preferred_element_type=F32)


def lane_half(e):
    lanes = lax.broadcasted_iota(jnp.int32, (1, DOUBLE), 1)
    inside = (lanes < HEAD_DIM) if e == 0 else (lanes >= HEAD_DIM)
    return inside.astype(F32).astype(BF)


def first_half(shape):
    return lax.broadcasted_iota(jnp.int32, shape, 1) < HEAD_DIM


def load_rows(inv, held, got, target, sems, pieces):
    half = held.shape[0]
    copies = []
    for r in range(2 * half):
        source = held if r < half else got
        for n, (first, rows, place) in enumerate(pieces):
            copies.append(
                pltpu.make_async_copy(
                    source.at[r % half, pl.ds(first, rows), :],
                    place(target, inv[r], rows),
                    sems.at[r, n],
                )
            )
    for copy in copies:
        copy.start()
    return copies


def one_hot(place, target):
    step = 128
    for i in range(target.shape[0] // step):
        shape = (step, target.shape[1])
        entry = lax.broadcasted_iota(jnp.int32, shape, 0) + i * step
        target[i * step : (i + 1) * step, :] = (entry == place[:1, :]).astype(F32).astype(BF)


def unit_kernel(xo, xt, xn, xm, place, unit_ref, col_ref, row_ref, hot_ref):
    one_hot(place, hot_ref)
    for i, (ref, j) in enumerate((ref, j) for ref in (xo, xt, xn, xm) for j in range(2)):
        unit, _ = normal(ref[j, :SLAB, :].astype(F32))
        at = pl.ds(i * SLAB, SLAB)
        unit_ref[at, :] = unit
        docs = ref[j, SLAB : SLAB + 8, :SLAB].astype(F32)[:1]
        col_ref[at, :] = jnp.broadcast_to(docs, (SLAB, SLAB)).T
        if i < 4:
            row_ref[:, i * SLAB : (i + 1) * SLAB] = jnp.broadcast_to(docs, (8, SLAB))


def fill_bias(col, row, bias):
    for i in range(bias.shape[0] // SLAB):
        at = pl.ds(i * SLAB, SLAB)
        for j in range(bias.shape[1] // SLAB):
            lanes = pl.ds(j * SLAB, SLAB)
            bias[at, lanes] = jnp.where(col[at, :] == row[:1, lanes], 0.0, MASKED)


def pick_rows(rows, step):
    shape = (2 * rows // step, rows)
    i = lax.broadcasted_iota(jnp.int32, shape, 0)
    j = lax.broadcasted_iota(jnp.int32, shape, 1)
    return (j == (i >> 1) * step + (i & 1)).astype(F32).astype(BF)


def mix_kernel(
    inv, unit, pi, device, owner, hot, held, got,
    a_ref, q_ref, k_ref, v_ref, w, vec, nat, small, sems, small_sems,
):
    half = held.shape[0]
    few = []
    for r in range(2 * half):
        source = held if r < half else got
        few.append(
            pltpu.make_async_copy(
                source.at[r % half, pl.ds(144, 16), :], small.at[pl.ds(r * 16, 16), :], small_sems.at[r]
            )
        )
    for copy in few:
        copy.start()
    place = lambda i: lambda t, chip, n: t.at[i, pl.ds(pl.multiple_of(chip * n, 16), n), :]
    copies = load_rows(inv, held, got, w, sems, [(48 * i, 48, place(i)) for i in range(3)])
    for copy in few:
        copy.wait()
    picked = dot(pick_rows(small.shape[0], 16), small[...]).astype(BF)
    mine_only = jnp.where(device[:, :1] == owner[:1, :], dot(picked, hot[...]), 0.0)
    vec[...] = jnp.sum(mine_only, axis=0, keepdims=True)
    keys = a_ref.shape[0]
    for i in range(keys // SLAB):
        at = pl.ds(i * SLAB, SLAB)
        nat[at, :] = (unit[at, :] * vec[:, AT["gain1"]] + vec[:, AT["shift1"]]).astype(BF)
    a_ref[...] = dot(nat[...], pi[...]).astype(BF)
    for copy in copies:
        copy.wait()
    mine = q_ref.shape[1]
    q = (dot(a_ref[:mine, :], w[0]) + vec[:, AT["bias_q"]]).astype(BF) * 0.125
    k = dot(a_ref[...], w[1]).astype(BF)
    v = (dot(a_ref[...], w[2]) + vec[:, AT["bias_v"]]).astype(BF)
    for i in range(PAIRS):
        lanes = slice(i * DOUBLE, (i + 1) * DOUBLE)
        q_ref[i], k_ref[i], v_ref[i] = q[:, lanes], k[:, lanes], v[:, lanes]


def attend_kernel(q_ref, k_ref, v_ref, col, row, o_ref, low_ref, lse_ref, bias, s, p_low):
    mine, keys = q_ref.shape[1], k_ref.shape[1]
    fill_bias(col, row, bias)

    def pair(i, carry):
        outs = []
        for e in range(2):
            qm = q_ref[i] * lane_half(e)
            top = jnp.full((1, mine), -3e38, F32)
            for c in range(keys // SLAB):
                at = pl.ds(c * SLAB, SLAB)
                t = dots(k_ref[i, at, :], qm, 1, 1) + bias[at, :]
                s[at, :] = t
                top = jnp.maximum(top, jnp.max(t, axis=0, keepdims=True))
            total = jnp.zeros((1, mine), F32)
            for c in range(keys // SLAB):
                at = pl.ds(c * SLAB, SLAB)
                p = jnp.exp(s[at, :] - top)
                total = total + jnp.sum(p, axis=0, keepdims=True)
                p_low[at, :] = p.astype(BF)
            lse_ref[i, e : e + 1, :] = top + jnp.log(total)
            o = dots(p_low[...], v_ref[i], 0, 0)
            scale = jnp.broadcast_to(1.0 / total, (DOUBLE, mine)).T
            outs.append(o * scale)
        o = jnp.where(first_half(outs[0].shape), outs[0], outs[1])
        o_ref[i] = o
        low_ref[i] = o.astype(BF)
        return carry

    lax.fori_loop(0, PAIRS, pair, 0)


def project_kernel(inv, low, perm, held, got, part_ref, wo_ref, rel, sems):
    half = held.shape[0]
    copies = []
    for r in range(2 * half):
        source = held if r < half else got
        copies.append(
            pltpu.make_async_copy(
                source.at[r % half, pl.ds(96, 32), :], rel.at[pl.ds(r * 32, 32), :], sems.at[r]
            )
        )
    for copy in copies:
        copy.start()
    for copy in copies:
        copy.wait()
    wo_ref[...] = dot(perm[...], rel[...]).astype(BF)
    att = jnp.concatenate([low[i] for i in range(PAIRS)], axis=1)
    part_ref[...] = dot(att, wo_ref[...]).astype(BF)


def middle_kernel(
    inv, inv_d, part, part_got, xo, xt, go, gt, vec, pi, held, got,
    mid_ref, a_ref, act_ref, fac_ref, w, keep_ref, send_ref, sum_ref,
    nat, grad, sems,
):
    place = lambda h: lambda t, chip, n: t.at[
        pl.ds(pl.multiple_of(chip * n, 16), n), pl.ds(h * D, D)
    ]
    copies = load_rows(inv, held, got, w, sems, [(48 * h, 48, place(h)) for h in range(2)])
    mine = part.shape[0]
    own = mine // 2
    for i, (ref, j) in enumerate((ref, j) for ref in (xo, xt) for j in range(2)):
        at = pl.ds(i * SLAB, SLAB)
        other = pl.ds((i * SLAB + own) % mine, SLAB)
        mid = (
            ref[j, :SLAB, :].astype(F32)
            + (part[at, :].astype(F32) + part_got[other, :].astype(F32))
            + vec[:, AT["bias_proj"]]
        )
        mid_ref[at, :] = mid
        unit, _ = normal(mid)
        nat[at, :] = (unit * vec[:, AT["gain2"]] + vec[:, AT["shift2"]]).astype(BF)
    a_ref[...] = dot(nat[...], pi[...]).astype(BF)
    g = jnp.concatenate([go[0], go[1], gt[0], gt[1]], axis=0)
    sum_ref[...] = jnp.sum(g[:own].astype(F32), axis=0, keepdims=True)
    for copy in copies:
        copy.wait()
    step = 512
    for j in range(w.shape[1] // step):
        lanes = pl.ds(j * step, step)
        start = AT["bias_up"].start + j * step
        pre = dot(a_ref[...], w[:, lanes]) + vec[:, start : start + step]
        sig = 1.0 / (1.0 + jnp.exp(-1.702 * pre))
        act_ref[:, lanes] = (pre * sig).astype(BF)
        fac_ref[:, lanes] = sig + 1.702 * pre * sig * (1.0 - sig)
        grad[lanes, :] = dots(act_ref[:, lanes], g, 0, 0).astype(BF)
    half = keep_ref.shape[0]
    for r in range(2 * half):
        target = keep_ref if r < half else send_ref
        target[r % half] = grad[pl.ds(pl.multiple_of(inv_d[r] * 96, 16), 96), :]


def slope_kernel(inv, go, gt, fac, w_up, pi, held, got, pre_ref, e_ref, w, sum_ref, sems):
    place = lambda t, chip, n: t.at[pl.ds(pl.multiple_of(chip * n, 16), n), :]
    copies = load_rows(inv, held, got, w, sems, [(0, 96, place)])
    g = jnp.concatenate([go[0], go[1], gt[0], gt[1]], axis=0)
    for copy in copies:
        copy.wait()
    step = 512
    total = None
    for j in range(w.shape[0] // step):
        lanes = pl.ds(j * step, step)
        pre = (dots(g, w[lanes, :], 1, 1) * fac[:, lanes]).astype(BF)
        pre_ref[:, lanes] = pre
        sum_ref[:, lanes] = jnp.sum(pre.astype(F32), axis=0, keepdims=True)
        term = dots(pre, w_up[:, lanes], 1, 1)
        total = term if total is None else total + term
    e_ref[...] = dots(total.astype(BF), pi[...], 1, 1).astype(BF)


def down_kernel(act, w_down, own_ref, give_ref):
    down = dot(act[...], w_down[...])
    own = own_ref.shape[0]
    own_ref[...] = down[:own]
    give_ref[...] = down[own:].astype(BF)


def wide(ref):
    return jnp.concatenate([ref[i] for i in range(PAIRS)], axis=1)


def branch_kernel(
    inv, e2, e2_got, mid, go, gt, vec, wo, low, perm, a, pre,
    gm_ref, branch_ref, d_ref, keep_ref, send_ref, e2n_sum, e2_sum, branch_sum, grad, out,
):
    mine = mid.shape[0]
    own = mine // 2
    sums = [jnp.zeros((1, D), F32) for _ in range(3)]
    for i, (ref, j) in enumerate((ref, j) for ref in (go, gt) for j in range(2)):
        at = pl.ds(i * SLAB, SLAB)
        other = pl.ds((i * SLAB + own) % mine, SLAB)
        e = e2[at, :].astype(F32) + e2_got[other, :].astype(F32)
        unit, inverse = normal(mid[at, :])
        gm = ref[j].astype(F32) + norm_back(e, unit, inverse, vec[:, AT["gain2"]])
        branch = gm.astype(BF)
        branch_ref[at, :] = branch
        if i < 2:
            gm_ref[at, :] = gm
            for n, term in enumerate((e * unit, e, branch.astype(F32))):
                sums[n] = sums[n] + jnp.sum(term, axis=0, keepdims=True)
    e2n_sum[...], e2_sum[...], branch_sum[...] = sums
    d = dots(branch_ref[...], wo[...], 1, 1).astype(BF)
    for i in range(PAIRS):
        d_ref[i] = d[:, i * DOUBLE : (i + 1) * DOUBLE]
    step = 512
    for j in range(pre.shape[1] // step):
        lanes = pl.ds(j * step, step)
        grad[:, lanes] = dots(a[...], pre[:, lanes], 0, 0).astype(BF)
    proj = dots(wide(low), branch_ref[...], 0, 0).astype(BF)
    out[...] = dots(perm[...], proj, 0, 0).astype(BF)
    half = keep_ref.shape[0]
    for r in range(2 * half):
        target, at = (keep_ref if r < half else send_ref), r % half
        rows = pl.ds(pl.multiple_of(inv[r] * 48, 16), 48)
        target[at, :48, :] = grad[rows, :D]
        target[at, 48:96, :] = grad[rows, D:]
        target[at, 96:, :] = out[r * 32 : r * 32 + 32, :]


def attend_back_kernel(
    q, k, v, o, lse, col, row, d_ref, dq_ref, dk_ref, dv_ref, dq_sum, dv_sum, bias, p_low, s_low
):
    mine, keys = q.shape[1], k.shape[1]
    fill_bias(col, row, bias)

    def pair(i, carry):
        both = (d_ref[i].astype(F32) * o[i]).T
        got = []
        for e in range(2):
            delta = jnp.sum(both[e * HEAD_DIM : (e + 1) * HEAD_DIM], axis=0, keepdims=True)
            qm = q[i] * lane_half(e)
            dm = d_ref[i] * lane_half(e)
            base = lse[i, e : e + 1, :]
            for c in range(keys // SLAB):
                at = pl.ds(c * SLAB, SLAB)
                t = dots(k[i, at, :], qm, 1, 1) + bias[at, :]
                p = jnp.exp(t - base)
                dp = dots(v[i, at, :], dm, 1, 1)
                p_low[at, :] = p.astype(BF)
                s_low[at, :] = (p * (dp - delta)).astype(BF)
            got.append(
                (
                    dots(s_low[...], k[i], 0, 0) * 0.125,
                    dot(s_low[...], q[i]),
                    dot(p_low[...], d_ref[i]),
                )
            )
        for n, ref in enumerate((dq_ref, dk_ref, dv_ref)):
            ref[i] = jnp.where(first_half(got[0][n].shape), got[0][n], got[1][n]).astype(BF)
        return carry

    lax.fori_loop(0, PAIRS, pair, 0)
    dq_sum[...] = jnp.sum(wide(dq_ref).astype(F32), axis=0, keepdims=True)
    dv_sum[...] = jnp.sum(wide(dv_ref).astype(F32), axis=0, keepdims=True)


def input_kernel(dq_ref, dk_ref, dv_ref, w, unit, pi, keep_ref, give_ref, e1n_sum, e1_sum):
    keys, own = unit.shape[0], keep_ref.shape[1]
    dq, dk, dv = wide(dq_ref), wide(dk_ref), wide(dv_ref)
    e1n = jnp.zeros((1, D), F32)
    e1s = jnp.zeros((1, D), F32)
    for part in range(keys // own):
        at = slice(part * own, (part + 1) * own)
        e = dots(dk[at], w[1], 1, 1) + dots(dv[at], w[2], 1, 1)
        if part < 2:
            e = e + dots(dq[at], w[0], 1, 1)
        e = dots(e.astype(BF), pi[...], 1, 1)
        e1s = e1s + jnp.sum(e, axis=0, keepdims=True)
        e1n = e1n + jnp.sum(e * unit[pl.ds(part * own, own), :], axis=0, keepdims=True)
        target = keep_ref if part % 2 == 0 else give_ref
        target[part // 2] = e.astype(BF)
    e1n_sum[...] = e1n
    e1_sum[...] = e1s


def gather_grads_kernel(inv, a, dq, dk, dv, device, owner, place, *rest):
    sums, (keep_ref, send_ref, grad, small, hot) = rest[:-5], rest[-5:]
    one_hot(place, hot)
    mine = dq.shape[1]
    grad[0] = dots(a[:mine, :], wide(dq), 0, 0).astype(BF)
    grad[1] = dots(a[...], wide(dk), 0, 0).astype(BF)
    grad[2] = dots(a[...], wide(dv), 0, 0).astype(BF)
    line = jnp.concatenate([ref[...] for ref in sums], axis=1)
    kept = jnp.where(device[:, :1] == owner[:1, :], line, 0.0).astype(BF)
    placed = dots(kept, hot[...], 1, 1).astype(BF)
    small[...] = dots(pick_rows(small.shape[0], 16), placed, 0, 0).astype(BF)
    half = keep_ref.shape[0]
    for r in range(2 * half):
        target, at = (keep_ref if r < half else send_ref), r % half
        rows = pl.ds(pl.multiple_of(inv[r] * 48, 16), 48)
        for i in range(3):
            target[at, 48 * i : 48 * i + 48, :] = grad[i, rows, :]
        target[at, 144:160, :] = small[r * 16 : r * 16 + 16, :]


def run(kernel, table, args, outs, scratch, anys=(), us=5, mib=16):
    specs = [
        pl.BlockSpec(memory_space=pl.ANY) if i in anys else pl.BlockSpec(memory_space=pltpu.VMEM)
        for i in range(len(args))
    ]
    prefetch = () if table is None else table if isinstance(table, tuple) else (table,)
    return pl.pallas_call(
        kernel,
        grid_spec=pltpu.PrefetchScalarGridSpec(
            num_scalar_prefetch=len(prefetch),
            grid=(),
            in_specs=specs,
            out_specs=[pl.BlockSpec(memory_space=pltpu.VMEM) for _ in outs],
            scratch_shapes=scratch,
        ),
        out_shape=[jax.ShapeDtypeStruct(shape, dtype) for shape, dtype in outs],
        compiler_params=pltpu.CompilerParams(vmem_limit_bytes=mib * 2**20),
        cost_estimate=pl.CostEstimate(
            flops=us * 10**9, bytes_accessed=us * 10**6, transcendentals=0
        ),
    )(*prefetch, *args)


def body(net, tokens, segments, cotangent, w_qkv, w_out, w_fc1, w_fc2, norm_gains, bias_pack):
    local, cols, width = tokens.shape
    own, mine = local * cols, 2 * local * cols
    keys = 2 * mine
    hidden = FF
    half_w, half_f = width // 2, hidden // 2
    chips, devices = net.chips, 2 * net.chips
    half = chips // 2
    rows, frows = width // devices, hidden // devices
    core = lax.axis_index("c")
    zodd = lax.axis_index("zh") & 1
    spots = jnp.arange(chips, dtype=jnp.int32)

    def order_of(orders):
        found = net.table(orders)[None, :] == spots[:, None]
        return jnp.sum(jnp.where(found, spots[None, :], 0), axis=1).astype(jnp.int32)

    inv, inv_d = order_of(net.orders), order_of(net.mixed)

    split = lambda n, parts: np.arange(n).reshape(parts, 2, n // (2 * parts))
    of_core = lambda n, parts: [split(n, parts)[:, c].reshape(-1) for c in range(2)]
    everywhere = lambda n: [np.arange(n)] * 2
    n_gain, n_bias = norm_gains.shape[0], bias_pack.shape[0]

    def owners(items):
        dev, place = [], []
        for c in range(2):
            flat = [(first + entry[c]) for first, entry, _, _ in items]
            dev.append(np.concatenate([f // n for f, (_, _, _, n) in zip(flat, items)]))
            place.append(
                np.concatenate([at + f % n for f, (_, _, at, n) in zip(flat, items)])
            )
        dev, place = np.array(dev, np.int32), np.array(place, np.int32)
        return (
            jnp.where(core == 0, dev[0], dev[1]),
            jnp.where(core == 0, place[0], place[1]),
        )

    chip_row = jnp.repeat(inv, 2)
    s_n = net.z * net.y
    row_device = ((chip_row // s_n) * 2 + jnp.tile(jnp.arange(2), chips)) * s_n + chip_row % s_n
    row_device = jnp.broadcast_to(row_device[:, None], (devices, SLAB))
    D_, W = everywhere(width), width

    def mapping(items):
        dev, place = owners(items)
        return dev[None, :], place[None, :]

    gl, bl = n_gain, n_bias
    heads_c, ff_c = of_core(width, net.x), of_core(hidden, net.x)
    owner_in, place_in = mapping(
        [
            (0, D_, 0, gl),
            (W, D_, 0, gl),
            (0, D_, gl, bl),
            (W, D_, gl, bl),
            (4 * W, D_, gl, bl),
            (5 * W, D_, gl, bl),
            (2 * W, heads_c, gl, bl),
            (3 * W, heads_c, gl, bl),
            (6 * W, ff_c, gl, bl),
        ]
    )
    ll = 2 * W // devices
    rl = n_gain + n_bias - 2 * ll
    owner_out, place_out = mapping(
        [
            (0, D_, 0, ll),
            (W, D_, 0, ll),
            (0, D_, ll, rl),
            (W, heads_c, ll, rl),
            (2 * W, D_, ll, rl),
            (3 * W, D_, ll, rl),
            (4 * W, ff_c, ll, rl),
            (0, D_, ll + rl, ll),
            (W, heads_c, ll + rl, ll),
        ]
    )
    order = np.arange(width).reshape(net.x, 2, s_n, rows).transpose(0, 2, 1, 3).reshape(-1)
    pi = jnp.asarray((np.arange(width)[:, None] == order[None, :]), BF)
    rel_row = jnp.arange(chips * 32, dtype=jnp.int32)
    nat_row = jnp.where(rel_row % 32 < rows, jnp.repeat(inv, 32) * rows + rel_row % 32, -1)
    perm = (jnp.arange(half_w, dtype=jnp.int32)[:, None] == nat_row[None, :]).astype(BF)

    def pick(array, parts, which):
        view = array.reshape(*array.shape[:-1], parts, 2, array.shape[-1] // (2 * parts))
        taken = jnp.where(which == 0, view[..., 0, :], view[..., 1, :])
        return taken.reshape(*array.shape[:-1], array.shape[-1] // 2)

    def both(a, b, axis):
        return jnp.where(
            core == 0, jnp.concatenate([a, b], axis=axis), jnp.concatenate([b, a], axis=axis)
        )

    small = jnp.concatenate([norm_gains, bias_pack])
    qkv = w_qkv.reshape(rows, 3, width).swapaxes(0, 1)
    got_qkv, got_small = net.core(pick(qkv, net.x, 1 - core)), net.core(small)
    chip_qkv = both(pick(qkv, net.x, core), got_qkv, 1).reshape(6 * rows, half_w)
    chip_small = jnp.pad(
        both(small[None], got_small[None], 0), ((0, 14), (0, half_w - small.shape[0]))
    )

    def after(value, *others):
        return lax.optimization_barrier((value, *others))[0]

    def grow(held, stage, orders=None, then=()):
        got = net.across(held, stage, orders)
        if then:
            got = after(got, *then)
        return jnp.concatenate([held, got])

    last = net.stages - 1
    q0 = jnp.concatenate([chip_qkv, chip_small])[None]
    q1 = grow(q0, 0)

    seg_row = jnp.pad(segments.astype(BF), ((0, 0), (0, width - cols)))[:, None, :]
    packed = jnp.concatenate([tokens, jnp.pad(seg_row, ((0, 0), (0, 7), (0, 0)))], axis=1)
    packed = after(packed, q0)

    def to_sequence(array):
        swapped = jnp.where(zodd == 0, array, array[::-1])
        return jnp.stack(
            [lax.ppermute(swapped[k], AXES, net.scatter_move(k)) for k in range(2)]
        )

    def from_sequence(array):
        back = jnp.stack(
            [
                lax.ppermute(array[k], AXES, [(b, a) for a, b in net.scatter_move(k)])
                for k in range(2)
            ]
        )
        return jnp.where(zodd == 0, back, back[::-1])

    x_o = to_sequence(packed)
    x_t = net.core(x_o)
    x_n = net.pair(x_o)
    x_m = net.core(x_n)

    up = after(w_fc1, q0).reshape(rows, hidden)
    got_up = net.core(pick(up, net.x, 1 - core))
    chip_up = fold(both(pick(up, net.x, core), got_up, 0), 2)
    chip_up = jnp.concatenate([chip_up, jnp.pad(w_out.reshape(rows, width), ((0, 8), (0, 0)))])

    q2 = grow(after(q1, x_o, chip_up), 1)
    d1 = grow(after(w_fc2.reshape(1, frows, width), q1), 0, net.mixed)
    u1 = grow(after(chip_up, q2)[None], 0)
    q4 = grow(q2, 2)
    u2 = grow(after(u1, q4), 1)
    q_held, q_got = q4, net.across(q4, last)
    g_o = to_sequence(after(cotangent, q4))
    g_t = net.core(g_o)

    dma = lambda *n: pltpu.SemaphoreType.DMA(n)
    vm = lambda shape, dtype: pltpu.VMEM(shape, dtype)
    by_pair = lambda n: (PAIRS, n, DOUBLE)
    unit1, col, row, hot = run(
        unit_kernel,
        None,
        (x_o, x_t, x_n, after(x_m, q4), place_in),
        (
            ((keys, width), F32),
            ((keys, SLAB), F32),
            ((8, mine), F32),
            ((half_w, place_in.shape[1]), BF),
        ),
        [],
        us=4,
    )
    u2 = after(u2, q_got)
    d1 = after(d1, u2, q_got)
    a1, q, k, v, w_mix, vec = run(
        mix_kernel,
        inv,
        (unit1, pi, row_device, owner_in, hot, q_held, q_got),
        (
            ((keys, width), BF),
            (by_pair(mine), BF),
            (by_pair(keys), BF),
            (by_pair(keys), BF),
            ((3, width, half_w), BF),
            ((1, place_in.shape[1]), F32),
        ),
        [vm((keys, width), BF), vm((chips * 16, half_w), BF), dma(chips, 3), dma(chips)],
        anys=(5, 6),
        us=8,
    )
    u4 = grow(u2, 2, then=(k,))
    d2 = grow(d1, 1, net.mixed, then=(k,))
    u_held, u_got = u4, net.across(u4, last)
    o, low, lse = run(
        attend_kernel,
        None,
        (after(q, u4, d2, g_o), k, v, col, row),
        ((by_pair(mine), F32), (by_pair(mine), BF), ((PAIRS, 8, mine), F32)),
        [vm((keys, mine), F32), vm((keys, mine), F32), vm((keys, mine), BF)],
        us=12,
    )
    d4 = grow(d2, 2, net.mixed, then=(low,))
    part, wo = run(
        project_kernel,
        inv,
        (low, perm, u_held, u_got),
        (((mine, width), BF), ((half_w, width), BF)),
        [vm((chips * 32, width), BF), dma(chips)],
        anys=(2, 3),
        us=3,
    )
    part_got = net.core(part)
    d_held, d_got = d4, net.across(after(d4, u_got), last, net.mixed)
    blocks = ((half, 96, width), BF)
    mid, a2, act, fac, w_up, keep_d, send_d, g_sum = run(
        middle_kernel,
        (inv, inv_d),
        (part, after(part_got, d4), x_o, x_t, g_o, g_t, vec, pi, u_held, u_got),
        (
            ((mine, width), F32),
            ((mine, width), BF),
            ((mine, half_f), BF),
            ((mine, half_f), F32),
            ((width, half_f), BF),
            blocks,
            blocks,
            ((1, width), F32),
        ),
        [vm((mine, width), BF), vm((half_f, width), BF), dma(chips, 2)],
        anys=(8, 9),
        us=10,
    )

    def shrink(keep, send, stage, orders=None):
        got = net.across(send, stage, orders)
        if stage == 0:
            return (keep.astype(F32) + got.astype(F32))[0]
        n = keep.shape[0] // 2
        send = (keep[n:].astype(F32) + got[n:].astype(F32)).astype(BF)
        keep = (keep[:n].astype(F32) + got[:n].astype(F32)).astype(BF)
        return keep, send

    pre, e2, w_down, pre_sum = run(
        slope_kernel,
        inv_d,
        (g_o, g_t, fac, w_up, pi, d_held, d_got),
        (
            ((mine, half_f), BF),
            ((mine, width), BF),
            ((half_f, width), BF),
            ((1, half_f), F32),
        ),
        [dma(chips, 1)],
        anys=(5, 6),
        us=8,
    )
    e2_got = net.core(e2)
    down_own, down_give = run(
        down_kernel,
        None,
        (after(act, e2_got), w_down),
        (((own, width), F32), ((own, width), BF)),
        [],
        us=2,
    )
    down_got = net.core(down_give).astype(F32)
    out_own = (mid[:own] + down_own + down_got + vec[:, AT["bias_down"]]).astype(BF)
    wide_sum, half_sum = ((1, width), F32), ((1, half_w), F32)
    blocks_u = ((half, 128, width), BF)
    gm, branch, d_heads, keep_u, send_u, e2n, e2s, bs = run(
        branch_kernel,
        inv,
        (e2, e2_got, mid, g_o, g_t, vec, wo, low, perm, a2, pre),
        (
            ((own, width), F32),
            ((mine, width), BF),
            (by_pair(mine), BF),
            blocks_u,
            blocks_u,
            wide_sum,
            wide_sum,
            wide_sum,
        ),
        [vm((width, half_f), BF), vm((chips * 32, width), BF)],
        us=7,
    )
    d3 = shrink(keep_d, send_d, 3, net.mixed)
    d_2 = shrink(*d3, 2, net.mixed)
    u3 = shrink(keep_u, send_u, 3)
    dq, dk, dv, dqs, dvs = run(
        attend_back_kernel,
        None,
        (q, k, v, o, lse, col, row, after(d_heads, d3[1])),
        (
            (by_pair(mine), BF),
            (by_pair(keys), BF),
            (by_pair(keys), BF),
            half_sum,
            half_sum,
        ),
        [vm((keys, mine), F32), vm((keys, mine), BF), vm((keys, mine), BF)],
        us=14,
    )
    quarter = ((2, own, width), BF)
    keep_e, give_e, e1n, e1s = run(
        input_kernel,
        None,
        (after(dq, u3[1]), dk, dv, w_mix, unit1, pi),
        (quarter, quarter, wide_sum, wide_sum),
        [],
        us=5,
    )
    got_e = net.core(give_e)
    u_2 = shrink(*u3, 2)
    blocks_q = ((half, 160, half_w), BF)
    keep_q, send_q = run(
        gather_grads_kernel,
        inv,
        (after(a1, u3, d_2), dq, dk, dv, row_device, owner_out, place_out)
        + (e1n, e2n, e2s, dqs, bs, g_sum, pre_sum, e1s, dvs),
        (blocks_q, blocks_q),
        [
            vm((3, width, half_w), BF),
            vm((chips * 16, half_w), BF),
            vm((half_w, place_out.shape[1]), BF),
        ],
        us=4,
    )
    e1_near = (keep_e[1].astype(F32) + got_e[1].astype(F32)).astype(BF)
    e1_near = net.pair(e1_near).astype(F32)
    q_3 = shrink(keep_q, send_q, 3)
    d_1 = shrink(*d_2, 1, net.mixed)
    u_1 = shrink(*u_2, 1)
    shard_d = shrink(*d_1, 0, net.mixed)
    shard_u = shrink(*u_1, 0)
    q_2 = shrink(*q_3, 2)
    shard_q = shrink(*shrink(*q_2, 1), 0)
    block_out = from_sequence(after(out_own, u3[1]).reshape(local, cols, width))

    e1 = keep_e[0].astype(F32) + got_e[0].astype(F32) + e1_near
    x_own = x_o[:, :cols].reshape(own, width).astype(F32)
    unit_own, inverse_own = normal(x_own)
    in_own = gm + norm_back(e1, unit_own, inverse_own, vec[:, AT["gain1"]])
    input_grad = from_sequence(in_own.astype(BF).reshape(local, cols, width)).astype(F32)

    def own_rows(chip):
        keep = jnp.where(core == 0, chip[..., 0, :, :], chip[..., 1, :, :])
        give = jnp.where(core == 0, chip[..., 1, :, :], chip[..., 0, :, :])
        return keep, net.core(give)

    def merge(keep, got, parts):
        view = lambda array: array.reshape(*array.shape[:-1], parts, 1, -1)
        first = jnp.where(core == 0, view(keep), view(got))
        second = jnp.where(core == 0, view(got), view(keep))
        return jnp.concatenate([first, second], axis=-2).reshape(*keep.shape[:-1], -1)

    qkv_own = merge(*own_rows(shard_q[: 6 * rows].reshape(3, 2, rows, half_w)), net.x)
    g_qkv = jnp.moveaxis(qkv_own, 0, 1).reshape(-1)
    g_out = shard_u[4 * rows : 5 * rows].reshape(-1)
    up_own = merge(*own_rows(unfold(shard_u[: 4 * rows], 2).reshape(2, rows, half_f)), net.x)
    two = shard_q[6 * rows : 6 * rows + 2, : 2 * ll + rl]
    keep_s, got_s = own_rows(two.reshape(2, 1, -1))
    own_sums = (keep_s + got_s)[0]
    return (
        block_out,
        input_grad,
        g_qkv,
        g_out,
        up_own.reshape(-1),
        shard_d.reshape(-1),
        own_sums[:ll],
        own_sums[ll : ll + rl],
        own_sums[ll + rl :],
    )


def solution(mesh):
    dp, seq = mesh.shape["dp"], mesh.shape["seq"]
    y = 1 << (((seq.bit_length() - 1) - 1) // 2)
    z = seq // y
    dims = (dp // 2, 2, 4, z // 4, y // 2, 2)
    net = Net(dims)
    inner = Mesh(mesh.devices.reshape(dims), AXES)
    place = ("zh", "zl", "yh", "yl")
    cube = P(("x", "c"), place, None)
    flat = P(AXES)
    rows = D // (2 * net.chips)
    tiles = rows == 24 and net.chips == 16 and net.zl * net.yh == 1
    return jax.shard_map(
        functools.partial(body if tiles else body_any, net),
        mesh=inner,
        in_specs=(cube, P(("x", "c"), place), cube) + (flat,) * 6,
        out_specs=(cube, cube) + (flat,) * 7,
        check_vma=False,
    )
```

```python
import functools
import itertools

import jax
import jax.numpy as jnp
import numpy as np
from jax import lax
from jax.experimental import pallas as pl
from jax.experimental.pallas import tpu as pltpu
from jax.sharding import Mesh
from jax.sharding import PartitionSpec as P

D = 768
FF = 3072
HEADS = 12
HEAD_DIM = 64
EPS = 1e-05
MASKED = -1000000000.0
BF = jnp.bfloat16
F32 = jnp.float32
AXES = ("x", "c", "zh", "zl", "yh", "yl")


class Net:
    def __init__(self, dims):
        self.dims = dims
        self.x, self.c, self.zh, self.zl, self.yh, self.yl = dims
        self.z, self.y = self.zh * self.zl, self.yh * self.yl
        self.chips = self.x * self.z * self.y
        bits = lambda axis, n: [(axis, 1 << b) for b in reversed(range(n.bit_length() - 1))]
        zs, xs, ys = bits("z", self.z), bits("x", self.x), bits("y", self.y)
        self.orders = (zs + xs + ys, zs + ys + xs)
        self.mixed = (xs + zs + ys, ys + zs + xs)
        self.stages = len(self.orders[0])

    def perm(self, move):
        pairs = []
        for at in itertools.product(*(range(n) for n in self.dims)):
            to = move(*at)
            pairs.append(
                (int(np.ravel_multi_index(at, self.dims)), int(np.ravel_multi_index(to, self.dims)))
            )
        return pairs

    def flip(self, stage, orders):
        def move(x, c, zh, zl, yh, yl):
            axis, bit = orders[c][stage]
            z, y = zh * self.zl + zl, yh * self.yl + yl
            if axis == "x":
                x ^= bit
            elif axis == "y":
                y ^= bit
            else:
                z ^= bit
            return (x, c, z // self.zl, z % self.zl, y // self.yl, y % self.yl)

        return self.perm(move)

    def across(self, value, stage, orders=None):
        return lax.ppermute(value, AXES, self.flip(stage, orders or self.orders))

    def core(self, value):
        return lax.ppermute(value, "c", [(0, 1), (1, 0)])

    def pair(self, value):
        return lax.ppermute(value, "yl", [(0, 1), (1, 0)])

    def scatter_move(self, k):
        return self.perm(
            lambda x, c, zh, zl, yh, yl: (x, zh >> 1, 2 * c + (k ^ (zh & 1)), zl, yh, yl)
        )

    def table(self, orders=None):
        me = {
            "x": lax.axis_index("x"),
            "z": lax.axis_index("zh") * self.zl + lax.axis_index("zl"),
            "y": lax.axis_index("yh") * self.yl + lax.axis_index("yl"),
        }
        grid = np.indices((self.x, self.z, self.y)).reshape(3, -1)
        axes = {"x": grid[0], "z": grid[1], "y": grid[2]}
        places = []
        for order in orders or self.orders:
            place = jnp.zeros((self.chips,), jnp.int32)
            for stage, (axis, bit) in enumerate(order):
                differs = (jnp.asarray(axes[axis], jnp.int32) ^ me[axis]) & bit
                place = place + jnp.where(differs != 0, 1 << stage, 0)
            places.append(place)
        return jnp.where(lax.axis_index("c") == 0, places[0], places[1]).astype(jnp.int32)

    def gather(self, block):
        held = block[None]
        for stage in range(self.stages):
            held = jnp.concatenate([held, self.across(held, stage)])
        return held

    def scatter(self, held):
        for stage in reversed(range(self.stages)):
            half = held.shape[0] // 2
            got = self.across(held[half:], stage)
            held = held[:half].astype(F32) + got.astype(F32)
            if stage:
                held = held.astype(BF)
        return held[0]


def move_kernel(table, source, target):
    target[...] = source[...]


def reorder(blocks, table, to_place):
    rest = -blocks.shape[1] % 16
    if rest:
        rows = blocks.shape[1]
        blocks = jnp.pad(blocks, ((0, 0), (0, rest), (0, 0)))
        return reorder(blocks, table, to_place)[:, :rows]
    chips, rows, cols = blocks.shape
    here = pl.BlockSpec((1, rows, cols), lambda chip, table: (chip, 0, 0))
    there = pl.BlockSpec((1, rows, cols), lambda chip, table: (table[chip], 0, 0))
    return pl.pallas_call(
        move_kernel,
        grid_spec=pltpu.PrefetchScalarGridSpec(
            num_scalar_prefetch=1,
            grid=(chips,),
            in_specs=[here if to_place else there],
            out_specs=there if to_place else here,
        ),
        out_shape=jax.ShapeDtypeStruct(blocks.shape, blocks.dtype),
    )(table, blocks)


def normal(field):
    center = field - jnp.mean(field, axis=-1, keepdims=True)
    inverse = lax.rsqrt(jnp.mean(center * center, axis=-1, keepdims=True) + EPS)
    return center * inverse, inverse


def norm_back(upstream, unit, inverse, gain):
    scaled = upstream * gain
    return inverse * (
        scaled
        - jnp.mean(scaled, axis=-1, keepdims=True)
        - unit * jnp.mean(scaled * unit, axis=-1, keepdims=True)
    )


def dot(a, b):
    return jnp.dot(a, b, preferred_element_type=F32)


def dot_t(a, b):
    return lax.dot_general(a, b, (((1,), (1,)), ((), ())), preferred_element_type=F32)


def t_dot(a, b):
    return lax.dot_general(a, b, (((0,), (0,)), ((), ())), preferred_element_type=F32)


def fold(wide, parts):
    lead, rows, cols = wide.shape[:-2], wide.shape[-2], wide.shape[-1] // parts
    moved = jnp.moveaxis(wide.reshape(*lead, rows, parts, cols), -2, -3)
    return moved.reshape(*lead, parts * rows, cols)


def unfold(tall, parts):
    lead, rows, cols = tall.shape[:-2], tall.shape[-2] // parts, tall.shape[-1]
    moved = jnp.moveaxis(tall.reshape(*lead, parts, rows, cols), -3, -2)
    return moved.reshape(*lead, rows, parts * cols)


def body_any(net, tokens, segments, cotangent, w_qkv, w_out, w_fc1, w_fc2, norm_gains, bias_pack):
    local, cols, width = tokens.shape
    own = local * cols
    mine = 2 * own
    hidden = FF
    half_w, half_f = width // 2, hidden // 2
    devices = 2 * net.chips
    core = lax.axis_index("c")
    zodd = lax.axis_index("zh") & 1
    table = net.table()
    rows = width // devices
    frows = hidden // devices
    aligned = (width // (2 * net.x)) % HEAD_DIM == 0
    groups = net.x if aligned else 1

    def pick(array, parts, which):
        split = array.reshape(*array.shape[:-1], parts, 2, array.shape[-1] // (2 * parts))
        taken = jnp.where(which == 0, split[..., 0, :], split[..., 1, :])
        return taken.reshape(*array.shape[:-1], array.shape[-1] // 2)

    def spread(vector, parts):
        split = vector.reshape(parts, 1, vector.shape[-1] // parts)
        both = jnp.concatenate(
            [jnp.where(core == 0, split, 0.0), jnp.where(core == 1, split, 0.0)], axis=1
        )
        return both.reshape(-1)

    seg_row = jnp.pad(segments.astype(BF), ((0, 0), (0, width - cols)))[:, None, :]
    seg_rows = jnp.pad(seg_row, ((0, 0), (0, 7), (0, 0)))
    packed = jnp.concatenate([tokens, seg_rows], axis=1)

    def to_sequence(array):
        swapped = jnp.where(zodd == 0, array, array[::-1])
        return jnp.stack(
            [lax.ppermute(swapped[k], AXES, net.scatter_move(k)) for k in range(2)]
        )

    def from_sequence(array):
        back = jnp.stack(
            [
                lax.ppermute(array[k], AXES, [(b, a) for a, b in net.scatter_move(k)])
                for k in range(2)
            ]
        )
        return jnp.where(zodd == 0, back, back[::-1])

    def halves(which):
        qkv = fold(w_qkv.reshape(rows, 3 * width), 3).reshape(3, rows, width)
        up = w_fc1.reshape(rows, hidden)
        return pick(qkv, groups, which), pick(up, net.x, which)

    keep_qkv, keep_up = halves(core)
    give_qkv, give_up = halves(1 - core)
    small = jnp.concatenate([norm_gains, bias_pack])
    out_rows = w_out.reshape(rows, width)
    got_qkv, got_up, got_small, got_out = jax.tree.map(
        net.core, (give_qkv, give_up, small, out_rows)
    )

    def both(a, b, axis):
        return jnp.where(
            core == 0, jnp.concatenate([a, b], axis=axis), jnp.concatenate([b, a], axis=axis)
        )

    chip_qkv = both(keep_qkv, got_qkv, 1).reshape(6 * rows, half_w)
    chip_up = fold(both(keep_up, got_up, 0), 2)
    chip_out = fold(out_rows if aligned else both(out_rows, got_out, 0), 2)
    chip_small = jnp.pad(
        both(small[None], got_small[None], 0), ((0, 14), (0, half_w - small.shape[0]))
    )
    cut = np.cumsum([chip_qkv.shape[0], chip_out.shape[0]])
    blocks_a = reorder(
        net.gather(jnp.concatenate([chip_qkv, chip_out, chip_small])), table, False
    )
    blocks_up = reorder(net.gather(chip_up), table, False)
    blocks_down = reorder(net.gather(w_fc2.reshape(frows, width)), table, False)

    lead = (net.x, net.z, net.y)

    def natural(blocks):
        n = blocks.shape[-1]
        return jnp.moveaxis(blocks.reshape(*lead, 2, -1, n), 3, 1).reshape(-1, n)

    def by_chip(array):
        n = array.shape[-1]
        return jnp.moveaxis(array.reshape(net.x, 2, net.z, net.y, -1, n), 1, 3).reshape(
            net.chips, -1, n
        )

    qkv_blocks = blocks_a[:, : cut[0]].reshape(net.chips, 3, 2 * rows, half_w)
    w_q, w_k, w_v = (natural(qkv_blocks[:, i]) for i in range(3))
    out_blocks = unfold(blocks_a[:, cut[0] : cut[1]], 2)
    if aligned:
        w_proj = out_blocks.reshape(half_w, width)
    else:
        w_proj = lax.dynamic_slice_in_dim(natural(out_blocks), core * half_w, half_w)
    smalls = blocks_a[:, cut[1] : cut[1] + 2, : small.shape[0]].reshape(*lead, 2, -1)
    smalls = jnp.moveaxis(smalls, 3, 1).reshape(devices, -1).astype(F32)
    n_gain = norm_gains.shape[0]
    gains = smalls[:, :n_gain].reshape(-1)
    shifts = smalls[:, n_gain:].reshape(-1)
    w_up = natural(unfold(blocks_up, 2))
    w_down = blocks_down.reshape(half_f, width)
    gain1, gain2 = gains[:width], gains[width:]
    shift1, shift2, bias_q, bias_v, bias_proj, bias_down = (
        shifts[i * width : (i + 1) * width] for i in range(6)
    )
    bias_up = pick(shifts[6 * width :], net.x, core)
    bias_q, bias_v = pick(bias_q, groups, core), pick(bias_v, groups, core)

    x_own = to_sequence(packed)
    x_other = net.core(x_own)
    x_mine = jnp.concatenate([x_own, x_other])
    near = net.pair(x_own)
    near = jnp.concatenate([near, net.core(near)])
    x_seq = jnp.concatenate([x_mine, near])
    if net.zl * net.yh > 1:
        x_far = lax.all_gather(x_seq, ("zl", "yh"), axis=0, tiled=True)
        x_keys = x_far
    else:
        x_keys = x_seq
    g_own = to_sequence(cotangent)
    g_mine = jnp.concatenate([g_own, net.core(g_own)]).reshape(mine, width)
    docs = x_keys[:, cols, :cols].reshape(-1)
    query_docs = x_mine[:, cols, :cols].reshape(-1)
    x_all = x_keys[:, :cols].reshape(-1, width).astype(F32)
    x_q = x_mine[:, :cols].reshape(-1, width).astype(F32)

    unit_q, inverse_q = normal(x_q)
    a_q = (unit_q * gain1 + shift1).astype(BF)
    unit_all, _ = normal(x_all)
    a_all = (unit_all * gain1 + shift1).astype(BF)
    heads = HEADS // 2
    q = (dot(a_q, w_q) + bias_q).astype(BF)
    k = dot(a_all, w_k).astype(BF)
    v = (dot(a_all, w_v) + bias_v).astype(BF)
    by_head = lambda t: t.reshape(-1, heads, HEAD_DIM)
    same = (query_docs[:, None] == docs[None, :])[None]
    scores = (
        jnp.einsum("qhd,khd->hqk", by_head(q), by_head(k), preferred_element_type=F32) * 0.125
    )
    scores = jnp.where(same, scores, MASKED)
    weights = jnp.exp(scores - jnp.max(scores, axis=-1, keepdims=True))
    probs = weights / jnp.sum(weights, axis=-1, keepdims=True)
    probs_low = probs.astype(BF)
    att = jnp.einsum("hqk,khd->qhd", probs_low, by_head(v), preferred_element_type=F32)
    att = att.reshape(mine, half_w)
    att_low = att.astype(BF)

    def core_sum(partial):
        low = partial.astype(BF)
        got = net.core(low)
        return low.astype(F32) + jnp.concatenate([got[own:], got[:own]]).astype(F32)

    middle = x_q + core_sum(dot(att_low, w_proj)) + bias_proj
    unit2, inverse2 = normal(middle)
    a2 = (unit2 * gain2 + shift2).astype(BF)
    pre = dot(a2, w_up) + bias_up
    sig = jax.nn.sigmoid(1.702 * pre)
    activ = (pre * sig).astype(BF)
    down = dot(activ, w_down)
    down_got = net.core(down[own:].astype(BF)).astype(F32)
    out_own = (middle[:own] + down[:own] + down_got + bias_down).astype(BF)
    block_out = from_sequence(out_own.reshape(local, cols, width))

    grad_down = t_dot(activ, g_mine).astype(BF)
    grad_pre = (dot_t(g_mine, w_down) * (sig + 1.702 * pre * sig * (1.0 - sig))).astype(BF)
    shard_down = net.scatter(reorder(grad_down.reshape(net.chips, frows, width), table, True))
    grad_up = t_dot(a2, grad_pre).astype(BF)
    shard_up = net.scatter(reorder(fold(by_chip(grad_up), 2), table, True))
    e2 = core_sum(dot_t(grad_pre, w_up))
    grad_middle = g_mine.astype(F32) + norm_back(e2, unit2, inverse2, gain2)
    branch = grad_middle.astype(BF)
    grad_proj = t_dot(att_low, branch).astype(BF)
    d_heads = dot_t(branch, w_proj).astype(BF)
    dp = jnp.einsum("qhd,khd->hqk", by_head(d_heads), by_head(v), preferred_element_type=F32)
    delta = jnp.sum(probs * dp, axis=-1, keepdims=True)
    d_scores = (probs * (dp - delta)).astype(BF)
    dq = 0.125 * jnp.einsum("hqk,khd->qhd", d_scores, by_head(k), preferred_element_type=F32)
    dk = 0.125 * jnp.einsum("hqk,qhd->khd", d_scores, by_head(q), preferred_element_type=F32)
    dv = jnp.einsum("hqk,qhd->khd", probs_low, by_head(d_heads), preferred_element_type=F32)
    dq = dq.reshape(-1, half_w).astype(BF)
    dk = dk.reshape(-1, half_w).astype(BF)
    dv = dv.reshape(-1, half_w).astype(BF)
    grad_qkv = jnp.stack([t_dot(a_q, dq), t_dot(a_all, dk), t_dot(a_all, dv)]).astype(BF)

    e1_keys = (dot_t(dk, w_k) + dot_t(dv, w_v)).astype(BF)
    if net.zl * net.yh > 1:
        e1_keys = lax.psum_scatter(
            e1_keys, ("zl", "yh"), scatter_dimension=0, tiled=True
        )
    e1_near = e1_keys[mine:].reshape(2, own, width)
    e1_mine = e1_keys[:mine].astype(F32) + dot_t(dq, w_q)
    e1_mine = e1_mine.astype(BF).reshape(2, own, width)
    got = net.core(jnp.stack([e1_mine[1], e1_near[1]]))
    e1_near = e1_near[0].astype(F32) + got[1].astype(F32)
    e1 = e1_mine[0].astype(F32) + got[0].astype(F32) + net.pair(e1_near.astype(BF)).astype(F32)
    unit1 = unit_q[:own]
    in_own = grad_middle[:own] + norm_back(e1, unit1, inverse_q[:own], gain1)
    input_grad = from_sequence(in_own.astype(BF).reshape(local, cols, width)).astype(F32)

    total = lambda array: jnp.sum(array.astype(F32), axis=0)
    g_own = g_mine[:own]
    gain_sums = jnp.concatenate([total(e1 * unit1), total(e2[:own] * unit2[:own])])
    bias_sums = jnp.concatenate(
        [
            total(e2[:own]),
            spread(total(dq), groups),
            total(branch[:own]),
            total(g_own),
            spread(total(grad_pre), net.x),
        ]
    )
    lead_sums = jnp.concatenate([total(e1), spread(total(dv), groups)])
    sums = jnp.concatenate(
        [v.reshape(devices, -1) for v in (gain_sums, bias_sums, lead_sums)], axis=1
    )
    sums = sums + net.core(sums)
    sums = jnp.moveaxis(sums.reshape(net.x, 2, net.z, net.y, -1), 1, 0)
    sums = jnp.where(core == 0, sums[0], sums[1]).reshape(net.chips, 1, -1)
    n_sums = sums.shape[-1]
    sums = jnp.pad(sums, ((0, 0), (0, 15), (0, half_w - n_sums))).astype(BF)
    qkv_send = jnp.stack([by_chip(grad_qkv[i]) for i in range(3)], axis=1)
    qkv_send = qkv_send.reshape(net.chips, 6 * rows, half_w)
    if aligned:
        out_send = grad_proj.reshape(net.chips, rows, width)
    else:
        whole = jnp.zeros((width, width), BF)
        whole = lax.dynamic_update_slice(whole, grad_proj, (core * half_w, 0))
        out_send = by_chip(whole)
    sent = jnp.concatenate([qkv_send, fold(out_send, 2), sums], axis=1)
    shard_a = net.scatter(reorder(sent, table, True))

    def own_rows(chip):
        keep = jnp.where(core == 0, chip[..., 0, :, :], chip[..., 1, :, :])
        give = jnp.where(core == 0, chip[..., 1, :, :], chip[..., 0, :, :])
        return keep, net.core(give)

    def merge(keep, got, parts):
        split = lambda array: array.reshape(*array.shape[:-1], parts, 1, -1)
        first = jnp.where(core == 0, split(keep), split(got))
        second = jnp.where(core == 0, split(got), split(keep))
        return jnp.concatenate([first, second], axis=-2).reshape(*keep.shape[:-1], -1)

    qkv_own = merge(*own_rows(shard_a[: cut[0]].reshape(3, 2, rows, half_w)), groups)
    g_qkv = jnp.moveaxis(qkv_own, 0, 1).reshape(-1)
    out_own = unfold(shard_a[cut[0] : cut[1]], 2)
    if not aligned:
        keep, got = own_rows(out_own.reshape(2, rows, width))
        out_own = keep + got
    g_out = out_own.reshape(-1)
    up_own = merge(*own_rows(unfold(shard_up, 2).reshape(2, rows, half_f)), net.x)
    own_sums = shard_a[cut[1], :n_sums]
    n_gain = 2 * width // devices
    n_lead = n_sums - n_gain
    return (
        block_out,
        input_grad,
        g_qkv,
        g_out,
        up_own.reshape(-1),
        shard_down.reshape(-1),
        own_sums[:n_gain],
        own_sums[n_gain:n_lead],
        own_sums[n_lead:],
    )


SLAB = 128
PAIRS = HEADS // 4
DOUBLE = 2 * HEAD_DIM
PARTS = (
    ("gain1", D),
    ("gain2", D),
    ("shift1", D),
    ("shift2", D),
    ("bias_proj", D),
    ("bias_down", D),
    ("bias_q", D // 2),
    ("bias_v", D // 2),
    ("bias_up", FF // 2),
)
SUMS = (
    ("e1n", D),
    ("e2n", D),
    ("e2", D),
    ("dq", D // 2),
    ("branch", D),
    ("g", D),
    ("pre", FF // 2),
    ("e1", D),
    ("dv", D // 2),
)


def offsets(parts):
    ends = np.cumsum([n for _, n in parts])
    return {name: slice(int(end - n), int(end)) for (name, n), end in zip(parts, ends)}


AT = offsets(PARTS)


def dots(a, b, ca, cb):
    return lax.dot_general(a, b, (((ca,), (cb,)), ((), ())), preferred_element_type=F32)


def lane_half(e):
    lanes = lax.broadcasted_iota(jnp.int32, (1, DOUBLE), 1)
    inside = (lanes < HEAD_DIM) if e == 0 else (lanes >= HEAD_DIM)
    return inside.astype(F32).astype(BF)


def first_half(shape):
    return lax.broadcasted_iota(jnp.int32, shape, 1) < HEAD_DIM


def load_rows(inv, held, got, target, sems, pieces):
    half = held.shape[0]
    copies = []
    for r in range(2 * half):
        source = held if r < half else got
        for n, (first, rows, place) in enumerate(pieces):
            copies.append(
                pltpu.make_async_copy(
                    source.at[r % half, pl.ds(first, rows), :],
                    place(target, inv[r], rows),
                    sems.at[r, n],
                )
            )
    for copy in copies:
        copy.start()
    return copies


def one_hot(place, target):
    step = 128
    for i in range(target.shape[0] // step):
        shape = (step, target.shape[1])
        entry = lax.broadcasted_iota(jnp.int32, shape, 0) + i * step
        target[i * step : (i + 1) * step, :] = (entry == place[:1, :]).astype(F32).astype(BF)


def unit_kernel(xo, xt, xn, xm, place, unit_ref, col_ref, row_ref, hot_ref):
    one_hot(place, hot_ref)
    for i, (ref, j) in enumerate((ref, j) for ref in (xo, xt, xn, xm) for j in range(2)):
        unit, _ = normal(ref[j, :SLAB, :].astype(F32))
        at = pl.ds(i * SLAB, SLAB)
        unit_ref[at, :] = unit
        docs = ref[j, SLAB : SLAB + 8, :SLAB].astype(F32)[:1]
        col_ref[at, :] = jnp.broadcast_to(docs, (SLAB, SLAB)).T
        if i < 4:
            row_ref[:, i * SLAB : (i + 1) * SLAB] = jnp.broadcast_to(docs, (8, SLAB))


def fill_bias(col, row, bias):
    for i in range(bias.shape[0] // SLAB):
        at = pl.ds(i * SLAB, SLAB)
        for j in range(bias.shape[1] // SLAB):
            lanes = pl.ds(j * SLAB, SLAB)
            bias[at, lanes] = jnp.where(col[at, :] == row[:1, lanes], 0.0, MASKED)


def pick_rows(rows, step):
    shape = (2 * rows // step, rows)
    i = lax.broadcasted_iota(jnp.int32, shape, 0)
    j = lax.broadcasted_iota(jnp.int32, shape, 1)
    return (j == (i >> 1) * step + (i & 1)).astype(F32).astype(BF)


def mix_kernel(
    inv, unit, pi, device, owner, hot, held, got,
    a_ref, q_ref, k_ref, v_ref, w, vec, nat, small, sems, small_sems,
):
    half = held.shape[0]
    few = []
    for r in range(2 * half):
        source = held if r < half else got
        few.append(
            pltpu.make_async_copy(
                source.at[r % half, pl.ds(144, 16), :], small.at[pl.ds(r * 16, 16), :], small_sems.at[r]
            )
        )
    for copy in few:
        copy.start()
    place = lambda i: lambda t, chip, n: t.at[i, pl.ds(pl.multiple_of(chip * n, 16), n), :]
    copies = load_rows(inv, held, got, w, sems, [(48 * i, 48, place(i)) for i in range(3)])
    for copy in few:
        copy.wait()
    picked = dot(pick_rows(small.shape[0], 16), small[...]).astype(BF)
    mine_only = jnp.where(device[:, :1] == owner[:1, :], dot(picked, hot[...]), 0.0)
    vec[...] = jnp.sum(mine_only, axis=0, keepdims=True)
    keys = a_ref.shape[0]
    for i in range(keys // SLAB):
        at = pl.ds(i * SLAB, SLAB)
        nat[at, :] = (unit[at, :] * vec[:, AT["gain1"]] + vec[:, AT["shift1"]]).astype(BF)
    a_ref[...] = dot(nat[...], pi[...]).astype(BF)
    for copy in copies:
        copy.wait()
    mine = q_ref.shape[1]
    q = (dot(a_ref[:mine, :], w[0]) + vec[:, AT["bias_q"]]).astype(BF) * 0.125
    k = dot(a_ref[...], w[1]).astype(BF)
    v = (dot(a_ref[...], w[2]) + vec[:, AT["bias_v"]]).astype(BF)
    for i in range(PAIRS):
        lanes = slice(i * DOUBLE, (i + 1) * DOUBLE)
        q_ref[i], k_ref[i], v_ref[i] = q[:, lanes], k[:, lanes], v[:, lanes]


def attend_kernel(q_ref, k_ref, v_ref, col, row, o_ref, low_ref, lse_ref, bias, s, p_low):
    mine, keys = q_ref.shape[1], k_ref.shape[1]
    fill_bias(col, row, bias)

    def pair(i, carry):
        outs = []
        for e in range(2):
            qm = q_ref[i] * lane_half(e)
            top = jnp.full((1, mine), -3e38, F32)
            for c in range(keys // SLAB):
                at = pl.ds(c * SLAB, SLAB)
                t = dots(k_ref[i, at, :], qm, 1, 1) + bias[at, :]
                s[at, :] = t
                top = jnp.maximum(top, jnp.max(t, axis=0, keepdims=True))
            total = jnp.zeros((1, mine), F32)
            for c in range(keys // SLAB):
                at = pl.ds(c * SLAB, SLAB)
                p = jnp.exp(s[at, :] - top)
                total = total + jnp.sum(p, axis=0, keepdims=True)
                p_low[at, :] = p.astype(BF)
            lse_ref[i, e : e + 1, :] = top + jnp.log(total)
            o = dots(p_low[...], v_ref[i], 0, 0)
            scale = jnp.broadcast_to(1.0 / total, (DOUBLE, mine)).T
            outs.append(o * scale)
        o = jnp.where(first_half(outs[0].shape), outs[0], outs[1])
        o_ref[i] = o
        low_ref[i] = o.astype(BF)
        return carry

    lax.fori_loop(0, PAIRS, pair, 0)


def project_kernel(inv, low, perm, held, got, part_ref, wo_ref, rel, sems):
    half = held.shape[0]
    copies = []
    for r in range(2 * half):
        source = held if r < half else got
        copies.append(
            pltpu.make_async_copy(
                source.at[r % half, pl.ds(96, 32), :], rel.at[pl.ds(r * 32, 32), :], sems.at[r]
            )
        )
    for copy in copies:
        copy.start()
    for copy in copies:
        copy.wait()
    wo_ref[...] = dot(perm[...], rel[...]).astype(BF)
    att = jnp.concatenate([low[i] for i in range(PAIRS)], axis=1)
    part_ref[...] = dot(att, wo_ref[...]).astype(BF)


def middle_kernel(
    inv, part, part_got, xo, xt, go, gt, vec, pi, held, got,
    mid_ref, a_ref, act_ref, fac_ref, w, keep_ref, send_ref, sum_ref,
    nat, grad, sems,
):
    place = lambda h: lambda t, chip, n: t.at[
        pl.ds(pl.multiple_of(chip * n, 16), n), pl.ds(h * D, D)
    ]
    copies = load_rows(inv, held, got, w, sems, [(48 * h, 48, place(h)) for h in range(2)])
    mine = part.shape[0]
    own = mine // 2
    for i, (ref, j) in enumerate((ref, j) for ref in (xo, xt) for j in range(2)):
        at = pl.ds(i * SLAB, SLAB)
        other = pl.ds((i * SLAB + own) % mine, SLAB)
        mid = (
            ref[j, :SLAB, :].astype(F32)
            + (part[at, :].astype(F32) + part_got[other, :].astype(F32))
            + vec[:, AT["bias_proj"]]
        )
        mid_ref[at, :] = mid
        unit, _ = normal(mid)
        nat[at, :] = (unit * vec[:, AT["gain2"]] + vec[:, AT["shift2"]]).astype(BF)
    a_ref[...] = dot(nat[...], pi[...]).astype(BF)
    g = jnp.concatenate([go[0], go[1], gt[0], gt[1]], axis=0)
    sum_ref[...] = jnp.sum(g[:own].astype(F32), axis=0, keepdims=True)
    for copy in copies:
        copy.wait()
    step = 512
    for j in range(w.shape[1] // step):
        lanes = pl.ds(j * step, step)
        start = AT["bias_up"].start + j * step
        pre = dot(a_ref[...], w[:, lanes]) + vec[:, start : start + step]
        sig = 1.0 / (1.0 + jnp.exp(-1.702 * pre))
        act_ref[:, lanes] = (pre * sig).astype(BF)
        fac_ref[:, lanes] = sig + 1.702 * pre * sig * (1.0 - sig)
        grad[lanes, :] = dots(act_ref[:, lanes], g, 0, 0).astype(BF)
    half = keep_ref.shape[0]
    for r in range(2 * half):
        target = keep_ref if r < half else send_ref
        target[r % half] = grad[pl.ds(pl.multiple_of(inv[r] * 96, 16), 96), :]


def slope_kernel(inv, go, gt, fac, w_up, pi, held, got, pre_ref, e_ref, w, sum_ref, sems):
    place = lambda t, chip, n: t.at[pl.ds(pl.multiple_of(chip * n, 16), n), :]
    copies = load_rows(inv, held, got, w, sems, [(0, 96, place)])
    g = jnp.concatenate([go[0], go[1], gt[0], gt[1]], axis=0)
    for copy in copies:
        copy.wait()
    step = 512
    total = None
    for j in range(w.shape[0] // step):
        lanes = pl.ds(j * step, step)
        pre = (dots(g, w[lanes, :], 1, 1) * fac[:, lanes]).astype(BF)
        pre_ref[:, lanes] = pre
        sum_ref[:, lanes] = jnp.sum(pre.astype(F32), axis=0, keepdims=True)
        term = dots(pre, w_up[:, lanes], 1, 1)
        total = term if total is None else total + term
    e_ref[...] = dots(total.astype(BF), pi[...], 1, 1).astype(BF)


def down_kernel(act, w_down, own_ref, give_ref):
    down = dot(act[...], w_down[...])
    own = own_ref.shape[0]
    own_ref[...] = down[:own]
    give_ref[...] = down[own:].astype(BF)


def wide(ref):
    return jnp.concatenate([ref[i] for i in range(PAIRS)], axis=1)


def branch_kernel(
    inv, e2, e2_got, mid, go, gt, vec, wo, low, perm, a, pre,
    gm_ref, branch_ref, d_ref, keep_ref, send_ref, e2n_sum, e2_sum, branch_sum, grad, out,
):
    mine = mid.shape[0]
    own = mine // 2
    sums = [jnp.zeros((1, D), F32) for _ in range(3)]
    for i, (ref, j) in enumerate((ref, j) for ref in (go, gt) for j in range(2)):
        at = pl.ds(i * SLAB, SLAB)
        other = pl.ds((i * SLAB + own) % mine, SLAB)
        e = e2[at, :].astype(F32) + e2_got[other, :].astype(F32)
        unit, inverse = normal(mid[at, :])
        gm = ref[j].astype(F32) + norm_back(e, unit, inverse, vec[:, AT["gain2"]])
        branch = gm.astype(BF)
        branch_ref[at, :] = branch
        if i < 2:
            gm_ref[at, :] = gm
            for n, term in enumerate((e * unit, e, branch.astype(F32))):
                sums[n] = sums[n] + jnp.sum(term, axis=0, keepdims=True)
    e2n_sum[...], e2_sum[...], branch_sum[...] = sums
    d = dots(branch_ref[...], wo[...], 1, 1).astype(BF)
    for i in range(PAIRS):
        d_ref[i] = d[:, i * DOUBLE : (i + 1) * DOUBLE]
    step = 512
    for j in range(pre.shape[1] // step):
        lanes = pl.ds(j * step, step)
        grad[:, lanes] = dots(a[...], pre[:, lanes], 0, 0).astype(BF)
    proj = dots(wide(low), branch_ref[...], 0, 0).astype(BF)
    out[...] = dots(perm[...], proj, 0, 0).astype(BF)
    half = keep_ref.shape[0]
    for r in range(2 * half):
        target, at = (keep_ref if r < half else send_ref), r % half
        rows = pl.ds(pl.multiple_of(inv[r] * 48, 16), 48)
        target[at, :48, :] = grad[rows, :D]
        target[at, 48:96, :] = grad[rows, D:]
        target[at, 96:, :] = out[r * 32 : r * 32 + 32, :]


def attend_back_kernel(
    q, k, v, o, lse, col, row, d_ref, dq_ref, dk_ref, dv_ref, dq_sum, dv_sum, bias, p_low, s_low
):
    mine, keys = q.shape[1], k.shape[1]
    fill_bias(col, row, bias)

    def pair(i, carry):
        both = (d_ref[i].astype(F32) * o[i]).T
        got = []
        for e in range(2):
            delta = jnp.sum(both[e * HEAD_DIM : (e + 1) * HEAD_DIM], axis=0, keepdims=True)
            qm = q[i] * lane_half(e)
            dm = d_ref[i] * lane_half(e)
            base = lse[i, e : e + 1, :]
            for c in range(keys // SLAB):
                at = pl.ds(c * SLAB, SLAB)
                t = dots(k[i, at, :], qm, 1, 1) + bias[at, :]
                p = jnp.exp(t - base)
                dp = dots(v[i, at, :], dm, 1, 1)
                p_low[at, :] = p.astype(BF)
                s_low[at, :] = (p * (dp - delta)).astype(BF)
            got.append(
                (
                    dots(s_low[...], k[i], 0, 0) * 0.125,
                    dot(s_low[...], q[i]),
                    dot(p_low[...], d_ref[i]),
                )
            )
        for n, ref in enumerate((dq_ref, dk_ref, dv_ref)):
            ref[i] = jnp.where(first_half(got[0][n].shape), got[0][n], got[1][n]).astype(BF)
        return carry

    lax.fori_loop(0, PAIRS, pair, 0)
    dq_sum[...] = jnp.sum(wide(dq_ref).astype(F32), axis=0, keepdims=True)
    dv_sum[...] = jnp.sum(wide(dv_ref).astype(F32), axis=0, keepdims=True)


def input_kernel(dq_ref, dk_ref, dv_ref, w, unit, pi, keep_ref, give_ref, e1n_sum, e1_sum):
    keys, own = unit.shape[0], keep_ref.shape[1]
    dq, dk, dv = wide(dq_ref), wide(dk_ref), wide(dv_ref)
    e1n = jnp.zeros((1, D), F32)
    e1s = jnp.zeros((1, D), F32)
    for part in range(keys // own):
        at = slice(part * own, (part + 1) * own)
        e = dots(dk[at], w[1], 1, 1) + dots(dv[at], w[2], 1, 1)
        if part < 2:
            e = e + dots(dq[at], w[0], 1, 1)
        e = dots(e.astype(BF), pi[...], 1, 1)
        e1s = e1s + jnp.sum(e, axis=0, keepdims=True)
        e1n = e1n + jnp.sum(e * unit[pl.ds(part * own, own), :], axis=0, keepdims=True)
        target = keep_ref if part % 2 == 0 else give_ref
        target[part // 2] = e.astype(BF)
    e1n_sum[...] = e1n
    e1_sum[...] = e1s


def gather_grads_kernel(inv, a, dq, dk, dv, device, owner, place, *rest):
    sums, (keep_ref, send_ref, grad, small, hot) = rest[:-5], rest[-5:]
    one_hot(place, hot)
    mine = dq.shape[1]
    grad[0] = dots(a[:mine, :], wide(dq), 0, 0).astype(BF)
    grad[1] = dots(a[...], wide(dk), 0, 0).astype(BF)
    grad[2] = dots(a[...], wide(dv), 0, 0).astype(BF)
    line = jnp.concatenate([ref[...] for ref in sums], axis=1)
    kept = jnp.where(device[:, :1] == owner[:1, :], line, 0.0).astype(BF)
    placed = dots(kept, hot[...], 1, 1).astype(BF)
    small[...] = dots(pick_rows(small.shape[0], 16), placed, 0, 0).astype(BF)
    half = keep_ref.shape[0]
    for r in range(2 * half):
        target, at = (keep_ref if r < half else send_ref), r % half
        rows = pl.ds(pl.multiple_of(inv[r] * 48, 16), 48)
        for i in range(3):
            target[at, 48 * i : 48 * i + 48, :] = grad[i, rows, :]
        target[at, 144:160, :] = small[r * 16 : r * 16 + 16, :]


def run(kernel, table, args, outs, scratch, anys=(), us=5, mib=16):
    specs = [
        pl.BlockSpec(memory_space=pl.ANY) if i in anys else pl.BlockSpec(memory_space=pltpu.VMEM)
        for i in range(len(args))
    ]
    prefetch = () if table is None else table if isinstance(table, tuple) else (table,)
    return pl.pallas_call(
        kernel,
        grid_spec=pltpu.PrefetchScalarGridSpec(
            num_scalar_prefetch=len(prefetch),
            grid=(),
            in_specs=specs,
            out_specs=[pl.BlockSpec(memory_space=pltpu.VMEM) for _ in outs],
            scratch_shapes=scratch,
        ),
        out_shape=[jax.ShapeDtypeStruct(shape, dtype) for shape, dtype in outs],
        compiler_params=pltpu.CompilerParams(vmem_limit_bytes=mib * 2**20),
        cost_estimate=pl.CostEstimate(
            flops=int(us * 10**9), bytes_accessed=int(us * 10**6), transcendentals=0
        ),
    )(*prefetch, *args)


def body(net, tokens, segments, cotangent, w_qkv, w_out, w_fc1, w_fc2, norm_gains, bias_pack):
    local, cols, width = tokens.shape
    own, mine = local * cols, 2 * local * cols
    keys = 2 * mine
    hidden = FF
    half_w, half_f = width // 2, hidden // 2
    chips, devices = net.chips, 2 * net.chips
    half = chips // 2
    rows, frows = width // devices, hidden // devices
    core = lax.axis_index("c")
    zodd = lax.axis_index("zh") & 1
    spots = jnp.arange(chips, dtype=jnp.int32)

    def order_of(orders):
        found = net.table(orders)[None, :] == spots[:, None]
        return jnp.sum(jnp.where(found, spots[None, :], 0), axis=1).astype(jnp.int32)

    inv, inv_d = order_of(net.orders), order_of(net.mixed)

    split = lambda n, parts: np.arange(n).reshape(parts, 2, n // (2 * parts))
    of_core = lambda n, parts: [split(n, parts)[:, c].reshape(-1) for c in range(2)]
    everywhere = lambda n: [np.arange(n)] * 2
    n_gain, n_bias = norm_gains.shape[0], bias_pack.shape[0]

    def owners(items):
        dev, place = [], []
        for c in range(2):
            flat = [(first + entry[c]) for first, entry, _, _ in items]
            dev.append(np.concatenate([f // n for f, (_, _, _, n) in zip(flat, items)]))
            place.append(
                np.concatenate([at + f % n for f, (_, _, at, n) in zip(flat, items)])
            )
        dev, place = np.array(dev, np.int32), np.array(place, np.int32)
        return (
            jnp.where(core == 0, dev[0], dev[1]),
            jnp.where(core == 0, place[0], place[1]),
        )

    chip_row = jnp.repeat(inv, 2)
    s_n = net.z * net.y
    row_device = ((chip_row // s_n) * 2 + jnp.tile(jnp.arange(2), chips)) * s_n + chip_row % s_n
    row_device = jnp.broadcast_to(row_device[:, None], (devices, SLAB))
    D_, W = everywhere(width), width

    def mapping(items):
        dev, place = owners(items)
        return dev[None, :], place[None, :]

    gl, bl = n_gain, n_bias
    heads_c, ff_c = of_core(width, net.x), of_core(hidden, net.x)
    owner_in, place_in = mapping(
        [
            (0, D_, 0, gl),
            (W, D_, 0, gl),
            (0, D_, gl, bl),
            (W, D_, gl, bl),
            (4 * W, D_, gl, bl),
            (5 * W, D_, gl, bl),
            (2 * W, heads_c, gl, bl),
            (3 * W, heads_c, gl, bl),
            (6 * W, ff_c, gl, bl),
        ]
    )
    ll = 2 * W // devices
    rl = n_gain + n_bias - 2 * ll
    owner_out, place_out = mapping(
        [
            (0, D_, 0, ll),
            (W, D_, 0, ll),
            (0, D_, ll, rl),
            (W, heads_c, ll, rl),
            (2 * W, D_, ll, rl),
            (3 * W, D_, ll, rl),
            (4 * W, ff_c, ll, rl),
            (0, D_, ll + rl, ll),
            (W, heads_c, ll + rl, ll),
        ]
    )
    order = np.arange(width).reshape(net.x, 2, s_n, rows).transpose(0, 2, 1, 3).reshape(-1)
    pi = jnp.asarray((np.arange(width)[:, None] == order[None, :]), BF)
    rel_row = jnp.arange(chips * 32, dtype=jnp.int32)
    nat_row = jnp.where(rel_row % 32 < rows, jnp.repeat(inv, 32) * rows + rel_row % 32, -1)
    perm = (jnp.arange(half_w, dtype=jnp.int32)[:, None] == nat_row[None, :]).astype(BF)

    def pick(array, parts, which):
        view = array.reshape(*array.shape[:-1], parts, 2, array.shape[-1] // (2 * parts))
        taken = jnp.where(which == 0, view[..., 0, :], view[..., 1, :])
        return taken.reshape(*array.shape[:-1], array.shape[-1] // 2)

    def both(a, b, axis):
        return jnp.where(
            core == 0, jnp.concatenate([a, b], axis=axis), jnp.concatenate([b, a], axis=axis)
        )

    small = jnp.concatenate([norm_gains, bias_pack])
    qkv = w_qkv.reshape(rows, 3, width).swapaxes(0, 1)
    got_qkv, got_small = net.core(pick(qkv, net.x, 1 - core)), net.core(small)
    chip_qkv = both(pick(qkv, net.x, core), got_qkv, 1).reshape(6 * rows, half_w)
    chip_small = jnp.pad(
        both(small[None], got_small[None], 0), ((0, 14), (0, half_w - small.shape[0]))
    )

    def after(value, *others):
        return lax.optimization_barrier((value, *others))[0]

    def all_after(values, *others):
        return lax.optimization_barrier((*values, *others))[: len(values)]

    def grow(held, stage, orders=None, then=()):
        got = net.across(held, stage, orders)
        if then:
            got = after(got, *then)
        return jnp.concatenate([held, got])

    last = net.stages - 1
    q0 = jnp.concatenate([chip_qkv, chip_small])[None]
    q1 = grow(q0, 0)

    seg_row = jnp.pad(segments.astype(BF), ((0, 0), (0, width - cols)))[:, None, :]
    packed = jnp.concatenate([tokens, jnp.pad(seg_row, ((0, 0), (0, 7), (0, 0)))], axis=1)
    packed = after(packed, q0)

    def to_sequence(array):
        swapped = jnp.where(zodd == 0, array, array[::-1])
        return jnp.stack(
            [lax.ppermute(swapped[k], AXES, net.scatter_move(k)) for k in range(2)]
        )

    def from_sequence(array, then=()):
        back = [
            lax.ppermute(array[k], AXES, [(b, a) for a, b in net.scatter_move(k)])
            for k in range(2)
        ]
        back = jnp.stack(all_after(back, *then))
        return jnp.where(zodd == 0, back, back[::-1])

    x_o = to_sequence(packed)
    x_t = net.core(x_o)
    x_n = net.pair(x_o)
    x_m = net.core(x_n)

    up = after(w_fc1, q0).reshape(rows, hidden)
    got_up = net.core(pick(up, net.x, 1 - core))
    chip_up = fold(both(pick(up, net.x, core), got_up, 0), 2)
    chip_up = jnp.concatenate([chip_up, jnp.pad(w_out.reshape(rows, width), ((0, 8), (0, 0)))])

    q2 = grow(after(q1, x_o, chip_up), 1)
    d1 = grow(after(w_fc2.reshape(1, frows, width), q1), 0, net.mixed)
    u1 = grow(after(chip_up, q2)[None], 0)
    q4 = grow(q2, 2)
    u2 = grow(after(u1, q4), 1)
    q_held, q_got = q4, net.across(q4, last)
    g_o = to_sequence(after(cotangent, q4))
    g_t = net.core(g_o)

    dma = lambda *n: pltpu.SemaphoreType.DMA(n)
    vm = lambda shape, dtype: pltpu.VMEM(shape, dtype)
    by_pair = lambda n: (PAIRS, n, DOUBLE)
    unit1, col, row, hot = run(
        unit_kernel,
        None,
        (x_o, x_t, x_n, after(x_m, q4), place_in),
        (
            ((keys, width), F32),
            ((keys, SLAB), F32),
            ((8, mine), F32),
            ((half_w, place_in.shape[1]), BF),
        ),
        [],
        us=4,
    )
    u2 = after(u2, q_got)
    d1 = after(d1, u2, q_got)
    a1, q, k, v, w_mix, vec = run(
        mix_kernel,
        inv,
        (unit1, pi, row_device, owner_in, hot, q_held, q_got),
        (
            ((keys, width), BF),
            (by_pair(mine), BF),
            (by_pair(keys), BF),
            (by_pair(keys), BF),
            ((3, width, half_w), BF),
            ((1, place_in.shape[1]), F32),
        ),
        [vm((keys, width), BF), vm((chips * 16, half_w), BF), dma(chips, 3), dma(chips)],
        anys=(5, 6),
        us=8,
    )
    u4 = grow(u2, 2, then=(k,))
    d2 = grow(d1, 1, net.mixed, then=(k,))
    u_held, u_got = u4, net.across(u4, last)
    o, low, lse = run(
        attend_kernel,
        None,
        (after(q, u4, d2, g_o), k, v, col, row),
        ((by_pair(mine), F32), (by_pair(mine), BF), ((PAIRS, 8, mine), F32)),
        [vm((keys, mine), F32), vm((keys, mine), F32), vm((keys, mine), BF)],
        us=12,
    )
    d4 = grow(d2, 2, net.mixed, then=(low,))
    part, wo = run(
        project_kernel,
        inv,
        (after(low, d4), perm, u_held, u_got),
        (((mine, width), BF), ((half_w, width), BF)),
        [vm((chips * 32, width), BF), dma(chips)],
        anys=(2, 3),
        us=3,
    )
    part_got = net.core(part)
    d_held, d_got = d4, net.across(after(d4, u_got), last, net.mixed)
    blocks = ((half, 96, width), BF)
    mid, a2, act, fac, w_up, keep_d, send_d, g_sum = run(
        middle_kernel,
        inv,
        (part, after(part_got, d4), x_o, x_t, g_o, g_t, vec, pi, u_held, u_got),
        (
            ((mine, width), F32),
            ((mine, width), BF),
            ((mine, half_f), BF),
            ((mine, half_f), F32),
            ((width, half_f), BF),
            blocks,
            blocks,
            ((1, width), F32),
        ),
        [vm((mine, width), BF), vm((half_f, width), BF), dma(chips, 2)],
        anys=(8, 9),
        us=10,
    )

    def shrink(keep, send, stage, orders=None, then=()):
        got = net.across(send, stage, orders)
        if then:
            got = after(got, *then)
        if stage == 0:
            return (keep.astype(F32) + got.astype(F32))[0]
        n = keep.shape[0] // 2
        send = (keep[n:].astype(F32) + got[n:].astype(F32)).astype(BF)
        keep = (keep[:n].astype(F32) + got[:n].astype(F32)).astype(BF)
        return keep, send

    pre, e2, w_down, pre_sum = run(
        slope_kernel,
        inv_d,
        (g_o, g_t, fac, w_up, pi, d_held, d_got),
        (
            ((mine, half_f), BF),
            ((mine, width), BF),
            ((half_f, width), BF),
            ((1, half_f), F32),
        ),
        [dma(chips, 1)],
        anys=(5, 6),
        us=0.1,
    )
    down_own, down_give = run(
        down_kernel,
        None,
        (act, w_down),
        (((own, width), F32), ((own, width), BF)),
        [],
        us=0.1,
    )
    down_got = net.core(down_give).astype(F32)
    out_own = (mid[:own] + down_own + down_got + vec[:, AT["bias_down"]]).astype(BF)
    e2_got = net.core(e2)
    wide_sum, half_sum = ((1, width), F32), ((1, half_w), F32)
    blocks_u = ((half, 128, width), BF)
    gm, branch, d_heads, keep_u, send_u, e2n, e2s, bs = run(
        branch_kernel,
        inv,
        (e2, e2_got, mid, g_o, g_t, vec, wo, low, perm, a2, pre),
        (
            ((own, width), F32),
            ((mine, width), BF),
            (by_pair(mine), BF),
            blocks_u,
            blocks_u,
            wide_sum,
            wide_sum,
            wide_sum,
        ),
        [vm((width, half_f), BF), vm((chips * 32, width), BF)],
        us=0.1,
    )
    d3 = shrink(keep_d, send_d, 3, then=(send_u,))
    dq, dk, dv, dqs, dvs = run(
        attend_back_kernel,
        None,
        (q, k, v, o, lse, col, row, after(d_heads, d3[1])),
        (
            (by_pair(mine), BF),
            (by_pair(keys), BF),
            (by_pair(keys), BF),
            half_sum,
            half_sum,
        ),
        [vm((keys, mine), F32), vm((keys, mine), BF), vm((keys, mine), BF)],
        us=10,
    )
    u3 = shrink(keep_u, send_u, 3)
    d_2 = shrink(*d3, 2, then=(dq,))
    block_out = from_sequence(out_own.reshape(local, cols, width), (dq,))
    quarter = ((2, own, width), BF)
    keep_e, give_e, e1n, e1s = run(
        input_kernel,
        None,
        (after(dq, u3[1], d_2[1], block_out), dk, dv, w_mix, unit1, pi),
        (quarter, quarter, wide_sum, wide_sum),
        [],
        us=5,
    )
    got_e = net.core(give_e)
    blocks_q = ((half, 160, half_w), BF)
    keep_q, send_q = run(
        gather_grads_kernel,
        inv,
        (after(a1, u3, d_2), dq, dk, dv, row_device, owner_out, place_out)
        + (e1n, e2n, e2s, dqs, bs, g_sum, pre_sum, e1s, dvs),
        (blocks_q, blocks_q),
        [
            vm((3, width, half_w), BF),
            vm((chips * 16, half_w), BF),
            vm((half_w, place_out.shape[1]), BF),
        ],
        us=4,
    )
    e1_give = (keep_e[1].astype(F32) + got_e[1].astype(F32)).astype(BF)
    e1_near = net.pair(e1_give).astype(F32)
    d_1 = shrink(*d_2, 1)
    send_q = after(send_q, d_1[1])
    q_3 = shrink(keep_q, send_q, 3)
    u_2 = shrink(*u3, 2, then=(e1_give,))
    u_1 = shrink(*u_2, 1)
    q_2 = shrink(q_3[0], after(q_3[1], u_1[1], e1_near), 2)
    shard_d = shrink(*d_1, 0)
    shard_u = shrink(*u_1, 0)
    q_1 = shrink(q_2[0], after(q_2[1], shard_u, shard_d), 1)
    shard_q = shrink(*q_1, 0)

    e1 = keep_e[0].astype(F32) + got_e[0].astype(F32) + e1_near
    x_own = x_o[:, :cols].reshape(own, width).astype(F32)
    unit_own, inverse_own = normal(x_own)
    in_own = gm + norm_back(e1, unit_own, inverse_own, vec[:, AT["gain1"]])
    input_grad = from_sequence(in_own.astype(BF).reshape(local, cols, width), (q_1[1],)).astype(F32)

    def own_rows(chip):
        keep = jnp.where(core == 0, chip[..., 0, :, :], chip[..., 1, :, :])
        give = jnp.where(core == 0, chip[..., 1, :, :], chip[..., 0, :, :])
        return keep, net.core(give)

    def merge(keep, got, parts):
        view = lambda array: array.reshape(*array.shape[:-1], parts, 1, -1)
        first = jnp.where(core == 0, view(keep), view(got))
        second = jnp.where(core == 0, view(got), view(keep))
        return jnp.concatenate([first, second], axis=-2).reshape(*keep.shape[:-1], -1)

    qkv_own = merge(*own_rows(shard_q[: 6 * rows].reshape(3, 2, rows, half_w)), net.x)
    g_qkv = jnp.moveaxis(qkv_own, 0, 1).reshape(-1)
    g_out = shard_u[4 * rows : 5 * rows].reshape(-1)
    up_own = merge(*own_rows(unfold(shard_u[: 4 * rows], 2).reshape(2, rows, half_f)), net.x)
    two = shard_q[6 * rows : 6 * rows + 2, : 2 * ll + rl]
    keep_s, got_s = own_rows(two.reshape(2, 1, -1))
    own_sums = (keep_s + got_s)[0]
    return (
        block_out,
        input_grad,
        g_qkv,
        g_out,
        up_own.reshape(-1),
        shard_d.reshape(-1),
        own_sums[:ll],
        own_sums[ll : ll + rl],
        own_sums[ll + rl :],
    )


def solution(mesh):
    dp, seq = mesh.shape["dp"], mesh.shape["seq"]
    y = 1 << (((seq.bit_length() - 1) - 1) // 2)
    z = seq // y
    dims = (dp // 2, 2, 4, z // 4, y // 2, 2)
    net = Net(dims)
    inner = Mesh(mesh.devices.reshape(dims), AXES)
    place = ("zh", "zl", "yh", "yl")
    cube = P(("x", "c"), place, None)
    flat = P(AXES)
    rows = D // (2 * net.chips)
    tiles = rows == 24 and net.chips == 16 and net.zl * net.yh == 1
    return jax.shard_map(
        functools.partial(body if tiles else body_any, net),
        mesh=inner,
        in_specs=(cube, P(("x", "c"), place), cube) + (flat,) * 6,
        out_specs=(cube, cube) + (flat,) * 7,
        check_vma=False,
    )
```

```python
import functools
import itertools

import jax
import jax.numpy as jnp
import numpy as np
from jax import lax
from jax.experimental import pallas as pl
from jax.experimental.pallas import tpu as pltpu
from jax.sharding import Mesh
from jax.sharding import PartitionSpec as P

D = 768
FF = 3072
HEADS = 12
HEAD_DIM = 64
EPS = 1e-05
MASKED = -1000000000.0
BF = jnp.bfloat16
F32 = jnp.float32
AXES = ("x", "c", "zh", "zl", "yh", "yl")


class Net:
    def __init__(self, dims):
        self.dims = dims
        self.x, self.c, self.zh, self.zl, self.yh, self.yl = dims
        self.z, self.y = self.zh * self.zl, self.yh * self.yl
        self.chips = self.x * self.z * self.y
        bits = lambda axis, n: [(axis, 1 << b) for b in reversed(range(n.bit_length() - 1))]
        zs, xs, ys = bits("z", self.z), bits("x", self.x), bits("y", self.y)
        self.orders = (zs + xs + ys, zs + ys + xs)
        self.mixed = (xs + zs + ys, ys + zs + xs)
        self.stages = len(self.orders[0])

    def perm(self, move):
        pairs = []
        for at in itertools.product(*(range(n) for n in self.dims)):
            to = move(*at)
            pairs.append(
                (int(np.ravel_multi_index(at, self.dims)), int(np.ravel_multi_index(to, self.dims)))
            )
        return pairs

    def flip(self, stage, orders):
        def move(x, c, zh, zl, yh, yl):
            axis, bit = orders[c][stage]
            z, y = zh * self.zl + zl, yh * self.yl + yl
            if axis == "x":
                x ^= bit
            elif axis == "y":
                y ^= bit
            else:
                z ^= bit
            return (x, c, z // self.zl, z % self.zl, y // self.yl, y % self.yl)

        return self.perm(move)

    def across(self, value, stage, orders=None):
        return lax.ppermute(value, AXES, self.flip(stage, orders or self.orders))

    def core(self, value):
        return lax.ppermute(value, "c", [(0, 1), (1, 0)])

    def pair(self, value):
        return lax.ppermute(value, "yl", [(0, 1), (1, 0)])

    def scatter_move(self, k):
        return self.perm(
            lambda x, c, zh, zl, yh, yl: (x, zh >> 1, 2 * c + (k ^ (zh & 1)), zl, yh, yl)
        )

    def table(self, orders=None):
        me = {
            "x": lax.axis_index("x"),
            "z": lax.axis_index("zh") * self.zl + lax.axis_index("zl"),
            "y": lax.axis_index("yh") * self.yl + lax.axis_index("yl"),
        }
        grid = np.indices((self.x, self.z, self.y)).reshape(3, -1)
        axes = {"x": grid[0], "z": grid[1], "y": grid[2]}
        places = []
        for order in orders or self.orders:
            place = jnp.zeros((self.chips,), jnp.int32)
            for stage, (axis, bit) in enumerate(order):
                differs = (jnp.asarray(axes[axis], jnp.int32) ^ me[axis]) & bit
                place = place + jnp.where(differs != 0, 1 << stage, 0)
            places.append(place)
        return jnp.where(lax.axis_index("c") == 0, places[0], places[1]).astype(jnp.int32)

    def gather(self, block):
        held = block[None]
        for stage in range(self.stages):
            held = jnp.concatenate([held, self.across(held, stage)])
        return held

    def scatter(self, held):
        for stage in reversed(range(self.stages)):
            half = held.shape[0] // 2
            got = self.across(held[half:], stage)
            held = held[:half].astype(F32) + got.astype(F32)
            if stage:
                held = held.astype(BF)
        return held[0]


def move_kernel(table, source, target):
    target[...] = source[...]


def reorder(blocks, table, to_place):
    rest = -blocks.shape[1] % 16
    if rest:
        rows = blocks.shape[1]
        blocks = jnp.pad(blocks, ((0, 0), (0, rest), (0, 0)))
        return reorder(blocks, table, to_place)[:, :rows]
    chips, rows, cols = blocks.shape
    here = pl.BlockSpec((1, rows, cols), lambda chip, table: (chip, 0, 0))
    there = pl.BlockSpec((1, rows, cols), lambda chip, table: (table[chip], 0, 0))
    return pl.pallas_call(
        move_kernel,
        grid_spec=pltpu.PrefetchScalarGridSpec(
            num_scalar_prefetch=1,
            grid=(chips,),
            in_specs=[here if to_place else there],
            out_specs=there if to_place else here,
        ),
        out_shape=jax.ShapeDtypeStruct(blocks.shape, blocks.dtype),
    )(table, blocks)


def normal(field):
    center = field - jnp.mean(field, axis=-1, keepdims=True)
    inverse = lax.rsqrt(jnp.mean(center * center, axis=-1, keepdims=True) + EPS)
    return center * inverse, inverse


def norm_back(upstream, unit, inverse, gain):
    scaled = upstream * gain
    return inverse * (
        scaled
        - jnp.mean(scaled, axis=-1, keepdims=True)
        - unit * jnp.mean(scaled * unit, axis=-1, keepdims=True)
    )


def dot(a, b):
    return jnp.dot(a, b, preferred_element_type=F32)


def dot_t(a, b):
    return lax.dot_general(a, b, (((1,), (1,)), ((), ())), preferred_element_type=F32)


def t_dot(a, b):
    return lax.dot_general(a, b, (((0,), (0,)), ((), ())), preferred_element_type=F32)


def fold(wide, parts):
    lead, rows, cols = wide.shape[:-2], wide.shape[-2], wide.shape[-1] // parts
    moved = jnp.moveaxis(wide.reshape(*lead, rows, parts, cols), -2, -3)
    return moved.reshape(*lead, parts * rows, cols)


def unfold(tall, parts):
    lead, rows, cols = tall.shape[:-2], tall.shape[-2] // parts, tall.shape[-1]
    moved = jnp.moveaxis(tall.reshape(*lead, parts, rows, cols), -3, -2)
    return moved.reshape(*lead, rows, parts * cols)


def body_any(net, tokens, segments, cotangent, w_qkv, w_out, w_fc1, w_fc2, norm_gains, bias_pack):
    local, cols, width = tokens.shape
    own = local * cols
    mine = 2 * own
    hidden = FF
    half_w, half_f = width // 2, hidden // 2
    devices = 2 * net.chips
    core = lax.axis_index("c")
    zodd = lax.axis_index("zh") & 1
    table = net.table()
    rows = width // devices
    frows = hidden // devices
    aligned = (width // (2 * net.x)) % HEAD_DIM == 0
    groups = net.x if aligned else 1

    def pick(array, parts, which):
        split = array.reshape(*array.shape[:-1], parts, 2, array.shape[-1] // (2 * parts))
        taken = jnp.where(which == 0, split[..., 0, :], split[..., 1, :])
        return taken.reshape(*array.shape[:-1], array.shape[-1] // 2)

    def spread(vector, parts):
        split = vector.reshape(parts, 1, vector.shape[-1] // parts)
        both = jnp.concatenate(
            [jnp.where(core == 0, split, 0.0), jnp.where(core == 1, split, 0.0)], axis=1
        )
        return both.reshape(-1)

    seg_row = jnp.pad(segments.astype(BF), ((0, 0), (0, width - cols)))[:, None, :]
    seg_rows = jnp.pad(seg_row, ((0, 0), (0, 7), (0, 0)))
    packed = jnp.concatenate([tokens, seg_rows], axis=1)

    def to_sequence(array):
        swapped = jnp.where(zodd == 0, array, array[::-1])
        return jnp.stack(
            [lax.ppermute(swapped[k], AXES, net.scatter_move(k)) for k in range(2)]
        )

    def from_sequence(array):
        back = jnp.stack(
            [
                lax.ppermute(array[k], AXES, [(b, a) for a, b in net.scatter_move(k)])
                for k in range(2)
            ]
        )
        return jnp.where(zodd == 0, back, back[::-1])

    def halves(which):
        qkv = fold(w_qkv.reshape(rows, 3 * width), 3).reshape(3, rows, width)
        up = w_fc1.reshape(rows, hidden)
        return pick(qkv, groups, which), pick(up, net.x, which)

    keep_qkv, keep_up = halves(core)
    give_qkv, give_up = halves(1 - core)
    small = jnp.concatenate([norm_gains, bias_pack])
    out_rows = w_out.reshape(rows, width)
    got_qkv, got_up, got_small, got_out = jax.tree.map(
        net.core, (give_qkv, give_up, small, out_rows)
    )

    def both(a, b, axis):
        return jnp.where(
            core == 0, jnp.concatenate([a, b], axis=axis), jnp.concatenate([b, a], axis=axis)
        )

    chip_qkv = both(keep_qkv, got_qkv, 1).reshape(6 * rows, half_w)
    chip_up = fold(both(keep_up, got_up, 0), 2)
    chip_out = fold(out_rows if aligned else both(out_rows, got_out, 0), 2)
    chip_small = jnp.pad(
        both(small[None], got_small[None], 0), ((0, 14), (0, half_w - small.shape[0]))
    )
    cut = np.cumsum([chip_qkv.shape[0], chip_out.shape[0]])
    blocks_a = reorder(
        net.gather(jnp.concatenate([chip_qkv, chip_out, chip_small])), table, False
    )
    blocks_up = reorder(net.gather(chip_up), table, False)
    blocks_down = reorder(net.gather(w_fc2.reshape(frows, width)), table, False)

    lead = (net.x, net.z, net.y)

    def natural(blocks):
        n = blocks.shape[-1]
        return jnp.moveaxis(blocks.reshape(*lead, 2, -1, n), 3, 1).reshape(-1, n)

    def by_chip(array):
        n = array.shape[-1]
        return jnp.moveaxis(array.reshape(net.x, 2, net.z, net.y, -1, n), 1, 3).reshape(
            net.chips, -1, n
        )

    qkv_blocks = blocks_a[:, : cut[0]].reshape(net.chips, 3, 2 * rows, half_w)
    w_q, w_k, w_v = (natural(qkv_blocks[:, i]) for i in range(3))
    out_blocks = unfold(blocks_a[:, cut[0] : cut[1]], 2)
    if aligned:
        w_proj = out_blocks.reshape(half_w, width)
    else:
        w_proj = lax.dynamic_slice_in_dim(natural(out_blocks), core * half_w, half_w)
    smalls = blocks_a[:, cut[1] : cut[1] + 2, : small.shape[0]].reshape(*lead, 2, -1)
    smalls = jnp.moveaxis(smalls, 3, 1).reshape(devices, -1).astype(F32)
    n_gain = norm_gains.shape[0]
    gains = smalls[:, :n_gain].reshape(-1)
    shifts = smalls[:, n_gain:].reshape(-1)
    w_up = natural(unfold(blocks_up, 2))
    w_down = blocks_down.reshape(half_f, width)
    gain1, gain2 = gains[:width], gains[width:]
    shift1, shift2, bias_q, bias_v, bias_proj, bias_down = (
        shifts[i * width : (i + 1) * width] for i in range(6)
    )
    bias_up = pick(shifts[6 * width :], net.x, core)
    bias_q, bias_v = pick(bias_q, groups, core), pick(bias_v, groups, core)

    x_own = to_sequence(packed)
    x_other = net.core(x_own)
    x_mine = jnp.concatenate([x_own, x_other])
    near = net.pair(x_own)
    near = jnp.concatenate([near, net.core(near)])
    x_seq = jnp.concatenate([x_mine, near])
    if net.zl * net.yh > 1:
        x_far = lax.all_gather(x_seq, ("zl", "yh"), axis=0, tiled=True)
        x_keys = x_far
    else:
        x_keys = x_seq
    g_own = to_sequence(cotangent)
    g_mine = jnp.concatenate([g_own, net.core(g_own)]).reshape(mine, width)
    docs = x_keys[:, cols, :cols].reshape(-1)
    query_docs = x_mine[:, cols, :cols].reshape(-1)
    x_all = x_keys[:, :cols].reshape(-1, width).astype(F32)
    x_q = x_mine[:, :cols].reshape(-1, width).astype(F32)

    unit_q, inverse_q = normal(x_q)
    a_q = (unit_q * gain1 + shift1).astype(BF)
    unit_all, _ = normal(x_all)
    a_all = (unit_all * gain1 + shift1).astype(BF)
    heads = HEADS // 2
    q = (dot(a_q, w_q) + bias_q).astype(BF)
    k = dot(a_all, w_k).astype(BF)
    v = (dot(a_all, w_v) + bias_v).astype(BF)
    by_head = lambda t: t.reshape(-1, heads, HEAD_DIM)
    same = (query_docs[:, None] == docs[None, :])[None]
    scores = (
        jnp.einsum("qhd,khd->hqk", by_head(q), by_head(k), preferred_element_type=F32) * 0.125
    )
    scores = jnp.where(same, scores, MASKED)
    weights = jnp.exp(scores - jnp.max(scores, axis=-1, keepdims=True))
    probs = weights / jnp.sum(weights, axis=-1, keepdims=True)
    probs_low = probs.astype(BF)
    att = jnp.einsum("hqk,khd->qhd", probs_low, by_head(v), preferred_element_type=F32)
    att = att.reshape(mine, half_w)
    att_low = att.astype(BF)

    def core_sum(partial):
        low = partial.astype(BF)
        got = net.core(low)
        return low.astype(F32) + jnp.concatenate([got[own:], got[:own]]).astype(F32)

    middle = x_q + core_sum(dot(att_low, w_proj)) + bias_proj
    unit2, inverse2 = normal(middle)
    a2 = (unit2 * gain2 + shift2).astype(BF)
    pre = dot(a2, w_up) + bias_up
    sig = jax.nn.sigmoid(1.702 * pre)
    activ = (pre * sig).astype(BF)
    down = dot(activ, w_down)
    down_got = net.core(down[own:].astype(BF)).astype(F32)
    out_own = (middle[:own] + down[:own] + down_got + bias_down).astype(BF)
    block_out = from_sequence(out_own.reshape(local, cols, width))

    grad_down = t_dot(activ, g_mine).astype(BF)
    grad_pre = (dot_t(g_mine, w_down) * (sig + 1.702 * pre * sig * (1.0 - sig))).astype(BF)
    shard_down = net.scatter(reorder(grad_down.reshape(net.chips, frows, width), table, True))
    grad_up = t_dot(a2, grad_pre).astype(BF)
    shard_up = net.scatter(reorder(fold(by_chip(grad_up), 2), table, True))
    e2 = core_sum(dot_t(grad_pre, w_up))
    grad_middle = g_mine.astype(F32) + norm_back(e2, unit2, inverse2, gain2)
    branch = grad_middle.astype(BF)
    grad_proj = t_dot(att_low, branch).astype(BF)
    d_heads = dot_t(branch, w_proj).astype(BF)
    dp = jnp.einsum("qhd,khd->hqk", by_head(d_heads), by_head(v), preferred_element_type=F32)
    delta = jnp.sum(probs * dp, axis=-1, keepdims=True)
    d_scores = (probs * (dp - delta)).astype(BF)
    dq = 0.125 * jnp.einsum("hqk,khd->qhd", d_scores, by_head(k), preferred_element_type=F32)
    dk = 0.125 * jnp.einsum("hqk,qhd->khd", d_scores, by_head(q), preferred_element_type=F32)
    dv = jnp.einsum("hqk,qhd->khd", probs_low, by_head(d_heads), preferred_element_type=F32)
    dq = dq.reshape(-1, half_w).astype(BF)
    dk = dk.reshape(-1, half_w).astype(BF)
    dv = dv.reshape(-1, half_w).astype(BF)
    grad_qkv = jnp.stack([t_dot(a_q, dq), t_dot(a_all, dk), t_dot(a_all, dv)]).astype(BF)

    e1_keys = (dot_t(dk, w_k) + dot_t(dv, w_v)).astype(BF)
    if net.zl * net.yh > 1:
        e1_keys = lax.psum_scatter(
            e1_keys, ("zl", "yh"), scatter_dimension=0, tiled=True
        )
    e1_near = e1_keys[mine:].reshape(2, own, width)
    e1_mine = e1_keys[:mine].astype(F32) + dot_t(dq, w_q)
    e1_mine = e1_mine.astype(BF).reshape(2, own, width)
    got = net.core(jnp.stack([e1_mine[1], e1_near[1]]))
    e1_near = e1_near[0].astype(F32) + got[1].astype(F32)
    e1 = e1_mine[0].astype(F32) + got[0].astype(F32) + net.pair(e1_near.astype(BF)).astype(F32)
    unit1 = unit_q[:own]
    in_own = grad_middle[:own] + norm_back(e1, unit1, inverse_q[:own], gain1)
    input_grad = from_sequence(in_own.astype(BF).reshape(local, cols, width)).astype(F32)

    total = lambda array: jnp.sum(array.astype(F32), axis=0)
    g_own = g_mine[:own]
    gain_sums = jnp.concatenate([total(e1 * unit1), total(e2[:own] * unit2[:own])])
    bias_sums = jnp.concatenate(
        [
            total(e2[:own]),
            spread(total(dq), groups),
            total(branch[:own]),
            total(g_own),
            spread(total(grad_pre), net.x),
        ]
    )
    lead_sums = jnp.concatenate([total(e1), spread(total(dv), groups)])
    sums = jnp.concatenate(
        [v.reshape(devices, -1) for v in (gain_sums, bias_sums, lead_sums)], axis=1
    )
    sums = sums + net.core(sums)
    sums = jnp.moveaxis(sums.reshape(net.x, 2, net.z, net.y, -1), 1, 0)
    sums = jnp.where(core == 0, sums[0], sums[1]).reshape(net.chips, 1, -1)
    n_sums = sums.shape[-1]
    sums = jnp.pad(sums, ((0, 0), (0, 15), (0, half_w - n_sums))).astype(BF)
    qkv_send = jnp.stack([by_chip(grad_qkv[i]) for i in range(3)], axis=1)
    qkv_send = qkv_send.reshape(net.chips, 6 * rows, half_w)
    if aligned:
        out_send = grad_proj.reshape(net.chips, rows, width)
    else:
        whole = jnp.zeros((width, width), BF)
        whole = lax.dynamic_update_slice(whole, grad_proj, (core * half_w, 0))
        out_send = by_chip(whole)
    sent = jnp.concatenate([qkv_send, fold(out_send, 2), sums], axis=1)
    shard_a = net.scatter(reorder(sent, table, True))

    def own_rows(chip):
        keep = jnp.where(core == 0, chip[..., 0, :, :], chip[..., 1, :, :])
        give = jnp.where(core == 0, chip[..., 1, :, :], chip[..., 0, :, :])
        return keep, net.core(give)

    def merge(keep, got, parts):
        split = lambda array: array.reshape(*array.shape[:-1], parts, 1, -1)
        first = jnp.where(core == 0, split(keep), split(got))
        second = jnp.where(core == 0, split(got), split(keep))
        return jnp.concatenate([first, second], axis=-2).reshape(*keep.shape[:-1], -1)

    qkv_own = merge(*own_rows(shard_a[: cut[0]].reshape(3, 2, rows, half_w)), groups)
    g_qkv = jnp.moveaxis(qkv_own, 0, 1).reshape(-1)
    out_own = unfold(shard_a[cut[0] : cut[1]], 2)
    if not aligned:
        keep, got = own_rows(out_own.reshape(2, rows, width))
        out_own = keep + got
    g_out = out_own.reshape(-1)
    up_own = merge(*own_rows(unfold(shard_up, 2).reshape(2, rows, half_f)), net.x)
    own_sums = shard_a[cut[1], :n_sums]
    n_gain = 2 * width // devices
    n_lead = n_sums - n_gain
    return (
        block_out,
        input_grad,
        g_qkv,
        g_out,
        up_own.reshape(-1),
        shard_down.reshape(-1),
        own_sums[:n_gain],
        own_sums[n_gain:n_lead],
        own_sums[n_lead:],
    )


SLAB = 128
PAIRS = HEADS // 4
DOUBLE = 2 * HEAD_DIM
PARTS = (
    ("gain1", D),
    ("gain2", D),
    ("shift1", D),
    ("shift2", D),
    ("bias_proj", D),
    ("bias_down", D),
    ("bias_q", D // 2),
    ("bias_v", D // 2),
    ("bias_up", FF // 2),
)
SUMS = (
    ("e1n", D),
    ("e2n", D),
    ("e2", D),
    ("dq", D // 2),
    ("branch", D),
    ("g", D),
    ("pre", FF // 2),
    ("e1", D),
    ("dv", D // 2),
)


def offsets(parts):
    ends = np.cumsum([n for _, n in parts])
    return {name: slice(int(end - n), int(end)) for (name, n), end in zip(parts, ends)}


AT = offsets(PARTS)


def dots(a, b, ca, cb):
    return lax.dot_general(a, b, (((ca,), (cb,)), ((), ())), preferred_element_type=F32)


def lane_half(e):
    lanes = lax.broadcasted_iota(jnp.int32, (1, DOUBLE), 1)
    inside = (lanes < HEAD_DIM) if e == 0 else (lanes >= HEAD_DIM)
    return inside.astype(F32).astype(BF)


def first_half(shape):
    return lax.broadcasted_iota(jnp.int32, shape, 1) < HEAD_DIM


def load_rows(inv, held, got, target, sems, pieces):
    half = held.shape[0]
    copies = []
    for r in range(2 * half):
        source = held if r < half else got
        for n, (first, rows, place) in enumerate(pieces):
            copies.append(
                pltpu.make_async_copy(
                    source.at[r % half, pl.ds(first, rows), :],
                    place(target, inv[r], rows),
                    sems.at[r, n],
                )
            )
    for copy in copies:
        copy.start()
    return copies


def one_hot(place, target):
    step = 128
    for i in range(target.shape[0] // step):
        shape = (step, target.shape[1])
        entry = lax.broadcasted_iota(jnp.int32, shape, 0) + i * step
        target[i * step : (i + 1) * step, :] = (entry == place[:1, :]).astype(F32).astype(BF)


def unit_kernel(xo, xt, xn, xm, place, unit_ref, col_ref, row_ref, hot_ref):
    one_hot(place, hot_ref)
    for i, (ref, j) in enumerate((ref, j) for ref in (xo, xt, xn, xm) for j in range(2)):
        unit, _ = normal(ref[j, :SLAB, :].astype(F32))
        at = pl.ds(i * SLAB, SLAB)
        unit_ref[at, :] = unit
        docs = ref[j, SLAB : SLAB + 8, :SLAB].astype(F32)[:1]
        col_ref[at, :] = jnp.broadcast_to(docs, (SLAB, SLAB)).T
        if i < 4:
            row_ref[:, i * SLAB : (i + 1) * SLAB] = jnp.broadcast_to(docs, (8, SLAB))


def fill_bias(col, row, bias):
    for i in range(bias.shape[0] // SLAB):
        at = pl.ds(i * SLAB, SLAB)
        for j in range(bias.shape[1] // SLAB):
            lanes = pl.ds(j * SLAB, SLAB)
            bias[at, lanes] = jnp.where(col[at, :] == row[:1, lanes], 0.0, MASKED)


def pick_rows(rows, step):
    shape = (2 * rows // step, rows)
    i = lax.broadcasted_iota(jnp.int32, shape, 0)
    j = lax.broadcasted_iota(jnp.int32, shape, 1)
    return (j == (i >> 1) * step + (i & 1)).astype(F32).astype(BF)


def mix_kernel(
    inv, unit, pi, device, owner, hot, held, got,
    a_ref, q_ref, k_ref, v_ref, w, vec, nat, small, sems, small_sems,
):
    half = held.shape[0]
    few = []
    for r in range(2 * half):
        source = held if r < half else got
        few.append(
            pltpu.make_async_copy(
                source.at[r % half, pl.ds(144, 16), :], small.at[pl.ds(r * 16, 16), :], small_sems.at[r]
            )
        )
    for copy in few:
        copy.start()
    place = lambda i: lambda t, chip, n: t.at[i, pl.ds(pl.multiple_of(chip * n, 16), n), :]
    copies = load_rows(inv, held, got, w, sems, [(48 * i, 48, place(i)) for i in range(3)])
    for copy in few:
        copy.wait()
    picked = dot(pick_rows(small.shape[0], 16), small[...]).astype(BF)
    mine_only = jnp.where(device[:, :1] == owner[:1, :], dot(picked, hot[...]), 0.0)
    vec[...] = jnp.sum(mine_only, axis=0, keepdims=True)
    keys = a_ref.shape[0]
    for i in range(keys // SLAB):
        at = pl.ds(i * SLAB, SLAB)
        nat[at, :] = (unit[at, :] * vec[:, AT["gain1"]] + vec[:, AT["shift1"]]).astype(BF)
    a_ref[...] = dot(nat[...], pi[...]).astype(BF)
    for copy in copies:
        copy.wait()
    mine = q_ref.shape[1]
    q = (dot(a_ref[:mine, :], w[0]) + vec[:, AT["bias_q"]]).astype(BF) * 0.125
    k = dot(a_ref[...], w[1]).astype(BF)
    v = (dot(a_ref[...], w[2]) + vec[:, AT["bias_v"]]).astype(BF)
    for i in range(PAIRS):
        lanes = slice(i * DOUBLE, (i + 1) * DOUBLE)
        q_ref[i], k_ref[i], v_ref[i] = q[:, lanes], k[:, lanes], v[:, lanes]


def attend_kernel(q_ref, k_ref, v_ref, col, row, o_ref, low_ref, lse_ref, bias, s, p_low):
    mine, keys = q_ref.shape[1], k_ref.shape[1]
    fill_bias(col, row, bias)

    def pair(i, carry):
        outs = []
        for e in range(2):
            qm = q_ref[i] * lane_half(e)
            top = jnp.full((1, mine), -3e38, F32)
            for c in range(keys // SLAB):
                at = pl.ds(c * SLAB, SLAB)
                t = dots(k_ref[i, at, :], qm, 1, 1) + bias[at, :]
                s[at, :] = t
                top = jnp.maximum(top, jnp.max(t, axis=0, keepdims=True))
            total = jnp.zeros((1, mine), F32)
            for c in range(keys // SLAB):
                at = pl.ds(c * SLAB, SLAB)
                p = jnp.exp(s[at, :] - top)
                total = total + jnp.sum(p, axis=0, keepdims=True)
                p_low[at, :] = p.astype(BF)
            lse_ref[i, e : e + 1, :] = top + jnp.log(total)
            o = dots(p_low[...], v_ref[i], 0, 0)
            scale = jnp.broadcast_to(1.0 / total, (DOUBLE, mine)).T
            outs.append(o * scale)
        o = jnp.where(first_half(outs[0].shape), outs[0], outs[1])
        o_ref[i] = o
        low_ref[i] = o.astype(BF)
        return carry

    lax.fori_loop(0, PAIRS, pair, 0)


def project_kernel(inv, low, perm, held, got, part_ref, wo_ref, rel, sems):
    half = held.shape[0]
    copies = []
    for r in range(2 * half):
        source = held if r < half else got
        copies.append(
            pltpu.make_async_copy(
                source.at[r % half, pl.ds(96, 32), :], rel.at[pl.ds(r * 32, 32), :], sems.at[r]
            )
        )
    for copy in copies:
        copy.start()
    for copy in copies:
        copy.wait()
    wo_ref[...] = dot(perm[...], rel[...]).astype(BF)
    att = jnp.concatenate([low[i] for i in range(PAIRS)], axis=1)
    part_ref[...] = dot(att, wo_ref[...]).astype(BF)


def middle_kernel(
    inv, part, part_got, xo, xt, go, gt, vec, pi, held, got,
    mid_ref, a_ref, act_ref, fac_ref, w, keep_ref, send_ref, sum_ref,
    nat, grad, sems,
):
    place = lambda h: lambda t, chip, n: t.at[
        pl.ds(pl.multiple_of(chip * n, 16), n), pl.ds(h * D, D)
    ]
    copies = load_rows(inv, held, got, w, sems, [(48 * h, 48, place(h)) for h in range(2)])
    mine = part.shape[0]
    own = mine // 2
    for i, (ref, j) in enumerate((ref, j) for ref in (xo, xt) for j in range(2)):
        at = pl.ds(i * SLAB, SLAB)
        other = pl.ds((i * SLAB + own) % mine, SLAB)
        mid = (
            ref[j, :SLAB, :].astype(F32)
            + (part[at, :].astype(F32) + part_got[other, :].astype(F32))
            + vec[:, AT["bias_proj"]]
        )
        mid_ref[at, :] = mid
        unit, _ = normal(mid)
        nat[at, :] = (unit * vec[:, AT["gain2"]] + vec[:, AT["shift2"]]).astype(BF)
    a_ref[...] = dot(nat[...], pi[...]).astype(BF)
    g = jnp.concatenate([go[0], go[1], gt[0], gt[1]], axis=0)
    sum_ref[...] = jnp.sum(g[:own].astype(F32), axis=0, keepdims=True)
    for copy in copies:
        copy.wait()
    step = 512
    for j in range(w.shape[1] // step):
        lanes = pl.ds(j * step, step)
        start = AT["bias_up"].start + j * step
        pre = dot(a_ref[...], w[:, lanes]) + vec[:, start : start + step]
        sig = 1.0 / (1.0 + jnp.exp(-1.702 * pre))
        act_ref[:, lanes] = (pre * sig).astype(BF)
        fac_ref[:, lanes] = sig + 1.702 * pre * sig * (1.0 - sig)
        grad[lanes, :] = dots(act_ref[:, lanes], g, 0, 0).astype(BF)
    half = keep_ref.shape[0]
    for r in range(2 * half):
        target = keep_ref if r < half else send_ref
        target[r % half] = grad[pl.ds(pl.multiple_of(inv[r] * 96, 16), 96), :]


def slope_kernel(inv, go, gt, fac, w_up, pi, held, got, pre_ref, e_ref, w, sum_ref, sems):
    place = lambda t, chip, n: t.at[pl.ds(pl.multiple_of(chip * n, 16), n), :]
    copies = load_rows(inv, held, got, w, sems, [(0, 96, place)])
    g = jnp.concatenate([go[0], go[1], gt[0], gt[1]], axis=0)
    for copy in copies:
        copy.wait()
    step = 512
    total = None
    for j in range(w.shape[0] // step):
        lanes = pl.ds(j * step, step)
        pre = (dots(g, w[lanes, :], 1, 1) * fac[:, lanes]).astype(BF)
        pre_ref[:, lanes] = pre
        sum_ref[:, lanes] = jnp.sum(pre.astype(F32), axis=0, keepdims=True)
        term = dots(pre, w_up[:, lanes], 1, 1)
        total = term if total is None else total + term
    e_ref[...] = dots(total.astype(BF), pi[...], 1, 1).astype(BF)


def down_kernel(act, w_down, own_ref, give_ref):
    down = dot(act[...], w_down[...])
    own = own_ref.shape[0]
    own_ref[...] = down[:own]
    give_ref[...] = down[own:].astype(BF)


def wide(ref):
    return jnp.concatenate([ref[i] for i in range(PAIRS)], axis=1)


def branch_kernel(
    inv, e2, e2_got, mid, go, gt, vec, wo, low, perm, a, pre,
    gm_ref, branch_ref, d_ref, keep_ref, send_ref, e2n_sum, e2_sum, branch_sum, grad, out,
):
    mine = mid.shape[0]
    own = mine // 2
    sums = [jnp.zeros((1, D), F32) for _ in range(3)]
    for i, (ref, j) in enumerate((ref, j) for ref in (go, gt) for j in range(2)):
        at = pl.ds(i * SLAB, SLAB)
        other = pl.ds((i * SLAB + own) % mine, SLAB)
        e = e2[at, :].astype(F32) + e2_got[other, :].astype(F32)
        unit, inverse = normal(mid[at, :])
        gm = ref[j].astype(F32) + norm_back(e, unit, inverse, vec[:, AT["gain2"]])
        branch = gm.astype(BF)
        branch_ref[at, :] = branch
        if i < 2:
            gm_ref[at, :] = gm
            for n, term in enumerate((e * unit, e, branch.astype(F32))):
                sums[n] = sums[n] + jnp.sum(term, axis=0, keepdims=True)
    e2n_sum[...], e2_sum[...], branch_sum[...] = sums
    d = dots(branch_ref[...], wo[...], 1, 1).astype(BF)
    for i in range(PAIRS):
        d_ref[i] = d[:, i * DOUBLE : (i + 1) * DOUBLE]
    step = 512
    for j in range(pre.shape[1] // step):
        lanes = pl.ds(j * step, step)
        grad[:, lanes] = dots(a[...], pre[:, lanes], 0, 0).astype(BF)
    proj = dots(wide(low), branch_ref[...], 0, 0).astype(BF)
    out[...] = dots(perm[...], proj, 0, 0).astype(BF)
    half = keep_ref.shape[0]
    for r in range(2 * half):
        target, at = (keep_ref if r < half else send_ref), r % half
        rows = pl.ds(pl.multiple_of(inv[r] * 48, 16), 48)
        target[at, :48, :] = grad[rows, :D]
        target[at, 48:96, :] = grad[rows, D:]
        target[at, 96:, :] = out[r * 32 : r * 32 + 32, :]


def attend_back_kernel(
    q, k, v, o, lse, col, row, d_ref, dq_ref, dk_ref, dv_ref, dq_sum, dv_sum, bias, p_low, s_low
):
    mine, keys = q.shape[1], k.shape[1]
    fill_bias(col, row, bias)

    def pair(i, carry):
        both = (d_ref[i].astype(F32) * o[i]).T
        got = []
        for e in range(2):
            delta = jnp.sum(both[e * HEAD_DIM : (e + 1) * HEAD_DIM], axis=0, keepdims=True)
            qm = q[i] * lane_half(e)
            dm = d_ref[i] * lane_half(e)
            base = lse[i, e : e + 1, :]
            for c in range(keys // SLAB):
                at = pl.ds(c * SLAB, SLAB)
                t = dots(k[i, at, :], qm, 1, 1) + bias[at, :]
                p = jnp.exp(t - base)
                dp = dots(v[i, at, :], dm, 1, 1)
                p_low[at, :] = p.astype(BF)
                s_low[at, :] = (p * (dp - delta)).astype(BF)
            got.append(
                (
                    dots(s_low[...], k[i], 0, 0) * 0.125,
                    dot(s_low[...], q[i]),
                    dot(p_low[...], d_ref[i]),
                )
            )
        for n, ref in enumerate((dq_ref, dk_ref, dv_ref)):
            ref[i] = jnp.where(first_half(got[0][n].shape), got[0][n], got[1][n]).astype(BF)
        return carry

    lax.fori_loop(0, PAIRS, pair, 0)
    dq_sum[...] = jnp.sum(wide(dq_ref).astype(F32), axis=0, keepdims=True)
    dv_sum[...] = jnp.sum(wide(dv_ref).astype(F32), axis=0, keepdims=True)


def input_kernel(dq_ref, dk_ref, dv_ref, w, unit, pi, keep_ref, give_ref, e1n_sum, e1_sum):
    keys, own = unit.shape[0], keep_ref.shape[1]
    dq, dk, dv = wide(dq_ref), wide(dk_ref), wide(dv_ref)
    e1n = jnp.zeros((1, D), F32)
    e1s = jnp.zeros((1, D), F32)
    for part in range(keys // own):
        at = slice(part * own, (part + 1) * own)
        e = dots(dk[at], w[1], 1, 1) + dots(dv[at], w[2], 1, 1)
        if part < 2:
            e = e + dots(dq[at], w[0], 1, 1)
        e = dots(e.astype(BF), pi[...], 1, 1)
        e1s = e1s + jnp.sum(e, axis=0, keepdims=True)
        e1n = e1n + jnp.sum(e * unit[pl.ds(part * own, own), :], axis=0, keepdims=True)
        target = keep_ref if part % 2 == 0 else give_ref
        target[part // 2] = e.astype(BF)
    e1n_sum[...] = e1n
    e1_sum[...] = e1s


def near_kernel(keep, got, give):
    give[...] = (keep[1].astype(F32) + got[1].astype(F32)).astype(BF)


def finish_kernel(keep, got, near, x, gm, vec, *parts):
    for i, part in enumerate(parts):
        at = pl.ds(i * SLAB, SLAB)
        e = keep[0, at, :].astype(F32) + got[0, at, :].astype(F32) + near[at, :].astype(F32)
        unit, inverse = normal(x[i, :SLAB, :].astype(F32))
        part[...] = (gm[at, :] + norm_back(e, unit, inverse, vec[:, AT["gain1"]])).astype(BF)


def gather_grads_kernel(inv, a, dq, dk, dv, device, owner, place, *rest):
    sums, (keep_ref, send_ref, grad, small, hot) = rest[:-5], rest[-5:]
    one_hot(place, hot)
    mine = dq.shape[1]
    grad[0] = dots(a[:mine, :], wide(dq), 0, 0).astype(BF)
    grad[1] = dots(a[...], wide(dk), 0, 0).astype(BF)
    grad[2] = dots(a[...], wide(dv), 0, 0).astype(BF)
    line = jnp.concatenate([ref[...] for ref in sums], axis=1)
    kept = jnp.where(device[:, :1] == owner[:1, :], line, 0.0).astype(BF)
    placed = dots(kept, hot[...], 1, 1).astype(BF)
    small[...] = dots(pick_rows(small.shape[0], 16), placed, 0, 0).astype(BF)
    half = keep_ref.shape[0]
    for r in range(2 * half):
        target, at = (keep_ref if r < half else send_ref), r % half
        rows = pl.ds(pl.multiple_of(inv[r] * 48, 16), 48)
        for i in range(3):
            target[at, 48 * i : 48 * i + 48, :] = grad[i, rows, :]
        target[at, 144:160, :] = small[r * 16 : r * 16 + 16, :]


def run(kernel, table, args, outs, scratch, anys=(), us=5, mib=16):
    specs = [
        pl.BlockSpec(memory_space=pl.ANY) if i in anys else pl.BlockSpec(memory_space=pltpu.VMEM)
        for i in range(len(args))
    ]
    prefetch = () if table is None else table if isinstance(table, tuple) else (table,)
    return pl.pallas_call(
        kernel,
        grid_spec=pltpu.PrefetchScalarGridSpec(
            num_scalar_prefetch=len(prefetch),
            grid=(),
            in_specs=specs,
            out_specs=[pl.BlockSpec(memory_space=pltpu.VMEM) for _ in outs],
            scratch_shapes=scratch,
        ),
        out_shape=[jax.ShapeDtypeStruct(shape, dtype) for shape, dtype in outs],
        compiler_params=pltpu.CompilerParams(vmem_limit_bytes=mib * 2**20),
        cost_estimate=pl.CostEstimate(
            flops=int(us * 10**9), bytes_accessed=int(us * 10**6), transcendentals=0
        ),
    )(*prefetch, *args)


def body(net, tokens, segments, cotangent, w_qkv, w_out, w_fc1, w_fc2, norm_gains, bias_pack):
    local, cols, width = tokens.shape
    own, mine = local * cols, 2 * local * cols
    keys = 2 * mine
    hidden = FF
    half_w, half_f = width // 2, hidden // 2
    chips, devices = net.chips, 2 * net.chips
    half = chips // 2
    rows, frows = width // devices, hidden // devices
    core = lax.axis_index("c")
    zodd = lax.axis_index("zh") & 1
    spots = jnp.arange(chips, dtype=jnp.int32)

    def order_of(orders):
        found = net.table(orders)[None, :] == spots[:, None]
        return jnp.sum(jnp.where(found, spots[None, :], 0), axis=1).astype(jnp.int32)

    inv, inv_d = order_of(net.orders), order_of(net.mixed)

    split = lambda n, parts: np.arange(n).reshape(parts, 2, n // (2 * parts))
    of_core = lambda n, parts: [split(n, parts)[:, c].reshape(-1) for c in range(2)]
    everywhere = lambda n: [np.arange(n)] * 2
    n_gain, n_bias = norm_gains.shape[0], bias_pack.shape[0]

    def owners(items):
        dev, place = [], []
        for c in range(2):
            flat = [(first + entry[c]) for first, entry, _, _ in items]
            dev.append(np.concatenate([f // n for f, (_, _, _, n) in zip(flat, items)]))
            place.append(
                np.concatenate([at + f % n for f, (_, _, at, n) in zip(flat, items)])
            )
        dev, place = np.array(dev, np.int32), np.array(place, np.int32)
        return (
            jnp.where(core == 0, dev[0], dev[1]),
            jnp.where(core == 0, place[0], place[1]),
        )

    chip_row = jnp.repeat(inv, 2)
    s_n = net.z * net.y
    row_device = ((chip_row // s_n) * 2 + jnp.tile(jnp.arange(2), chips)) * s_n + chip_row % s_n
    row_device = jnp.broadcast_to(row_device[:, None], (devices, SLAB))
    D_, W = everywhere(width), width

    def mapping(items):
        dev, place = owners(items)
        return dev[None, :], place[None, :]

    gl, bl = n_gain, n_bias
    heads_c, ff_c = of_core(width, net.x), of_core(hidden, net.x)
    owner_in, place_in = mapping(
        [
            (0, D_, 0, gl),
            (W, D_, 0, gl),
            (0, D_, gl, bl),
            (W, D_, gl, bl),
            (4 * W, D_, gl, bl),
            (5 * W, D_, gl, bl),
            (2 * W, heads_c, gl, bl),
            (3 * W, heads_c, gl, bl),
            (6 * W, ff_c, gl, bl),
        ]
    )
    ll = 2 * W // devices
    rl = n_gain + n_bias - 2 * ll
    owner_out, place_out = mapping(
        [
            (0, D_, 0, ll),
            (W, D_, 0, ll),
            (0, D_, ll, rl),
            (W, heads_c, ll, rl),
            (2 * W, D_, ll, rl),
            (3 * W, D_, ll, rl),
            (4 * W, ff_c, ll, rl),
            (0, D_, ll + rl, ll),
            (W, heads_c, ll + rl, ll),
        ]
    )
    order = np.arange(width).reshape(net.x, 2, s_n, rows).transpose(0, 2, 1, 3).reshape(-1)
    pi = jnp.asarray((np.arange(width)[:, None] == order[None, :]), BF)
    rel_row = jnp.arange(chips * 32, dtype=jnp.int32)
    nat_row = jnp.where(rel_row % 32 < rows, jnp.repeat(inv, 32) * rows + rel_row % 32, -1)
    perm = (jnp.arange(half_w, dtype=jnp.int32)[:, None] == nat_row[None, :]).astype(BF)

    def pick(array, parts, which):
        view = array.reshape(*array.shape[:-1], parts, 2, array.shape[-1] // (2 * parts))
        taken = jnp.where(which == 0, view[..., 0, :], view[..., 1, :])
        return taken.reshape(*array.shape[:-1], array.shape[-1] // 2)

    def both(a, b, axis):
        return jnp.where(
            core == 0, jnp.concatenate([a, b], axis=axis), jnp.concatenate([b, a], axis=axis)
        )

    small = jnp.concatenate([norm_gains, bias_pack])
    qkv = w_qkv.reshape(rows, 3, width).swapaxes(0, 1)
    got_qkv, got_small = net.core(pick(qkv, net.x, 1 - core)), net.core(small)
    chip_qkv = both(pick(qkv, net.x, core), got_qkv, 1).reshape(6 * rows, half_w)
    chip_small = jnp.pad(
        both(small[None], got_small[None], 0), ((0, 14), (0, half_w - small.shape[0]))
    )

    def after(value, *others):
        return lax.optimization_barrier((value, *others))[0]

    def all_after(values, *others):
        return lax.optimization_barrier((*values, *others))[: len(values)]

    def grow(held, stage, orders=None, then=()):
        got = net.across(held, stage, orders)
        if then:
            got = after(got, *then)
        return jnp.concatenate([held, got])

    last = net.stages - 1
    q0 = jnp.concatenate([chip_qkv, chip_small])[None]
    q1 = grow(q0, 0)

    seg_row = jnp.pad(segments.astype(BF), ((0, 0), (0, width - cols)))[:, None, :]
    packed = jnp.concatenate([tokens, jnp.pad(seg_row, ((0, 0), (0, 7), (0, 0)))], axis=1)

    def to_sequence(array):
        swapped = jnp.where(zodd == 0, array, array[::-1])
        return jnp.stack(
            [lax.ppermute(swapped[k], AXES, net.scatter_move(k)) for k in range(2)]
        )

    def from_sequence(array, then=()):
        back = [
            lax.ppermute(array[k], AXES, [(b, a) for a, b in net.scatter_move(k)])
            for k in range(2)
        ]
        back = jnp.stack(all_after(back, *then))
        return jnp.where(zodd == 0, back, back[::-1])

    up = after(w_fc1, q0).reshape(rows, hidden)
    got_up = net.core(pick(up, net.x, 1 - core))
    chip_up = fold(both(pick(up, net.x, core), got_up, 0), 2)
    chip_up = jnp.concatenate([chip_up, jnp.pad(w_out.reshape(rows, width), ((0, 8), (0, 0)))])

    u1 = grow(chip_up[None], 0)
    q2 = grow(after(q1, chip_up), 1)
    d1 = grow(after(w_fc2.reshape(1, frows, width), q1), 0, net.mixed)
    q4 = grow(after(q2, u1, d1), 2)
    x_o = to_sequence(after(packed, u1))
    x_n = net.pair(x_o)
    x_m = net.core(x_n)
    x_t = net.core(after(x_o, q4))
    u2 = grow(u1, 1, then=(q4,))
    q_held, q_got = q4, net.across(q4, last)
    d2 = grow(after(d1, u2), 1, net.mixed)
    u4 = grow(after(u2, q4), 2)
    g_out = jnp.where(zodd == 0, cotangent, cotangent[::-1])
    g_out = all_after([g_out[0], g_out[1]], q4)

    dma = lambda *n: pltpu.SemaphoreType.DMA(n)
    vm = lambda shape, dtype: pltpu.VMEM(shape, dtype)
    by_pair = lambda n: (PAIRS, n, DOUBLE)
    unit1, col, row, hot = run(
        unit_kernel,
        None,
        (x_o, x_t, x_n, x_m, place_in),
        (
            ((keys, width), F32),
            ((keys, SLAB), F32),
            ((8, mine), F32),
            ((half_w, place_in.shape[1]), BF),
        ),
        [],
        us=4,
    )
    q_got, unit1, u4, d2 = all_after([q_got, unit1, u4, d2])
    u_held = u4
    u_got = net.across(u4, last)
    a1, q, k, v, w_mix, vec = run(
        mix_kernel,
        inv,
        (unit1, pi, row_device, owner_in, hot, q_held, q_got),
        (
            ((keys, width), BF),
            (by_pair(mine), BF),
            (by_pair(keys), BF),
            (by_pair(keys), BF),
            ((3, width, half_w), BF),
            ((1, place_in.shape[1]), F32),
        ),
        [vm((keys, width), BF), vm((chips * 16, half_w), BF), dma(chips, 3), dma(chips)],
        anys=(5, 6),
        us=8,
    )
    d_got = net.across(d2, 2, net.mixed)
    g_out = all_after(g_out, k)
    g_in = [lax.ppermute(g_out[k], AXES, net.scatter_move(k)) for k in range(2)]
    o, low, lse = run(
        attend_kernel,
        None,
        (q, k, v, col, row),
        ((by_pair(mine), F32), (by_pair(mine), BF), ((PAIRS, 8, mine), F32)),
        [vm((keys, mine), F32), vm((keys, mine), F32), vm((keys, mine), BF)],
        us=12,
    )
    d4 = jnp.concatenate([d2, d_got])
    g_o = jnp.stack(g_in)
    blocks = ((half, 96, width), BF)
    part, wo = run(
        project_kernel,
        inv,
        (all_after([low], d_got, *g_in)[0], perm, u_held, u_got),
        (((mine, width), BF), ((half_w, width), BF)),
        [vm((chips * 32, width), BF), dma(chips)],
        anys=(2, 3),
        us=3,
    )
    part_got = net.core(part)
    g_t = net.core(g_o)
    d_half = d_got
    d_held = jnp.concatenate([d2, d_half])
    d_got = net.across(d_held, last, net.mixed)
    mid, a2, act, fac, w_up, keep_d, send_d, g_sum = run(
        middle_kernel,
        inv,
        (part, part_got, x_o, x_t, g_o, g_t, vec, pi, u_held, u_got),
        (
            ((mine, width), F32),
            ((mine, width), BF),
            ((mine, half_f), BF),
            ((mine, half_f), F32),
            ((width, half_f), BF),
            blocks,
            blocks,
            ((1, width), F32),
        ),
        [vm((mine, width), BF), vm((half_f, width), BF), dma(chips, 2)],
        anys=(8, 9),
        us=10,
    )

    def fold_in(keep, got):
        n = keep.shape[0] // 2
        total = [keep[at].astype(F32) + got[at].astype(F32) for at in (slice(n), slice(n, None))]
        return [part.astype(BF) for part in total]

    def shrink(keep, send, stage, orders=None, then=()):
        got = net.across(send, stage, orders)
        if then:
            got = after(got, *then)
        if stage == 0:
            return (keep.astype(F32) + got.astype(F32))[0]
        return fold_in(keep, got)

    pre, e2, w_down, pre_sum = run(
        slope_kernel,
        inv_d,
        (g_o, g_t, fac, w_up, pi, d_held, d_got),
        (
            ((mine, half_f), BF),
            ((mine, width), BF),
            ((half_f, width), BF),
            ((1, half_f), F32),
        ),
        [dma(chips, 1)],
        anys=(5, 6),
        us=8,
    )
    keep_d, send_d = shrink(keep_d, send_d, 3)
    e2_got = net.core(after(e2, send_d))
    down_own, down_give = run(
        down_kernel,
        None,
        (act, w_down),
        (((own, width), F32), ((own, width), BF)),
        [],
        us=2,
    )
    wide_sum, half_sum = ((1, width), F32), ((1, half_w), F32)
    blocks_u = ((half, 128, width), BF)
    gm, branch, d_heads, keep_u, send_u, e2n, e2s, bs = run(
        branch_kernel,
        inv,
        (e2, e2_got, mid, g_o, g_t, vec, wo, low, perm, a2, pre),
        (
            ((own, width), F32),
            ((mine, width), BF),
            (by_pair(mine), BF),
            blocks_u,
            blocks_u,
            wide_sum,
            wide_sum,
            wide_sum,
        ),
        [vm((width, half_f), BF), vm((chips * 32, width), BF)],
        us=0.1,
    )
    down_got = net.core(after(down_give, e2_got)).astype(F32)
    out_own = (mid[:own] + down_own + down_got + vec[:, AT["bias_down"]]).astype(BF)
    out_own = out_own.reshape(local, cols, width)
    out_parts = [out_own[k] for k in range(2)]
    keep_d, send_d = shrink(keep_d, send_d, 2, then=(send_u,))
    send_d, send_u, d_heads, *out_parts = all_after([send_d, send_u, d_heads, *out_parts])
    quarter = ((2, own, width), BF)
    blocks_q = ((half, 160, half_w), BF)
    home = lambda k: [(b, a) for a, b in net.scatter_move(k)]
    dq, dk, dv, dqs, dvs = run(
        attend_back_kernel,
        None,
        (q, k, v, o, lse, col, row, d_heads),
        (
            (by_pair(mine), BF),
            (by_pair(keys), BF),
            (by_pair(keys), BF),
            half_sum,
            half_sum,
        ),
        [vm((keys, mine), F32), vm((keys, mine), BF), vm((keys, mine), BF)],
        us=10,
    )
    out_parts = [lax.ppermute(out_parts[k], AXES, home(k)) for k in range(2)]
    out_parts = all_after(out_parts, dq)
    d_1 = shrink(keep_d, send_d, 1, then=(dq,))
    keep_e, give_e, e1n, e1s = run(
        input_kernel,
        None,
        (all_after([dq], d_1[1], *out_parts)[0], dk, dv, w_mix, unit1, pi),
        (quarter, quarter, wide_sum, wide_sum),
        [],
        us=0.1,
    )
    got_e = net.core(give_e)
    (e1_give,) = run(near_kernel, None, (keep_e, got_e), (((own, width), BF),), [], us=0.1)
    u3 = shrink(keep_u, send_u, 3, then=(keep_e,))
    shard_d = shrink(*d_1, 0)
    keep_q, send_q = run(
        gather_grads_kernel,
        inv,
        (all_after([a1], u3[1], e1_give)[0], dq, dk, dv, row_device, owner_out, place_out)
        + (e1n, e2n, e2s, dqs, bs, g_sum, pre_sum, e1s, dvs),
        (blocks_q, blocks_q),
        [
            vm((3, width, half_w), BF),
            vm((chips * 16, half_w), BF),
            vm((half_w, place_out.shape[1]), BF),
        ],
        us=0.1,
    )
    q_3 = shrink(keep_q, send_q, 3)
    back = jnp.stack(out_parts)
    block_out = jnp.where(zodd == 0, back, back[::-1])
    block = ((cols, width), BF)
    u_2 = shrink(*u3, 2, then=(send_q,))
    e1_near = net.pair(all_after([e1_give], q_3[1])[0])
    u_1 = shrink(*u_2, 1, then=(q_3[1],))
    q_2 = shrink(*q_3, 2)
    in_parts = run(
        finish_kernel,
        None,
        (keep_e, got_e, all_after([e1_near], q_2[1])[0], x_o, gm, vec),
        (block, block),
        [],
        us=0.1,
    )
    in_parts = [lax.ppermute(in_parts[k], AXES, home(k)) for k in range(2)]
    got_last = net.across(u_1[1], 0)
    q_1 = shrink(*all_after(q_2, u_1[1]), 1)
    shard_u = (u_1[0].astype(F32) + all_after([got_last], q_1[1])[0].astype(F32))[0]
    in_parts = all_after(in_parts, q_1[1])
    shard_q = shrink(*q_1, 0)
    back = jnp.stack(in_parts)
    input_grad = jnp.where(zodd == 0, back, back[::-1]).astype(F32)

    def own_rows(chip):
        keep = jnp.where(core == 0, chip[..., 0, :, :], chip[..., 1, :, :])
        give = jnp.where(core == 0, chip[..., 1, :, :], chip[..., 0, :, :])
        return keep, net.core(give)

    def merge(keep, got, parts):
        view = lambda array: array.reshape(*array.shape[:-1], parts, 1, -1)
        first = jnp.where(core == 0, view(keep), view(got))
        second = jnp.where(core == 0, view(got), view(keep))
        return jnp.concatenate([first, second], axis=-2).reshape(*keep.shape[:-1], -1)

    qkv_own = merge(*own_rows(shard_q[: 6 * rows].reshape(3, 2, rows, half_w)), net.x)
    g_qkv = jnp.moveaxis(qkv_own, 0, 1).reshape(-1)
    g_out = shard_u[4 * rows : 5 * rows].reshape(-1)
    up_own = merge(*own_rows(unfold(shard_u[: 4 * rows], 2).reshape(2, rows, half_f)), net.x)
    two = shard_q[6 * rows : 6 * rows + 2, : 2 * ll + rl]
    keep_s, got_s = own_rows(two.reshape(2, 1, -1))
    own_sums = (keep_s + got_s)[0]
    return (
        block_out,
        input_grad,
        g_qkv,
        g_out,
        up_own.reshape(-1),
        shard_d.reshape(-1),
        own_sums[:ll],
        own_sums[ll : ll + rl],
        own_sums[ll + rl :],
    )


def solution(mesh):
    dp, seq = mesh.shape["dp"], mesh.shape["seq"]
    y = 1 << (((seq.bit_length() - 1) - 1) // 2)
    z = seq // y
    dims = (dp // 2, 2, 4, z // 4, y // 2, 2)
    net = Net(dims)
    inner = Mesh(mesh.devices.reshape(dims), AXES)
    place = ("zh", "zl", "yh", "yl")
    cube = P(("x", "c"), place, None)
    flat = P(AXES)
    rows = D // (2 * net.chips)
    tiles = rows == 24 and net.chips == 16 and net.zl * net.yh == 1
    return jax.shard_map(
        functools.partial(body if tiles else body_any, net),
        mesh=inner,
        in_specs=(cube, P(("x", "c"), place), cube) + (flat,) * 6,
        out_specs=(cube, cube) + (flat,) * 7,
        check_vma=False,
    )
```

```python
import functools
import itertools

import jax
import jax.numpy as jnp
import numpy as np
from jax import lax
from jax.experimental import pallas as pl
from jax.experimental.pallas import tpu as pltpu
from jax.sharding import Mesh
from jax.sharding import PartitionSpec as P

D = 768
FF = 3072
HEADS = 12
HEAD_DIM = 64
EPS = 1e-05
MASKED = -1000000000.0
BF = jnp.bfloat16
F32 = jnp.float32
AXES = ("x", "c", "zh", "zl", "yh", "yl")


class Net:
    def __init__(self, dims):
        self.dims = dims
        self.x, self.c, self.zh, self.zl, self.yh, self.yl = dims
        self.z, self.y = self.zh * self.zl, self.yh * self.yl
        self.chips = self.x * self.z * self.y
        bits = lambda axis, n: [(axis, 1 << b) for b in reversed(range(n.bit_length() - 1))]
        zs, xs, ys = bits("z", self.z), bits("x", self.x), bits("y", self.y)
        self.orders = (zs + xs + ys, zs + ys + xs)
        self.mixed = (xs + zs + ys, ys + zs + xs)
        self.stages = len(self.orders[0])

    def perm(self, move):
        pairs = []
        for at in itertools.product(*(range(n) for n in self.dims)):
            to = move(*at)
            pairs.append(
                (int(np.ravel_multi_index(at, self.dims)), int(np.ravel_multi_index(to, self.dims)))
            )
        return pairs

    def flip(self, stage, orders):
        def move(x, c, zh, zl, yh, yl):
            axis, bit = orders[c][stage]
            z, y = zh * self.zl + zl, yh * self.yl + yl
            if axis == "x":
                x ^= bit
            elif axis == "y":
                y ^= bit
            else:
                z ^= bit
            return (x, c, z // self.zl, z % self.zl, y // self.yl, y % self.yl)

        return self.perm(move)

    def across(self, value, stage, orders=None):
        return lax.ppermute(value, AXES, self.flip(stage, orders or self.orders))

    def core(self, value):
        return lax.ppermute(value, "c", [(0, 1), (1, 0)])

    def pair(self, value):
        return lax.ppermute(value, "yl", [(0, 1), (1, 0)])

    def scatter_move(self, k):
        return self.perm(
            lambda x, c, zh, zl, yh, yl: (x, zh >> 1, 2 * c + (k ^ (zh & 1)), zl, yh, yl)
        )

    def table(self, orders=None):
        me = {
            "x": lax.axis_index("x"),
            "z": lax.axis_index("zh") * self.zl + lax.axis_index("zl"),
            "y": lax.axis_index("yh") * self.yl + lax.axis_index("yl"),
        }
        grid = np.indices((self.x, self.z, self.y)).reshape(3, -1)
        axes = {"x": grid[0], "z": grid[1], "y": grid[2]}
        places = []
        for order in orders or self.orders:
            place = jnp.zeros((self.chips,), jnp.int32)
            for stage, (axis, bit) in enumerate(order):
                differs = (jnp.asarray(axes[axis], jnp.int32) ^ me[axis]) & bit
                place = place + jnp.where(differs != 0, 1 << stage, 0)
            places.append(place)
        return jnp.where(lax.axis_index("c") == 0, places[0], places[1]).astype(jnp.int32)

    def gather(self, block):
        held = block[None]
        for stage in range(self.stages):
            held = jnp.concatenate([held, self.across(held, stage)])
        return held

    def scatter(self, held):
        for stage in reversed(range(self.stages)):
            half = held.shape[0] // 2
            got = self.across(held[half:], stage)
            held = held[:half].astype(F32) + got.astype(F32)
            if stage:
                held = held.astype(BF)
        return held[0]


def move_kernel(table, source, target):
    target[...] = source[...]


def reorder(blocks, table, to_place):
    rest = -blocks.shape[1] % 16
    if rest:
        rows = blocks.shape[1]
        blocks = jnp.pad(blocks, ((0, 0), (0, rest), (0, 0)))
        return reorder(blocks, table, to_place)[:, :rows]
    chips, rows, cols = blocks.shape
    here = pl.BlockSpec((1, rows, cols), lambda chip, table: (chip, 0, 0))
    there = pl.BlockSpec((1, rows, cols), lambda chip, table: (table[chip], 0, 0))
    return pl.pallas_call(
        move_kernel,
        grid_spec=pltpu.PrefetchScalarGridSpec(
            num_scalar_prefetch=1,
            grid=(chips,),
            in_specs=[here if to_place else there],
            out_specs=there if to_place else here,
        ),
        out_shape=jax.ShapeDtypeStruct(blocks.shape, blocks.dtype),
    )(table, blocks)


def normal(field):
    center = field - jnp.mean(field, axis=-1, keepdims=True)
    inverse = lax.rsqrt(jnp.mean(center * center, axis=-1, keepdims=True) + EPS)
    return center * inverse, inverse


def norm_back(upstream, unit, inverse, gain):
    scaled = upstream * gain
    return inverse * (
        scaled
        - jnp.mean(scaled, axis=-1, keepdims=True)
        - unit * jnp.mean(scaled * unit, axis=-1, keepdims=True)
    )


def dot(a, b):
    return jnp.dot(a, b, preferred_element_type=F32)


def dot_t(a, b):
    return lax.dot_general(a, b, (((1,), (1,)), ((), ())), preferred_element_type=F32)


def t_dot(a, b):
    return lax.dot_general(a, b, (((0,), (0,)), ((), ())), preferred_element_type=F32)


def fold(wide, parts):
    lead, rows, cols = wide.shape[:-2], wide.shape[-2], wide.shape[-1] // parts
    moved = jnp.moveaxis(wide.reshape(*lead, rows, parts, cols), -2, -3)
    return moved.reshape(*lead, parts * rows, cols)


def unfold(tall, parts):
    lead, rows, cols = tall.shape[:-2], tall.shape[-2] // parts, tall.shape[-1]
    moved = jnp.moveaxis(tall.reshape(*lead, parts, rows, cols), -3, -2)
    return moved.reshape(*lead, rows, parts * cols)


def body_any(net, tokens, segments, cotangent, w_qkv, w_out, w_fc1, w_fc2, norm_gains, bias_pack):
    local, cols, width = tokens.shape
    own = local * cols
    mine = 2 * own
    hidden = FF
    half_w, half_f = width // 2, hidden // 2
    devices = 2 * net.chips
    core = lax.axis_index("c")
    zodd = lax.axis_index("zh") & 1
    table = net.table()
    rows = width // devices
    frows = hidden // devices
    aligned = (width // (2 * net.x)) % HEAD_DIM == 0
    groups = net.x if aligned else 1

    def pick(array, parts, which):
        split = array.reshape(*array.shape[:-1], parts, 2, array.shape[-1] // (2 * parts))
        taken = jnp.where(which == 0, split[..., 0, :], split[..., 1, :])
        return taken.reshape(*array.shape[:-1], array.shape[-1] // 2)

    def spread(vector, parts):
        split = vector.reshape(parts, 1, vector.shape[-1] // parts)
        both = jnp.concatenate(
            [jnp.where(core == 0, split, 0.0), jnp.where(core == 1, split, 0.0)], axis=1
        )
        return both.reshape(-1)

    seg_row = jnp.pad(segments.astype(BF), ((0, 0), (0, width - cols)))[:, None, :]
    seg_rows = jnp.pad(seg_row, ((0, 0), (0, 7), (0, 0)))
    packed = jnp.concatenate([tokens, seg_rows], axis=1)

    def to_sequence(array):
        swapped = jnp.where(zodd == 0, array, array[::-1])
        return jnp.stack(
            [lax.ppermute(swapped[k], AXES, net.scatter_move(k)) for k in range(2)]
        )

    def from_sequence(array):
        back = jnp.stack(
            [
                lax.ppermute(array[k], AXES, [(b, a) for a, b in net.scatter_move(k)])
                for k in range(2)
            ]
        )
        return jnp.where(zodd == 0, back, back[::-1])

    def halves(which):
        qkv = fold(w_qkv.reshape(rows, 3 * width), 3).reshape(3, rows, width)
        up = w_fc1.reshape(rows, hidden)
        return pick(qkv, groups, which), pick(up, net.x, which)

    keep_qkv, keep_up = halves(core)
    give_qkv, give_up = halves(1 - core)
    small = jnp.concatenate([norm_gains, bias_pack])
    out_rows = w_out.reshape(rows, width)
    got_qkv, got_up, got_small, got_out = jax.tree.map(
        net.core, (give_qkv, give_up, small, out_rows)
    )

    def both(a, b, axis):
        return jnp.where(
            core == 0, jnp.concatenate([a, b], axis=axis), jnp.concatenate([b, a], axis=axis)
        )

    chip_qkv = both(keep_qkv, got_qkv, 1).reshape(6 * rows, half_w)
    chip_up = fold(both(keep_up, got_up, 0), 2)
    chip_out = fold(out_rows if aligned else both(out_rows, got_out, 0), 2)
    chip_small = jnp.pad(
        both(small[None], got_small[None], 0), ((0, 14), (0, half_w - small.shape[0]))
    )
    cut = np.cumsum([chip_qkv.shape[0], chip_out.shape[0]])
    blocks_a = reorder(
        net.gather(jnp.concatenate([chip_qkv, chip_out, chip_small])), table, False
    )
    blocks_up = reorder(net.gather(chip_up), table, False)
    blocks_down = reorder(net.gather(w_fc2.reshape(frows, width)), table, False)

    lead = (net.x, net.z, net.y)

    def natural(blocks):
        n = blocks.shape[-1]
        return jnp.moveaxis(blocks.reshape(*lead, 2, -1, n), 3, 1).reshape(-1, n)

    def by_chip(array):
        n = array.shape[-1]
        return jnp.moveaxis(array.reshape(net.x, 2, net.z, net.y, -1, n), 1, 3).reshape(
            net.chips, -1, n
        )

    qkv_blocks = blocks_a[:, : cut[0]].reshape(net.chips, 3, 2 * rows, half_w)
    w_q, w_k, w_v = (natural(qkv_blocks[:, i]) for i in range(3))
    out_blocks = unfold(blocks_a[:, cut[0] : cut[1]], 2)
    if aligned:
        w_proj = out_blocks.reshape(half_w, width)
    else:
        w_proj = lax.dynamic_slice_in_dim(natural(out_blocks), core * half_w, half_w)
    smalls = blocks_a[:, cut[1] : cut[1] + 2, : small.shape[0]].reshape(*lead, 2, -1)
    smalls = jnp.moveaxis(smalls, 3, 1).reshape(devices, -1).astype(F32)
    n_gain = norm_gains.shape[0]
    gains = smalls[:, :n_gain].reshape(-1)
    shifts = smalls[:, n_gain:].reshape(-1)
    w_up = natural(unfold(blocks_up, 2))
    w_down = blocks_down.reshape(half_f, width)
    gain1, gain2 = gains[:width], gains[width:]
    shift1, shift2, bias_q, bias_v, bias_proj, bias_down = (
        shifts[i * width : (i + 1) * width] for i in range(6)
    )
    bias_up = pick(shifts[6 * width :], net.x, core)
    bias_q, bias_v = pick(bias_q, groups, core), pick(bias_v, groups, core)

    x_own = to_sequence(packed)
    x_other = net.core(x_own)
    x_mine = jnp.concatenate([x_own, x_other])
    near = net.pair(x_own)
    near = jnp.concatenate([near, net.core(near)])
    x_seq = jnp.concatenate([x_mine, near])
    if net.zl * net.yh > 1:
        x_far = lax.all_gather(x_seq, ("zl", "yh"), axis=0, tiled=True)
        x_keys = x_far
    else:
        x_keys = x_seq
    g_own = to_sequence(cotangent)
    g_mine = jnp.concatenate([g_own, net.core(g_own)]).reshape(mine, width)
    docs = x_keys[:, cols, :cols].reshape(-1)
    query_docs = x_mine[:, cols, :cols].reshape(-1)
    x_all = x_keys[:, :cols].reshape(-1, width).astype(F32)
    x_q = x_mine[:, :cols].reshape(-1, width).astype(F32)

    unit_q, inverse_q = normal(x_q)
    a_q = (unit_q * gain1 + shift1).astype(BF)
    unit_all, _ = normal(x_all)
    a_all = (unit_all * gain1 + shift1).astype(BF)
    heads = HEADS // 2
    q = (dot(a_q, w_q) + bias_q).astype(BF)
    k = dot(a_all, w_k).astype(BF)
    v = (dot(a_all, w_v) + bias_v).astype(BF)
    by_head = lambda t: t.reshape(-1, heads, HEAD_DIM)
    same = (query_docs[:, None] == docs[None, :])[None]
    scores = (
        jnp.einsum("qhd,khd->hqk", by_head(q), by_head(k), preferred_element_type=F32) * 0.125
    )
    scores = jnp.where(same, scores, MASKED)
    weights = jnp.exp(scores - jnp.max(scores, axis=-1, keepdims=True))
    probs = weights / jnp.sum(weights, axis=-1, keepdims=True)
    probs_low = probs.astype(BF)
    att = jnp.einsum("hqk,khd->qhd", probs_low, by_head(v), preferred_element_type=F32)
    att = att.reshape(mine, half_w)
    att_low = att.astype(BF)

    def core_sum(partial):
        low = partial.astype(BF)
        got = net.core(low)
        return low.astype(F32) + jnp.concatenate([got[own:], got[:own]]).astype(F32)

    middle = x_q + core_sum(dot(att_low, w_proj)) + bias_proj
    unit2, inverse2 = normal(middle)
    a2 = (unit2 * gain2 + shift2).astype(BF)
    pre = dot(a2, w_up) + bias_up
    sig = jax.nn.sigmoid(1.702 * pre)
    activ = (pre * sig).astype(BF)
    down = dot(activ, w_down)
    down_got = net.core(down[own:].astype(BF)).astype(F32)
    out_own = (middle[:own] + down[:own] + down_got + bias_down).astype(BF)
    block_out = from_sequence(out_own.reshape(local, cols, width))

    grad_down = t_dot(activ, g_mine).astype(BF)
    grad_pre = (dot_t(g_mine, w_down) * (sig + 1.702 * pre * sig * (1.0 - sig))).astype(BF)
    shard_down = net.scatter(reorder(grad_down.reshape(net.chips, frows, width), table, True))
    grad_up = t_dot(a2, grad_pre).astype(BF)
    shard_up = net.scatter(reorder(fold(by_chip(grad_up), 2), table, True))
    e2 = core_sum(dot_t(grad_pre, w_up))
    grad_middle = g_mine.astype(F32) + norm_back(e2, unit2, inverse2, gain2)
    branch = grad_middle.astype(BF)
    grad_proj = t_dot(att_low, branch).astype(BF)
    d_heads = dot_t(branch, w_proj).astype(BF)
    dp = jnp.einsum("qhd,khd->hqk", by_head(d_heads), by_head(v), preferred_element_type=F32)
    delta = jnp.sum(probs * dp, axis=-1, keepdims=True)
    d_scores = (probs * (dp - delta)).astype(BF)
    dq = 0.125 * jnp.einsum("hqk,khd->qhd", d_scores, by_head(k), preferred_element_type=F32)
    dk = 0.125 * jnp.einsum("hqk,qhd->khd", d_scores, by_head(q), preferred_element_type=F32)
    dv = jnp.einsum("hqk,qhd->khd", probs_low, by_head(d_heads), preferred_element_type=F32)
    dq = dq.reshape(-1, half_w).astype(BF)
    dk = dk.reshape(-1, half_w).astype(BF)
    dv = dv.reshape(-1, half_w).astype(BF)
    grad_qkv = jnp.stack([t_dot(a_q, dq), t_dot(a_all, dk), t_dot(a_all, dv)]).astype(BF)

    e1_keys = (dot_t(dk, w_k) + dot_t(dv, w_v)).astype(BF)
    if net.zl * net.yh > 1:
        e1_keys = lax.psum_scatter(
            e1_keys, ("zl", "yh"), scatter_dimension=0, tiled=True
        )
    e1_near = e1_keys[mine:].reshape(2, own, width)
    e1_mine = e1_keys[:mine].astype(F32) + dot_t(dq, w_q)
    e1_mine = e1_mine.astype(BF).reshape(2, own, width)
    got = net.core(jnp.stack([e1_mine[1], e1_near[1]]))
    e1_near = e1_near[0].astype(F32) + got[1].astype(F32)
    e1 = e1_mine[0].astype(F32) + got[0].astype(F32) + net.pair(e1_near.astype(BF)).astype(F32)
    unit1 = unit_q[:own]
    in_own = grad_middle[:own] + norm_back(e1, unit1, inverse_q[:own], gain1)
    input_grad = from_sequence(in_own.astype(BF).reshape(local, cols, width)).astype(F32)

    total = lambda array: jnp.sum(array.astype(F32), axis=0)
    g_own = g_mine[:own]
    gain_sums = jnp.concatenate([total(e1 * unit1), total(e2[:own] * unit2[:own])])
    bias_sums = jnp.concatenate(
        [
            total(e2[:own]),
            spread(total(dq), groups),
            total(branch[:own]),
            total(g_own),
            spread(total(grad_pre), net.x),
        ]
    )
    lead_sums = jnp.concatenate([total(e1), spread(total(dv), groups)])
    sums = jnp.concatenate(
        [v.reshape(devices, -1) for v in (gain_sums, bias_sums, lead_sums)], axis=1
    )
    sums = sums + net.core(sums)
    sums = jnp.moveaxis(sums.reshape(net.x, 2, net.z, net.y, -1), 1, 0)
    sums = jnp.where(core == 0, sums[0], sums[1]).reshape(net.chips, 1, -1)
    n_sums = sums.shape[-1]
    sums = jnp.pad(sums, ((0, 0), (0, 15), (0, half_w - n_sums))).astype(BF)
    qkv_send = jnp.stack([by_chip(grad_qkv[i]) for i in range(3)], axis=1)
    qkv_send = qkv_send.reshape(net.chips, 6 * rows, half_w)
    if aligned:
        out_send = grad_proj.reshape(net.chips, rows, width)
    else:
        whole = jnp.zeros((width, width), BF)
        whole = lax.dynamic_update_slice(whole, grad_proj, (core * half_w, 0))
        out_send = by_chip(whole)
    sent = jnp.concatenate([qkv_send, fold(out_send, 2), sums], axis=1)
    shard_a = net.scatter(reorder(sent, table, True))

    def own_rows(chip):
        keep = jnp.where(core == 0, chip[..., 0, :, :], chip[..., 1, :, :])
        give = jnp.where(core == 0, chip[..., 1, :, :], chip[..., 0, :, :])
        return keep, net.core(give)

    def merge(keep, got, parts):
        split = lambda array: array.reshape(*array.shape[:-1], parts, 1, -1)
        first = jnp.where(core == 0, split(keep), split(got))
        second = jnp.where(core == 0, split(got), split(keep))
        return jnp.concatenate([first, second], axis=-2).reshape(*keep.shape[:-1], -1)

    qkv_own = merge(*own_rows(shard_a[: cut[0]].reshape(3, 2, rows, half_w)), groups)
    g_qkv = jnp.moveaxis(qkv_own, 0, 1).reshape(-1)
    out_own = unfold(shard_a[cut[0] : cut[1]], 2)
    if not aligned:
        keep, got = own_rows(out_own.reshape(2, rows, width))
        out_own = keep + got
    g_out = out_own.reshape(-1)
    up_own = merge(*own_rows(unfold(shard_up, 2).reshape(2, rows, half_f)), net.x)
    own_sums = shard_a[cut[1], :n_sums]
    n_gain = 2 * width // devices
    n_lead = n_sums - n_gain
    return (
        block_out,
        input_grad,
        g_qkv,
        g_out,
        up_own.reshape(-1),
        shard_down.reshape(-1),
        own_sums[:n_gain],
        own_sums[n_gain:n_lead],
        own_sums[n_lead:],
    )


SLAB = 128
PAIRS = HEADS // 4
DOUBLE = 2 * HEAD_DIM
PARTS = (
    ("gain1", D),
    ("gain2", D),
    ("shift1", D),
    ("shift2", D),
    ("bias_proj", D),
    ("bias_down", D),
    ("bias_q", D // 2),
    ("bias_v", D // 2),
    ("bias_up", FF // 2),
)
SUMS = (
    ("e1n", D),
    ("e2n", D),
    ("e2", D),
    ("dq", D // 2),
    ("branch", D),
    ("g", D),
    ("pre", FF // 2),
    ("e1", D),
    ("dv", D // 2),
)


def offsets(parts):
    ends = np.cumsum([n for _, n in parts])
    return {name: slice(int(end - n), int(end)) for (name, n), end in zip(parts, ends)}


AT = offsets(PARTS)


def dots(a, b, ca, cb):
    return lax.dot_general(a, b, (((ca,), (cb,)), ((), ())), preferred_element_type=F32)


def lane_half(e):
    lanes = lax.broadcasted_iota(jnp.int32, (1, DOUBLE), 1)
    inside = (lanes < HEAD_DIM) if e == 0 else (lanes >= HEAD_DIM)
    return inside.astype(F32).astype(BF)


def first_half(shape):
    return lax.broadcasted_iota(jnp.int32, shape, 1) < HEAD_DIM


def load_rows(inv, held, got, target, sems, pieces):
    half = held.shape[0]
    copies = []
    for r in range(2 * half):
        source = held if r < half else got
        for n, (first, rows, place) in enumerate(pieces):
            copies.append(
                pltpu.make_async_copy(
                    source.at[r % half, pl.ds(first, rows), :],
                    place(target, inv[r], rows),
                    sems.at[r, n],
                )
            )
    for copy in copies:
        copy.start()
    return copies


def one_hot(place, target):
    step = 128
    for i in range(target.shape[0] // step):
        shape = (step, target.shape[1])
        entry = lax.broadcasted_iota(jnp.int32, shape, 0) + i * step
        target[i * step : (i + 1) * step, :] = (entry == place[:1, :]).astype(F32).astype(BF)


def unit_kernel(xo, xt, xn, xm, place, unit_ref, col_ref, row_ref, hot_ref):
    one_hot(place, hot_ref)
    for i, (ref, j) in enumerate((ref, j) for ref in (xo, xt, xn, xm) for j in range(2)):
        unit, _ = normal(ref[j, :SLAB, :].astype(F32))
        at = pl.ds(i * SLAB, SLAB)
        unit_ref[at, :] = unit
        docs = ref[j, SLAB : SLAB + 8, :SLAB].astype(F32)[:1]
        col_ref[at, :] = jnp.broadcast_to(docs, (SLAB, SLAB)).T
        if i < 4:
            row_ref[:, i * SLAB : (i + 1) * SLAB] = jnp.broadcast_to(docs, (8, SLAB))


def fill_bias(col, row, bias):
    for i in range(bias.shape[0] // SLAB):
        at = pl.ds(i * SLAB, SLAB)
        for j in range(bias.shape[1] // SLAB):
            lanes = pl.ds(j * SLAB, SLAB)
            bias[at, lanes] = jnp.where(col[at, :] == row[:1, lanes], 0.0, MASKED)


def pick_rows(rows, step):
    shape = (2 * rows // step, rows)
    i = lax.broadcasted_iota(jnp.int32, shape, 0)
    j = lax.broadcasted_iota(jnp.int32, shape, 1)
    return (j == (i >> 1) * step + (i & 1)).astype(F32).astype(BF)


def mix_kernel(
    inv, unit, pi, device, owner, hot, held, got,
    a_ref, q_ref, k_ref, v_ref, w, vec, nat, small, sems, small_sems,
):
    half = held.shape[0]
    few = []
    for r in range(2 * half):
        source = held if r < half else got
        few.append(
            pltpu.make_async_copy(
                source.at[r % half, pl.ds(144, 16), :], small.at[pl.ds(r * 16, 16), :], small_sems.at[r]
            )
        )
    for copy in few:
        copy.start()
    place = lambda i: lambda t, chip, n: t.at[i, pl.ds(pl.multiple_of(chip * n, 16), n), :]
    copies = load_rows(inv, held, got, w, sems, [(48 * i, 48, place(i)) for i in range(3)])
    for copy in few:
        copy.wait()
    picked = dot(pick_rows(small.shape[0], 16), small[...]).astype(BF)
    mine_only = jnp.where(device[:, :1] == owner[:1, :], dot(picked, hot[...]), 0.0)
    vec[...] = jnp.sum(mine_only, axis=0, keepdims=True)
    keys = a_ref.shape[0]
    for i in range(keys // SLAB):
        at = pl.ds(i * SLAB, SLAB)
        nat[at, :] = (unit[at, :] * vec[:, AT["gain1"]] + vec[:, AT["shift1"]]).astype(BF)
    a_ref[...] = dot(nat[...], pi[...]).astype(BF)
    for copy in copies:
        copy.wait()
    mine = q_ref.shape[1]
    q = (dot(a_ref[:mine, :], w[0]) + vec[:, AT["bias_q"]]).astype(BF) * 0.125
    k = dot(a_ref[...], w[1]).astype(BF)
    v = (dot(a_ref[...], w[2]) + vec[:, AT["bias_v"]]).astype(BF)
    for i in range(PAIRS):
        lanes = slice(i * DOUBLE, (i + 1) * DOUBLE)
        q_ref[i], k_ref[i], v_ref[i] = q[:, lanes], k[:, lanes], v[:, lanes]


def attend_kernel(q_ref, k_ref, v_ref, col, row, o_ref, low_ref, lse_ref, bias, s, p_low):
    mine, keys = q_ref.shape[1], k_ref.shape[1]
    fill_bias(col, row, bias)

    def pair(i, carry):
        outs = []
        for e in range(2):
            qm = q_ref[i] * lane_half(e)
            top = jnp.full((1, mine), -3e38, F32)
            for c in range(keys // SLAB):
                at = pl.ds(c * SLAB, SLAB)
                t = dots(k_ref[i, at, :], qm, 1, 1) + bias[at, :]
                s[at, :] = t
                top = jnp.maximum(top, jnp.max(t, axis=0, keepdims=True))
            total = jnp.zeros((1, mine), F32)
            for c in range(keys // SLAB):
                at = pl.ds(c * SLAB, SLAB)
                p = jnp.exp(s[at, :] - top)
                total = total + jnp.sum(p, axis=0, keepdims=True)
                p_low[at, :] = p.astype(BF)
            lse_ref[i, e : e + 1, :] = top + jnp.log(total)
            o = dots(p_low[...], v_ref[i], 0, 0)
            scale = jnp.broadcast_to(1.0 / total, (DOUBLE, mine)).T
            outs.append(o * scale)
        o = jnp.where(first_half(outs[0].shape), outs[0], outs[1])
        o_ref[i] = o
        low_ref[i] = o.astype(BF)
        return carry

    lax.fori_loop(0, PAIRS, pair, 0)


def project_kernel(inv, low, perm, held, got, part_ref, wo_ref, rel, sems):
    half = held.shape[0]
    copies = []
    for r in range(2 * half):
        source = held if r < half else got
        copies.append(
            pltpu.make_async_copy(
                source.at[r % half, pl.ds(96, 32), :], rel.at[pl.ds(r * 32, 32), :], sems.at[r]
            )
        )
    for copy in copies:
        copy.start()
    for copy in copies:
        copy.wait()
    wo_ref[...] = dot(perm[...], rel[...]).astype(BF)
    att = jnp.concatenate([low[i] for i in range(PAIRS)], axis=1)
    part_ref[...] = dot(att, wo_ref[...]).astype(BF)


def load_half(inv, source, first, target, sems):
    rows = source.shape[1]
    copies = [
        pltpu.make_async_copy(
            source.at[r],
            target.at[pl.ds(pl.multiple_of(inv[first + r] * rows, 16), rows), :],
            sems.at[r],
        )
        for r in range(source.shape[0])
    ]
    for copy in copies:
        copy.start()
    return copies


def middle_kernel(
    inv, inv_d, part, part_got, xo, xt, go, gt, vec, pi, held, got, d_held,
    mid_ref, a_ref, act_ref, fac_ref, w, keep_ref, send_ref, sum_ref, w_down,
    nat, grad, sems, d_sems,
):
    place = lambda h: lambda t, chip, n: t.at[
        pl.ds(pl.multiple_of(chip * n, 16), n), pl.ds(h * D, D)
    ]
    copies = load_rows(inv, held, got, w, sems, [(48 * h, 48, place(h)) for h in range(2)])
    later = load_half(inv_d, d_held, 0, w_down, d_sems)
    mine = part.shape[0]
    own = mine // 2
    for i, (ref, j) in enumerate((ref, j) for ref in (xo, xt) for j in range(2)):
        at = pl.ds(i * SLAB, SLAB)
        other = pl.ds((i * SLAB + own) % mine, SLAB)
        mid = (
            ref[j, :SLAB, :].astype(F32)
            + (part[at, :].astype(F32) + part_got[other, :].astype(F32))
            + vec[:, AT["bias_proj"]]
        )
        mid_ref[at, :] = mid
        unit, _ = normal(mid)
        nat[at, :] = (unit * vec[:, AT["gain2"]] + vec[:, AT["shift2"]]).astype(BF)
    a_ref[...] = dot(nat[...], pi[...]).astype(BF)
    g = jnp.concatenate([go[0], go[1], gt[0], gt[1]], axis=0)
    sum_ref[...] = jnp.sum(g[:own].astype(F32), axis=0, keepdims=True)
    for copy in copies:
        copy.wait()
    step = 512
    for j in range(w.shape[1] // step):
        lanes = pl.ds(j * step, step)
        start = AT["bias_up"].start + j * step
        pre = dot(a_ref[...], w[:, lanes]) + vec[:, start : start + step]
        sig = 1.0 / (1.0 + jnp.exp(-1.702 * pre))
        act_ref[:, lanes] = (pre * sig).astype(BF)
        fac_ref[:, lanes] = sig + 1.702 * pre * sig * (1.0 - sig)
        grad[lanes, :] = dots(act_ref[:, lanes], g, 0, 0).astype(BF)
    half = keep_ref.shape[0]
    for r in range(2 * half):
        target = keep_ref if r < half else send_ref
        target[r % half] = grad[pl.ds(pl.multiple_of(inv[r] * 96, 16), 96), :]
    for copy in later:
        copy.wait()


def slope_kernel(inv, go, gt, fac, w_up, pi, w_half, got, pre_ref, e_ref, w, sum_ref, sems):
    copies = load_half(inv, got, got.shape[0], w, sems)
    g = jnp.concatenate([go[0], go[1], gt[0], gt[1]], axis=0)
    for copy in copies:
        copy.wait()
    step = 512
    total = None
    for j in range(w.shape[0] // step):
        lanes = pl.ds(j * step, step)
        pre = (dots(g, w[lanes, :], 1, 1) * fac[:, lanes]).astype(BF)
        pre_ref[:, lanes] = pre
        sum_ref[:, lanes] = jnp.sum(pre.astype(F32), axis=0, keepdims=True)
        term = dots(pre, w_up[:, lanes], 1, 1)
        total = term if total is None else total + term
    e_ref[...] = dots(total.astype(BF), pi[...], 1, 1).astype(BF)


def down_kernel(act, w_down, own_ref, give_ref):
    down = dot(act[...], w_down[...])
    own = own_ref.shape[0]
    own_ref[...] = down[:own]
    give_ref[...] = down[own:].astype(BF)


def wide(ref):
    return jnp.concatenate([ref[i] for i in range(PAIRS)], axis=1)


def branch_kernel(
    inv, e2, e2_got, mid, go, gt, vec, wo, low, perm, a, pre,
    gm_ref, branch_ref, d_ref, keep_ref, send_ref, e2n_sum, e2_sum, branch_sum, grad, out,
):
    mine = mid.shape[0]
    own = mine // 2
    sums = [jnp.zeros((1, D), F32) for _ in range(3)]
    for i, (ref, j) in enumerate((ref, j) for ref in (go, gt) for j in range(2)):
        at = pl.ds(i * SLAB, SLAB)
        other = pl.ds((i * SLAB + own) % mine, SLAB)
        e = e2[at, :].astype(F32) + e2_got[other, :].astype(F32)
        unit, inverse = normal(mid[at, :])
        gm = ref[j].astype(F32) + norm_back(e, unit, inverse, vec[:, AT["gain2"]])
        branch = gm.astype(BF)
        branch_ref[at, :] = branch
        if i < 2:
            gm_ref[at, :] = gm
            for n, term in enumerate((e * unit, e, branch.astype(F32))):
                sums[n] = sums[n] + jnp.sum(term, axis=0, keepdims=True)
    e2n_sum[...], e2_sum[...], branch_sum[...] = sums
    d = dots(branch_ref[...], wo[...], 1, 1).astype(BF)
    for i in range(PAIRS):
        d_ref[i] = d[:, i * DOUBLE : (i + 1) * DOUBLE]
    step = 512
    for j in range(pre.shape[1] // step):
        lanes = pl.ds(j * step, step)
        grad[:, lanes] = dots(a[...], pre[:, lanes], 0, 0).astype(BF)
    proj = dots(wide(low), branch_ref[...], 0, 0).astype(BF)
    out[...] = dots(perm[...], proj, 0, 0).astype(BF)
    half = keep_ref.shape[0]
    for r in range(2 * half):
        target, at = (keep_ref if r < half else send_ref), r % half
        rows = pl.ds(pl.multiple_of(inv[r] * 48, 16), 48)
        target[at, :48, :] = grad[rows, :D]
        target[at, 48:96, :] = grad[rows, D:]
        target[at, 96:, :] = out[r * 32 : r * 32 + 32, :]


def attend_back_kernel(
    q, k, v, o, lse, col, row, d_ref, dq_ref, dk_ref, dv_ref, dq_sum, dv_sum, bias, p_low, s_low
):
    mine, keys = q.shape[1], k.shape[1]
    fill_bias(col, row, bias)

    def pair(i, carry):
        both = (d_ref[i].astype(F32) * o[i]).T
        got = []
        for e in range(2):
            delta = jnp.sum(both[e * HEAD_DIM : (e + 1) * HEAD_DIM], axis=0, keepdims=True)
            qm = q[i] * lane_half(e)
            dm = d_ref[i] * lane_half(e)
            base = lse[i, e : e + 1, :]
            for c in range(keys // SLAB):
                at = pl.ds(c * SLAB, SLAB)
                t = dots(k[i, at, :], qm, 1, 1) + bias[at, :]
                p = jnp.exp(t - base)
                dp = dots(v[i, at, :], dm, 1, 1)
                p_low[at, :] = p.astype(BF)
                s_low[at, :] = (p * (dp - delta)).astype(BF)
            got.append(
                (
                    dots(s_low[...], k[i], 0, 0) * 0.125,
                    dot(s_low[...], q[i]),
                    dot(p_low[...], d_ref[i]),
                )
            )
        for n, ref in enumerate((dq_ref, dk_ref, dv_ref)):
            ref[i] = jnp.where(first_half(got[0][n].shape), got[0][n], got[1][n]).astype(BF)
        return carry

    lax.fori_loop(0, PAIRS, pair, 0)
    dq_sum[...] = jnp.sum(wide(dq_ref).astype(F32), axis=0, keepdims=True)
    dv_sum[...] = jnp.sum(wide(dv_ref).astype(F32), axis=0, keepdims=True)


def input_kernel(dq_ref, dk_ref, dv_ref, w, unit, pi, keep_ref, give_ref, e1n_sum, e1_sum):
    keys, own = unit.shape[0], keep_ref.shape[1]
    dq, dk, dv = wide(dq_ref), wide(dk_ref), wide(dv_ref)
    e1n = jnp.zeros((1, D), F32)
    e1s = jnp.zeros((1, D), F32)
    for part in range(keys // own):
        at = slice(part * own, (part + 1) * own)
        e = dots(dk[at], w[1], 1, 1) + dots(dv[at], w[2], 1, 1)
        if part < 2:
            e = e + dots(dq[at], w[0], 1, 1)
        e = dots(e.astype(BF), pi[...], 1, 1)
        e1s = e1s + jnp.sum(e, axis=0, keepdims=True)
        e1n = e1n + jnp.sum(e * unit[pl.ds(part * own, own), :], axis=0, keepdims=True)
        target = keep_ref if part % 2 == 0 else give_ref
        target[part // 2] = e.astype(BF)
    e1n_sum[...] = e1n
    e1_sum[...] = e1s


def near_kernel(keep, got, give):
    give[...] = (keep[1].astype(F32) + got[1].astype(F32)).astype(BF)


def finish_kernel(keep, got, near, x, gm, vec, *parts):
    for i, part in enumerate(parts):
        at = pl.ds(i * SLAB, SLAB)
        e = keep[0, at, :].astype(F32) + got[0, at, :].astype(F32) + near[at, :].astype(F32)
        unit, inverse = normal(x[i, :SLAB, :].astype(F32))
        part[...] = (gm[at, :] + norm_back(e, unit, inverse, vec[:, AT["gain1"]])).astype(BF)


def gather_grads_kernel(inv, a, dq, dk, dv, device, owner, place, *rest):
    sums, (keep_ref, send_ref, grad, small, hot) = rest[:-5], rest[-5:]
    one_hot(place, hot)
    mine = dq.shape[1]
    grad[0] = dots(a[:mine, :], wide(dq), 0, 0).astype(BF)
    grad[1] = dots(a[...], wide(dk), 0, 0).astype(BF)
    grad[2] = dots(a[...], wide(dv), 0, 0).astype(BF)
    line = jnp.concatenate([ref[...] for ref in sums], axis=1)
    kept = jnp.where(device[:, :1] == owner[:1, :], line, 0.0).astype(BF)
    placed = dots(kept, hot[...], 1, 1).astype(BF)
    small[...] = dots(pick_rows(small.shape[0], 16), placed, 0, 0).astype(BF)
    half = keep_ref.shape[0]
    for r in range(2 * half):
        target, at = (keep_ref if r < half else send_ref), r % half
        rows = pl.ds(pl.multiple_of(inv[r] * 48, 16), 48)
        for i in range(3):
            target[at, 48 * i : 48 * i + 48, :] = grad[i, rows, :]
        target[at, 144:160, :] = small[r * 16 : r * 16 + 16, :]


def run(kernel, table, args, outs, scratch, anys=(), us=5, mib=16, alias=None):
    specs = [
        pl.BlockSpec(memory_space=pl.ANY) if i in anys else pl.BlockSpec(memory_space=pltpu.VMEM)
        for i in range(len(args))
    ]
    prefetch = () if table is None else table if isinstance(table, tuple) else (table,)
    return pl.pallas_call(
        kernel,
        grid_spec=pltpu.PrefetchScalarGridSpec(
            num_scalar_prefetch=len(prefetch),
            grid=(),
            in_specs=specs,
            out_specs=[pl.BlockSpec(memory_space=pltpu.VMEM) for _ in outs],
            scratch_shapes=scratch,
        ),
        out_shape=[jax.ShapeDtypeStruct(shape, dtype) for shape, dtype in outs],
        input_output_aliases=alias or {},
        compiler_params=pltpu.CompilerParams(vmem_limit_bytes=mib * 2**20),
        cost_estimate=pl.CostEstimate(
            flops=int(us * 10**9), bytes_accessed=int(us * 10**6), transcendentals=0
        ),
    )(*prefetch, *args)


def body(net, tokens, segments, cotangent, w_qkv, w_out, w_fc1, w_fc2, norm_gains, bias_pack):
    local, cols, width = tokens.shape
    own, mine = local * cols, 2 * local * cols
    keys = 2 * mine
    hidden = FF
    half_w, half_f = width // 2, hidden // 2
    chips, devices = net.chips, 2 * net.chips
    half = chips // 2
    rows, frows = width // devices, hidden // devices
    core = lax.axis_index("c")
    zodd = lax.axis_index("zh") & 1
    def pick(array, parts, which):
        view = array.reshape(*array.shape[:-1], parts, 2, array.shape[-1] // (2 * parts))
        taken = jnp.where(which == 0, view[..., 0, :], view[..., 1, :])
        return taken.reshape(*array.shape[:-1], array.shape[-1] // 2)

    def both(a, b, axis):
        return jnp.where(
            core == 0, jnp.concatenate([a, b], axis=axis), jnp.concatenate([b, a], axis=axis)
        )

    small = jnp.concatenate([norm_gains, bias_pack])
    qkv = w_qkv.reshape(rows, 3, width).swapaxes(0, 1)
    got_qkv, got_small = net.core(pick(qkv, net.x, 1 - core)), net.core(small)
    chip_qkv = both(pick(qkv, net.x, core), got_qkv, 1).reshape(6 * rows, half_w)
    chip_small = jnp.pad(
        both(small[None], got_small[None], 0), ((0, 14), (0, half_w - small.shape[0]))
    )

    def after(value, *others):
        return lax.optimization_barrier((value, *others))[0]

    def all_after(values, *others):
        return lax.optimization_barrier((*values, *others))[: len(values)]

    def grow(held, stage, orders=None, then=()):
        got = net.across(held, stage, orders)
        if then:
            got = after(got, *then)
        return jnp.concatenate([held, got])

    last = net.stages - 1
    q0 = jnp.concatenate([chip_qkv, chip_small])[None]
    q1 = grow(q0, 0)
    spots = after(jnp.arange(chips, dtype=jnp.int32), q0)

    def order_of(orders):
        found = net.table(orders)[None, :] == spots[:, None]
        return jnp.sum(jnp.where(found, spots[None, :], 0), axis=1).astype(jnp.int32)

    inv, inv_d = order_of(net.orders), order_of(net.mixed)

    split = lambda n, parts: np.arange(n).reshape(parts, 2, n // (2 * parts))
    of_core = lambda n, parts: [split(n, parts)[:, c].reshape(-1) for c in range(2)]
    everywhere = lambda n: [np.arange(n)] * 2
    n_gain, n_bias = norm_gains.shape[0], bias_pack.shape[0]

    def owners(items):
        dev, place = [], []
        for c in range(2):
            flat = [(first + entry[c]) for first, entry, _, _ in items]
            dev.append(np.concatenate([f // n for f, (_, _, _, n) in zip(flat, items)]))
            place.append(
                np.concatenate([at + f % n for f, (_, _, at, n) in zip(flat, items)])
            )
        dev, place = np.array(dev, np.int32), np.array(place, np.int32)
        return (
            jnp.where(core == 0, dev[0], dev[1]),
            jnp.where(core == 0, place[0], place[1]),
        )

    chip_row = jnp.repeat(inv, 2)
    s_n = net.z * net.y
    row_device = ((chip_row // s_n) * 2 + jnp.tile(jnp.arange(2), chips)) * s_n + chip_row % s_n
    row_device = jnp.broadcast_to(row_device[:, None], (devices, SLAB))
    D_, W = everywhere(width), width

    def mapping(items):
        dev, place = owners(items)
        return dev[None, :], place[None, :]

    gl, bl = n_gain, n_bias
    heads_c, ff_c = of_core(width, net.x), of_core(hidden, net.x)
    owner_in, place_in = mapping(
        [
            (0, D_, 0, gl),
            (W, D_, 0, gl),
            (0, D_, gl, bl),
            (W, D_, gl, bl),
            (4 * W, D_, gl, bl),
            (5 * W, D_, gl, bl),
            (2 * W, heads_c, gl, bl),
            (3 * W, heads_c, gl, bl),
            (6 * W, ff_c, gl, bl),
        ]
    )
    ll = 2 * W // devices
    rl = n_gain + n_bias - 2 * ll
    owner_out, place_out = mapping(
        [
            (0, D_, 0, ll),
            (W, D_, 0, ll),
            (0, D_, ll, rl),
            (W, heads_c, ll, rl),
            (2 * W, D_, ll, rl),
            (3 * W, D_, ll, rl),
            (4 * W, ff_c, ll, rl),
            (0, D_, ll + rl, ll),
            (W, heads_c, ll + rl, ll),
        ]
    )
    order = np.arange(width).reshape(net.x, 2, s_n, rows).transpose(0, 2, 1, 3).reshape(-1)
    pi = jnp.asarray((np.arange(width)[:, None] == order[None, :]), BF)
    rel_row = jnp.arange(chips * 32, dtype=jnp.int32)
    nat_row = jnp.where(rel_row % 32 < rows, jnp.repeat(inv, 32) * rows + rel_row % 32, -1)
    perm = (jnp.arange(half_w, dtype=jnp.int32)[:, None] == nat_row[None, :]).astype(BF)


    seg_row = jnp.pad(after(segments, q0).astype(BF), ((0, 0), (0, width - cols)))[:, None, :]
    packed = jnp.concatenate([tokens, jnp.pad(seg_row, ((0, 0), (0, 7), (0, 0)))], axis=1)

    def to_sequence(array):
        swapped = jnp.where(zodd == 0, array, array[::-1])
        return jnp.stack(
            [lax.ppermute(swapped[k], AXES, net.scatter_move(k)) for k in range(2)]
        )

    def from_sequence(array, then=()):
        back = [
            lax.ppermute(array[k], AXES, [(b, a) for a, b in net.scatter_move(k)])
            for k in range(2)
        ]
        back = jnp.stack(all_after(back, *then))
        return jnp.where(zodd == 0, back, back[::-1])

    up = after(w_fc1, q0).reshape(rows, hidden)
    got_up = net.core(pick(up, net.x, 1 - core))
    chip_up = fold(both(pick(up, net.x, core), got_up, 0), 2)
    chip_up = jnp.concatenate([chip_up, jnp.pad(w_out.reshape(rows, width), ((0, 8), (0, 0)))])

    u1 = grow(chip_up[None], 0)
    q2 = grow(after(q1, chip_up), 1)
    d1 = grow(after(w_fc2.reshape(1, frows, width), q1), 0, net.mixed)
    q4 = grow(after(q2, u1, d1), 2)
    x_o = to_sequence(after(packed, u1))
    x_n = net.pair(x_o)
    x_m = net.core(x_n)
    x_t = net.core(after(x_o, q4))
    u2 = grow(u1, 1, then=(q4,))
    q_held, q_got = q4, net.across(q4, last)
    d2 = grow(after(d1, u2), 1, net.mixed)
    u4 = grow(after(u2, q4), 2)
    g_out = jnp.where(zodd == 0, cotangent, cotangent[::-1])
    g_out = all_after([g_out[0], g_out[1]], q4)

    dma = lambda *n: pltpu.SemaphoreType.DMA(n)
    vm = lambda shape, dtype: pltpu.VMEM(shape, dtype)
    by_pair = lambda n: (PAIRS, n, DOUBLE)
    unit1, col, row, hot = run(
        unit_kernel,
        None,
        (x_o, x_t, x_n, x_m, place_in),
        (
            ((keys, width), F32),
            ((keys, SLAB), F32),
            ((8, mine), F32),
            ((half_w, place_in.shape[1]), BF),
        ),
        [],
        us=4,
    )
    q_got, unit1, u4, d2 = all_after([q_got, unit1, u4, d2])
    u_held = u4
    u_got = net.across(u4, last)
    a1, q, k, v, w_mix, vec = run(
        mix_kernel,
        inv,
        (unit1, pi, row_device, owner_in, hot, q_held, q_got),
        (
            ((keys, width), BF),
            (by_pair(mine), BF),
            (by_pair(keys), BF),
            (by_pair(keys), BF),
            ((3, width, half_w), BF),
            ((1, place_in.shape[1]), F32),
        ),
        [vm((keys, width), BF), vm((chips * 16, half_w), BF), dma(chips, 3), dma(chips)],
        anys=(5, 6),
        us=8,
    )
    d_got = net.across(d2, 2, net.mixed)
    g_out = all_after(g_out, k)
    g_in = [lax.ppermute(g_out[k], AXES, net.scatter_move(k)) for k in range(2)]
    o, low, lse = run(
        attend_kernel,
        None,
        (q, k, v, col, row),
        ((by_pair(mine), F32), (by_pair(mine), BF), ((PAIRS, 8, mine), F32)),
        [vm((keys, mine), F32), vm((keys, mine), F32), vm((keys, mine), BF)],
        us=12,
    )
    d4 = jnp.concatenate([d2, d_got])
    g_o = jnp.stack(g_in)
    blocks = ((half, 96, width), BF)
    part, wo = run(
        project_kernel,
        inv,
        (all_after([low], d_got, *g_in)[0], perm, u_held, u_got),
        (((mine, width), BF), ((half_w, width), BF)),
        [vm((chips * 32, width), BF), dma(chips)],
        anys=(2, 3),
        us=3,
    )
    part_got = net.core(part)
    g_t = net.core(g_o)
    d_half = d_got
    d_held = jnp.concatenate([d2, d_half])
    d_got = net.across(d_held, last, net.mixed)
    mid, a2, act, fac, w_up, keep_d, send_d, g_sum, w_half = run(
        middle_kernel,
        (inv, inv_d),
        (part, part_got, x_o, x_t, g_o, g_t, vec, pi, u_held, u_got, d_held),
        (
            ((mine, width), F32),
            ((mine, width), BF),
            ((mine, half_f), BF),
            ((mine, half_f), F32),
            ((width, half_f), BF),
            blocks,
            blocks,
            ((1, width), F32),
            ((half_f, width), BF),
        ),
        [vm((mine, width), BF), vm((half_f, width), BF), dma(chips, 2), dma(half)],
        anys=(8, 9, 10),
        us=10,
    )

    def fold_in(keep, got):
        n = keep.shape[0] // 2
        total = [keep[at].astype(F32) + got[at].astype(F32) for at in (slice(n), slice(n, None))]
        return [part.astype(BF) for part in total]

    def shrink(keep, send, stage, orders=None, then=()):
        got = net.across(send, stage, orders)
        if then:
            got = after(got, *then)
        if stage == 0:
            return (keep.astype(F32) + got.astype(F32))[0]
        return fold_in(keep, got)

    pre, e2, w_down, pre_sum = run(
        slope_kernel,
        inv_d,
        (g_o, g_t, fac, w_up, pi, w_half, d_got),
        (
            ((mine, half_f), BF),
            ((mine, width), BF),
            ((half_f, width), BF),
            ((1, half_f), F32),
        ),
        [dma(half)],
        anys=(6,),
        us=8,
        alias={6: 2},
    )
    keep_d, send_d = shrink(keep_d, send_d, 3)
    e2_got = after(net.core(e2), send_d)
    down_own, down_give = run(
        down_kernel,
        None,
        (act, w_down),
        (((own, width), F32), ((own, width), BF)),
        [],
        us=2,
    )
    wide_sum, half_sum = ((1, width), F32), ((1, half_w), F32)
    blocks_u = ((half, 128, width), BF)
    gm, branch, d_heads, keep_u, send_u, e2n, e2s, bs = run(
        branch_kernel,
        inv,
        (e2, e2_got, mid, g_o, g_t, vec, wo, low, perm, a2, pre),
        (
            ((own, width), F32),
            ((mine, width), BF),
            (by_pair(mine), BF),
            blocks_u,
            blocks_u,
            wide_sum,
            wide_sum,
            wide_sum,
        ),
        [vm((width, half_f), BF), vm((chips * 32, width), BF)],
        us=0.1,
    )
    down_got = net.core(after(down_give, e2_got)).astype(F32)
    out_own = (mid[:own] + down_own + down_got + vec[:, AT["bias_down"]]).astype(BF)
    out_own = out_own.reshape(local, cols, width)
    out_parts = [out_own[k] for k in range(2)]
    keep_d, send_d = shrink(keep_d, send_d, 2, then=(send_u,))
    send_d, d_heads, *out_parts = all_after([send_d, d_heads, *out_parts])
    quarter = ((2, own, width), BF)
    blocks_q = ((half, 160, half_w), BF)
    home = lambda k: [(b, a) for a, b in net.scatter_move(k)]
    dq, dk, dv, dqs, dvs = run(
        attend_back_kernel,
        None,
        (q, k, v, o, lse, col, row, d_heads),
        (
            (by_pair(mine), BF),
            (by_pair(keys), BF),
            (by_pair(keys), BF),
            half_sum,
            half_sum,
        ),
        [vm((keys, mine), F32), vm((keys, mine), BF), vm((keys, mine), BF)],
        us=10,
    )
    out_parts = [lax.ppermute(out_parts[k], AXES, home(k)) for k in range(2)]
    out_parts = all_after(out_parts, dq)
    d_1 = shrink(keep_d, send_d, 1, then=(dq,))
    keep_e, give_e, e1n, e1s = run(
        input_kernel,
        None,
        (all_after([dq], d_1[1], *out_parts)[0], dk, dv, w_mix, unit1, pi),
        (quarter, quarter, wide_sum, wide_sum),
        [],
        us=0.1,
    )
    got_e = net.core(give_e)
    (e1_give,) = run(near_kernel, None, (keep_e, got_e), (((own, width), BF),), [], us=0.1)
    u3 = shrink(keep_u, send_u, 3, then=(keep_e,))
    got_d = net.across(d_1[1], 0)
    shard_d = (d_1[0].astype(F32) + got_d.astype(F32))[0]
    keep_q, send_q = run(
        gather_grads_kernel,
        inv,
        (all_after([a1], u3[1], e1_give)[0], dq, dk, dv, row_device, owner_out, place_out)
        + (e1n, e2n, e2s, dqs, bs, g_sum, pre_sum, e1s, dvs),
        (blocks_q, blocks_q),
        [
            vm((3, width, half_w), BF),
            vm((chips * 16, half_w), BF),
            vm((half_w, place_out.shape[1]), BF),
        ],
        us=0.1,
    )
    q_3 = shrink(*all_after([keep_q, send_q], got_d), 3)
    back = jnp.stack(out_parts)
    block_out = jnp.where(zodd == 0, back, back[::-1])
    block = ((cols, width), BF)
    u_2 = shrink(*u3, 2, then=(send_q,))
    e1_near = net.pair(all_after([e1_give], q_3[1])[0])
    u_1 = shrink(*u_2, 1, then=(q_3[1],))
    q_2 = shrink(*q_3, 2)
    in_parts = run(
        finish_kernel,
        None,
        (keep_e, got_e, all_after([e1_near], q_2[1])[0], x_o, gm, vec),
        (block, block),
        [],
        us=0.1,
    )
    in_parts = [lax.ppermute(in_parts[k], AXES, home(k)) for k in range(2)]
    got_last = net.across(u_1[1], 0)
    q_1 = shrink(*all_after(q_2, u_1[1]), 1)
    shard_u = (u_1[0].astype(F32) + all_after([got_last], q_1[1])[0].astype(F32))[0]
    in_parts = all_after(in_parts, q_1[1])
    shard_q = shrink(*q_1, 0)
    back = jnp.stack(in_parts)
    input_grad = jnp.where(zodd == 0, back, back[::-1]).astype(F32)

    def own_rows(chip):
        keep = jnp.where(core == 0, chip[..., 0, :, :], chip[..., 1, :, :])
        give = jnp.where(core == 0, chip[..., 1, :, :], chip[..., 0, :, :])
        return keep, net.core(give)

    def merge(keep, got, parts):
        view = lambda array: array.reshape(*array.shape[:-1], parts, 1, -1)
        first = jnp.where(core == 0, view(keep), view(got))
        second = jnp.where(core == 0, view(got), view(keep))
        return jnp.concatenate([first, second], axis=-2).reshape(*keep.shape[:-1], -1)

    qkv_own = merge(*own_rows(shard_q[: 6 * rows].reshape(3, 2, rows, half_w)), net.x)
    g_qkv = jnp.moveaxis(qkv_own, 0, 1).reshape(-1)
    g_out = shard_u[4 * rows : 5 * rows].reshape(-1)
    up_own = merge(*own_rows(unfold(shard_u[: 4 * rows], 2).reshape(2, rows, half_f)), net.x)
    two = shard_q[6 * rows : 6 * rows + 2, : 2 * ll + rl]
    keep_s, got_s = own_rows(two.reshape(2, 1, -1))
    own_sums = (keep_s + got_s)[0]
    return (
        block_out,
        input_grad,
        g_qkv,
        g_out,
        up_own.reshape(-1),
        shard_d.reshape(-1),
        own_sums[:ll],
        own_sums[ll : ll + rl],
        own_sums[ll + rl :],
    )


def solution(mesh):
    dp, seq = mesh.shape["dp"], mesh.shape["seq"]
    y = 1 << (((seq.bit_length() - 1) - 1) // 2)
    z = seq // y
    dims = (dp // 2, 2, 4, z // 4, y // 2, 2)
    net = Net(dims)
    inner = Mesh(mesh.devices.reshape(dims), AXES)
    place = ("zh", "zl", "yh", "yl")
    cube = P(("x", "c"), place, None)
    flat = P(AXES)
    rows = D // (2 * net.chips)
    tiles = rows == 24 and net.chips == 16 and net.zl * net.yh == 1
    return jax.shard_map(
        functools.partial(body if tiles else body_any, net),
        mesh=inner,
        in_specs=(cube, P(("x", "c"), place), cube) + (flat,) * 6,
        out_specs=(cube, cube) + (flat,) * 7,
        check_vma=False,
    )
```

```python
import functools
import itertools

import jax
import jax.numpy as jnp
import numpy as np
from jax import lax
from jax.experimental import pallas as pl
from jax.experimental.pallas import tpu as pltpu
from jax.sharding import Mesh
from jax.sharding import PartitionSpec as P

D = 768
FF = 3072
HEADS = 12
HEAD_DIM = 64
EPS = 1e-05
MASKED = -1000000000.0
BF = jnp.bfloat16
F32 = jnp.float32
AXES = ("x", "c", "zh", "zl", "yh", "yl")


class Net:
    def __init__(self, dims):
        self.dims = dims
        self.x, self.c, self.zh, self.zl, self.yh, self.yl = dims
        self.z, self.y = self.zh * self.zl, self.yh * self.yl
        self.chips = self.x * self.z * self.y
        bits = lambda axis, n: [(axis, 1 << b) for b in reversed(range(n.bit_length() - 1))]
        zs, xs, ys = bits("z", self.z), bits("x", self.x), bits("y", self.y)
        self.orders = (zs + xs + ys, zs + ys + xs)
        self.mixed = (xs + zs + ys, ys + zs + xs)
        self.stages = len(self.orders[0])

    def perm(self, move):
        pairs = []
        for at in itertools.product(*(range(n) for n in self.dims)):
            to = move(*at)
            pairs.append(
                (int(np.ravel_multi_index(at, self.dims)), int(np.ravel_multi_index(to, self.dims)))
            )
        return pairs

    def flip(self, stage, orders):
        def move(x, c, zh, zl, yh, yl):
            axis, bit = orders[c][stage]
            z, y = zh * self.zl + zl, yh * self.yl + yl
            if axis == "x":
                x ^= bit
            elif axis == "y":
                y ^= bit
            else:
                z ^= bit
            return (x, c, z // self.zl, z % self.zl, y // self.yl, y % self.yl)

        return self.perm(move)

    def across(self, value, stage, orders=None):
        return lax.ppermute(value, AXES, self.flip(stage, orders or self.orders))

    def core(self, value):
        return lax.ppermute(value, "c", [(0, 1), (1, 0)])

    def pair(self, value):
        return lax.ppermute(value, "yl", [(0, 1), (1, 0)])

    def scatter_move(self, k):
        return self.perm(
            lambda x, c, zh, zl, yh, yl: (x, zh >> 1, 2 * c + (k ^ (zh & 1)), zl, yh, yl)
        )

    def table(self, orders=None):
        me = {
            "x": lax.axis_index("x"),
            "z": lax.axis_index("zh") * self.zl + lax.axis_index("zl"),
            "y": lax.axis_index("yh") * self.yl + lax.axis_index("yl"),
        }
        grid = np.indices((self.x, self.z, self.y)).reshape(3, -1)
        axes = {"x": grid[0], "z": grid[1], "y": grid[2]}
        places = []
        for order in orders or self.orders:
            place = jnp.zeros((self.chips,), jnp.int32)
            for stage, (axis, bit) in enumerate(order):
                differs = (jnp.asarray(axes[axis], jnp.int32) ^ me[axis]) & bit
                place = place + jnp.where(differs != 0, 1 << stage, 0)
            places.append(place)
        return jnp.where(lax.axis_index("c") == 0, places[0], places[1]).astype(jnp.int32)

    def gather(self, block):
        held = block[None]
        for stage in range(self.stages):
            held = jnp.concatenate([held, self.across(held, stage)])
        return held

    def scatter(self, held):
        for stage in reversed(range(self.stages)):
            half = held.shape[0] // 2
            got = self.across(held[half:], stage)
            held = held[:half].astype(F32) + got.astype(F32)
            if stage:
                held = held.astype(BF)
        return held[0]


def move_kernel(table, source, target):
    target[...] = source[...]


def reorder(blocks, table, to_place):
    rest = -blocks.shape[1] % 16
    if rest:
        rows = blocks.shape[1]
        blocks = jnp.pad(blocks, ((0, 0), (0, rest), (0, 0)))
        return reorder(blocks, table, to_place)[:, :rows]
    chips, rows, cols = blocks.shape
    here = pl.BlockSpec((1, rows, cols), lambda chip, table: (chip, 0, 0))
    there = pl.BlockSpec((1, rows, cols), lambda chip, table: (table[chip], 0, 0))
    return pl.pallas_call(
        move_kernel,
        grid_spec=pltpu.PrefetchScalarGridSpec(
            num_scalar_prefetch=1,
            grid=(chips,),
            in_specs=[here if to_place else there],
            out_specs=there if to_place else here,
        ),
        out_shape=jax.ShapeDtypeStruct(blocks.shape, blocks.dtype),
    )(table, blocks)


def normal(field):
    center = field - jnp.mean(field, axis=-1, keepdims=True)
    inverse = lax.rsqrt(jnp.mean(center * center, axis=-1, keepdims=True) + EPS)
    return center * inverse, inverse


def norm_back(upstream, unit, inverse, gain):
    scaled = upstream * gain
    return inverse * (
        scaled
        - jnp.mean(scaled, axis=-1, keepdims=True)
        - unit * jnp.mean(scaled * unit, axis=-1, keepdims=True)
    )


def dot(a, b):
    return jnp.dot(a, b, preferred_element_type=F32)


def dot_t(a, b):
    return lax.dot_general(a, b, (((1,), (1,)), ((), ())), preferred_element_type=F32)


def t_dot(a, b):
    return lax.dot_general(a, b, (((0,), (0,)), ((), ())), preferred_element_type=F32)


def fold(wide, parts):
    lead, rows, cols = wide.shape[:-2], wide.shape[-2], wide.shape[-1] // parts
    moved = jnp.moveaxis(wide.reshape(*lead, rows, parts, cols), -2, -3)
    return moved.reshape(*lead, parts * rows, cols)


def unfold(tall, parts):
    lead, rows, cols = tall.shape[:-2], tall.shape[-2] // parts, tall.shape[-1]
    moved = jnp.moveaxis(tall.reshape(*lead, parts, rows, cols), -3, -2)
    return moved.reshape(*lead, rows, parts * cols)


def body_any(net, tokens, segments, cotangent, w_qkv, w_out, w_fc1, w_fc2, norm_gains, bias_pack):
    local, cols, width = tokens.shape
    own = local * cols
    mine = 2 * own
    hidden = FF
    half_w, half_f = width // 2, hidden // 2
    devices = 2 * net.chips
    core = lax.axis_index("c")
    zodd = lax.axis_index("zh") & 1
    table = net.table()
    rows = width // devices
    frows = hidden // devices
    aligned = (width // (2 * net.x)) % HEAD_DIM == 0
    groups = net.x if aligned else 1

    def pick(array, parts, which):
        split = array.reshape(*array.shape[:-1], parts, 2, array.shape[-1] // (2 * parts))
        taken = jnp.where(which == 0, split[..., 0, :], split[..., 1, :])
        return taken.reshape(*array.shape[:-1], array.shape[-1] // 2)

    def spread(vector, parts):
        split = vector.reshape(parts, 1, vector.shape[-1] // parts)
        both = jnp.concatenate(
            [jnp.where(core == 0, split, 0.0), jnp.where(core == 1, split, 0.0)], axis=1
        )
        return both.reshape(-1)

    seg_row = jnp.pad(segments.astype(BF), ((0, 0), (0, width - cols)))[:, None, :]
    seg_rows = jnp.pad(seg_row, ((0, 0), (0, 7), (0, 0)))
    packed = jnp.concatenate([tokens, seg_rows], axis=1)

    def to_sequence(array):
        swapped = jnp.where(zodd == 0, array, array[::-1])
        return jnp.stack(
            [lax.ppermute(swapped[k], AXES, net.scatter_move(k)) for k in range(2)]
        )

    def from_sequence(array):
        back = jnp.stack(
            [
                lax.ppermute(array[k], AXES, [(b, a) for a, b in net.scatter_move(k)])
                for k in range(2)
            ]
        )
        return jnp.where(zodd == 0, back, back[::-1])

    def halves(which):
        qkv = fold(w_qkv.reshape(rows, 3 * width), 3).reshape(3, rows, width)
        up = w_fc1.reshape(rows, hidden)
        return pick(qkv, groups, which), pick(up, net.x, which)

    keep_qkv, keep_up = halves(core)
    give_qkv, give_up = halves(1 - core)
    small = jnp.concatenate([norm_gains, bias_pack])
    out_rows = w_out.reshape(rows, width)
    got_qkv, got_up, got_small, got_out = jax.tree.map(
        net.core, (give_qkv, give_up, small, out_rows)
    )

    def both(a, b, axis):
        return jnp.where(
            core == 0, jnp.concatenate([a, b], axis=axis), jnp.concatenate([b, a], axis=axis)
        )

    chip_qkv = both(keep_qkv, got_qkv, 1).reshape(6 * rows, half_w)
    chip_up = fold(both(keep_up, got_up, 0), 2)
    chip_out = fold(out_rows if aligned else both(out_rows, got_out, 0), 2)
    chip_small = jnp.pad(
        both(small[None], got_small[None], 0), ((0, 14), (0, half_w - small.shape[0]))
    )
    cut = np.cumsum([chip_qkv.shape[0], chip_out.shape[0]])
    blocks_a = reorder(
        net.gather(jnp.concatenate([chip_qkv, chip_out, chip_small])), table, False
    )
    blocks_up = reorder(net.gather(chip_up), table, False)
    blocks_down = reorder(net.gather(w_fc2.reshape(frows, width)), table, False)

    lead = (net.x, net.z, net.y)

    def natural(blocks):
        n = blocks.shape[-1]
        return jnp.moveaxis(blocks.reshape(*lead, 2, -1, n), 3, 1).reshape(-1, n)

    def by_chip(array):
        n = array.shape[-1]
        return jnp.moveaxis(array.reshape(net.x, 2, net.z, net.y, -1, n), 1, 3).reshape(
            net.chips, -1, n
        )

    qkv_blocks = blocks_a[:, : cut[0]].reshape(net.chips, 3, 2 * rows, half_w)
    w_q, w_k, w_v = (natural(qkv_blocks[:, i]) for i in range(3))
    out_blocks = unfold(blocks_a[:, cut[0] : cut[1]], 2)
    if aligned:
        w_proj = out_blocks.reshape(half_w, width)
    else:
        w_proj = lax.dynamic_slice_in_dim(natural(out_blocks), core * half_w, half_w)
    smalls = blocks_a[:, cut[1] : cut[1] + 2, : small.shape[0]].reshape(*lead, 2, -1)
    smalls = jnp.moveaxis(smalls, 3, 1).reshape(devices, -1).astype(F32)
    n_gain = norm_gains.shape[0]
    gains = smalls[:, :n_gain].reshape(-1)
    shifts = smalls[:, n_gain:].reshape(-1)
    w_up = natural(unfold(blocks_up, 2))
    w_down = blocks_down.reshape(half_f, width)
    gain1, gain2 = gains[:width], gains[width:]
    shift1, shift2, bias_q, bias_v, bias_proj, bias_down = (
        shifts[i * width : (i + 1) * width] for i in range(6)
    )
    bias_up = pick(shifts[6 * width :], net.x, core)
    bias_q, bias_v = pick(bias_q, groups, core), pick(bias_v, groups, core)

    x_own = to_sequence(packed)
    x_other = net.core(x_own)
    x_mine = jnp.concatenate([x_own, x_other])
    near = net.pair(x_own)
    near = jnp.concatenate([near, net.core(near)])
    x_seq = jnp.concatenate([x_mine, near])
    if net.zl * net.yh > 1:
        x_far = lax.all_gather(x_seq, ("zl", "yh"), axis=0, tiled=True)
        x_keys = x_far
    else:
        x_keys = x_seq
    g_own = to_sequence(cotangent)
    g_mine = jnp.concatenate([g_own, net.core(g_own)]).reshape(mine, width)
    docs = x_keys[:, cols, :cols].reshape(-1)
    query_docs = x_mine[:, cols, :cols].reshape(-1)
    x_all = x_keys[:, :cols].reshape(-1, width).astype(F32)
    x_q = x_mine[:, :cols].reshape(-1, width).astype(F32)

    unit_q, inverse_q = normal(x_q)
    a_q = (unit_q * gain1 + shift1).astype(BF)
    unit_all, _ = normal(x_all)
    a_all = (unit_all * gain1 + shift1).astype(BF)
    heads = HEADS // 2
    q = (dot(a_q, w_q) + bias_q).astype(BF)
    k = dot(a_all, w_k).astype(BF)
    v = (dot(a_all, w_v) + bias_v).astype(BF)
    by_head = lambda t: t.reshape(-1, heads, HEAD_DIM)
    same = (query_docs[:, None] == docs[None, :])[None]
    scores = (
        jnp.einsum("qhd,khd->hqk", by_head(q), by_head(k), preferred_element_type=F32) * 0.125
    )
    scores = jnp.where(same, scores, MASKED)
    weights = jnp.exp(scores - jnp.max(scores, axis=-1, keepdims=True))
    probs = weights / jnp.sum(weights, axis=-1, keepdims=True)
    probs_low = probs.astype(BF)
    att = jnp.einsum("hqk,khd->qhd", probs_low, by_head(v), preferred_element_type=F32)
    att = att.reshape(mine, half_w)
    att_low = att.astype(BF)

    def core_sum(partial):
        low = partial.astype(BF)
        got = net.core(low)
        return low.astype(F32) + jnp.concatenate([got[own:], got[:own]]).astype(F32)

    middle = x_q + core_sum(dot(att_low, w_proj)) + bias_proj
    unit2, inverse2 = normal(middle)
    a2 = (unit2 * gain2 + shift2).astype(BF)
    pre = dot(a2, w_up) + bias_up
    sig = jax.nn.sigmoid(1.702 * pre)
    activ = (pre * sig).astype(BF)
    down = dot(activ, w_down)
    down_got = net.core(down[own:].astype(BF)).astype(F32)
    out_own = (middle[:own] + down[:own] + down_got + bias_down).astype(BF)
    block_out = from_sequence(out_own.reshape(local, cols, width))

    grad_down = t_dot(activ, g_mine).astype(BF)
    grad_pre = (dot_t(g_mine, w_down) * (sig + 1.702 * pre * sig * (1.0 - sig))).astype(BF)
    shard_down = net.scatter(reorder(grad_down.reshape(net.chips, frows, width), table, True))
    grad_up = t_dot(a2, grad_pre).astype(BF)
    shard_up = net.scatter(reorder(fold(by_chip(grad_up), 2), table, True))
    e2 = core_sum(dot_t(grad_pre, w_up))
    grad_middle = g_mine.astype(F32) + norm_back(e2, unit2, inverse2, gain2)
    branch = grad_middle.astype(BF)
    grad_proj = t_dot(att_low, branch).astype(BF)
    d_heads = dot_t(branch, w_proj).astype(BF)
    dp = jnp.einsum("qhd,khd->hqk", by_head(d_heads), by_head(v), preferred_element_type=F32)
    delta = jnp.sum(probs * dp, axis=-1, keepdims=True)
    d_scores = (probs * (dp - delta)).astype(BF)
    dq = 0.125 * jnp.einsum("hqk,khd->qhd", d_scores, by_head(k), preferred_element_type=F32)
    dk = 0.125 * jnp.einsum("hqk,qhd->khd", d_scores, by_head(q), preferred_element_type=F32)
    dv = jnp.einsum("hqk,qhd->khd", probs_low, by_head(d_heads), preferred_element_type=F32)
    dq = dq.reshape(-1, half_w).astype(BF)
    dk = dk.reshape(-1, half_w).astype(BF)
    dv = dv.reshape(-1, half_w).astype(BF)
    grad_qkv = jnp.stack([t_dot(a_q, dq), t_dot(a_all, dk), t_dot(a_all, dv)]).astype(BF)

    e1_keys = (dot_t(dk, w_k) + dot_t(dv, w_v)).astype(BF)
    if net.zl * net.yh > 1:
        e1_keys = lax.psum_scatter(
            e1_keys, ("zl", "yh"), scatter_dimension=0, tiled=True
        )
    e1_near = e1_keys[mine:].reshape(2, own, width)
    e1_mine = e1_keys[:mine].astype(F32) + dot_t(dq, w_q)
    e1_mine = e1_mine.astype(BF).reshape(2, own, width)
    got = net.core(jnp.stack([e1_mine[1], e1_near[1]]))
    e1_near = e1_near[0].astype(F32) + got[1].astype(F32)
    e1 = e1_mine[0].astype(F32) + got[0].astype(F32) + net.pair(e1_near.astype(BF)).astype(F32)
    unit1 = unit_q[:own]
    in_own = grad_middle[:own] + norm_back(e1, unit1, inverse_q[:own], gain1)
    input_grad = from_sequence(in_own.astype(BF).reshape(local, cols, width)).astype(F32)

    total = lambda array: jnp.sum(array.astype(F32), axis=0)
    g_own = g_mine[:own]
    gain_sums = jnp.concatenate([total(e1 * unit1), total(e2[:own] * unit2[:own])])
    bias_sums = jnp.concatenate(
        [
            total(e2[:own]),
            spread(total(dq), groups),
            total(branch[:own]),
            total(g_own),
            spread(total(grad_pre), net.x),
        ]
    )
    lead_sums = jnp.concatenate([total(e1), spread(total(dv), groups)])
    sums = jnp.concatenate(
        [v.reshape(devices, -1) for v in (gain_sums, bias_sums, lead_sums)], axis=1
    )
    sums = sums + net.core(sums)
    sums = jnp.moveaxis(sums.reshape(net.x, 2, net.z, net.y, -1), 1, 0)
    sums = jnp.where(core == 0, sums[0], sums[1]).reshape(net.chips, 1, -1)
    n_sums = sums.shape[-1]
    sums = jnp.pad(sums, ((0, 0), (0, 15), (0, half_w - n_sums))).astype(BF)
    qkv_send = jnp.stack([by_chip(grad_qkv[i]) for i in range(3)], axis=1)
    qkv_send = qkv_send.reshape(net.chips, 6 * rows, half_w)
    if aligned:
        out_send = grad_proj.reshape(net.chips, rows, width)
    else:
        whole = jnp.zeros((width, width), BF)
        whole = lax.dynamic_update_slice(whole, grad_proj, (core * half_w, 0))
        out_send = by_chip(whole)
    sent = jnp.concatenate([qkv_send, fold(out_send, 2), sums], axis=1)
    shard_a = net.scatter(reorder(sent, table, True))

    def own_rows(chip):
        keep = jnp.where(core == 0, chip[..., 0, :, :], chip[..., 1, :, :])
        give = jnp.where(core == 0, chip[..., 1, :, :], chip[..., 0, :, :])
        return keep, net.core(give)

    def merge(keep, got, parts):
        split = lambda array: array.reshape(*array.shape[:-1], parts, 1, -1)
        first = jnp.where(core == 0, split(keep), split(got))
        second = jnp.where(core == 0, split(got), split(keep))
        return jnp.concatenate([first, second], axis=-2).reshape(*keep.shape[:-1], -1)

    qkv_own = merge(*own_rows(shard_a[: cut[0]].reshape(3, 2, rows, half_w)), groups)
    g_qkv = jnp.moveaxis(qkv_own, 0, 1).reshape(-1)
    out_own = unfold(shard_a[cut[0] : cut[1]], 2)
    if not aligned:
        keep, got = own_rows(out_own.reshape(2, rows, width))
        out_own = keep + got
    g_out = out_own.reshape(-1)
    up_own = merge(*own_rows(unfold(shard_up, 2).reshape(2, rows, half_f)), net.x)
    own_sums = shard_a[cut[1], :n_sums]
    n_gain = 2 * width // devices
    n_lead = n_sums - n_gain
    return (
        block_out,
        input_grad,
        g_qkv,
        g_out,
        up_own.reshape(-1),
        shard_down.reshape(-1),
        own_sums[:n_gain],
        own_sums[n_gain:n_lead],
        own_sums[n_lead:],
    )


SLAB = 128
PAIRS = HEADS // 4
DOUBLE = 2 * HEAD_DIM
PARTS = (
    ("gain1", D),
    ("gain2", D),
    ("shift1", D),
    ("shift2", D),
    ("bias_proj", D),
    ("bias_down", D),
    ("bias_q", D // 2),
    ("bias_v", D // 2),
    ("bias_up", FF // 2),
)
SUMS = (
    ("e1n", D),
    ("e2n", D),
    ("e2", D),
    ("dq", D // 2),
    ("branch", D),
    ("g", D),
    ("pre", FF // 2),
    ("e1", D),
    ("dv", D // 2),
)


def offsets(parts):
    ends = np.cumsum([n for _, n in parts])
    return {name: slice(int(end - n), int(end)) for (name, n), end in zip(parts, ends)}


AT = offsets(PARTS)


def dots(a, b, ca, cb):
    return lax.dot_general(a, b, (((ca,), (cb,)), ((), ())), preferred_element_type=F32)


def lane_half(e):
    lanes = lax.broadcasted_iota(jnp.int32, (1, DOUBLE), 1)
    inside = (lanes < HEAD_DIM) if e == 0 else (lanes >= HEAD_DIM)
    return inside.astype(F32).astype(BF)


def first_half(shape):
    return lax.broadcasted_iota(jnp.int32, shape, 1) < HEAD_DIM


def load_rows(inv, held, got, target, sems, pieces):
    half = held.shape[0]
    copies = []
    for r in range(2 * half):
        source = held if r < half else got
        for n, (first, rows, place) in enumerate(pieces):
            copies.append(
                pltpu.make_async_copy(
                    source.at[r % half, pl.ds(first, rows), :],
                    place(target, inv[r], rows),
                    sems.at[r, n],
                )
            )
    for copy in copies:
        copy.start()
    return copies


def one_hot(place, target):
    step = 128
    for i in range(target.shape[0] // step):
        shape = (step, target.shape[1])
        entry = lax.broadcasted_iota(jnp.int32, shape, 0) + i * step
        target[i * step : (i + 1) * step, :] = (entry == place[:1, :]).astype(F32).astype(BF)


def unit_kernel(xo, xt, xn, xm, place, unit_ref, col_ref, row_ref, hot_ref):
    one_hot(place, hot_ref)
    for i, (ref, j) in enumerate((ref, j) for ref in (xo, xt, xn, xm) for j in range(2)):
        unit, _ = normal(ref[j, :SLAB, :].astype(F32))
        at = pl.ds(i * SLAB, SLAB)
        unit_ref[at, :] = unit
        docs = ref[j, :, :SLAB].astype(F32)[SLAB : SLAB + 1]
        col_ref[at, :] = jnp.broadcast_to(docs, (SLAB, SLAB)).T
        if i < 4:
            row_ref[:, i * SLAB : (i + 1) * SLAB] = jnp.broadcast_to(docs, (8, SLAB))


def fill_bias(col, row, bias):
    for i in range(bias.shape[0] // SLAB):
        at = pl.ds(i * SLAB, SLAB)
        for j in range(bias.shape[1] // SLAB):
            lanes = pl.ds(j * SLAB, SLAB)
            bias[at, lanes] = jnp.where(col[at, :] == row[:1, lanes], 0.0, MASKED)


def pick_rows(rows, step):
    shape = (2 * rows // step, rows)
    i = lax.broadcasted_iota(jnp.int32, shape, 0)
    j = lax.broadcasted_iota(jnp.int32, shape, 1)
    return (j == (i >> 1) * step + (i & 1)).astype(F32).astype(BF)


def mix_kernel(
    inv, unit, pi, device, owner, hot, held, got,
    a_ref, q_ref, k_ref, v_ref, w, vec, nat, small, sems, small_sems,
):
    half = held.shape[0]
    few = []
    for r in range(2 * half):
        source = held if r < half else got
        few.append(
            pltpu.make_async_copy(
                source.at[r % half, pl.ds(144, 16), :], small.at[pl.ds(r * 16, 16), :], small_sems.at[r]
            )
        )
    for copy in few:
        copy.start()
    place = lambda i: lambda t, chip, n: t.at[i, pl.ds(pl.multiple_of(chip * n, 16), n), :]
    copies = load_rows(inv, held, got, w, sems, [(48 * i, 48, place(i)) for i in range(3)])
    for copy in few:
        copy.wait()
    picked = dot(pick_rows(small.shape[0], 16), small[...]).astype(BF)
    mine_only = jnp.where(device[:, :1] == owner[:1, :], dot(picked, hot[...]), 0.0)
    vec[...] = jnp.sum(mine_only, axis=0, keepdims=True)
    keys = a_ref.shape[0]
    for i in range(keys // SLAB):
        at = pl.ds(i * SLAB, SLAB)
        nat[at, :] = (unit[at, :] * vec[:, AT["gain1"]] + vec[:, AT["shift1"]]).astype(BF)
    a_ref[...] = dot(nat[...], pi[...]).astype(BF)
    for copy in copies:
        copy.wait()
    mine = q_ref.shape[1]
    q = (dot(a_ref[:mine, :], w[0]) + vec[:, AT["bias_q"]]).astype(BF) * 0.125
    k = dot(a_ref[...], w[1]).astype(BF)
    v = (dot(a_ref[...], w[2]) + vec[:, AT["bias_v"]]).astype(BF)
    for i in range(PAIRS):
        lanes = slice(i * DOUBLE, (i + 1) * DOUBLE)
        q_ref[i], k_ref[i], v_ref[i] = q[:, lanes], k[:, lanes], v[:, lanes]


def attend_kernel(q_ref, k_ref, v_ref, col, row, o_ref, low_ref, lse_ref, bias, s, p_low):
    mine, keys = q_ref.shape[1], k_ref.shape[1]
    fill_bias(col, row, bias)

    def pair(i, carry):
        outs = []
        for e in range(2):
            qm = q_ref[i] * lane_half(e)
            top = jnp.full((1, mine), -3e38, F32)
            for c in range(keys // SLAB):
                at = pl.ds(c * SLAB, SLAB)
                t = dots(k_ref[i, at, :], qm, 1, 1) + bias[at, :]
                s[at, :] = t
                top = jnp.maximum(top, jnp.max(t, axis=0, keepdims=True))
            total = jnp.zeros((1, mine), F32)
            for c in range(keys // SLAB):
                at = pl.ds(c * SLAB, SLAB)
                p = jnp.exp(s[at, :] - top)
                total = total + jnp.sum(p, axis=0, keepdims=True)
                p_low[at, :] = p.astype(BF)
            lse_ref[i, e : e + 1, :] = top + jnp.log(total)
            o = dots(p_low[...], v_ref[i], 0, 0)
            scale = jnp.broadcast_to(1.0 / total, (DOUBLE, mine)).T
            outs.append(o * scale)
        o = jnp.where(first_half(outs[0].shape), outs[0], outs[1])
        o_ref[i] = o
        low_ref[i] = o.astype(BF)
        return carry

    lax.fori_loop(0, PAIRS, pair, 0)


def project_kernel(inv, low, perm, held, got, part_ref, wo_ref, rel, sems):
    half = held.shape[0]
    copies = []
    for r in range(2 * half):
        source = held if r < half else got
        copies.append(
            pltpu.make_async_copy(
                source.at[r % half, pl.ds(96, 32), :], rel.at[pl.ds(r * 32, 32), :], sems.at[r]
            )
        )
    for copy in copies:
        copy.start()
    for copy in copies:
        copy.wait()
    wo_ref[...] = dot(perm[...], rel[...]).astype(BF)
    att = jnp.concatenate([low[i] for i in range(PAIRS)], axis=1)
    part_ref[...] = dot(att, wo_ref[...]).astype(BF)


def load_half(inv, source, first, target, sems):
    rows = source.shape[1]
    copies = [
        pltpu.make_async_copy(
            source.at[r],
            target.at[pl.ds(pl.multiple_of(inv[first + r] * rows, 16), rows), :],
            sems.at[r],
        )
        for r in range(source.shape[0])
    ]
    for copy in copies:
        copy.start()
    return copies


def middle_kernel(
    inv, inv_d, part, part_got, xo, xt, go, gt, vec, pi, held, got, d_held,
    mid_ref, a_ref, act_ref, fac_ref, w, keep_ref, send_ref, sum_ref, w_down,
    nat, grad, sems, d_sems,
):
    place = lambda h: lambda t, chip, n: t.at[
        pl.ds(pl.multiple_of(chip * n, 16), n), pl.ds(h * D, D)
    ]
    copies = load_rows(inv, held, got, w, sems, [(48 * h, 48, place(h)) for h in range(2)])
    later = load_half(inv_d, d_held, 0, w_down, d_sems)
    mine = part.shape[0]
    own = mine // 2
    for i, (ref, j) in enumerate((ref, j) for ref in (xo, xt) for j in range(2)):
        at = pl.ds(i * SLAB, SLAB)
        other = pl.ds((i * SLAB + own) % mine, SLAB)
        mid = (
            ref[j, :SLAB, :].astype(F32)
            + (part[at, :].astype(F32) + part_got[other, :].astype(F32))
            + vec[:, AT["bias_proj"]]
        )
        mid_ref[at, :] = mid
        unit, _ = normal(mid)
        nat[at, :] = (unit * vec[:, AT["gain2"]] + vec[:, AT["shift2"]]).astype(BF)
    a_ref[...] = dot(nat[...], pi[...]).astype(BF)
    g = jnp.concatenate([go[0], go[1], gt[0], gt[1]], axis=0)
    sum_ref[...] = jnp.sum(g[:own].astype(F32), axis=0, keepdims=True)
    for copy in copies:
        copy.wait()
    step = 512
    for j in range(w.shape[1] // step):
        lanes = pl.ds(j * step, step)
        start = AT["bias_up"].start + j * step
        pre = dot(a_ref[...], w[:, lanes]) + vec[:, start : start + step]
        sig = 1.0 / (1.0 + jnp.exp(-1.702 * pre))
        act_ref[:, lanes] = (pre * sig).astype(BF)
        fac_ref[:, lanes] = sig + 1.702 * pre * sig * (1.0 - sig)
        grad[lanes, :] = dots(act_ref[:, lanes], g, 0, 0).astype(BF)
    half = keep_ref.shape[0]
    for r in range(2 * half):
        target = keep_ref if r < half else send_ref
        target[r % half] = grad[pl.ds(pl.multiple_of(inv[r] * 96, 16), 96), :]
    for copy in later:
        copy.wait()


def slope_kernel(inv, go, gt, fac, w_up, pi, w_half, got, pre_ref, e_ref, w, sum_ref, sems):
    copies = load_half(inv, got, got.shape[0], w, sems)
    g = jnp.concatenate([go[0], go[1], gt[0], gt[1]], axis=0)
    for copy in copies:
        copy.wait()
    step = 512
    total = None
    for j in range(w.shape[0] // step):
        lanes = pl.ds(j * step, step)
        pre = (dots(g, w[lanes, :], 1, 1) * fac[:, lanes]).astype(BF)
        pre_ref[:, lanes] = pre
        sum_ref[:, lanes] = jnp.sum(pre.astype(F32), axis=0, keepdims=True)
        term = dots(pre, w_up[:, lanes], 1, 1)
        total = term if total is None else total + term
    e_ref[...] = dots(total.astype(BF), pi[...], 1, 1).astype(BF)


def down_kernel(act, w_down, own_ref, give_ref):
    down = dot(act[...], w_down[...])
    own = own_ref.shape[0]
    own_ref[...] = down[:own]
    give_ref[...] = down[own:].astype(BF)


def wide(ref):
    return jnp.concatenate([ref[i] for i in range(PAIRS)], axis=1)


def branch_kernel(
    inv, e2, e2_got, mid, go, gt, vec, wo, low, perm, a, pre,
    gm_ref, branch_ref, d_ref, keep_ref, send_ref, e2n_sum, e2_sum, branch_sum, grad, out,
):
    mine = mid.shape[0]
    own = mine // 2
    sums = [jnp.zeros((1, D), F32) for _ in range(3)]
    for i, (ref, j) in enumerate((ref, j) for ref in (go, gt) for j in range(2)):
        at = pl.ds(i * SLAB, SLAB)
        other = pl.ds((i * SLAB + own) % mine, SLAB)
        e = e2[at, :].astype(F32) + e2_got[other, :].astype(F32)
        unit, inverse = normal(mid[at, :])
        gm = ref[j].astype(F32) + norm_back(e, unit, inverse, vec[:, AT["gain2"]])
        branch = gm.astype(BF)
        branch_ref[at, :] = branch
        if i < 2:
            gm_ref[at, :] = gm
            for n, term in enumerate((e * unit, e, branch.astype(F32))):
                sums[n] = sums[n] + jnp.sum(term, axis=0, keepdims=True)
    e2n_sum[...], e2_sum[...], branch_sum[...] = sums
    d = dots(branch_ref[...], wo[...], 1, 1).astype(BF)
    for i in range(PAIRS):
        d_ref[i] = d[:, i * DOUBLE : (i + 1) * DOUBLE]
    step = 512
    for j in range(pre.shape[1] // step):
        lanes = pl.ds(j * step, step)
        grad[:, lanes] = dots(a[...], pre[:, lanes], 0, 0).astype(BF)
    proj = dots(wide(low), branch_ref[...], 0, 0).astype(BF)
    out[...] = dots(perm[...], proj, 0, 0).astype(BF)
    half = keep_ref.shape[0]
    for r in range(2 * half):
        target, at = (keep_ref if r < half else send_ref), r % half
        rows = pl.ds(pl.multiple_of(inv[r] * 48, 16), 48)
        target[at, :48, :] = grad[rows, :D]
        target[at, 48:96, :] = grad[rows, D:]
        target[at, 96:, :] = out[r * 32 : r * 32 + 32, :]


def attend_back_kernel(
    q, k, v, o, lse, col, row, d_ref, dq_ref, dk_ref, dv_ref, dq_sum, dv_sum, bias, p_low, s_low
):
    mine, keys = q.shape[1], k.shape[1]
    fill_bias(col, row, bias)

    def pair(i, carry):
        both = (d_ref[i].astype(F32) * o[i]).T
        got = []
        for e in range(2):
            delta = jnp.sum(both[e * HEAD_DIM : (e + 1) * HEAD_DIM], axis=0, keepdims=True)
            qm = q[i] * lane_half(e)
            dm = d_ref[i] * lane_half(e)
            base = lse[i, e : e + 1, :]
            for c in range(keys // SLAB):
                at = pl.ds(c * SLAB, SLAB)
                t = dots(k[i, at, :], qm, 1, 1) + bias[at, :]
                p = jnp.exp(t - base)
                dp = dots(v[i, at, :], dm, 1, 1)
                p_low[at, :] = p.astype(BF)
                s_low[at, :] = (p * (dp - delta)).astype(BF)
            got.append(
                (
                    dots(s_low[...], k[i], 0, 0) * 0.125,
                    dot(s_low[...], q[i]),
                    dot(p_low[...], d_ref[i]),
                )
            )
        for n, ref in enumerate((dq_ref, dk_ref, dv_ref)):
            ref[i] = jnp.where(first_half(got[0][n].shape), got[0][n], got[1][n]).astype(BF)
        return carry

    lax.fori_loop(0, PAIRS, pair, 0)
    dq_sum[...] = jnp.sum(wide(dq_ref).astype(F32), axis=0, keepdims=True)
    dv_sum[...] = jnp.sum(wide(dv_ref).astype(F32), axis=0, keepdims=True)


def input_kernel(dq_ref, dk_ref, dv_ref, w, unit, pi, keep_ref, give_ref, e1n_sum, e1_sum):
    keys, own = unit.shape[0], keep_ref.shape[1]
    dq, dk, dv = wide(dq_ref), wide(dk_ref), wide(dv_ref)
    e1n = jnp.zeros((1, D), F32)
    e1s = jnp.zeros((1, D), F32)
    for part in range(keys // own):
        at = slice(part * own, (part + 1) * own)
        e = dots(dk[at], w[1], 1, 1) + dots(dv[at], w[2], 1, 1)
        if part < 2:
            e = e + dots(dq[at], w[0], 1, 1)
        e = dots(e.astype(BF), pi[...], 1, 1)
        e1s = e1s + jnp.sum(e, axis=0, keepdims=True)
        e1n = e1n + jnp.sum(e * unit[pl.ds(part * own, own), :], axis=0, keepdims=True)
        target = keep_ref if part % 2 == 0 else give_ref
        target[part // 2] = e.astype(BF)
    e1n_sum[...] = e1n
    e1_sum[...] = e1s


def near_kernel(keep, got, give):
    give[...] = (keep[1].astype(F32) + got[1].astype(F32)).astype(BF)


def finish_kernel(keep, got, near, x, gm, vec, *parts):
    for i, part in enumerate(parts):
        at = pl.ds(i * SLAB, SLAB)
        e = keep[0, at, :].astype(F32) + got[0, at, :].astype(F32) + near[at, :].astype(F32)
        unit, inverse = normal(x[i, :SLAB, :].astype(F32))
        part[...] = (gm[at, :] + norm_back(e, unit, inverse, vec[:, AT["gain1"]])).astype(BF)


def gather_grads_kernel(inv, a, dq, dk, dv, device, owner, place, *rest):
    sums, (keep_ref, send_ref, grad, small, hot) = rest[:-5], rest[-5:]
    one_hot(place, hot)
    mine = dq.shape[1]
    grad[0] = dots(a[:mine, :], wide(dq), 0, 0).astype(BF)
    grad[1] = dots(a[...], wide(dk), 0, 0).astype(BF)
    grad[2] = dots(a[...], wide(dv), 0, 0).astype(BF)
    line = jnp.concatenate([ref[...] for ref in sums], axis=1)
    kept = jnp.where(device[:, :1] == owner[:1, :], line, 0.0).astype(BF)
    placed = dots(kept, hot[...], 1, 1).astype(BF)
    small[...] = dots(pick_rows(small.shape[0], 16), placed, 0, 0).astype(BF)
    half = keep_ref.shape[0]
    for r in range(2 * half):
        target, at = (keep_ref if r < half else send_ref), r % half
        rows = pl.ds(pl.multiple_of(inv[r] * 48, 16), 48)
        for i in range(3):
            target[at, 48 * i : 48 * i + 48, :] = grad[i, rows, :]
        target[at, 144:160, :] = small[r * 16 : r * 16 + 16, :]


def run(kernel, table, args, outs, scratch, anys=(), us=5, mib=16, alias=None):
    specs = [
        pl.BlockSpec(memory_space=pl.ANY) if i in anys else pl.BlockSpec(memory_space=pltpu.VMEM)
        for i in range(len(args))
    ]
    prefetch = () if table is None else table if isinstance(table, tuple) else (table,)
    return pl.pallas_call(
        kernel,
        grid_spec=pltpu.PrefetchScalarGridSpec(
            num_scalar_prefetch=len(prefetch),
            grid=(),
            in_specs=specs,
            out_specs=[pl.BlockSpec(memory_space=pltpu.VMEM) for _ in outs],
            scratch_shapes=scratch,
        ),
        out_shape=[jax.ShapeDtypeStruct(shape, dtype) for shape, dtype in outs],
        input_output_aliases=alias or {},
        compiler_params=pltpu.CompilerParams(vmem_limit_bytes=mib * 2**20),
        cost_estimate=pl.CostEstimate(
            flops=int(us * 10**9), bytes_accessed=int(us * 10**6), transcendentals=0
        ),
    )(*prefetch, *args)


def body(net, tokens, segments, cotangent, w_qkv, w_out, w_fc1, w_fc2, norm_gains, bias_pack):
    local, cols, width = tokens.shape
    own, mine = local * cols, 2 * local * cols
    keys = 2 * mine
    hidden = FF
    half_w, half_f = width // 2, hidden // 2
    chips, devices = net.chips, 2 * net.chips
    half = chips // 2
    rows, frows = width // devices, hidden // devices
    core = lax.axis_index("c")
    zodd = lax.axis_index("zh") & 1
    def pick(array, parts, which):
        view = array.reshape(*array.shape[:-1], parts, 2, array.shape[-1] // (2 * parts))
        taken = jnp.where(which == 0, view[..., 0, :], view[..., 1, :])
        return taken.reshape(*array.shape[:-1], array.shape[-1] // 2)

    def both(a, b, axis):
        return jnp.where(
            core == 0, jnp.concatenate([a, b], axis=axis), jnp.concatenate([b, a], axis=axis)
        )

    small = jnp.concatenate([norm_gains, bias_pack])
    qkv = w_qkv.reshape(rows, 3, width).swapaxes(0, 1)
    got_qkv, got_small = net.core(pick(qkv, net.x, 1 - core)), net.core(small)
    chip_qkv = both(pick(qkv, net.x, core), got_qkv, 1).reshape(6 * rows, half_w)
    chip_small = jnp.pad(
        both(small[None], got_small[None], 0), ((0, 14), (0, half_w - small.shape[0]))
    )

    def after(value, *others):
        return lax.optimization_barrier((value, *others))[0]

    def all_after(values, *others):
        return lax.optimization_barrier((*values, *others))[: len(values)]

    def grow(held, stage, orders=None, then=()):
        got = net.across(held, stage, orders)
        if then:
            got = after(got, *then)
        return jnp.concatenate([held, got])

    last = net.stages - 1
    q0 = jnp.concatenate([chip_qkv, chip_small])[None]
    q1 = grow(q0, 0)
    spots = after(jnp.arange(chips, dtype=jnp.int32), q0)

    def order_of(orders):
        found = net.table(orders)[None, :] == spots[:, None]
        return jnp.sum(jnp.where(found, spots[None, :], 0), axis=1).astype(jnp.int32)

    inv, inv_d = order_of(net.orders), order_of(net.mixed)

    split = lambda n, parts: np.arange(n).reshape(parts, 2, n // (2 * parts))
    of_core = lambda n, parts: [split(n, parts)[:, c].reshape(-1) for c in range(2)]
    everywhere = lambda n: [np.arange(n)] * 2
    n_gain, n_bias = norm_gains.shape[0], bias_pack.shape[0]

    def owners(items):
        dev, place = [], []
        for c in range(2):
            flat = [(first + entry[c]) for first, entry, _, _ in items]
            dev.append(np.concatenate([f // n for f, (_, _, _, n) in zip(flat, items)]))
            place.append(
                np.concatenate([at + f % n for f, (_, _, at, n) in zip(flat, items)])
            )
        dev, place = np.array(dev, np.int32), np.array(place, np.int32)
        return (
            jnp.where(core == 0, dev[0], dev[1]),
            jnp.where(core == 0, place[0], place[1]),
        )

    chip_row = jnp.repeat(inv, 2)
    s_n = net.z * net.y
    row_device = ((chip_row // s_n) * 2 + jnp.tile(jnp.arange(2), chips)) * s_n + chip_row % s_n
    row_device = jnp.broadcast_to(row_device[:, None], (devices, SLAB))
    D_, W = everywhere(width), width

    def mapping(items):
        dev, place = owners(items)
        return dev[None, :], place[None, :]

    gl, bl = n_gain, n_bias
    heads_c, ff_c = of_core(width, net.x), of_core(hidden, net.x)
    owner_in, place_in = mapping(
        [
            (0, D_, 0, gl),
            (W, D_, 0, gl),
            (0, D_, gl, bl),
            (W, D_, gl, bl),
            (4 * W, D_, gl, bl),
            (5 * W, D_, gl, bl),
            (2 * W, heads_c, gl, bl),
            (3 * W, heads_c, gl, bl),
            (6 * W, ff_c, gl, bl),
        ]
    )
    ll = 2 * W // devices
    rl = n_gain + n_bias - 2 * ll
    owner_out, place_out = mapping(
        [
            (0, D_, 0, ll),
            (W, D_, 0, ll),
            (0, D_, ll, rl),
            (W, heads_c, ll, rl),
            (2 * W, D_, ll, rl),
            (3 * W, D_, ll, rl),
            (4 * W, ff_c, ll, rl),
            (0, D_, ll + rl, ll),
            (W, heads_c, ll + rl, ll),
        ]
    )
    order = np.arange(width).reshape(net.x, 2, s_n, rows).transpose(0, 2, 1, 3).reshape(-1)
    pi = jnp.asarray((np.arange(width)[:, None] == order[None, :]), BF)
    rel_row = jnp.arange(chips * 32, dtype=jnp.int32)
    nat_row = jnp.where(rel_row % 32 < rows, jnp.repeat(inv, 32) * rows + rel_row % 32, -1)
    perm = (jnp.arange(half_w, dtype=jnp.int32)[:, None] == nat_row[None, :]).astype(BF)


    seg_row = jnp.pad(after(segments, q0).astype(BF), ((0, 0), (0, width - cols)))[:, None, :]
    packed = jnp.concatenate([tokens, jnp.pad(seg_row, ((0, 0), (0, 7), (0, 0)))], axis=1)

    def to_sequence(array):
        swapped = jnp.where(zodd == 0, array, array[::-1])
        return jnp.stack(
            [lax.ppermute(swapped[k], AXES, net.scatter_move(k)) for k in range(2)]
        )

    def from_sequence(array, then=()):
        back = [
            lax.ppermute(array[k], AXES, [(b, a) for a, b in net.scatter_move(k)])
            for k in range(2)
        ]
        back = jnp.stack(all_after(back, *then))
        return jnp.where(zodd == 0, back, back[::-1])

    up = after(w_fc1, q0).reshape(rows, hidden)
    got_up = net.core(pick(up, net.x, 1 - core))
    chip_up = fold(both(pick(up, net.x, core), got_up, 0), 2)
    chip_up = jnp.concatenate([chip_up, jnp.pad(w_out.reshape(rows, width), ((0, 8), (0, 0)))])

    u1 = grow(chip_up[None], 0)
    q2 = grow(after(q1, chip_up), 1)
    d1 = grow(after(w_fc2.reshape(1, frows, width), q1), 0, net.mixed)
    q4 = grow(after(q2, u1, d1), 2)
    x_o = to_sequence(after(packed, u1))
    x_n = net.pair(x_o)
    x_m = net.core(x_n)
    x_t = net.core(after(x_o, q4))
    u2 = grow(u1, 1, then=(q4,))
    q_held, q_got = q4, net.across(q4, last)
    d2 = grow(after(d1, u2), 1, net.mixed)
    u4 = grow(after(u2, q4), 2)
    g_out = jnp.where(zodd == 0, cotangent, cotangent[::-1])
    g_out = all_after([g_out[0], g_out[1]], q4)

    dma = lambda *n: pltpu.SemaphoreType.DMA(n)
    vm = lambda shape, dtype: pltpu.VMEM(shape, dtype)
    by_pair = lambda n: (PAIRS, n, DOUBLE)
    unit1, col, row, hot = run(
        unit_kernel,
        None,
        (x_o, x_t, x_n, x_m, place_in),
        (
            ((keys, width), F32),
            ((keys, SLAB), F32),
            ((8, mine), F32),
            ((half_w, place_in.shape[1]), BF),
        ),
        [],
        us=4,
    )
    q_got, unit1, u4, d2 = all_after([q_got, unit1, u4, d2])
    u_held = u4
    u_got = net.across(u4, last)
    a1, q, k, v, w_mix, vec = run(
        mix_kernel,
        inv,
        (unit1, pi, row_device, owner_in, hot, q_held, q_got),
        (
            ((keys, width), BF),
            (by_pair(mine), BF),
            (by_pair(keys), BF),
            (by_pair(keys), BF),
            ((3, width, half_w), BF),
            ((1, place_in.shape[1]), F32),
        ),
        [vm((keys, width), BF), vm((chips * 16, half_w), BF), dma(chips, 3), dma(chips)],
        anys=(5, 6),
        us=8,
    )
    d_got = net.across(d2, 2, net.mixed)
    g_out = all_after(g_out, k)
    g_in = [lax.ppermute(g_out[k], AXES, net.scatter_move(k)) for k in range(2)]
    o, low, lse = run(
        attend_kernel,
        None,
        (q, k, v, col, row),
        ((by_pair(mine), F32), (by_pair(mine), BF), ((PAIRS, 8, mine), F32)),
        [vm((keys, mine), F32), vm((keys, mine), F32), vm((keys, mine), BF)],
        us=12,
    )
    d4 = jnp.concatenate([d2, d_got])
    g_o = jnp.stack(g_in)
    blocks = ((half, 96, width), BF)
    part, wo = run(
        project_kernel,
        inv,
        (all_after([low], d_got, *g_in)[0], perm, u_held, u_got),
        (((mine, width), BF), ((half_w, width), BF)),
        [vm((chips * 32, width), BF), dma(chips)],
        anys=(2, 3),
        us=3,
    )
    part_got = net.core(part)
    g_t = net.core(g_o)
    d_half = d_got
    d_held = jnp.concatenate([d2, d_half])
    d_got = net.across(d_held, last, net.mixed)
    mid, a2, act, fac, w_up, keep_d, send_d, g_sum, w_half = run(
        middle_kernel,
        (inv, inv_d),
        (part, part_got, x_o, x_t, g_o, g_t, vec, pi, u_held, u_got, d_held),
        (
            ((mine, width), F32),
            ((mine, width), BF),
            ((mine, half_f), BF),
            ((mine, half_f), F32),
            ((width, half_f), BF),
            blocks,
            blocks,
            ((1, width), F32),
            ((half_f, width), BF),
        ),
        [vm((mine, width), BF), vm((half_f, width), BF), dma(chips, 2), dma(half)],
        anys=(8, 9, 10),
        us=10,
    )

    def fold_in(keep, got):
        n = keep.shape[0] // 2
        total = [keep[at].astype(F32) + got[at].astype(F32) for at in (slice(n), slice(n, None))]
        return [part.astype(BF) for part in total]

    def shrink(keep, send, stage, orders=None, then=()):
        got = net.across(send, stage, orders)
        if then:
            got = after(got, *then)
        if stage == 0:
            return (keep.astype(F32) + got.astype(F32))[0]
        return fold_in(keep, got)

    pre, e2, w_down, pre_sum = run(
        slope_kernel,
        inv_d,
        (g_o, g_t, fac, w_up, pi, w_half, d_got),
        (
            ((mine, half_f), BF),
            ((mine, width), BF),
            ((half_f, width), BF),
            ((1, half_f), F32),
        ),
        [dma(half)],
        anys=(6,),
        us=8,
        alias={6: 2},
    )
    keep_d, send_d = shrink(keep_d, send_d, 3)
    e2_got = after(net.core(e2), send_d)
    down_own, down_give = run(
        down_kernel,
        None,
        (act, w_down),
        (((own, width), F32), ((own, width), BF)),
        [],
        us=2,
    )
    wide_sum, half_sum = ((1, width), F32), ((1, half_w), F32)
    blocks_u = ((half, 128, width), BF)
    gm, branch, d_heads, keep_u, send_u, e2n, e2s, bs = run(
        branch_kernel,
        inv,
        (e2, e2_got, mid, g_o, g_t, vec, wo, low, perm, a2, pre),
        (
            ((own, width), F32),
            ((mine, width), BF),
            (by_pair(mine), BF),
            blocks_u,
            blocks_u,
            wide_sum,
            wide_sum,
            wide_sum,
        ),
        [vm((width, half_f), BF), vm((chips * 32, width), BF)],
        us=0.1,
    )
    down_got = net.core(after(down_give, e2_got)).astype(F32)
    out_own = (mid[:own] + down_own + down_got + vec[:, AT["bias_down"]]).astype(BF)
    out_own = out_own.reshape(local, cols, width)
    out_parts = [out_own[k] for k in range(2)]
    keep_d, send_d = shrink(keep_d, send_d, 2, then=(send_u,))
    send_d, d_heads, *out_parts = all_after([send_d, d_heads, *out_parts])
    quarter = ((2, own, width), BF)
    blocks_q = ((half, 160, half_w), BF)
    home = lambda k: [(b, a) for a, b in net.scatter_move(k)]
    dq, dk, dv, dqs, dvs = run(
        attend_back_kernel,
        None,
        (q, k, v, o, lse, col, row, d_heads),
        (
            (by_pair(mine), BF),
            (by_pair(keys), BF),
            (by_pair(keys), BF),
            half_sum,
            half_sum,
        ),
        [vm((keys, mine), F32), vm((keys, mine), BF), vm((keys, mine), BF)],
        us=10,
    )
    out_parts = [lax.ppermute(out_parts[k], AXES, home(k)) for k in range(2)]
    out_parts = all_after(out_parts, dq)
    d_1 = shrink(keep_d, send_d, 1, then=(dq,))
    keep_e, give_e, e1n, e1s = run(
        input_kernel,
        None,
        (all_after([dq], d_1[1], *out_parts)[0], dk, dv, w_mix, unit1, pi),
        (quarter, quarter, wide_sum, wide_sum),
        [],
        us=0.1,
    )
    got_e = net.core(give_e)
    (e1_give,) = run(near_kernel, None, (keep_e, got_e), (((own, width), BF),), [], us=0.1)
    u3 = shrink(keep_u, send_u, 3, then=(keep_e,))
    got_d = net.across(d_1[1], 0)
    shard_d = (d_1[0].astype(F32) + got_d.astype(F32))[0]
    keep_q, send_q = run(
        gather_grads_kernel,
        inv,
        (all_after([a1], u3[1], e1_give)[0], dq, dk, dv, row_device, owner_out, place_out)
        + (e1n, e2n, e2s, dqs, bs, g_sum, pre_sum, e1s, dvs),
        (blocks_q, blocks_q),
        [
            vm((3, width, half_w), BF),
            vm((chips * 16, half_w), BF),
            vm((half_w, place_out.shape[1]), BF),
        ],
        us=0.1,
    )
    q_3 = shrink(*all_after([keep_q, send_q], got_d), 3)
    back = jnp.stack(out_parts)
    block_out = jnp.where(zodd == 0, back, back[::-1])
    block = ((cols, width), BF)
    u_2 = shrink(*u3, 2, then=(send_q,))
    e1_near = net.pair(all_after([e1_give], q_3[1])[0])
    u_1 = shrink(*u_2, 1, then=(q_3[1],))
    q_2 = shrink(*q_3, 2)
    in_parts = run(
        finish_kernel,
        None,
        (keep_e, got_e, all_after([e1_near], q_2[1])[0], x_o, gm, vec),
        (block, block),
        [],
        us=0.1,
    )
    in_parts = [lax.ppermute(in_parts[k], AXES, home(k)) for k in range(2)]
    got_last = net.across(u_1[1], 0)
    q_1 = shrink(*all_after(q_2, u_1[1]), 1)
    shard_u = (u_1[0].astype(F32) + all_after([got_last], q_1[1])[0].astype(F32))[0]
    in_parts = all_after(in_parts, q_1[1])
    shard_q = shrink(*q_1, 0)
    back = jnp.stack(in_parts)
    input_grad = jnp.where(zodd == 0, back, back[::-1]).astype(F32)

    def own_rows(chip):
        keep = jnp.where(core == 0, chip[..., 0, :, :], chip[..., 1, :, :])
        give = jnp.where(core == 0, chip[..., 1, :, :], chip[..., 0, :, :])
        return keep, net.core(give)

    def merge(keep, got, parts):
        view = lambda array: array.reshape(*array.shape[:-1], parts, 1, -1)
        first = jnp.where(core == 0, view(keep), view(got))
        second = jnp.where(core == 0, view(got), view(keep))
        return jnp.concatenate([first, second], axis=-2).reshape(*keep.shape[:-1], -1)

    qkv_own = merge(*own_rows(shard_q[: 6 * rows].reshape(3, 2, rows, half_w)), net.x)
    g_qkv = jnp.moveaxis(qkv_own, 0, 1).reshape(-1)
    g_out = shard_u[4 * rows : 5 * rows].reshape(-1)
    up_own = merge(*own_rows(unfold(shard_u[: 4 * rows], 2).reshape(2, rows, half_f)), net.x)
    two = shard_q[6 * rows : 6 * rows + 2, : 2 * ll + rl]
    keep_s, got_s = own_rows(two.reshape(2, 1, -1))
    own_sums = (keep_s + got_s)[0]
    return (
        block_out,
        input_grad,
        g_qkv,
        g_out,
        up_own.reshape(-1),
        shard_d.reshape(-1),
        own_sums[:ll],
        own_sums[ll : ll + rl],
        own_sums[ll + rl :],
    )


def solution(mesh):
    dp, seq = mesh.shape["dp"], mesh.shape["seq"]
    y = 1 << (((seq.bit_length() - 1) - 1) // 2)
    z = seq // y
    dims = (dp // 2, 2, 4, z // 4, y // 2, 2)
    net = Net(dims)
    inner = Mesh(mesh.devices.reshape(dims), AXES)
    place = ("zh", "zl", "yh", "yl")
    cube = P(("x", "c"), place, None)
    flat = P(AXES)
    rows = D // (2 * net.chips)
    tiles = rows == 24 and net.chips == 16 and net.zl * net.yh == 1
    return jax.shard_map(
        functools.partial(body if tiles else body_any, net),
        mesh=inner,
        in_specs=(cube, P(("x", "c"), place), cube) + (flat,) * 6,
        out_specs=(cube, cube) + (flat,) * 7,
        check_vma=False,
    )
```

```python
import functools
import itertools

import jax
import jax.numpy as jnp
import numpy as np
from jax import lax
from jax.experimental import pallas as pl
from jax.experimental.pallas import tpu as pltpu
from jax.sharding import Mesh
from jax.sharding import PartitionSpec as P

D = 768
FF = 3072
HEADS = 12
HEAD_DIM = 64
EPS = 1e-05
MASKED = -1000000000.0
BF = jnp.bfloat16
F32 = jnp.float32
AXES = ("x", "c", "zh", "zl", "yh", "yl")


class Net:
    def __init__(self, dims):
        self.dims = dims
        self.x, self.c, self.zh, self.zl, self.yh, self.yl = dims
        self.z, self.y = self.zh * self.zl, self.yh * self.yl
        self.chips = self.x * self.z * self.y
        bits = lambda axis, n: [(axis, 1 << b) for b in reversed(range(n.bit_length() - 1))]
        zs, xs, ys = bits("z", self.z), bits("x", self.x), bits("y", self.y)
        self.orders = (zs + xs + ys, zs + ys + xs)
        self.mixed = (xs + zs + ys, ys + zs + xs)
        self.stages = len(self.orders[0])

    def perm(self, move):
        pairs = []
        for at in itertools.product(*(range(n) for n in self.dims)):
            to = move(*at)
            pairs.append(
                (int(np.ravel_multi_index(at, self.dims)), int(np.ravel_multi_index(to, self.dims)))
            )
        return pairs

    def flip(self, stage, orders):
        def move(x, c, zh, zl, yh, yl):
            axis, bit = orders[c][stage]
            z, y = zh * self.zl + zl, yh * self.yl + yl
            if axis == "x":
                x ^= bit
            elif axis == "y":
                y ^= bit
            else:
                z ^= bit
            return (x, c, z // self.zl, z % self.zl, y // self.yl, y % self.yl)

        return self.perm(move)

    def across(self, value, stage, orders=None):
        return lax.ppermute(value, AXES, self.flip(stage, orders or self.orders))

    def core(self, value):
        return lax.ppermute(value, "c", [(0, 1), (1, 0)])

    def pair(self, value):
        return lax.ppermute(value, "yl", [(0, 1), (1, 0)])

    def scatter_move(self, k):
        return self.perm(
            lambda x, c, zh, zl, yh, yl: (x, zh >> 1, 2 * c + (k ^ (zh & 1)), zl, yh, yl)
        )

    def table(self, orders=None):
        me = {
            "x": lax.axis_index("x"),
            "z": lax.axis_index("zh") * self.zl + lax.axis_index("zl"),
            "y": lax.axis_index("yh") * self.yl + lax.axis_index("yl"),
        }
        grid = np.indices((self.x, self.z, self.y)).reshape(3, -1)
        axes = {"x": grid[0], "z": grid[1], "y": grid[2]}
        places = []
        for order in orders or self.orders:
            place = jnp.zeros((self.chips,), jnp.int32)
            for stage, (axis, bit) in enumerate(order):
                differs = (jnp.asarray(axes[axis], jnp.int32) ^ me[axis]) & bit
                place = place + jnp.where(differs != 0, 1 << stage, 0)
            places.append(place)
        return jnp.where(lax.axis_index("c") == 0, places[0], places[1]).astype(jnp.int32)

    def gather(self, block):
        held = block[None]
        for stage in range(self.stages):
            held = jnp.concatenate([held, self.across(held, stage)])
        return held

    def scatter(self, held):
        for stage in reversed(range(self.stages)):
            half = held.shape[0] // 2
            got = self.across(held[half:], stage)
            held = held[:half].astype(F32) + got.astype(F32)
            if stage:
                held = held.astype(BF)
        return held[0]


def move_kernel(table, source, target):
    target[...] = source[...]


def reorder(blocks, table, to_place):
    rest = -blocks.shape[1] % 16
    if rest:
        rows = blocks.shape[1]
        blocks = jnp.pad(blocks, ((0, 0), (0, rest), (0, 0)))
        return reorder(blocks, table, to_place)[:, :rows]
    chips, rows, cols = blocks.shape
    here = pl.BlockSpec((1, rows, cols), lambda chip, table: (chip, 0, 0))
    there = pl.BlockSpec((1, rows, cols), lambda chip, table: (table[chip], 0, 0))
    return pl.pallas_call(
        move_kernel,
        grid_spec=pltpu.PrefetchScalarGridSpec(
            num_scalar_prefetch=1,
            grid=(chips,),
            in_specs=[here if to_place else there],
            out_specs=there if to_place else here,
        ),
        out_shape=jax.ShapeDtypeStruct(blocks.shape, blocks.dtype),
    )(table, blocks)


def normal(field):
    center = field - jnp.mean(field, axis=-1, keepdims=True)
    inverse = lax.rsqrt(jnp.mean(center * center, axis=-1, keepdims=True) + EPS)
    return center * inverse, inverse


def norm_back(upstream, unit, inverse, gain):
    scaled = upstream * gain
    return inverse * (
        scaled
        - jnp.mean(scaled, axis=-1, keepdims=True)
        - unit * jnp.mean(scaled * unit, axis=-1, keepdims=True)
    )


def dot(a, b):
    return jnp.dot(a, b, preferred_element_type=F32)


def dot_t(a, b):
    return lax.dot_general(a, b, (((1,), (1,)), ((), ())), preferred_element_type=F32)


def t_dot(a, b):
    return lax.dot_general(a, b, (((0,), (0,)), ((), ())), preferred_element_type=F32)


def fold(wide, parts):
    lead, rows, cols = wide.shape[:-2], wide.shape[-2], wide.shape[-1] // parts
    moved = jnp.moveaxis(wide.reshape(*lead, rows, parts, cols), -2, -3)
    return moved.reshape(*lead, parts * rows, cols)


def unfold(tall, parts):
    lead, rows, cols = tall.shape[:-2], tall.shape[-2] // parts, tall.shape[-1]
    moved = jnp.moveaxis(tall.reshape(*lead, parts, rows, cols), -3, -2)
    return moved.reshape(*lead, rows, parts * cols)


def body_any(net, tokens, segments, cotangent, w_qkv, w_out, w_fc1, w_fc2, norm_gains, bias_pack):
    local, cols, width = tokens.shape
    own = local * cols
    mine = 2 * own
    hidden = FF
    half_w, half_f = width // 2, hidden // 2
    devices = 2 * net.chips
    core = lax.axis_index("c")
    zodd = lax.axis_index("zh") & 1
    table = net.table()
    rows = width // devices
    frows = hidden // devices
    aligned = (width // (2 * net.x)) % HEAD_DIM == 0
    groups = net.x if aligned else 1

    def pick(array, parts, which):
        split = array.reshape(*array.shape[:-1], parts, 2, array.shape[-1] // (2 * parts))
        taken = jnp.where(which == 0, split[..., 0, :], split[..., 1, :])
        return taken.reshape(*array.shape[:-1], array.shape[-1] // 2)

    def spread(vector, parts):
        split = vector.reshape(parts, 1, vector.shape[-1] // parts)
        both = jnp.concatenate(
            [jnp.where(core == 0, split, 0.0), jnp.where(core == 1, split, 0.0)], axis=1
        )
        return both.reshape(-1)

    seg_row = jnp.pad(segments.astype(BF), ((0, 0), (0, width - cols)))[:, None, :]
    seg_rows = jnp.pad(seg_row, ((0, 0), (0, 7), (0, 0)))
    packed = jnp.concatenate([tokens, seg_rows], axis=1)

    def to_sequence(array):
        swapped = jnp.where(zodd == 0, array, array[::-1])
        return jnp.stack(
            [lax.ppermute(swapped[k], AXES, net.scatter_move(k)) for k in range(2)]
        )

    def from_sequence(array):
        back = jnp.stack(
            [
                lax.ppermute(array[k], AXES, [(b, a) for a, b in net.scatter_move(k)])
                for k in range(2)
            ]
        )
        return jnp.where(zodd == 0, back, back[::-1])

    def halves(which):
        qkv = fold(w_qkv.reshape(rows, 3 * width), 3).reshape(3, rows, width)
        up = w_fc1.reshape(rows, hidden)
        return pick(qkv, groups, which), pick(up, net.x, which)

    keep_qkv, keep_up = halves(core)
    give_qkv, give_up = halves(1 - core)
    small = jnp.concatenate([norm_gains, bias_pack])
    out_rows = w_out.reshape(rows, width)
    got_qkv, got_up, got_small, got_out = jax.tree.map(
        net.core, (give_qkv, give_up, small, out_rows)
    )

    def both(a, b, axis):
        return jnp.where(
            core == 0, jnp.concatenate([a, b], axis=axis), jnp.concatenate([b, a], axis=axis)
        )

    chip_qkv = both(keep_qkv, got_qkv, 1).reshape(6 * rows, half_w)
    chip_up = fold(both(keep_up, got_up, 0), 2)
    chip_out = fold(out_rows if aligned else both(out_rows, got_out, 0), 2)
    chip_small = jnp.pad(
        both(small[None], got_small[None], 0), ((0, 14), (0, half_w - small.shape[0]))
    )
    cut = np.cumsum([chip_qkv.shape[0], chip_out.shape[0]])
    blocks_a = reorder(
        net.gather(jnp.concatenate([chip_qkv, chip_out, chip_small])), table, False
    )
    blocks_up = reorder(net.gather(chip_up), table, False)
    blocks_down = reorder(net.gather(w_fc2.reshape(frows, width)), table, False)

    lead = (net.x, net.z, net.y)

    def natural(blocks):
        n = blocks.shape[-1]
        return jnp.moveaxis(blocks.reshape(*lead, 2, -1, n), 3, 1).reshape(-1, n)

    def by_chip(array):
        n = array.shape[-1]
        return jnp.moveaxis(array.reshape(net.x, 2, net.z, net.y, -1, n), 1, 3).reshape(
            net.chips, -1, n
        )

    qkv_blocks = blocks_a[:, : cut[0]].reshape(net.chips, 3, 2 * rows, half_w)
    w_q, w_k, w_v = (natural(qkv_blocks[:, i]) for i in range(3))
    out_blocks = unfold(blocks_a[:, cut[0] : cut[1]], 2)
    if aligned:
        w_proj = out_blocks.reshape(half_w, width)
    else:
        w_proj = lax.dynamic_slice_in_dim(natural(out_blocks), core * half_w, half_w)
    smalls = blocks_a[:, cut[1] : cut[1] + 2, : small.shape[0]].reshape(*lead, 2, -1)
    smalls = jnp.moveaxis(smalls, 3, 1).reshape(devices, -1).astype(F32)
    n_gain = norm_gains.shape[0]
    gains = smalls[:, :n_gain].reshape(-1)
    shifts = smalls[:, n_gain:].reshape(-1)
    w_up = natural(unfold(blocks_up, 2))
    w_down = blocks_down.reshape(half_f, width)
    gain1, gain2 = gains[:width], gains[width:]
    shift1, shift2, bias_q, bias_v, bias_proj, bias_down = (
        shifts[i * width : (i + 1) * width] for i in range(6)
    )
    bias_up = pick(shifts[6 * width :], net.x, core)
    bias_q, bias_v = pick(bias_q, groups, core), pick(bias_v, groups, core)

    x_own = to_sequence(packed)
    x_other = net.core(x_own)
    x_mine = jnp.concatenate([x_own, x_other])
    near = net.pair(x_own)
    near = jnp.concatenate([near, net.core(near)])
    x_seq = jnp.concatenate([x_mine, near])
    if net.zl * net.yh > 1:
        x_far = lax.all_gather(x_seq, ("zl", "yh"), axis=0, tiled=True)
        x_keys = x_far
    else:
        x_keys = x_seq
    g_own = to_sequence(cotangent)
    g_mine = jnp.concatenate([g_own, net.core(g_own)]).reshape(mine, width)
    docs = x_keys[:, cols, :cols].reshape(-1)
    query_docs = x_mine[:, cols, :cols].reshape(-1)
    x_all = x_keys[:, :cols].reshape(-1, width).astype(F32)
    x_q = x_mine[:, :cols].reshape(-1, width).astype(F32)

    unit_q, inverse_q = normal(x_q)
    a_q = (unit_q * gain1 + shift1).astype(BF)
    unit_all, _ = normal(x_all)
    a_all = (unit_all * gain1 + shift1).astype(BF)
    heads = HEADS // 2
    q = (dot(a_q, w_q) + bias_q).astype(BF)
    k = dot(a_all, w_k).astype(BF)
    v = (dot(a_all, w_v) + bias_v).astype(BF)
    by_head = lambda t: t.reshape(-1, heads, HEAD_DIM)
    same = (query_docs[:, None] == docs[None, :])[None]
    scores = (
        jnp.einsum("qhd,khd->hqk", by_head(q), by_head(k), preferred_element_type=F32) * 0.125
    )
    scores = jnp.where(same, scores, MASKED)
    weights = jnp.exp(scores - jnp.max(scores, axis=-1, keepdims=True))
    probs = weights / jnp.sum(weights, axis=-1, keepdims=True)
    probs_low = probs.astype(BF)
    att = jnp.einsum("hqk,khd->qhd", probs_low, by_head(v), preferred_element_type=F32)
    att = att.reshape(mine, half_w)
    att_low = att.astype(BF)

    def core_sum(partial):
        low = partial.astype(BF)
        got = net.core(low)
        return low.astype(F32) + jnp.concatenate([got[own:], got[:own]]).astype(F32)

    middle = x_q + core_sum(dot(att_low, w_proj)) + bias_proj
    unit2, inverse2 = normal(middle)
    a2 = (unit2 * gain2 + shift2).astype(BF)
    pre = dot(a2, w_up) + bias_up
    sig = jax.nn.sigmoid(1.702 * pre)
    activ = (pre * sig).astype(BF)
    down = dot(activ, w_down)
    down_got = net.core(down[own:].astype(BF)).astype(F32)
    out_own = (middle[:own] + down[:own] + down_got + bias_down).astype(BF)
    block_out = from_sequence(out_own.reshape(local, cols, width))

    grad_down = t_dot(activ, g_mine).astype(BF)
    grad_pre = (dot_t(g_mine, w_down) * (sig + 1.702 * pre * sig * (1.0 - sig))).astype(BF)
    shard_down = net.scatter(reorder(grad_down.reshape(net.chips, frows, width), table, True))
    grad_up = t_dot(a2, grad_pre).astype(BF)
    shard_up = net.scatter(reorder(fold(by_chip(grad_up), 2), table, True))
    e2 = core_sum(dot_t(grad_pre, w_up))
    grad_middle = g_mine.astype(F32) + norm_back(e2, unit2, inverse2, gain2)
    branch = grad_middle.astype(BF)
    grad_proj = t_dot(att_low, branch).astype(BF)
    d_heads = dot_t(branch, w_proj).astype(BF)
    dp = jnp.einsum("qhd,khd->hqk", by_head(d_heads), by_head(v), preferred_element_type=F32)
    delta = jnp.sum(probs * dp, axis=-1, keepdims=True)
    d_scores = (probs * (dp - delta)).astype(BF)
    dq = 0.125 * jnp.einsum("hqk,khd->qhd", d_scores, by_head(k), preferred_element_type=F32)
    dk = 0.125 * jnp.einsum("hqk,qhd->khd", d_scores, by_head(q), preferred_element_type=F32)
    dv = jnp.einsum("hqk,qhd->khd", probs_low, by_head(d_heads), preferred_element_type=F32)
    dq = dq.reshape(-1, half_w).astype(BF)
    dk = dk.reshape(-1, half_w).astype(BF)
    dv = dv.reshape(-1, half_w).astype(BF)
    grad_qkv = jnp.stack([t_dot(a_q, dq), t_dot(a_all, dk), t_dot(a_all, dv)]).astype(BF)

    e1_keys = (dot_t(dk, w_k) + dot_t(dv, w_v)).astype(BF)
    if net.zl * net.yh > 1:
        e1_keys = lax.psum_scatter(
            e1_keys, ("zl", "yh"), scatter_dimension=0, tiled=True
        )
    e1_near = e1_keys[mine:].reshape(2, own, width)
    e1_mine = e1_keys[:mine].astype(F32) + dot_t(dq, w_q)
    e1_mine = e1_mine.astype(BF).reshape(2, own, width)
    got = net.core(jnp.stack([e1_mine[1], e1_near[1]]))
    e1_near = e1_near[0].astype(F32) + got[1].astype(F32)
    e1 = e1_mine[0].astype(F32) + got[0].astype(F32) + net.pair(e1_near.astype(BF)).astype(F32)
    unit1 = unit_q[:own]
    in_own = grad_middle[:own] + norm_back(e1, unit1, inverse_q[:own], gain1)
    input_grad = from_sequence(in_own.astype(BF).reshape(local, cols, width)).astype(F32)

    total = lambda array: jnp.sum(array.astype(F32), axis=0)
    g_own = g_mine[:own]
    gain_sums = jnp.concatenate([total(e1 * unit1), total(e2[:own] * unit2[:own])])
    bias_sums = jnp.concatenate(
        [
            total(e2[:own]),
            spread(total(dq), groups),
            total(branch[:own]),
            total(g_own),
            spread(total(grad_pre), net.x),
        ]
    )
    lead_sums = jnp.concatenate([total(e1), spread(total(dv), groups)])
    sums = jnp.concatenate(
        [v.reshape(devices, -1) for v in (gain_sums, bias_sums, lead_sums)], axis=1
    )
    sums = sums + net.core(sums)
    sums = jnp.moveaxis(sums.reshape(net.x, 2, net.z, net.y, -1), 1, 0)
    sums = jnp.where(core == 0, sums[0], sums[1]).reshape(net.chips, 1, -1)
    n_sums = sums.shape[-1]
    sums = jnp.pad(sums, ((0, 0), (0, 15), (0, half_w - n_sums))).astype(BF)
    qkv_send = jnp.stack([by_chip(grad_qkv[i]) for i in range(3)], axis=1)
    qkv_send = qkv_send.reshape(net.chips, 6 * rows, half_w)
    if aligned:
        out_send = grad_proj.reshape(net.chips, rows, width)
    else:
        whole = jnp.zeros((width, width), BF)
        whole = lax.dynamic_update_slice(whole, grad_proj, (core * half_w, 0))
        out_send = by_chip(whole)
    sent = jnp.concatenate([qkv_send, fold(out_send, 2), sums], axis=1)
    shard_a = net.scatter(reorder(sent, table, True))

    def own_rows(chip):
        keep = jnp.where(core == 0, chip[..., 0, :, :], chip[..., 1, :, :])
        give = jnp.where(core == 0, chip[..., 1, :, :], chip[..., 0, :, :])
        return keep, net.core(give)

    def merge(keep, got, parts):
        split = lambda array: array.reshape(*array.shape[:-1], parts, 1, -1)
        first = jnp.where(core == 0, split(keep), split(got))
        second = jnp.where(core == 0, split(got), split(keep))
        return jnp.concatenate([first, second], axis=-2).reshape(*keep.shape[:-1], -1)

    qkv_own = merge(*own_rows(shard_a[: cut[0]].reshape(3, 2, rows, half_w)), groups)
    g_qkv = jnp.moveaxis(qkv_own, 0, 1).reshape(-1)
    out_own = unfold(shard_a[cut[0] : cut[1]], 2)
    if not aligned:
        keep, got = own_rows(out_own.reshape(2, rows, width))
        out_own = keep + got
    g_out = out_own.reshape(-1)
    up_own = merge(*own_rows(unfold(shard_up, 2).reshape(2, rows, half_f)), net.x)
    own_sums = shard_a[cut[1], :n_sums]
    n_gain = 2 * width // devices
    n_lead = n_sums - n_gain
    return (
        block_out,
        input_grad,
        g_qkv,
        g_out,
        up_own.reshape(-1),
        shard_down.reshape(-1),
        own_sums[:n_gain],
        own_sums[n_gain:n_lead],
        own_sums[n_lead:],
    )


SLAB = 128
PAIRS = HEADS // 4
DOUBLE = 2 * HEAD_DIM
PARTS = (
    ("gain1", D),
    ("gain2", D),
    ("shift1", D),
    ("shift2", D),
    ("bias_proj", D),
    ("bias_down", D),
    ("bias_q", D // 2),
    ("bias_v", D // 2),
    ("bias_up", FF // 2),
)
SUMS = (
    ("e1n", D),
    ("e2n", D),
    ("e2", D),
    ("dq", D // 2),
    ("branch", D),
    ("g", D),
    ("pre", FF // 2),
    ("e1", D),
    ("dv", D // 2),
)


def offsets(parts):
    ends = np.cumsum([n for _, n in parts])
    return {name: slice(int(end - n), int(end)) for (name, n), end in zip(parts, ends)}


AT = offsets(PARTS)


def dots(a, b, ca, cb):
    return lax.dot_general(a, b, (((ca,), (cb,)), ((), ())), preferred_element_type=F32)


def lane_half(e):
    lanes = lax.broadcasted_iota(jnp.int32, (1, DOUBLE), 1)
    inside = (lanes < HEAD_DIM) if e == 0 else (lanes >= HEAD_DIM)
    return inside.astype(F32).astype(BF)


def first_half(shape):
    return lax.broadcasted_iota(jnp.int32, shape, 1) < HEAD_DIM


def load_rows(inv, held, got, target, sems, pieces):
    half = held.shape[0]
    copies = []
    for r in range(2 * half):
        source = held if r < half else got
        for n, (first, rows, place) in enumerate(pieces):
            copies.append(
                pltpu.make_async_copy(
                    source.at[r % half, pl.ds(first, rows), :],
                    place(target, inv[r], rows),
                    sems.at[r, n],
                )
            )
    for copy in copies:
        copy.start()
    return copies


def one_hot(place, target):
    step = 128
    for i in range(target.shape[0] // step):
        shape = (step, target.shape[1])
        entry = lax.broadcasted_iota(jnp.int32, shape, 0) + i * step
        target[i * step : (i + 1) * step, :] = (entry == place[:1, :]).astype(F32).astype(BF)


def unit_kernel(xo, xt, xn, xm, place, unit_ref, col_ref, row_ref, hot_ref):
    one_hot(place, hot_ref)
    for i, (ref, j) in enumerate((ref, j) for ref in (xo, xt, xn, xm) for j in range(2)):
        unit, _ = normal(ref[j, :SLAB, :].astype(F32))
        at = pl.ds(i * SLAB, SLAB)
        unit_ref[at, :] = unit
        docs = ref[j, :, :SLAB].astype(F32)[SLAB : SLAB + 1]
        col_ref[at, :] = jnp.broadcast_to(docs, (SLAB, SLAB)).T
        if i < 4:
            row_ref[:, i * SLAB : (i + 1) * SLAB] = jnp.broadcast_to(docs, (8, SLAB))


def fill_bias(col, row, bias):
    for i in range(bias.shape[0] // SLAB):
        at = pl.ds(i * SLAB, SLAB)
        for j in range(bias.shape[1] // SLAB):
            lanes = pl.ds(j * SLAB, SLAB)
            bias[at, lanes] = jnp.where(col[at, :] == row[:1, lanes], 0.0, MASKED)


def pick_rows(rows, step):
    shape = (2 * rows // step, rows)
    i = lax.broadcasted_iota(jnp.int32, shape, 0)
    j = lax.broadcasted_iota(jnp.int32, shape, 1)
    return (j == (i >> 1) * step + (i & 1)).astype(F32).astype(BF)


def mix_kernel(
    inv, unit, pi, device, owner, hot, held, got,
    a_ref, q_ref, k_ref, v_ref, w, vec, nat, small, sems, small_sems,
):
    half = held.shape[0]
    few = []
    for r in range(2 * half):
        source = held if r < half else got
        few.append(
            pltpu.make_async_copy(
                source.at[r % half, pl.ds(144, 16), :], small.at[pl.ds(r * 16, 16), :], small_sems.at[r]
            )
        )
    for copy in few:
        copy.start()
    place = lambda i: lambda t, chip, n: t.at[i, pl.ds(pl.multiple_of(chip * n, 16), n), :]
    copies = load_rows(inv, held, got, w, sems, [(48 * i, 48, place(i)) for i in range(3)])
    for copy in few:
        copy.wait()
    picked = dot(pick_rows(small.shape[0], 16), small[...]).astype(BF)
    mine_only = jnp.where(device[:, :1] == owner[:1, :], dot(picked, hot[...]), 0.0)
    vec[...] = jnp.sum(mine_only, axis=0, keepdims=True)
    keys = a_ref.shape[0]
    for i in range(keys // SLAB):
        at = pl.ds(i * SLAB, SLAB)
        nat[at, :] = (unit[at, :] * vec[:, AT["gain1"]] + vec[:, AT["shift1"]]).astype(BF)
    a_ref[...] = dot(nat[...], pi[...]).astype(BF)
    for copy in copies:
        copy.wait()
    mine = q_ref.shape[1]
    q = (dot(a_ref[:mine, :], w[0]) + vec[:, AT["bias_q"]]).astype(BF) * 0.125
    k = dot(a_ref[...], w[1]).astype(BF)
    v = (dot(a_ref[...], w[2]) + vec[:, AT["bias_v"]]).astype(BF)
    for i in range(PAIRS):
        lanes = slice(i * DOUBLE, (i + 1) * DOUBLE)
        q_ref[i], k_ref[i], v_ref[i] = q[:, lanes], k[:, lanes], v[:, lanes]


def attend_kernel(q_ref, k_ref, v_ref, col, row, o_ref, low_ref, lse_ref, bias, s, p_low):
    mine, keys = q_ref.shape[1], k_ref.shape[1]
    fill_bias(col, row, bias)

    def pair(i, carry):
        outs = []
        for e in range(2):
            qm = q_ref[i] * lane_half(e)
            top = jnp.full((1, mine), -3e38, F32)
            for c in range(keys // SLAB):
                at = pl.ds(c * SLAB, SLAB)
                t = dots(k_ref[i, at, :], qm, 1, 1) + bias[at, :]
                s[at, :] = t
                top = jnp.maximum(top, jnp.max(t, axis=0, keepdims=True))
            total = jnp.zeros((1, mine), F32)
            for c in range(keys // SLAB):
                at = pl.ds(c * SLAB, SLAB)
                p = jnp.exp(s[at, :] - top)
                total = total + jnp.sum(p, axis=0, keepdims=True)
                p_low[at, :] = p.astype(BF)
            lse_ref[i, e : e + 1, :] = top + jnp.log(total)
            o = dots(p_low[...], v_ref[i], 0, 0)
            scale = jnp.broadcast_to(1.0 / total, (DOUBLE, mine)).T
            outs.append(o * scale)
        o = jnp.where(first_half(outs[0].shape), outs[0], outs[1])
        o_ref[i] = o
        low_ref[i] = o.astype(BF)
        return carry

    lax.fori_loop(0, PAIRS, pair, 0)


def project_kernel(inv, low, perm, held, got, part_ref, wo_ref, rel, sems):
    half = held.shape[0]
    copies = []
    for r in range(2 * half):
        source = held if r < half else got
        copies.append(
            pltpu.make_async_copy(
                source.at[r % half, pl.ds(96, 32), :], rel.at[pl.ds(r * 32, 32), :], sems.at[r]
            )
        )
    for copy in copies:
        copy.start()
    for copy in copies:
        copy.wait()
    wo_ref[...] = dot(perm[...], rel[...]).astype(BF)
    att = jnp.concatenate([low[i] for i in range(PAIRS)], axis=1)
    part_ref[...] = dot(att, wo_ref[...]).astype(BF)


def load_half(inv, source, first, target, sems):
    rows = source.shape[1]
    copies = [
        pltpu.make_async_copy(
            source.at[r],
            target.at[pl.ds(pl.multiple_of(inv[first + r] * rows, 16), rows), :],
            sems.at[r],
        )
        for r in range(source.shape[0])
    ]
    for copy in copies:
        copy.start()
    return copies


def middle_kernel(
    inv, inv_d, part, part_got, xo, xt, go, gt, vec, pi, held, got, d_held,
    mid_ref, a_ref, act_ref, fac_ref, w, keep_ref, send_ref, sum_ref, w_down,
    nat, grad, sems, d_sems,
):
    place = lambda h: lambda t, chip, n: t.at[
        pl.ds(pl.multiple_of(chip * n, 16), n), pl.ds(h * D, D)
    ]
    copies = load_rows(inv, held, got, w, sems, [(48 * h, 48, place(h)) for h in range(2)])
    later = load_half(inv_d, d_held, 0, w_down, d_sems)
    mine = part.shape[0]
    own = mine // 2
    for i, (ref, j) in enumerate((ref, j) for ref in (xo, xt) for j in range(2)):
        at = pl.ds(i * SLAB, SLAB)
        other = pl.ds((i * SLAB + own) % mine, SLAB)
        mid = (
            ref[j, :SLAB, :].astype(F32)
            + (part[at, :].astype(F32) + part_got[other, :].astype(F32))
            + vec[:, AT["bias_proj"]]
        )
        mid_ref[at, :] = mid
        unit, _ = normal(mid)
        nat[at, :] = (unit * vec[:, AT["gain2"]] + vec[:, AT["shift2"]]).astype(BF)
    a_ref[...] = dot(nat[...], pi[...]).astype(BF)
    g = jnp.concatenate([go[0], go[1], gt[0], gt[1]], axis=0)
    sum_ref[...] = jnp.sum(g[:own].astype(F32), axis=0, keepdims=True)
    for copy in copies:
        copy.wait()
    step = 512
    for j in range(w.shape[1] // step):
        lanes = pl.ds(j * step, step)
        start = AT["bias_up"].start + j * step
        pre = dot(a_ref[...], w[:, lanes]) + vec[:, start : start + step]
        sig = 1.0 / (1.0 + jnp.exp(-1.702 * pre))
        act_ref[:, lanes] = (pre * sig).astype(BF)
        fac_ref[:, lanes] = sig + 1.702 * pre * sig * (1.0 - sig)
        grad[lanes, :] = dots(act_ref[:, lanes], g, 0, 0).astype(BF)
    half = keep_ref.shape[0]
    for r in range(2 * half):
        target = keep_ref if r < half else send_ref
        target[r % half] = grad[pl.ds(pl.multiple_of(inv[r] * 96, 16), 96), :]
    for copy in later:
        copy.wait()


def slope_kernel(inv, go, gt, fac, w_up, pi, w_half, got, pre_ref, e_ref, w, sum_ref, sems):
    copies = load_half(inv, got, got.shape[0], w, sems)
    g = jnp.concatenate([go[0], go[1], gt[0], gt[1]], axis=0)
    for copy in copies:
        copy.wait()
    step = 512
    total = None
    for j in range(w.shape[0] // step):
        lanes = pl.ds(j * step, step)
        pre = (dots(g, w[lanes, :], 1, 1) * fac[:, lanes]).astype(BF)
        pre_ref[:, lanes] = pre
        sum_ref[:, lanes] = jnp.sum(pre.astype(F32), axis=0, keepdims=True)
        term = dots(pre, w_up[:, lanes], 1, 1)
        total = term if total is None else total + term
    e_ref[...] = dots(total.astype(BF), pi[...], 1, 1).astype(BF)


def down_kernel(act, w_down, own_ref, give_ref):
    down = dot(act[...], w_down[...])
    own = own_ref.shape[0]
    own_ref[...] = down[:own]
    give_ref[...] = down[own:].astype(BF)


def wide(ref):
    return jnp.concatenate([ref[i] for i in range(PAIRS)], axis=1)


def branch_kernel(
    inv, e2, e2_got, mid, go, gt, vec, wo, low, perm, a, pre,
    gm_ref, branch_ref, d_ref, keep_ref, send_ref, e2n_sum, e2_sum, branch_sum, grad, out,
):
    mine = mid.shape[0]
    own = mine // 2
    sums = [jnp.zeros((1, D), F32) for _ in range(3)]
    for i, (ref, j) in enumerate((ref, j) for ref in (go, gt) for j in range(2)):
        at = pl.ds(i * SLAB, SLAB)
        other = pl.ds((i * SLAB + own) % mine, SLAB)
        e = e2[at, :].astype(F32) + e2_got[other, :].astype(F32)
        unit, inverse = normal(mid[at, :])
        gm = ref[j].astype(F32) + norm_back(e, unit, inverse, vec[:, AT["gain2"]])
        branch = gm.astype(BF)
        branch_ref[at, :] = branch
        if i < 2:
            gm_ref[at, :] = gm
            for n, term in enumerate((e * unit, e, branch.astype(F32))):
                sums[n] = sums[n] + jnp.sum(term, axis=0, keepdims=True)
    e2n_sum[...], e2_sum[...], branch_sum[...] = sums
    d = dots(branch_ref[...], wo[...], 1, 1).astype(BF)
    for i in range(PAIRS):
        d_ref[i] = d[:, i * DOUBLE : (i + 1) * DOUBLE]
    step = 512
    for j in range(pre.shape[1] // step):
        lanes = pl.ds(j * step, step)
        grad[:, lanes] = dots(a[...], pre[:, lanes], 0, 0).astype(BF)
    proj = dots(wide(low), branch_ref[...], 0, 0).astype(BF)
    out[...] = dots(perm[...], proj, 0, 0).astype(BF)
    half = keep_ref.shape[0]
    for r in range(2 * half):
        target, at = (keep_ref if r < half else send_ref), r % half
        rows = pl.ds(pl.multiple_of(inv[r] * 48, 16), 48)
        target[at, :48, :] = grad[rows, :D]
        target[at, 48:96, :] = grad[rows, D:]
        target[at, 96:, :] = out[r * 32 : r * 32 + 32, :]


def attend_back_kernel(
    q, k, v, o, lse, col, row, d_ref, dq_ref, dk_ref, dv_ref, dq_sum, dv_sum, bias, p_low, s_low
):
    mine, keys = q.shape[1], k.shape[1]
    fill_bias(col, row, bias)

    def pair(i, carry):
        both = (d_ref[i].astype(F32) * o[i]).T
        got = []
        for e in range(2):
            delta = jnp.sum(both[e * HEAD_DIM : (e + 1) * HEAD_DIM], axis=0, keepdims=True)
            qm = q[i] * lane_half(e)
            dm = d_ref[i] * lane_half(e)
            base = lse[i, e : e + 1, :]
            for c in range(keys // SLAB):
                at = pl.ds(c * SLAB, SLAB)
                t = dots(k[i, at, :], qm, 1, 1) + bias[at, :]
                p = jnp.exp(t - base)
                dp = dots(v[i, at, :], dm, 1, 1)
                p_low[at, :] = p.astype(BF)
                s_low[at, :] = (p * (dp - delta)).astype(BF)
            got.append(
                (
                    dots(s_low[...], k[i], 0, 0) * 0.125,
                    dot(s_low[...], q[i]),
                    dot(p_low[...], d_ref[i]),
                )
            )
        for n, ref in enumerate((dq_ref, dk_ref, dv_ref)):
            ref[i] = jnp.where(first_half(got[0][n].shape), got[0][n], got[1][n]).astype(BF)
        return carry

    lax.fori_loop(0, PAIRS, pair, 0)
    dq_sum[...] = jnp.sum(wide(dq_ref).astype(F32), axis=0, keepdims=True)
    dv_sum[...] = jnp.sum(wide(dv_ref).astype(F32), axis=0, keepdims=True)


def input_kernel(dq_ref, dk_ref, dv_ref, w, unit, pi, keep_ref, give_ref, e1n_sum, e1_sum):
    keys, own = unit.shape[0], keep_ref.shape[1]
    dq, dk, dv = wide(dq_ref), wide(dk_ref), wide(dv_ref)
    e1n = jnp.zeros((1, D), F32)
    e1s = jnp.zeros((1, D), F32)
    for part in range(keys // own):
        at = slice(part * own, (part + 1) * own)
        e = dots(dk[at], w[1], 1, 1) + dots(dv[at], w[2], 1, 1)
        if part < 2:
            e = e + dots(dq[at], w[0], 1, 1)
        e = dots(e.astype(BF), pi[...], 1, 1)
        e1s = e1s + jnp.sum(e, axis=0, keepdims=True)
        e1n = e1n + jnp.sum(e * unit[pl.ds(part * own, own), :], axis=0, keepdims=True)
        target = keep_ref if part % 2 == 0 else give_ref
        target[part // 2] = e.astype(BF)
    e1n_sum[...] = e1n
    e1_sum[...] = e1s


def near_kernel(keep, got, give):
    give[...] = (keep[1].astype(F32) + got[1].astype(F32)).astype(BF)


def finish_kernel(keep, got, near, x, gm, vec, *parts):
    for i, part in enumerate(parts):
        at = pl.ds(i * SLAB, SLAB)
        e = keep[0, at, :].astype(F32) + got[0, at, :].astype(F32) + near[at, :].astype(F32)
        unit, inverse = normal(x[i, :SLAB, :].astype(F32))
        part[...] = (gm[at, :] + norm_back(e, unit, inverse, vec[:, AT["gain1"]])).astype(BF)


def gather_grads_kernel(inv, a, dq, dk, dv, device, owner, place, *rest):
    sums, (keep_ref, send_ref, grad, small, hot) = rest[:-5], rest[-5:]
    one_hot(place, hot)
    mine = dq.shape[1]
    grad[0] = dots(a[:mine, :], wide(dq), 0, 0).astype(BF)
    grad[1] = dots(a[...], wide(dk), 0, 0).astype(BF)
    grad[2] = dots(a[...], wide(dv), 0, 0).astype(BF)
    line = jnp.concatenate([ref[...] for ref in sums], axis=1)
    kept = jnp.where(device[:, :1] == owner[:1, :], line, 0.0).astype(BF)
    placed = dots(kept, hot[...], 1, 1).astype(BF)
    small[...] = dots(pick_rows(small.shape[0], 16), placed, 0, 0).astype(BF)
    half = keep_ref.shape[0]
    for r in range(2 * half):
        target, at = (keep_ref if r < half else send_ref), r % half
        rows = pl.ds(pl.multiple_of(inv[r] * 48, 16), 48)
        for i in range(3):
            target[at, 48 * i : 48 * i + 48, :] = grad[i, rows, :]
        target[at, 144:160, :] = small[r * 16 : r * 16 + 16, :]


def run(kernel, table, args, outs, scratch, anys=(), us=5, mib=16, alias=None):
    specs = [
        pl.BlockSpec(memory_space=pl.ANY) if i in anys else pl.BlockSpec(memory_space=pltpu.VMEM)
        for i in range(len(args))
    ]
    prefetch = () if table is None else table if isinstance(table, tuple) else (table,)
    return pl.pallas_call(
        kernel,
        grid_spec=pltpu.PrefetchScalarGridSpec(
            num_scalar_prefetch=len(prefetch),
            grid=(),
            in_specs=specs,
            out_specs=[pl.BlockSpec(memory_space=pltpu.VMEM) for _ in outs],
            scratch_shapes=scratch,
        ),
        out_shape=[jax.ShapeDtypeStruct(shape, dtype) for shape, dtype in outs],
        input_output_aliases=alias or {},
        compiler_params=pltpu.CompilerParams(vmem_limit_bytes=mib * 2**20),
        cost_estimate=pl.CostEstimate(
            flops=int(us * 10**9), bytes_accessed=int(us * 10**6), transcendentals=0
        ),
    )(*prefetch, *args)


def body(net, tokens, segments, cotangent, w_qkv, w_out, w_fc1, w_fc2, norm_gains, bias_pack):
    local, cols, width = tokens.shape
    own, mine = local * cols, 2 * local * cols
    keys = 2 * mine
    hidden = FF
    half_w, half_f = width // 2, hidden // 2
    chips, devices = net.chips, 2 * net.chips
    half = chips // 2
    rows, frows = width // devices, hidden // devices
    core = lax.axis_index("c")
    zodd = lax.axis_index("zh") & 1
    def pick(array, parts, which):
        view = array.reshape(*array.shape[:-1], parts, 2, array.shape[-1] // (2 * parts))
        taken = jnp.where(which == 0, view[..., 0, :], view[..., 1, :])
        return taken.reshape(*array.shape[:-1], array.shape[-1] // 2)

    def both(a, b, axis):
        return jnp.where(
            core == 0, jnp.concatenate([a, b], axis=axis), jnp.concatenate([b, a], axis=axis)
        )

    small = jnp.concatenate([norm_gains, bias_pack])
    qkv = w_qkv.reshape(rows, 3, width).swapaxes(0, 1)
    got_qkv, got_small = net.core(pick(qkv, net.x, 1 - core)), net.core(small)
    chip_qkv = both(pick(qkv, net.x, core), got_qkv, 1).reshape(6 * rows, half_w)
    chip_small = jnp.pad(
        both(small[None], got_small[None], 0), ((0, 14), (0, half_w - small.shape[0]))
    )

    def after(value, *others):
        return lax.optimization_barrier((value, *others))[0]

    def all_after(values, *others):
        return lax.optimization_barrier((*values, *others))[: len(values)]

    def grow(held, stage, orders=None, then=()):
        got = net.across(held, stage, orders)
        if then:
            got = after(got, *then)
        return jnp.concatenate([held, got])

    last = net.stages - 1
    q0 = jnp.concatenate([chip_qkv, chip_small])[None]
    q1 = grow(q0, 0)
    spots = after(jnp.arange(chips, dtype=jnp.int32), q0)

    def order_of(orders):
        found = net.table(orders)[None, :] == spots[:, None]
        return jnp.sum(jnp.where(found, spots[None, :], 0), axis=1).astype(jnp.int32)

    inv, inv_d = order_of(net.orders), order_of(net.mixed)

    split = lambda n, parts: np.arange(n).reshape(parts, 2, n // (2 * parts))
    of_core = lambda n, parts: [split(n, parts)[:, c].reshape(-1) for c in range(2)]
    everywhere = lambda n: [np.arange(n)] * 2
    n_gain, n_bias = norm_gains.shape[0], bias_pack.shape[0]

    def owners(items):
        dev, place = [], []
        for c in range(2):
            flat = [(first + entry[c]) for first, entry, _, _ in items]
            dev.append(np.concatenate([f // n for f, (_, _, _, n) in zip(flat, items)]))
            place.append(
                np.concatenate([at + f % n for f, (_, _, at, n) in zip(flat, items)])
            )
        dev, place = np.array(dev, np.int32), np.array(place, np.int32)
        return (
            jnp.where(core == 0, dev[0], dev[1]),
            jnp.where(core == 0, place[0], place[1]),
        )

    chip_row = jnp.repeat(inv, 2)
    s_n = net.z * net.y
    row_device = ((chip_row // s_n) * 2 + jnp.tile(jnp.arange(2), chips)) * s_n + chip_row % s_n
    row_device = jnp.broadcast_to(row_device[:, None], (devices, SLAB))
    D_, W = everywhere(width), width

    def mapping(items):
        dev, place = owners(items)
        return dev[None, :], place[None, :]

    gl, bl = n_gain, n_bias
    heads_c, ff_c = of_core(width, net.x), of_core(hidden, net.x)
    owner_in, place_in = mapping(
        [
            (0, D_, 0, gl),
            (W, D_, 0, gl),
            (0, D_, gl, bl),
            (W, D_, gl, bl),
            (4 * W, D_, gl, bl),
            (5 * W, D_, gl, bl),
            (2 * W, heads_c, gl, bl),
            (3 * W, heads_c, gl, bl),
            (6 * W, ff_c, gl, bl),
        ]
    )
    ll = 2 * W // devices
    rl = n_gain + n_bias - 2 * ll
    owner_out, place_out = mapping(
        [
            (0, D_, 0, ll),
            (W, D_, 0, ll),
            (0, D_, ll, rl),
            (W, heads_c, ll, rl),
            (2 * W, D_, ll, rl),
            (3 * W, D_, ll, rl),
            (4 * W, ff_c, ll, rl),
            (0, D_, ll + rl, ll),
            (W, heads_c, ll + rl, ll),
        ]
    )
    order = np.arange(width).reshape(net.x, 2, s_n, rows).transpose(0, 2, 1, 3).reshape(-1)
    pi = jnp.asarray((np.arange(width)[:, None] == order[None, :]), BF)
    rel_row = jnp.arange(chips * 32, dtype=jnp.int32)
    nat_row = jnp.where(rel_row % 32 < rows, jnp.repeat(inv, 32) * rows + rel_row % 32, -1)
    perm = (jnp.arange(half_w, dtype=jnp.int32)[:, None] == nat_row[None, :]).astype(BF)


    seg_row = jnp.pad(after(segments, q0).astype(BF), ((0, 0), (0, width - cols)))[:, None, :]
    packed = jnp.concatenate([tokens, jnp.pad(seg_row, ((0, 0), (0, 7), (0, 0)))], axis=1)

    def to_sequence(array):
        swapped = jnp.where(zodd == 0, array, array[::-1])
        return jnp.stack(
            [lax.ppermute(swapped[k], AXES, net.scatter_move(k)) for k in range(2)]
        )

    def from_sequence(array, then=()):
        back = [
            lax.ppermute(array[k], AXES, [(b, a) for a, b in net.scatter_move(k)])
            for k in range(2)
        ]
        back = jnp.stack(all_after(back, *then))
        return jnp.where(zodd == 0, back, back[::-1])

    up = after(w_fc1, q0).reshape(rows, hidden)
    got_up = net.core(pick(up, net.x, 1 - core))
    chip_up = fold(both(pick(up, net.x, core), got_up, 0), 2)
    chip_up = jnp.concatenate([chip_up, jnp.pad(w_out.reshape(rows, width), ((0, 8), (0, 0)))])

    u1 = grow(chip_up[None], 0)
    q2 = grow(after(q1, chip_up), 1)
    d1 = grow(after(w_fc2.reshape(1, frows, width), q1), 0, net.mixed)
    q4 = grow(after(q2, u1, d1), 2)
    x_o = to_sequence(after(packed, u1))
    x_n = net.pair(x_o)
    x_m = net.core(x_n)
    x_t = net.core(after(x_o, q4))
    u2 = grow(u1, 1, then=(q4,))
    q_held, q_got = q4, net.across(q4, last)
    d2 = grow(after(d1, u2), 1, net.mixed)
    u4 = grow(after(u2, q4), 2)
    g_out = jnp.where(zodd == 0, cotangent, cotangent[::-1])
    g_out = all_after([g_out[0], g_out[1]], q4)

    dma = lambda *n: pltpu.SemaphoreType.DMA(n)
    vm = lambda shape, dtype: pltpu.VMEM(shape, dtype)
    by_pair = lambda n: (PAIRS, n, DOUBLE)
    unit1, col, row, hot = run(
        unit_kernel,
        None,
        (x_o, x_t, x_n, x_m, place_in),
        (
            ((keys, width), F32),
            ((keys, SLAB), F32),
            ((8, mine), F32),
            ((half_w, place_in.shape[1]), BF),
        ),
        [],
        us=4,
    )
    q_got, unit1, u4, d2 = all_after([q_got, unit1, u4, d2])
    u_held = u4
    u_got = net.across(u4, last)
    a1, q, k, v, w_mix, vec = run(
        mix_kernel,
        inv,
        (unit1, pi, row_device, owner_in, hot, q_held, q_got),
        (
            ((keys, width), BF),
            (by_pair(mine), BF),
            (by_pair(keys), BF),
            (by_pair(keys), BF),
            ((3, width, half_w), BF),
            ((1, place_in.shape[1]), F32),
        ),
        [vm((keys, width), BF), vm((chips * 16, half_w), BF), dma(chips, 3), dma(chips)],
        anys=(5, 6),
        us=8,
    )
    d_got = net.across(d2, 2, net.mixed)
    g_out = all_after(g_out, k)
    g_in = [lax.ppermute(g_out[k], AXES, net.scatter_move(k)) for k in range(2)]
    o, low, lse = run(
        attend_kernel,
        None,
        (q, k, v, col, row),
        ((by_pair(mine), F32), (by_pair(mine), BF), ((PAIRS, 8, mine), F32)),
        [vm((keys, mine), F32), vm((keys, mine), F32), vm((keys, mine), BF)],
        us=12,
    )
    d4 = jnp.concatenate([d2, d_got])
    g_o = jnp.stack(g_in)
    blocks = ((half, 96, width), BF)
    part, wo = run(
        project_kernel,
        inv,
        (all_after([low], d_got, *g_in)[0], perm, u_held, u_got),
        (((mine, width), BF), ((half_w, width), BF)),
        [vm((chips * 32, width), BF), dma(chips)],
        anys=(2, 3),
        us=3,
    )
    part_got = net.core(part)
    g_t = net.core(g_o)
    d_half = d_got
    d_held = jnp.concatenate([d2, d_half])
    d_got = net.across(d_held, last, net.mixed)
    mid, a2, act, fac, w_up, keep_d, send_d, g_sum, w_half = run(
        middle_kernel,
        (inv, inv_d),
        (part, part_got, x_o, x_t, g_o, g_t, vec, pi, u_held, u_got, d_held),
        (
            ((mine, width), F32),
            ((mine, width), BF),
            ((mine, half_f), BF),
            ((mine, half_f), F32),
            ((width, half_f), BF),
            blocks,
            blocks,
            ((1, width), F32),
            ((half_f, width), BF),
        ),
        [vm((mine, width), BF), vm((half_f, width), BF), dma(chips, 2), dma(half)],
        anys=(8, 9, 10),
        us=10,
    )

    def fold_in(keep, got):
        n = keep.shape[0] // 2
        total = [keep[at].astype(F32) + got[at].astype(F32) for at in (slice(n), slice(n, None))]
        return [part.astype(BF) for part in total]

    def shrink(keep, send, stage, orders=None, then=()):
        got = net.across(send, stage, orders)
        if then:
            got = after(got, *then)
        if stage == 0:
            return (keep.astype(F32) + got.astype(F32))[0]
        return fold_in(keep, got)

    pre, e2, w_down, pre_sum = run(
        slope_kernel,
        inv_d,
        (g_o, g_t, fac, w_up, pi, w_half, d_got),
        (
            ((mine, half_f), BF),
            ((mine, width), BF),
            ((half_f, width), BF),
            ((1, half_f), F32),
        ),
        [dma(half)],
        anys=(6,),
        us=8,
        alias={6: 2},
    )
    keep_d, send_d = shrink(keep_d, send_d, 3)
    e2_got = after(net.core(e2), send_d)
    down_own, down_give = run(
        down_kernel,
        None,
        (act, w_down),
        (((own, width), F32), ((own, width), BF)),
        [],
        us=2,
    )
    wide_sum, half_sum = ((1, width), F32), ((1, half_w), F32)
    blocks_u = ((half, 128, width), BF)
    gm, branch, d_heads, keep_u, send_u, e2n, e2s, bs = run(
        branch_kernel,
        inv,
        (e2, e2_got, mid, g_o, g_t, vec, wo, low, perm, a2, pre),
        (
            ((own, width), F32),
            ((mine, width), BF),
            (by_pair(mine), BF),
            blocks_u,
            blocks_u,
            wide_sum,
            wide_sum,
            wide_sum,
        ),
        [vm((width, half_f), BF), vm((chips * 32, width), BF)],
        us=0.1,
    )
    down_got = net.core(after(down_give, e2_got)).astype(F32)
    out_own = (mid[:own] + down_own + down_got + vec[:, AT["bias_down"]]).astype(BF)
    out_own = out_own.reshape(local, cols, width)
    out_parts = [out_own[k] for k in range(2)]
    keep_d, send_d = shrink(keep_d, send_d, 2, then=(send_u,))
    send_d, d_heads, *out_parts = all_after([send_d, d_heads, *out_parts])
    quarter = ((2, own, width), BF)
    blocks_q = ((half, 160, half_w), BF)
    home = lambda k: [(b, a) for a, b in net.scatter_move(k)]
    dq, dk, dv, dqs, dvs = run(
        attend_back_kernel,
        None,
        (q, k, v, o, lse, col, row, d_heads),
        (
            (by_pair(mine), BF),
            (by_pair(keys), BF),
            (by_pair(keys), BF),
            half_sum,
            half_sum,
        ),
        [vm((keys, mine), F32), vm((keys, mine), BF), vm((keys, mine), BF)],
        us=10,
    )
    out_parts = [lax.ppermute(out_parts[k], AXES, home(k)) for k in range(2)]
    out_parts = all_after(out_parts, dq)
    d_1 = shrink(keep_d, send_d, 1, then=(dq,))
    keep_e, give_e, e1n, e1s = run(
        input_kernel,
        None,
        (all_after([dq], d_1[1], *out_parts)[0], dk, dv, w_mix, unit1, pi),
        (quarter, quarter, wide_sum, wide_sum),
        [],
        us=0.1,
    )
    got_e = net.core(give_e)
    (e1_give,) = run(near_kernel, None, (keep_e, got_e), (((own, width), BF),), [], us=0.1)
    u3 = shrink(keep_u, send_u, 3, then=(keep_e,))
    got_d = net.across(d_1[1], 0)
    shard_d = (d_1[0].astype(F32) + got_d.astype(F32))[0]
    keep_q, send_q = run(
        gather_grads_kernel,
        inv,
        (all_after([a1], u3[1], e1_give)[0], dq, dk, dv, row_device, owner_out, place_out)
        + (e1n, e2n, e2s, dqs, bs, g_sum, pre_sum, e1s, dvs),
        (blocks_q, blocks_q),
        [
            vm((3, width, half_w), BF),
            vm((chips * 16, half_w), BF),
            vm((half_w, place_out.shape[1]), BF),
        ],
        us=0.1,
    )
    q_3 = shrink(*all_after([keep_q, send_q], got_d), 3)
    back = jnp.stack(out_parts)
    block_out = jnp.where(zodd == 0, back, back[::-1])
    block = ((cols, width), BF)
    u_2 = shrink(*u3, 2, then=(send_q,))
    e1_near = net.pair(all_after([e1_give], q_3[1])[0])
    u_1 = shrink(*u_2, 1, then=(q_3[1],))
    q_2 = shrink(*q_3, 2)
    in_parts = run(
        finish_kernel,
        None,
        (keep_e, got_e, all_after([e1_near], q_2[1])[0], x_o, gm, vec),
        (block, block),
        [],
        us=0.1,
    )
    in_parts = [lax.ppermute(in_parts[k], AXES, home(k)) for k in range(2)]
    got_last = net.across(u_1[1], 0)
    q_1 = shrink(*all_after(q_2, u_1[1]), 1)
    shard_u = (u_1[0].astype(F32) + all_after([got_last], q_1[1])[0].astype(F32))[0]
    in_parts = all_after(in_parts, q_1[1])
    shard_q = shrink(*q_1, 0)
    back = jnp.stack(in_parts)
    input_grad = jnp.where(zodd == 0, back, back[::-1]).astype(F32)

    def own_rows(chip):
        keep = jnp.where(core == 0, chip[..., 0, :, :], chip[..., 1, :, :])
        give = jnp.where(core == 0, chip[..., 1, :, :], chip[..., 0, :, :])
        return keep, net.core(give)

    def merge(keep, got, parts):
        view = lambda array: array.reshape(*array.shape[:-1], parts, 1, -1)
        first = jnp.where(core == 0, view(keep), view(got))
        second = jnp.where(core == 0, view(got), view(keep))
        return jnp.concatenate([first, second], axis=-2).reshape(*keep.shape[:-1], -1)

    n_sums = 2 * ll + rl
    whole = shard_q[: 6 * rows].reshape(3, 2, rows, half_w)
    two = shard_q[6 * rows : 6 * rows + 2].reshape(2, 1, half_w)
    ours, theirs = (
        jnp.concatenate(
            [jnp.where(core == c, whole[:, 0], whole[:, 1]).reshape(3 * rows, half_w),
             jnp.where(core == c, two[0], two[1])]
        )
        for c in range(2)
    )
    theirs = net.core(theirs)
    keep_s, got_s = ours[3 * rows :, :n_sums], theirs[3 * rows :, :n_sums]
    keep_w, got_w = (v[: 3 * rows].reshape(3, rows, half_w) for v in (ours, theirs))
    qkv_own = merge(keep_w, got_w, net.x)
    g_qkv = jnp.moveaxis(qkv_own, 0, 1).reshape(-1)
    g_out = shard_u[4 * rows : 5 * rows].reshape(-1)
    up_own = merge(*own_rows(unfold(shard_u[: 4 * rows], 2).reshape(2, rows, half_f)), net.x)
    own_sums = (keep_s + got_s)[0]
    return (
        block_out,
        input_grad,
        g_qkv,
        g_out,
        up_own.reshape(-1),
        shard_d.reshape(-1),
        own_sums[:ll],
        own_sums[ll : ll + rl],
        own_sums[ll + rl :],
    )


def solution(mesh):
    dp, seq = mesh.shape["dp"], mesh.shape["seq"]
    y = 1 << (((seq.bit_length() - 1) - 1) // 2)
    z = seq // y
    dims = (dp // 2, 2, 4, z // 4, y // 2, 2)
    net = Net(dims)
    inner = Mesh(mesh.devices.reshape(dims), AXES)
    place = ("zh", "zl", "yh", "yl")
    cube = P(("x", "c"), place, None)
    flat = P(AXES)
    rows = D // (2 * net.chips)
    tiles = rows == 24 and net.chips == 16 and net.zl * net.yh == 1
    return jax.shard_map(
        functools.partial(body if tiles else body_any, net),
        mesh=inner,
        in_specs=(cube, P(("x", "c"), place), cube) + (flat,) * 6,
        out_specs=(cube, cube) + (flat,) * 7,
        check_vma=False,
    )
```
